32 devices in a mesh: dp: 2 (over core), code: 16 (over z, y, x).
Axes of the slice: x: 2, y: 2, z: 4, core: 2. Of those that a mesh axis runs over, the one named last changes fastest.
Arguments:
- tokens: bfloat16 [1024, 256], P('dp'), may hold values from -0.59765625 to 0.59765625
- codebook: bfloat16 [131072, 256], P('code'), may hold values from -3 to 3
- gumbel_perturbation: bfloat16 [1024, 131072], P('dp', 'code'), may hold values from -1 to 120
- grad_out: bfloat16 [1024, 256], P('dp'), may hold values from -1.5 to 1.5
Outputs:
- quantized: float32 [1024, 256], P('dp')
- token_gradient: float32 [1024, 256], P('dp')
- grad_codebook: float32 [16, 8192, 256], P('code', 'dp')
The draws below stay inside these ranges and needn't reach their ends.
All inputs are finite; a program needn't handle non-finite values.
Results may differ from the reference program's by a relative error of at most 0.017.
Values may be sent and summed in bfloat16 or wider, within the bound.
No kernel may reach another device: no remote copies, remote signals or barrier semaphores. Data moves between devices by JAX's collectives and lax.ppermute only.
A program may use at most 128 MiB of HBM per device.

```python
import jax
import jax.numpy as jnp
from jax import lax

D = 256
K = 131072
TOK_DP = 512
TOKENS = 1024
N_DP = 2
N_CODE = 16


def draw_gumbel_perturbation(key, part):
    key = jax.random.fold_in(key, 11)
    uniform = jax.random.uniform(key, (TOKENS, K), jnp.float32, 0.01, 0.99)
    base = -jnp.log(-jnp.log(uniform))
    noise = 0.25 * base
    return noise.astype(jnp.bfloat16)


def steps_of(rng, extent, split, low, largest):
    factor_of = 1.0
    for axis_at, parts in split:
        heights = jax.random.uniform(jax.random.fold_in(jax.random.fold_in(rng, 6), axis_at), (parts,), jnp.float32, low / len(split), largest / len(split))
        factor_of = factor_of * jnp.repeat(jnp.exp(heights), extent[axis_at] // parts).reshape((-1,) + (1,) * (len(extent) - 1 - axis_at))
    return factor_of


def scatter_about(own_key, shape, width, limit, pieces=(), kind=jnp.bfloat16):
    values = jax.random.normal(own_key, shape, jnp.float32) * width
    if len(pieces) > 0:
        values = steps_of(own_key, shape, pieces, -0.22, 0.18) * values
    return jnp.clip(values, min=-limit, max=limit).astype(kind)


def setup_inputs(seed: int = 0) -> dict:
    seeds = jax.random.split(jax.random.key(seed), 5)
    tokens = scatter_about(seeds[0], (TOKENS, D), 0.1, 0.59765625, ((0, 2),))
    codebook = scatter_about(seeds[1], (K, D), 0.5, 3.0, ((0, 16),))
    gumbel_perturbation = draw_gumbel_perturbation(jax.random.fold_in(seeds[4], 71), 0)
    grad_out = scatter_about(seeds[3], (TOKENS, D), 0.25, 1.5, ((0, 2),))
    return dict(tokens=tokens, codebook=codebook, gumbel_perturbation=gumbel_perturbation, grad_out=grad_out)


SOFTMAX_HEAT = 0.5


def reference(tokens, codebook, gumbel_perturbation, grad_out):
    def one_group(running, items):
        tokens_per_group, noise_per_group, group_grad = items
        code_scores = (jnp.dot(tokens_per_group, codebook.T, preferred_element_type=jnp.float32) + noise_per_group.astype(jnp.float32)) / SOFTMAX_HEAT
        row_max = jnp.max(code_scores, axis=1)
        weights = jnp.exp(code_scores - row_max[:, None])
        row_total = jnp.sum(weights, axis=1)
        relaxed_codes = (weights / row_total[:, None]).astype(jnp.bfloat16)
        quantized = jnp.dot(relaxed_codes, codebook, preferred_element_type=jnp.float32)
        relaxed_gradient = jnp.dot(group_grad, codebook.T, preferred_element_type=jnp.float32)
        product = relaxed_codes.astype(jnp.float32) * relaxed_gradient
        weighted_inner_total = jnp.sum(product, axis=1)
        weighted = product.astype(jnp.bfloat16)
        gathered_codes = jnp.dot(weighted, codebook, preferred_element_type=jnp.float32)
        token_gradient = (gathered_codes - weighted_inner_total[:, None] * quantized) / SOFTMAX_HEAT
        score_gradient = (relaxed_codes.astype(jnp.float32) * (relaxed_gradient - weighted_inner_total[:, None]) / SOFTMAX_HEAT).astype(jnp.bfloat16)
        partial_grad = jnp.dot(relaxed_codes.T, group_grad, preferred_element_type=jnp.float32)
        partial_grad = partial_grad + jnp.dot(score_gradient.T, tokens_per_group, preferred_element_type=jnp.float32)
        rounded = lax.optimization_barrier(partial_grad.astype(jnp.bfloat16)).astype(jnp.float32)
        return running + rounded, (quantized, token_gradient)

    items = (tokens.reshape(N_DP, TOK_DP, D), gumbel_perturbation.reshape(N_DP, TOK_DP, K), grad_out.reshape(N_DP, TOK_DP, D))
    summed, outputs = lax.scan(one_group, jnp.zeros((K, D), jnp.float32), items)
    quantized, token_gradient = outputs
    return quantized.reshape(TOKENS, D), token_gradient.reshape(TOKENS, D), summed.reshape(N_CODE, K // N_CODE, D)
```

```python
import jax
import jax.numpy as jnp
from jax import lax
from jax.sharding import PartitionSpec as P

SOFTMAX_HEAT = 0.5
BF16 = jnp.bfloat16
F32 = jnp.float32


def token_code_scores(left, codebook):
    return lax.dot_general(left, codebook, (((1,), (1,)), ((), ())), preferred_element_type=F32)


def over_tokens(left, right):
    return lax.dot_general(left, right, (((0,), (0,)), ((), ())), preferred_element_type=F32)


def swap(value, axis, size, mask):
    return lax.ppermute(value, axis, [(i, i ^ mask) for i in range(size)])


def halving_sum(value, axis, size):
    at = lax.axis_index(axis)
    rows = value.shape[0]
    mask = 1
    while mask < size:
        rows //= 2
        upper = (at // mask) % 2
        keep = lax.dynamic_slice_in_dim(value, upper * rows, rows, 0)
        give = lax.dynamic_slice_in_dim(value, (1 - upper) * rows, rows, 0)
        got = swap(give, axis, size, mask)
        value = (keep.astype(F32) + got.astype(F32)).astype(BF16)
        mask *= 2
    mask = size // 2
    while mask:
        upper = (at // mask) % 2
        got = swap(value, axis, size, mask)
        low = jnp.where(upper == 0, value, got)
        high = jnp.where(upper == 0, got, value)
        value = jnp.concatenate([low, high], axis=0)
        mask //= 2
    return value


def local(n_dp, n_code, tokens, codebook, gumbel_perturbation, grad_out):
    scores = (
        token_code_scores(tokens, codebook) + gumbel_perturbation.astype(F32)
    ) / SOFTMAX_HEAT
    own_max = jnp.max(scores, axis=1)
    weights = jnp.exp(scores - own_max[:, None])
    own_total = jnp.sum(weights, axis=1)
    codes = weights.astype(BF16)
    gradient = token_code_scores(grad_out, codebook)
    product = codes.astype(F32) * gradient
    own_inner = jnp.sum(product, axis=1)

    own = jnp.stack([own_max, own_total, own_inner])
    stats = [own] + [swap(own, "code", n_code, d) for d in range(1, n_code)]
    stats = jnp.stack(stats)
    row_max = jnp.max(stats[:, 0], axis=0)
    shift = jnp.exp(stats[:, 0] - row_max)
    total = jnp.sum(stats[:, 1] * shift, axis=0)
    inner = jnp.sum(stats[:, 2] * shift, axis=0) / total
    scale = (shift[0] / total)[:, None]

    mix = jnp.dot(codes, codebook, preferred_element_type=F32)
    pulled = jnp.dot(product.astype(BF16), codebook, preferred_element_type=F32)
    part = jnp.concatenate(
        [scale * mix, (pulled - inner[:, None] * mix) * (scale / SOFTMAX_HEAT)], axis=1
    ).astype(BF16)
    summed = halving_sum(part, "code", n_code).astype(F32)
    width = tokens.shape[1]
    quantized, token_gradient = summed[:, :width], summed[:, width:]

    score_gradient = (codes.astype(F32) * (gradient - inner[:, None])).astype(BF16)
    group = (
        over_tokens(codes, (scale * grad_out.astype(F32)).astype(BF16))
        + over_tokens(score_gradient, (scale / SOFTMAX_HEAT * tokens.astype(F32)).astype(BF16))
    ).astype(BF16)
    at = lax.axis_index("dp")
    rows = group.shape[0] // n_dp
    own_rows = lax.dynamic_slice_in_dim(group, at * rows, rows, 0).astype(F32)
    for d in range(1, n_dp):
        give = lax.dynamic_slice_in_dim(group, (at ^ d) * rows, rows, 0)
        own_rows = own_rows + swap(give, "dp", n_dp, d).astype(F32)
    return (quantized, token_gradient, own_rows[None])


def solution(mesh):
    n_dp, n_code = mesh.shape["dp"], mesh.shape["code"]

    def call(*args):
        return local(n_dp, n_code, *args)

    in_specs = (P("dp", None), P("code", None), P("dp", "code"), P("dp", None))
    out_specs = (P("dp", None), P("dp", None), P("code", "dp", None))
    return jax.shard_map(call, mesh=mesh, in_specs=in_specs, out_specs=out_specs, check_vma=False)
```

```python
import jax
import jax.numpy as jnp
from jax import lax
from jax.sharding import PartitionSpec as P

SOFTMAX_HEAT = 0.5
BF16 = jnp.bfloat16
F32 = jnp.float32


def token_code_scores(left, codebook):
    return lax.dot_general(left, codebook, (((1,), (1,)), ((), ())), preferred_element_type=F32)


def over_tokens(left, right):
    return lax.dot_general(left, right, (((0,), (0,)), ((), ())), preferred_element_type=F32)


def swap(value, axis, size, mask):
    return lax.ppermute(value, axis, [(i, i ^ mask) for i in range(size)])


def spread(value, axis, size):
    whole = jnp.broadcast_to(value[None], (size,) + value.shape)
    return lax.all_to_all(whole, axis, 0, 0, tiled=True)


def sum_over(value, axis, size):
    rows = value.shape[0] // size
    pieces = lax.all_to_all(
        value.reshape(size, rows, value.shape[1]), axis, 0, 0, tiled=True
    )
    own = jnp.sum(pieces.astype(F32), axis=0).astype(BF16)
    return spread(own, axis, size).reshape(value.shape)


def local(n_dp, n_code, tokens, codebook, gumbel_perturbation, grad_out):
    scores = (
        token_code_scores(tokens, codebook) + gumbel_perturbation.astype(F32)
    ) / SOFTMAX_HEAT
    own_max = jnp.max(scores, axis=1)
    weights = jnp.exp(scores - own_max[:, None])
    own_total = jnp.sum(weights, axis=1)
    codes = weights.astype(BF16)
    gradient = token_code_scores(grad_out, codebook)
    product = codes.astype(F32) * gradient
    own_inner = jnp.sum(product, axis=1)

    own = jnp.stack([own_max, own_total, own_inner])
    stats = spread(own, "code", n_code)
    row_max = jnp.max(stats[:, 0], axis=0)
    shift = jnp.exp(stats[:, 0] - row_max)
    total = jnp.sum(stats[:, 1] * shift, axis=0)
    inner = jnp.sum(stats[:, 2] * shift, axis=0) / total
    scale = (jnp.exp(own_max - row_max) / total)[:, None]

    mix = jnp.dot(codes, codebook, preferred_element_type=F32)
    pulled = jnp.dot(product.astype(BF16), codebook, preferred_element_type=F32)
    part = jnp.concatenate(
        [scale * mix, (pulled - inner[:, None] * mix) * (scale / SOFTMAX_HEAT)], axis=1
    ).astype(BF16)
    summed = sum_over(part, "code", n_code).astype(F32)
    width = tokens.shape[1]
    quantized, token_gradient = summed[:, :width], summed[:, width:]

    score_gradient = (codes.astype(F32) * (gradient - inner[:, None])).astype(BF16)
    group = (
        over_tokens(codes, (scale * grad_out.astype(F32)).astype(BF16))
        + over_tokens(score_gradient, (scale / SOFTMAX_HEAT * tokens.astype(F32)).astype(BF16))
    ).astype(BF16)
    at = lax.axis_index("dp")
    rows = group.shape[0] // n_dp
    own_rows = lax.dynamic_slice_in_dim(group, at * rows, rows, 0).astype(F32)
    for d in range(1, n_dp):
        give = lax.dynamic_slice_in_dim(group, (at ^ d) * rows, rows, 0)
        own_rows = own_rows + swap(give, "dp", n_dp, d).astype(F32)
    return (quantized, token_gradient, own_rows[None])


def solution(mesh):
    n_dp, n_code = mesh.shape["dp"], mesh.shape["code"]

    def call(*args):
        return local(n_dp, n_code, *args)

    in_specs = (P("dp", None), P("code", None), P("dp", "code"), P("dp", None))
    out_specs = (P("dp", None), P("dp", None), P("code", "dp", None))
    return jax.shard_map(call, mesh=mesh, in_specs=in_specs, out_specs=out_specs, check_vma=False)
```

```python
import functools
import math

import jax
import jax.numpy as jnp
from jax import lax
from jax.experimental import pallas as pl
from jax.experimental.pallas import tpu as pltpu
from jax.sharding import PartitionSpec as P

SOFTMAX_HEAT = 0.5
TO_LOG2 = math.log2(math.e) / SOFTMAX_HEAT
BF16 = jnp.bfloat16
F32 = jnp.float32
MIB = 1 << 20
VMEM = pl.BlockSpec(memory_space=pltpu.VMEM)
SMEM = pl.BlockSpec(memory_space=pltpu.SMEM)
ANY = pl.BlockSpec(memory_space=pl.ANY)


def dot(left, right, left_dim=1, right_dim=0):
    return lax.dot_general(
        left, right, (((left_dim,), (right_dim,)), ((), ())), preferred_element_type=F32
    )


def lane_groups(value):
    return [value[:, j : j + 128] for j in range(0, value.shape[1], 128)]


def stat_lanes(n_code):
    return max(8 * n_code, 128)


def high_low(value):
    high = value.astype(BF16).astype(F32)
    return high, (value - high).astype(BF16).astype(F32)


def forward_kernel(
    n_code, tokens, grad_out, codebook, noise, codes, sent,
    book, noise_in, scores, top, total, mix, pulled, book_sem, noise_sem,
):
    tiles, n_tokens, width = codes.shape
    dim = tokens.shape[1]

    def fetch(t):
        at = pl.multiple_of(t * width, width)
        return (
            pltpu.make_async_copy(codebook.at[pl.ds(at, width)], book.at[t], book_sem.at[t]),
            pltpu.make_async_copy(noise.at[:, pl.ds(at, width)], noise_in.at[t], noise_sem.at[t]),
        )

    for t in range(tiles):
        for copy in fetch(t):
            copy.start()
    top[...] = jnp.full(top.shape, -jnp.inf, F32)

    def score(t, carry):
        for copy in fetch(t):
            copy.wait()
        value = (dot(tokens[...], book[t], 1, 1) + noise_in[t].astype(F32)) * TO_LOG2
        scores[t] = value
        top[...] = functools.reduce(jnp.maximum, lane_groups(value), top[...])
        return carry

    lax.fori_loop(0, tiles, score, 0)
    shift = jnp.max(top[...], axis=1, keepdims=True).astype(BF16).astype(F32)
    top[...] = jnp.broadcast_to(shift, top.shape)
    total[...] = jnp.zeros(total.shape, F32)
    mix[...] = jnp.zeros(mix.shape, F32)
    pulled[...] = jnp.zeros(pulled.shape, F32)

    def soften(t, carry):
        shifts = jnp.concatenate([top[...]] * (width // 128), axis=1)
        weight = jnp.exp2(scores[t] - shifts)
        code = weight.astype(BF16)
        codes[t] = code
        total[...] += sum(lane_groups(weight))
        gradient = dot(grad_out[...], book[t], 1, 1)
        weighted = (weight * gradient).astype(BF16)
        mix[...] += dot(code, book[t])
        pulled[...] += dot(weighted, book[t])
        return carry

    lax.fori_loop(0, tiles, soften, 0)
    own_total = jnp.sum(total[...], axis=1, keepdims=True)
    own_inner = jnp.sum(grad_out[...].astype(F32) * mix[...], axis=1, keepdims=True)
    mean = own_inner / own_total
    rows = n_tokens // n_code
    lanes = stat_lanes(n_code)
    half = lanes // 2
    lane = lax.broadcasted_iota(jnp.int32, (rows, lanes), 1)
    stats = jnp.zeros((rows, lanes), F32)
    columns = high_low(own_total) + high_low(own_inner)
    for g in range(n_code):
        part = slice(g * rows, (g + 1) * rows)
        for i, column in enumerate(columns):
            stats = jnp.where(lane == 4 * g + i, column[part], stats)
        stats = jnp.where((lane - half) // 4 == g, shift[part], stats)
    stats = stats.astype(BF16)
    for g in range(n_code):
        part = slice(g * rows, (g + 1) * rows)
        sent[g, :, :dim] = mix[part].astype(BF16)
        sent[g, :, dim : 2 * dim] = (pulled[part] - mean[part] * mix[part]).astype(BF16)
        sent[g, :, 2 * dim :] = stats


def roll_left(value, by):
    return pltpu.roll(value, value.shape[1] - by, 1)


def merged_stats(received):
    n_code = received.shape[0]
    lanes = stat_lanes(n_code)
    stats = [received[p, :, received.shape[2] - lanes :].astype(F32) for p in range(n_code)]
    top = functools.reduce(jnp.maximum, stats)
    scales = [roll_left(jnp.exp2(s - top), lanes // 2) for s in stats]
    pairs = [s + roll_left(s, 1) for s in stats]
    inners = [roll_left(s, 2) for s in pairs]
    total = sum(a * s for a, s in zip(scales, pairs))
    inner = sum(a * s for a, s in zip(scales, inners)) / total
    means = [i / s for i, s in zip(inners, pairs)]
    return [a / total for a in scales], means, inner


def merge_kernel(me, received, spread):
    n_code, rows, _ = received.shape
    dim = spread.shape[2] // 2
    scales, means, inner = merged_stats(received)
    lane = lax.broadcasted_iota(jnp.int32, inner.shape, 1)
    mine = lane == 4 * me[0]

    def column(value):
        return jnp.sum(jnp.where(mine, value, 0.0), axis=1, keepdims=True)

    quantized = jnp.zeros((rows, dim), F32)
    gradient = jnp.zeros((rows, dim), F32)
    for p in range(n_code):
        scale = column(scales[p])
        offset = column(scales[p] * (means[p] - inner))
        mix = received[p, :, :dim].astype(F32)
        quantized += scale * mix
        gradient += scale * received[p, :, dim : 2 * dim].astype(F32) + offset * mix
    quantized = quantized.astype(BF16)
    gradient = (gradient / SOFTMAX_HEAT).astype(BF16)
    for p in range(n_code):
        spread[p, :, :dim] = quantized
        spread[p, :, dim:] = gradient


def backward_kernel(
    add, where, tokens, grad_out, codebook, codes, received, *rest
):
    if add:
        other, out, book, result, upper, lower, inner_in, book_sem, out_sem = rest
    else:
        out, book, result, upper, lower, inner_in, book_sem = rest
    tiles = book.shape[0]
    n_code, rows, _ = received.shape
    n_tokens, dim = tokens.shape
    width = book.shape[1]
    first = where[1] * tiles

    def fetch(t):
        at = pl.multiple_of((first + t) * width, width)
        return pltpu.make_async_copy(codebook.at[pl.ds(at, width)], book.at[t], book_sem.at[t])

    for t in range(tiles):
        fetch(t).start()

    scales, _, inner = merged_stats(received)
    scale = jnp.zeros(inner.shape, F32)
    for p in range(n_code):
        scale = jnp.where(where[0] == p, scales[p], scale)
    for g in range(n_code):
        part = slice(g * rows, (g + 1) * rows)
        column = scale[:, 4 * g : 4 * g + 1]
        upper[part] = column * grad_out[part].astype(F32)
        lower[part] = column * (tokens[part].astype(F32) / SOFTMAX_HEAT)
        inner_in[part] = jnp.broadcast_to(inner[:, 4 * g : 4 * g + 1], (rows, 128))
    left = upper[...].T.astype(BF16)
    right = lower[...].T.astype(BF16)

    def send(t):
        return pltpu.make_async_copy(
            result.at[t % 2], out.at[pl.ds(pl.multiple_of(t * width, width), width)],
            out_sem.at[t % 2],
        )

    def block(t, carry):
        fetch(t).wait()
        gradient = dot(grad_out[...], book[t], 1, 1)
        code = codes[first + t]
        inners = jnp.concatenate([inner_in[...]] * (width // 128), axis=1)
        score_gradient = (code.astype(F32) * (gradient - inners)).astype(BF16)
        value = dot(left, code) + dot(right, score_gradient)
        value = value.astype(BF16).T
        at = pl.ds(pl.multiple_of(t * width, width), width)
        if add:
            @pl.when(t >= 2)
            def _():
                send(t - 2).wait()
            result[t % 2] = value.astype(F32) + other[at].astype(F32)
            send(t).start()
        else:
            out[at] = value
        return carry

    lax.fori_loop(0, tiles, block, 0)
    if add:
        for t in range(max(tiles - 2, 0), tiles):
            send(t).wait()


def swap(value, axis, size, mask):
    return lax.ppermute(value, axis, [(i, i ^ mask) for i in range(size)])


def local(n_dp, n_code, tokens, codebook, noise, grad_out):
    n_tokens, dim = tokens.shape
    n_codes = codebook.shape[0]
    rows = n_tokens // n_code
    block = n_codes // n_dp
    width = min(1024, block)
    tiles = n_codes // width
    lanes = stat_lanes(n_code)
    products = 2 * n_tokens * n_codes * dim

    codes, sent = pl.pallas_call(
        functools.partial(forward_kernel, n_code),
        out_shape=(
            pltpu.VMEM((tiles, n_tokens, width), BF16),
            jax.ShapeDtypeStruct((n_code, rows, 2 * dim + lanes), BF16),
        ),
        in_specs=[VMEM, VMEM, ANY, ANY],
        out_specs=(VMEM, VMEM),
        scratch_shapes=[
            pltpu.VMEM((tiles, width, dim), BF16),
            pltpu.VMEM((tiles, n_tokens, width), BF16),
            pltpu.VMEM((tiles, n_tokens, width), F32),
            pltpu.VMEM((n_tokens, 128), F32),
            pltpu.VMEM((n_tokens, 128), F32),
            pltpu.VMEM((n_tokens, dim), F32),
            pltpu.VMEM((n_tokens, dim), F32),
            pltpu.SemaphoreType.DMA((tiles,)),
            pltpu.SemaphoreType.DMA((tiles,)),
        ],
        compiler_params=pltpu.CompilerParams(vmem_limit_bytes=46 * MIB),
        cost_estimate=pl.CostEstimate(
            flops=4 * products, bytes_accessed=16 * MIB, transcendentals=n_tokens * n_codes
        ),
        name="forward",
    )(tokens, grad_out, codebook, noise)

    received = lax.all_to_all(sent, "code", 0, 0, tiled=True)
    code_at = lax.axis_index("code")
    spread = pl.pallas_call(
        merge_kernel,
        out_shape=jax.ShapeDtypeStruct((n_code, rows, 2 * dim), BF16),
        in_specs=[SMEM, VMEM],
        out_specs=VMEM,
        name="merge",
    )(code_at[None], received)
    gathered = lax.all_to_all(spread, "code", 0, 0, tiled=True)
    gathered = gathered.reshape(n_tokens, 2 * dim).astype(F32)
    quantized, token_gradient = gathered[:, :dim], gathered[:, dim:]

    def backward(at, other=None):
        add = other is not None
        scratch = [
            pltpu.VMEM((block // width, width, dim), BF16),
            pltpu.VMEM((2, width, dim), F32),
            pltpu.VMEM((n_tokens, dim), F32),
            pltpu.VMEM((n_tokens, dim), F32),
            pltpu.VMEM((n_tokens, 128), F32),
            pltpu.SemaphoreType.DMA((block // width,)),
        ]
        extra = (other,) if add else ()
        return pl.pallas_call(
            functools.partial(backward_kernel, add),
            out_shape=jax.ShapeDtypeStruct((block, dim), F32 if add else BF16),
            in_specs=[SMEM, VMEM, VMEM, ANY, VMEM, VMEM] + [VMEM] * add,
            out_specs=ANY if add else VMEM,
            scratch_shapes=scratch + [pltpu.SemaphoreType.DMA((2,))] * add,
            compiler_params=pltpu.CompilerParams(vmem_limit_bytes=36 * MIB),
            cost_estimate=pl.CostEstimate(
                flops=3 * products // n_dp, bytes_accessed=16 * MIB // n_dp, transcendentals=0
            ),
            name="backward",
        )(jnp.stack([code_at, at]), tokens, grad_out, codebook, codes, received, *extra)

    dp_at = lax.axis_index("dp")
    other = None
    for d in range(1, n_dp):
        got = swap(backward(dp_at ^ d), "dp", n_dp, d)
        other = got if other is None else other.astype(F32) + got.astype(F32)
    return quantized, token_gradient, backward(dp_at, other)[None]


def solution(mesh):
    n_dp, n_code = mesh.shape["dp"], mesh.shape["code"]
    in_specs = (P("dp", None), P("code", None), P("dp", "code"), P("dp", None))
    out_specs = (P("dp", None), P("dp", None), P("code", "dp", None))
    return jax.shard_map(
        functools.partial(local, n_dp, n_code),
        mesh=mesh, in_specs=in_specs, out_specs=out_specs, check_vma=False,
    )
```

```python
import functools
import math

import jax
import jax.numpy as jnp
from jax import lax
from jax.experimental import pallas as pl
from jax.experimental.pallas import tpu as pltpu
from jax.sharding import PartitionSpec as P

SOFTMAX_HEAT = 0.5
TO_LOG2 = math.log2(math.e) / SOFTMAX_HEAT
BF16 = jnp.bfloat16
F32 = jnp.float32
MIB = 1 << 20
CHUNK = 256
AHEAD = 3
VMEM = pl.BlockSpec(memory_space=pltpu.VMEM)
SMEM = pl.BlockSpec(memory_space=pltpu.SMEM)
ANY = pl.BlockSpec(memory_space=pl.ANY)


def dot(left, right, left_dim=1, right_dim=0):
    return lax.dot_general(
        left, right, (((left_dim,), (right_dim,)), ((), ())), preferred_element_type=F32
    )


def lane_groups(value):
    return [value[:, j : j + 128] for j in range(0, value.shape[1], 128)]


def stat_lanes(n_code):
    return max(8 * n_code, 128)


def high_low(value):
    high = value.astype(BF16).astype(F32)
    return high, (value - high).astype(BF16).astype(F32)


def forward_kernel(
    n_code, tokens, grad_out, codebook, noise, codes, sent,
    book, noise_in, scores, gradients, code_slots, weighted_slots, top, total, mix, pulled,
    book_sem, noise_sem,
):
    tiles, n_tokens, width = codes.shape
    dim = tokens.shape[1]
    columns = [slice(c, c + CHUNK) for c in range(0, width, CHUNK)]

    def fetch(t):
        at = pl.multiple_of(t * width, width)
        return (
            pltpu.make_async_copy(codebook.at[pl.ds(at, width)], book.at[t], book_sem.at[t]),
            pltpu.make_async_copy(noise.at[:, pl.ds(at, width)], noise_in.at[t], noise_sem.at[t]),
        )

    def start(t):
        for copy in fetch(t):
            copy.start()

    for t in range(min(AHEAD, tiles)):
        start(t)
    top[...] = jnp.full(top.shape, -jnp.inf, F32)

    def score(t):
        for copy in fetch(t):
            copy.wait()

        @pl.when(t + AHEAD < tiles)
        def _():
            start(t + AHEAD)

        for c in columns:
            keys = book[t, c]
            value = (dot(tokens[...], keys, 1, 1) + noise_in[t, :, c].astype(F32)) * TO_LOG2
            scores[t, :, c] = value
            top[...] = functools.reduce(jnp.maximum, lane_groups(value), top[...])
            gradients[t, :, c] = dot(grad_out[...], keys, 1, 1)

    def score_pair(i, carry):
        score(2 * i)
        score(2 * i + 1)
        return carry

    lax.fori_loop(0, tiles // 2, score_pair, 0)
    shift = jnp.max(top[...], axis=1, keepdims=True).astype(BF16).astype(F32)
    top[...] = jnp.broadcast_to(shift, top.shape)
    total[...] = jnp.zeros(total.shape, F32)
    mix[...] = jnp.zeros(mix.shape, F32)
    pulled[...] = jnp.zeros(pulled.shape, F32)

    def store(t):
        return pltpu.make_async_copy(noise_in.at[t], codes.at[t], noise_sem.at[t])

    def soften(t, slot):
        for c in columns:
            shifts = jnp.concatenate([top[...]] * (CHUNK // 128), axis=1)
            weight = jnp.exp2(scores[t, :, c] - shifts)
            total[...] += sum(lane_groups(weight))
            code = weight.astype(BF16)
            code_slots[slot, :, c] = code
            noise_in[t, :, c] = code
            weighted_slots[slot, :, c] = (weight * gradients[t, :, c]).astype(BF16)
        store(t).start()

    def accumulate(t, slot):
        mix[...] += dot(code_slots[slot], book[t])
        pulled[...] += dot(weighted_slots[slot], book[t])

    def soften_pair(i, carry):
        soften(2 * i + 1, 1)
        accumulate(2 * i, 0)
        soften(2 * i + 2, 0)
        accumulate(2 * i + 1, 1)
        return carry

    soften(0, 0)
    lax.fori_loop(0, tiles // 2 - 1, soften_pair, 0)
    soften(tiles - 1, 1)
    accumulate(tiles - 2, 0)
    accumulate(tiles - 1, 1)

    own_total = jnp.sum(total[...], axis=1, keepdims=True)
    own_inner = jnp.sum(grad_out[...].astype(F32) * mix[...], axis=1, keepdims=True)
    mean = own_inner / own_total
    rows = n_tokens // n_code
    lanes = stat_lanes(n_code)
    half = lanes // 2
    lane = lax.broadcasted_iota(jnp.int32, (rows, lanes), 1)
    stats = jnp.zeros((rows, lanes), F32)
    parts = high_low(own_total) + high_low(own_inner)
    for g in range(n_code):
        at = slice(g * rows, (g + 1) * rows)
        for i, part in enumerate(parts):
            stats = jnp.where(lane == 4 * g + i, part[at], stats)
        stats = jnp.where((lane - half) // 4 == g, shift[at], stats)
    stats = stats.astype(BF16)
    for g in range(n_code):
        at = slice(g * rows, (g + 1) * rows)
        sent[g, :, :dim] = mix[at].astype(BF16)
        sent[g, :, dim : 2 * dim] = (pulled[at] - mean[at] * mix[at]).astype(BF16)
        sent[g, :, 2 * dim :] = stats
    for t in range(tiles):
        store(t).wait()


def roll_left(value, by):
    return pltpu.roll(value, value.shape[1] - by, 1)


def merged_stats(received):
    n_code = received.shape[0]
    lanes = stat_lanes(n_code)
    stats = [received[p, :, received.shape[2] - lanes :].astype(F32) for p in range(n_code)]
    top = functools.reduce(jnp.maximum, stats)
    scales = [roll_left(jnp.exp2(s - top), lanes // 2) for s in stats]
    pairs = [s + roll_left(s, 1) for s in stats]
    inners = [roll_left(s, 2) for s in pairs]
    total = sum(a * s for a, s in zip(scales, pairs))
    inner = sum(a * s for a, s in zip(scales, inners)) / total
    means = [i / s for i, s in zip(inners, pairs)]
    return [a / total for a in scales], means, inner


def merge_kernel(me, received, spread):
    n_code, rows, _ = received.shape
    dim = spread.shape[2] // 2
    scales, means, inner = merged_stats(received)
    lane = lax.broadcasted_iota(jnp.int32, inner.shape, 1)
    mine = lane == 4 * me[0]

    def column(value):
        return jnp.sum(jnp.where(mine, value, 0.0), axis=1, keepdims=True)

    quantized = jnp.zeros((rows, dim), F32)
    gradient = jnp.zeros((rows, dim), F32)
    for p in range(n_code):
        scale = column(scales[p])
        offset = column(scales[p] * (means[p] - inner))
        mix = received[p, :, :dim].astype(F32)
        quantized += scale * mix
        gradient += scale * received[p, :, dim : 2 * dim].astype(F32) + offset * mix
    quantized = quantized.astype(BF16)
    gradient = (gradient / SOFTMAX_HEAT).astype(BF16)
    for p in range(n_code):
        spread[p, :, :dim] = quantized
        spread[p, :, dim:] = gradient


def backward_kernel(add, where, tokens, grad_out, codebook, codes, received, *rest):
    if add:
        other, out, book, code_in, upper, lower, inner_in, book_sem, code_sem, result, out_sem = rest
    else:
        out, book, code_in, upper, lower, inner_in, book_sem, code_sem = rest
    tiles, width, dim = book.shape
    n_code, rows, _ = received.shape
    first = where[1] * tiles

    def fetch(t):
        at = pl.multiple_of((first + t) * width, width)
        return (
            pltpu.make_async_copy(codebook.at[pl.ds(at, width)], book.at[t], book_sem.at[t]),
            pltpu.make_async_copy(codes.at[first + t], code_in.at[t], code_sem.at[t]),
        )

    for t in range(tiles):
        for copy in fetch(t):
            copy.start()

    scales, _, inner = merged_stats(received)
    scale = jnp.zeros(inner.shape, F32)
    for p in range(n_code):
        scale = jnp.where(where[0] == p, scales[p], scale)
    for g in range(n_code):
        part = slice(g * rows, (g + 1) * rows)
        column = scale[:, 4 * g : 4 * g + 1]
        upper[part] = column * grad_out[part].astype(F32)
        lower[part] = column * (tokens[part].astype(F32) / SOFTMAX_HEAT)
        inner_in[part] = jnp.broadcast_to(inner[:, 4 * g : 4 * g + 1], (rows, 128))
    left = upper[...].T.astype(BF16)
    right = lower[...].T.astype(BF16)

    def send(t):
        return pltpu.make_async_copy(
            result.at[t], out.at[pl.ds(pl.multiple_of(t * width, width), width)], out_sem.at[t]
        )

    def block(t, carry):
        for copy in fetch(t):
            copy.wait()
        for c in range(0, width, CHUNK):
            gradient = dot(grad_out[...], book[t, c : c + CHUNK], 1, 1)
            code = code_in[t, :, c : c + CHUNK]
            inners = jnp.concatenate([inner_in[...]] * (CHUNK // 128), axis=1)
            score_gradient = (code.astype(F32) * (gradient - inners)).astype(BF16)
            value = (dot(left, code) + dot(right, score_gradient)).astype(BF16).T
            at = pl.ds(pl.multiple_of(t * width + c, CHUNK), CHUNK)
            if add:
                result[t, c : c + CHUNK] = value.astype(F32) + other[at].astype(F32)
            else:
                out[at] = value
        if add:
            send(t).start()
        return carry

    lax.fori_loop(0, tiles, block, 0)
    if add:
        for t in range(tiles):
            send(t).wait()


def unpack_kernel(gathered, quantized, gradient):
    n_code, rows, both = gathered.shape
    dim = both // 2
    for g in range(n_code):
        at = slice(g * rows, (g + 1) * rows)
        quantized[at] = gathered[g, :, :dim].astype(F32)
        gradient[at] = gathered[g, :, dim:].astype(F32)


def swap(value, axis, size, mask):
    return lax.ppermute(value, axis, [(i, i ^ mask) for i in range(size)])


def local(n_dp, n_code, tokens, codebook, noise, grad_out):
    n_tokens, dim = tokens.shape
    n_codes = codebook.shape[0]
    rows = n_tokens // n_code
    block = n_codes // n_dp
    width = min(1024, block)
    tiles = n_codes // width
    lanes = stat_lanes(n_code)
    products = 2 * n_tokens * n_codes * dim

    codes, sent = pl.pallas_call(
        functools.partial(forward_kernel, n_code),
        out_shape=(
            pltpu.HBM((tiles, n_tokens, width), BF16),
            jax.ShapeDtypeStruct((n_code, rows, 2 * dim + lanes), BF16),
        ),
        in_specs=[VMEM, VMEM, ANY, ANY],
        out_specs=(ANY, VMEM),
        scratch_shapes=[
            pltpu.VMEM((tiles, width, dim), BF16),
            pltpu.VMEM((tiles, n_tokens, width), BF16),
            pltpu.VMEM((tiles, n_tokens, width), F32),
            pltpu.VMEM((tiles, n_tokens, width), F32),
            pltpu.VMEM((2, n_tokens, width), BF16),
            pltpu.VMEM((2, n_tokens, width), BF16),
            pltpu.VMEM((n_tokens, 128), F32),
            pltpu.VMEM((n_tokens, 128), F32),
            pltpu.VMEM((n_tokens, dim), F32),
            pltpu.VMEM((n_tokens, dim), F32),
            pltpu.SemaphoreType.DMA((tiles,)),
            pltpu.SemaphoreType.DMA((tiles,)),
        ],
        compiler_params=pltpu.CompilerParams(vmem_limit_bytes=60 * MIB),
        cost_estimate=pl.CostEstimate(
            flops=4 * products, bytes_accessed=24 * MIB, transcendentals=n_tokens * n_codes
        ),
        name="forward",
    )(tokens, grad_out, codebook, noise)

    received = lax.all_to_all(sent, "code", 0, 0, tiled=True)
    code_at = lax.axis_index("code")
    spread = pl.pallas_call(
        merge_kernel,
        out_shape=jax.ShapeDtypeStruct((n_code, rows, 2 * dim), BF16),
        in_specs=[SMEM, VMEM],
        out_specs=VMEM,
        name="merge",
    )(code_at[None], received)
    received, spread = lax.optimization_barrier((received, spread))
    gathered = lax.all_to_all(spread, "code", 0, 0, tiled=True)
    quantized, token_gradient = pl.pallas_call(
        unpack_kernel,
        out_shape=(jax.ShapeDtypeStruct((n_tokens, dim), F32),) * 2,
        in_specs=[VMEM],
        out_specs=(VMEM, VMEM),
        name="unpack",
    )(gathered)

    def backward(at, other=None):
        add = other is not None
        scratch = [
            pltpu.VMEM((block // width, width, dim), BF16),
            pltpu.VMEM((block // width, n_tokens, width), BF16),
            pltpu.VMEM((n_tokens, dim), F32),
            pltpu.VMEM((n_tokens, dim), F32),
            pltpu.VMEM((n_tokens, 128), F32),
            pltpu.SemaphoreType.DMA((block // width,)),
            pltpu.SemaphoreType.DMA((block // width,)),
        ]
        if add:
            scratch += [
                pltpu.VMEM((block // width, width, dim), F32),
                pltpu.SemaphoreType.DMA((block // width,)),
            ]
        extra = (other,) if add else ()
        return pl.pallas_call(
            functools.partial(backward_kernel, add),
            out_shape=jax.ShapeDtypeStruct((block, dim), F32 if add else BF16),
            in_specs=[SMEM, VMEM, VMEM, ANY, ANY, VMEM] + [VMEM] * add,
            out_specs=ANY if add else VMEM,
            scratch_shapes=scratch,
            compiler_params=pltpu.CompilerParams(vmem_limit_bytes=60 * MIB),
            cost_estimate=pl.CostEstimate(
                flops=3 * products // n_dp, bytes_accessed=16 * MIB // n_dp, transcendentals=0
            ),
            name="backward",
        )(jnp.stack([code_at, at]), tokens, grad_out, codebook, codes, received, *extra)

    dp_at = lax.axis_index("dp")
    other = None
    for d in range(1, n_dp):
        got = swap(backward(dp_at ^ d), "dp", n_dp, d)
        other = got if other is None else other.astype(F32) + got.astype(F32)
    return quantized, token_gradient, backward(dp_at, other)[None]


def solution(mesh):
    n_dp, n_code = mesh.shape["dp"], mesh.shape["code"]
    in_specs = (P("dp", None), P("code", None), P("dp", "code"), P("dp", None))
    out_specs = (P("dp", None), P("dp", None), P("code", "dp", None))
    return jax.shard_map(
        functools.partial(local, n_dp, n_code),
        mesh=mesh, in_specs=in_specs, out_specs=out_specs, check_vma=False,
    )
```

```python
import functools
import math

import jax
import jax.numpy as jnp
from jax import lax
from jax.experimental import pallas as pl
from jax.experimental.pallas import tpu as pltpu
from jax.sharding import PartitionSpec as P

SOFTMAX_HEAT = 0.5
TO_LOG2 = math.log2(math.e) / SOFTMAX_HEAT
BF16 = jnp.bfloat16
F32 = jnp.float32
MIB = 1 << 20
CHUNK = 256
AHEAD = 3
ROWS = 64
LARGEST = 2.0**60
VMEM = pl.BlockSpec(memory_space=pltpu.VMEM)
SMEM = pl.BlockSpec(memory_space=pltpu.SMEM)
ANY = pl.BlockSpec(memory_space=pl.ANY)


def dot(left, right, left_dim=1, right_dim=0):
    return lax.dot_general(
        left, right, (((left_dim,), (right_dim,)), ((), ())), preferred_element_type=F32
    )


def lane_groups(value):
    return [value[:, j : j + 128] for j in range(0, value.shape[1], 128)]


def stat_lanes(n_code):
    return max(8 * n_code, 128)


def high_low(value):
    high = value.astype(BF16).astype(F32)
    return high, (value - high).astype(BF16).astype(F32)


def forward_kernel(
    n_code, tokens, grad_out, codebook, noise, codes, sent,
    pair, book, noise_in, slot_a, slot_b, shifts, total, sums, book_sem, noise_sem, code_sem,
):
    tiles, n_tokens, width = codes.shape
    dim = tokens.shape[1]
    columns = [slice(c, c + CHUNK) for c in range(0, width, CHUNK)]
    slots = (slot_a, slot_b)

    def fetch(t):
        at = pl.multiple_of(t * width, width)
        return (
            pltpu.make_async_copy(codebook.at[pl.ds(at, width)], book.at[t], book_sem.at[t]),
            pltpu.make_async_copy(noise.at[:, pl.ds(at, width)], noise_in.at[t], noise_sem.at[t]),
        )

    def start(t):
        for copy in fetch(t):
            copy.start()

    def arrive(t):
        for copy in fetch(t):
            copy.wait()

    for t in range(min(AHEAD + 1, tiles)):
        start(t)
    for r in range(0, n_tokens, ROWS):
        pair[2 * r : 2 * r + ROWS] = tokens[r : r + ROWS]
        pair[2 * r + ROWS : 2 * r + 2 * ROWS] = grad_out[r : r + ROWS]

    def raise_shift(t, some):
        for c in some:
            value = (dot(tokens[...], book[t, c], 1, 1) + noise_in[t, :, c].astype(F32)) * TO_LOG2
            shifts[...] = functools.reduce(jnp.maximum, lane_groups(value), shifts[...])

    def store(t, s):
        return pltpu.make_async_copy(
            slots[s].at[pl.ds(0, n_tokens)], codes.at[t], code_sem.at[s]
        )

    def soften(t, s, fresh):
        if fresh is not None:
            @pl.when(fresh)
            def _():
                arrive(t)

                @pl.when(t + AHEAD < tiles)
                def _():
                    start(t + AHEAD)

        slot = slots[s]
        for c in columns:
            both = dot(pair[...], book[t, c], 1, 1)
            for r in range(0, n_tokens, ROWS):
                at = slice(r, r + ROWS)
                score = both[2 * r : 2 * r + ROWS] + noise_in[t, at, c].astype(F32)
                shift = jnp.concatenate([shifts[at]] * (CHUNK // 128), axis=1)
                weight = jnp.exp2(score * TO_LOG2 - shift)
                total[at] += sum(lane_groups(weight))
                slot[at, c] = weight.astype(BF16)
                gradient = both[2 * r + ROWS : 2 * r + 2 * ROWS]
                slot[n_tokens + r : n_tokens + r + ROWS, c] = (weight * gradient).astype(BF16)
        store(t, s).start()

    def accumulate(t, s):
        sums[...] += dot(slots[s][...], book[t])

    def attempt(state):
        again, _ = state
        fresh = again == 0
        shifts[...] = jnp.full(shifts.shape, -jnp.inf, F32)

        @pl.when(fresh)
        def _():
            raise_shift(0, columns[:2])

        @pl.when(jnp.logical_not(fresh))
        def _():
            def over(t, carry):
                raise_shift(t, columns)
                return carry

            lax.fori_loop(0, tiles, over, 0)

        shift = jnp.max(shifts[...], axis=1, keepdims=True).astype(BF16).astype(F32)
        shifts[...] = jnp.broadcast_to(shift, shifts.shape)
        total[...] = jnp.zeros(total.shape, F32)
        sums[...] = jnp.zeros(sums.shape, F32)
        soften(0, 0, None)

        def soften_pair(i, carry):
            @pl.when(i > 0)
            def _():
                store(2 * i - 1, 1).wait()

            soften(2 * i + 1, 1, fresh)
            accumulate(2 * i, 0)
            store(2 * i, 0).wait()
            soften(2 * i + 2, 0, fresh)
            accumulate(2 * i + 1, 1)
            return carry

        lax.fori_loop(0, tiles // 2 - 1, soften_pair, 0)
        if tiles > 2:
            store(tiles - 3, 1).wait()
        soften(tiles - 1, 1, fresh)
        accumulate(tiles - 2, 0)
        accumulate(tiles - 1, 1)
        store(tiles - 2, 0).wait()
        store(tiles - 1, 1).wait()
        fits = jnp.max(total[...]) < LARGEST
        return again + 1, jnp.logical_and(fresh, jnp.logical_not(fits))

    arrive(0)
    lax.while_loop(lambda state: state[1], attempt, (jnp.int32(0), jnp.bool_(True)))

    shift = shifts[:, :1]
    mix = sums[:n_tokens]
    pulled = sums[n_tokens:]
    own_total = jnp.sum(total[...], axis=1, keepdims=True)
    own_inner = jnp.sum(grad_out[...].astype(F32) * mix, axis=1, keepdims=True)
    mean = own_inner / own_total
    rows = n_tokens // n_code
    lanes = stat_lanes(n_code)
    half = lanes // 2
    lane = lax.broadcasted_iota(jnp.int32, (rows, lanes), 1)
    stats = jnp.zeros((rows, lanes), F32)
    parts = high_low(own_total) + high_low(own_inner)
    for g in range(n_code):
        at = slice(g * rows, (g + 1) * rows)
        for i, part in enumerate(parts):
            stats = jnp.where(lane == 4 * g + i, part[at], stats)
        stats = jnp.where((lane - half) // 4 == g, shift[at], stats)
    stats = stats.astype(BF16)
    for g in range(n_code):
        at = slice(g * rows, (g + 1) * rows)
        sent[g, :, :dim] = mix[at].astype(BF16)
        sent[g, :, dim : 2 * dim] = (pulled[at] - mean[at] * mix[at]).astype(BF16)
        sent[g, :, 2 * dim :] = stats


def roll_left(value, by):
    return pltpu.roll(value, value.shape[1] - by, 1)


def merged_stats(received):
    n_code = received.shape[0]
    lanes = stat_lanes(n_code)
    stats = [received[p, :, received.shape[2] - lanes :].astype(F32) for p in range(n_code)]
    top = functools.reduce(jnp.maximum, stats)
    scales = [roll_left(jnp.exp2(s - top), lanes // 2) for s in stats]
    pairs = [s + roll_left(s, 1) for s in stats]
    inners = [roll_left(s, 2) for s in pairs]
    total = sum(a * s for a, s in zip(scales, pairs))
    inner = sum(a * s for a, s in zip(scales, inners)) / total
    means = [i / s for i, s in zip(inners, pairs)]
    return [a / total for a in scales], means, inner


def merge_kernel(me, received, spread):
    n_code, rows, _ = received.shape
    dim = spread.shape[2] // 2
    scales, means, inner = merged_stats(received)
    lane = lax.broadcasted_iota(jnp.int32, inner.shape, 1)
    mine = lane == 4 * me[0]

    def column(value):
        return jnp.sum(jnp.where(mine, value, 0.0), axis=1, keepdims=True)

    quantized = jnp.zeros((rows, dim), F32)
    gradient = jnp.zeros((rows, dim), F32)
    for p in range(n_code):
        scale = column(scales[p])
        offset = column(scales[p] * (means[p] - inner))
        mix = received[p, :, :dim].astype(F32)
        quantized += scale * mix
        gradient += scale * received[p, :, dim : 2 * dim].astype(F32) + offset * mix
    quantized = quantized.astype(BF16)
    gradient = (gradient / SOFTMAX_HEAT).astype(BF16)
    for p in range(n_code):
        spread[p, :, :dim] = quantized
        spread[p, :, dim:] = gradient


def backward_kernel(prepared, where, *rest):
    if prepared:
        grad_out, codebook, codes, operands, inners, out, *rest = rest
    else:
        tokens, grad_out, codebook, codes, received, out, operands, inners, upper, lower, *rest = rest
    book, code_in, result, book_sem, code_sem, out_sem = rest
    tiles, width, dim = book.shape
    n_tokens = grad_out.shape[0]
    first = where[1] * tiles

    def fetch(t):
        at = pl.multiple_of((first + t) * width, width)
        return (
            pltpu.make_async_copy(codebook.at[pl.ds(at, width)], book.at[t], book_sem.at[t]),
            pltpu.make_async_copy(codes.at[first + t], code_in.at[t], code_sem.at[t]),
        )

    def start(t):
        for copy in fetch(t):
            copy.start()

    for t in range(min(AHEAD, tiles)):
        start(t)

    if not prepared:
        n_code, rows, _ = received.shape
        scales, _, inner = merged_stats(received)
        scale = jnp.zeros(inner.shape, F32)
        for p in range(n_code):
            scale = jnp.where(where[0] == p, scales[p], scale)
        for g in range(n_code):
            part = slice(g * rows, (g + 1) * rows)
            column = scale[:, 4 * g : 4 * g + 1]
            upper[part] = column * grad_out[part].astype(F32)
            lower[part] = column * (tokens[part].astype(F32) / SOFTMAX_HEAT)
            inners[part] = jnp.broadcast_to(inner[:, 4 * g : 4 * g + 1], (rows, 128))
        operands[0] = upper[...].T.astype(BF16)
        operands[1] = lower[...].T.astype(BF16)

    def send(t):
        return pltpu.make_async_copy(
            result.at[t], out.at[pl.ds(pl.multiple_of(t * width, width), width)], out_sem.at[t]
        )

    def block(t, carry):
        for copy in fetch(t):
            copy.wait()

        @pl.when(t + AHEAD < tiles)
        def _():
            start(t + AHEAD)

        for c in range(0, width, CHUNK):
            gradient = dot(grad_out[...], book[t, c : c + CHUNK], 1, 1)
            code = code_in[t, :, c : c + CHUNK]
            inner = jnp.concatenate([inners[...]] * (CHUNK // 128), axis=1)
            score_gradient = (code.astype(F32) * (gradient - inner)).astype(BF16)
            value = dot(operands[0], code) + dot(operands[1], score_gradient)
            result[t, c : c + CHUNK] = value.astype(BF16).T
        send(t).start()
        return carry

    lax.fori_loop(0, tiles, block, 0)
    for t in range(tiles):
        send(t).wait()


def add_kernel(*refs):
    out = refs[-1]
    out[...] = sum(ref[...].astype(F32) for ref in refs[:-1])


def unpack_kernel(gathered, quantized, gradient):
    n_code, rows, both = gathered.shape
    dim = both // 2
    for g in range(n_code):
        at = slice(g * rows, (g + 1) * rows)
        quantized[at] = gathered[g, :, :dim].astype(F32)
        gradient[at] = gathered[g, :, dim:].astype(F32)


def swap(value, axis, size, mask):
    return lax.ppermute(value, axis, [(i, i ^ mask) for i in range(size)])


def local(n_dp, n_code, tokens, codebook, noise, grad_out):
    n_tokens, dim = tokens.shape
    n_codes = codebook.shape[0]
    rows = n_tokens // n_code
    block = n_codes // n_dp
    width = min(1024, block)
    tiles = n_codes // width
    lanes = stat_lanes(n_code)
    products = 2 * n_tokens * n_codes * dim

    codes, sent = pl.pallas_call(
        functools.partial(forward_kernel, n_code),
        out_shape=(
            pltpu.HBM((tiles, n_tokens, width), BF16),
            jax.ShapeDtypeStruct((n_code, rows, 2 * dim + lanes), BF16),
        ),
        in_specs=[VMEM, VMEM, ANY, ANY],
        out_specs=(ANY, VMEM),
        scratch_shapes=[
            pltpu.VMEM((2 * n_tokens, dim), BF16),
            pltpu.VMEM((tiles, width, dim), BF16),
            pltpu.VMEM((tiles, n_tokens, width), BF16),
            pltpu.VMEM((2 * n_tokens, width), BF16),
            pltpu.VMEM((2 * n_tokens, width), BF16),
            pltpu.VMEM((n_tokens, 128), F32),
            pltpu.VMEM((n_tokens, 128), F32),
            pltpu.VMEM((2 * n_tokens, dim), F32),
            pltpu.SemaphoreType.DMA((tiles,)),
            pltpu.SemaphoreType.DMA((tiles,)),
            pltpu.SemaphoreType.DMA((2,)),
        ],
        compiler_params=pltpu.CompilerParams(vmem_limit_bytes=60 * MIB),
        cost_estimate=pl.CostEstimate(
            flops=4 * products, bytes_accessed=24 * MIB, transcendentals=n_tokens * n_codes
        ),
        name="forward",
    )(tokens, grad_out, codebook, noise)

    received = lax.all_to_all(sent, "code", 0, 0, tiled=True)
    code_at = lax.axis_index("code")
    spread = pl.pallas_call(
        merge_kernel,
        out_shape=jax.ShapeDtypeStruct((n_code, rows, 2 * dim), BF16),
        in_specs=[SMEM, VMEM],
        out_specs=VMEM,
        name="merge",
    )(code_at[None], received)
    received, spread = lax.optimization_barrier((received, spread))
    gathered = lax.all_to_all(spread, "code", 0, 0, tiled=True)
    quantized, token_gradient = pl.pallas_call(
        unpack_kernel,
        out_shape=(jax.ShapeDtypeStruct((n_tokens, dim), F32),) * 2,
        in_specs=[VMEM],
        out_specs=(VMEM, VMEM),
        cost_estimate=pl.CostEstimate(flops=0, bytes_accessed=64 * MIB, transcendentals=0),
        name="unpack",
    )(gathered)

    block_tiles = block // width
    streams = [
        pltpu.VMEM((block_tiles, width, dim), BF16),
        pltpu.VMEM((block_tiles, n_tokens, width), BF16),
        pltpu.VMEM((block_tiles, width, dim), BF16),
        pltpu.SemaphoreType.DMA((block_tiles,)),
        pltpu.SemaphoreType.DMA((block_tiles,)),
        pltpu.SemaphoreType.DMA((block_tiles,)),
    ]
    block_shape = jax.ShapeDtypeStruct((block, dim), BF16)
    common = dict(
        compiler_params=pltpu.CompilerParams(vmem_limit_bytes=60 * MIB),
        cost_estimate=pl.CostEstimate(
            flops=3 * products // n_dp, bytes_accessed=16 * MIB // n_dp, transcendentals=0
        ),
    )
    dp_at = lax.axis_index("dp")
    first, operands, inners = pl.pallas_call(
        functools.partial(backward_kernel, False),
        out_shape=(
            block_shape,
            jax.ShapeDtypeStruct((2, dim, n_tokens), BF16),
            jax.ShapeDtypeStruct((n_tokens, 128), F32),
        ),
        in_specs=[SMEM, VMEM, VMEM, ANY, ANY, VMEM],
        out_specs=(ANY, VMEM, VMEM),
        scratch_shapes=[
            pltpu.VMEM((n_tokens, dim), F32), pltpu.VMEM((n_tokens, dim), F32),
        ] + streams,
        name="backward_first",
        **common,
    )(jnp.stack([code_at, dp_at ^ (n_dp - 1)]), tokens, grad_out, codebook, codes, received)

    def backward(at):
        return pl.pallas_call(
            functools.partial(backward_kernel, True),
            out_shape=block_shape,
            in_specs=[SMEM, VMEM, ANY, ANY, VMEM, VMEM],
            out_specs=ANY,
            scratch_shapes=streams,
            name="backward",
            **common,
        )(jnp.stack([code_at, at]), grad_out, codebook, codes, operands, inners)

    blocks = [swap(first, "dp", n_dp, n_dp - 1)]
    blocks += [swap(backward(dp_at ^ d), "dp", n_dp, d) for d in range(1, n_dp - 1)]
    blocks.append(backward(dp_at))
    rows_spec = pl.BlockSpec((min(1024, block), dim), lambda i: (i, 0))
    own_rows = pl.pallas_call(
        add_kernel,
        out_shape=jax.ShapeDtypeStruct((block, dim), F32),
        grid=(block // min(1024, block),),
        in_specs=[rows_spec] * n_dp,
        out_specs=rows_spec,
        cost_estimate=pl.CostEstimate(
            flops=0, bytes_accessed=(2 * n_dp + 4) * block * dim, transcendentals=0
        ),
        name="add",
    )(*blocks)
    return quantized, token_gradient, own_rows[None]


def solution(mesh):
    n_dp, n_code = mesh.shape["dp"], mesh.shape["code"]
    in_specs = (P("dp", None), P("code", None), P("dp", "code"), P("dp", None))
    out_specs = (P("dp", None), P("dp", None), P("code", "dp", None))
    return jax.shard_map(
        functools.partial(local, n_dp, n_code),
        mesh=mesh, in_specs=in_specs, out_specs=out_specs, check_vma=False,
    )
```

```python
import functools
import math

import jax
import jax.numpy as jnp
from jax import lax
from jax.experimental import pallas as pl
from jax.experimental.pallas import tpu as pltpu
from jax.sharding import PartitionSpec as P

SOFTMAX_HEAT = 0.5
TO_LOG2 = math.log2(math.e) / SOFTMAX_HEAT
BF16 = jnp.bfloat16
F32 = jnp.float32
MIB = 1 << 20
CHUNK = 256
AHEAD = 3
ROWS = 64
LARGEST = 2.0**60
VMEM = pl.BlockSpec(memory_space=pltpu.VMEM)
SMEM = pl.BlockSpec(memory_space=pltpu.SMEM)
ANY = pl.BlockSpec(memory_space=pl.ANY)
FULL = pltpu.CompilerParams(vmem_limit_bytes=60 * MIB)


def dot(left, right, left_dim=1, right_dim=0):
    return lax.dot_general(
        left, right, (((left_dim,), (right_dim,)), ((), ())), preferred_element_type=F32
    )


def lane_groups(value):
    return [value[:, j : j + 128] for j in range(0, value.shape[1], 128)]


def stat_lanes(n_code):
    return max(8 * n_code, 128)


def high_low(value):
    high = value.astype(BF16).astype(F32)
    return high, (value - high).astype(BF16).astype(F32)


def forward_kernel(
    n_code, tokens, grad_out, codebook, noise, codes, sent,
    pair, book, noise_in, slot_a, slot_b, shifts, total, sums,
    pair_sem, book_sem, noise_sem, code_sem,
):
    tiles, n_tokens, width = codes.shape
    dim = tokens.shape[1]
    columns = [slice(c, c + CHUNK) for c in range(0, width, CHUNK)]
    slots = (slot_a, slot_b)

    def fetch(t):
        at = pl.multiple_of(t * width, width)
        return (
            pltpu.make_async_copy(codebook.at[pl.ds(at, width)], book.at[t], book_sem.at[t]),
            pltpu.make_async_copy(noise.at[:, pl.ds(at, width)], noise_in.at[t], noise_sem.at[t]),
        )

    def start(t):
        for copy in fetch(t):
            copy.start()

    def arrive(t):
        for copy in fetch(t):
            copy.wait()

    pair_copies = []
    for r in range(0, n_tokens, ROWS):
        for half, source in enumerate((tokens, grad_out)):
            pair_copies.append(
                pltpu.make_async_copy(
                    source.at[pl.ds(r, ROWS)],
                    pair.at[pl.ds(2 * r + half * ROWS, ROWS)],
                    pair_sem.at[len(pair_copies)],
                )
            )
    start(0)
    for copy in pair_copies:
        copy.start()
    for t in range(1, min(AHEAD + 1, tiles)):
        start(t)

    def raise_shift(t, some):
        for c in some:
            both = dot(pair[...], book[t, c], 1, 1)
            for r in range(0, n_tokens, ROWS):
                at = slice(r, r + ROWS)
                score = both[2 * r : 2 * r + ROWS] + noise_in[t, at, c].astype(F32)
                shifts[at] = functools.reduce(
                    jnp.maximum, lane_groups(score * TO_LOG2), shifts[at]
                )

    def store(t, s):
        return pltpu.make_async_copy(
            slots[s].at[pl.ds(0, n_tokens)], codes.at[t], code_sem.at[s]
        )

    def soften(t, s, fresh):
        if fresh is not None:
            @pl.when(fresh)
            def _():
                arrive(t)

                @pl.when(t + AHEAD < tiles)
                def _():
                    start(t + AHEAD)

        slot = slots[s]
        for c in columns:
            both = dot(pair[...], book[t, c], 1, 1)
            for r in range(0, n_tokens, ROWS):
                at = slice(r, r + ROWS)
                score = both[2 * r : 2 * r + ROWS] + noise_in[t, at, c].astype(F32)
                shift = jnp.concatenate([shifts[at]] * (CHUNK // 128), axis=1)
                weight = jnp.exp2(score * TO_LOG2 - shift)
                total[at] += sum(lane_groups(weight))
                slot[at, c] = weight.astype(BF16)
                gradient = both[2 * r + ROWS : 2 * r + 2 * ROWS]
                slot[n_tokens + r : n_tokens + r + ROWS, c] = (weight * gradient).astype(BF16)
        store(t, s).start()

    def accumulate(t, s):
        sums[...] += dot(slots[s][...], book[t])

    def attempt(state):
        again, _ = state
        fresh = again == 0
        shifts[...] = jnp.full(shifts.shape, -jnp.inf, F32)

        @pl.when(fresh)
        def _():
            raise_shift(0, columns[:2])

        @pl.when(jnp.logical_not(fresh))
        def _():
            def over(t, carry):
                raise_shift(t, columns)
                return carry

            lax.fori_loop(0, tiles, over, 0)

        shift = jnp.max(shifts[...], axis=1, keepdims=True).astype(BF16).astype(F32)
        shifts[...] = jnp.broadcast_to(shift, shifts.shape)
        total[...] = jnp.zeros(total.shape, F32)
        sums[...] = jnp.zeros(sums.shape, F32)
        soften(0, 0, None)

        def soften_pair(i, carry):
            @pl.when(i > 0)
            def _():
                store(2 * i - 1, 1).wait()

            soften(2 * i + 1, 1, fresh)
            accumulate(2 * i, 0)
            store(2 * i, 0).wait()
            soften(2 * i + 2, 0, fresh)
            accumulate(2 * i + 1, 1)
            return carry

        lax.fori_loop(0, tiles // 2 - 1, soften_pair, 0)
        if tiles > 2:
            store(tiles - 3, 1).wait()
        soften(tiles - 1, 1, fresh)
        accumulate(tiles - 2, 0)
        accumulate(tiles - 1, 1)
        store(tiles - 2, 0).wait()
        store(tiles - 1, 1).wait()
        fits = jnp.max(total[...]) < LARGEST
        return again + 1, jnp.logical_and(fresh, jnp.logical_not(fits))

    for copy in pair_copies:
        copy.wait()
    arrive(0)
    lax.while_loop(lambda state: state[1], attempt, (jnp.int32(0), jnp.bool_(True)))

    shift = shifts[:, :1]
    mix = sums[:n_tokens]
    pulled = sums[n_tokens:]
    own_total = jnp.sum(total[...], axis=1, keepdims=True)
    own_grad = jnp.concatenate(
        [pair[2 * r + ROWS : 2 * r + 2 * ROWS] for r in range(0, n_tokens, ROWS)], axis=0
    )
    own_inner = jnp.sum(own_grad.astype(F32) * mix, axis=1, keepdims=True)
    mean = own_inner / own_total
    rows = n_tokens // n_code
    lanes = stat_lanes(n_code)
    half = lanes // 2
    lane = lax.broadcasted_iota(jnp.int32, (rows, lanes), 1)
    stats = jnp.zeros((rows, lanes), F32)
    parts = high_low(own_total) + high_low(own_inner)
    for g in range(n_code):
        at = slice(g * rows, (g + 1) * rows)
        for i, part in enumerate(parts):
            stats = jnp.where(lane == 4 * g + i, part[at], stats)
        stats = jnp.where((lane - half) // 4 == g, shift[at], stats)
    stats = stats.astype(BF16)
    for g in range(n_code):
        at = slice(g * rows, (g + 1) * rows)
        sent[g, :, :dim] = mix[at].astype(BF16)
        sent[g, :, dim : 2 * dim] = (pulled[at] - mean[at] * mix[at]).astype(BF16)
        sent[g, :, 2 * dim :] = stats


def roll_left(value, by):
    return pltpu.roll(value, value.shape[1] - by, 1)


def merged_stats(received):
    n_code = received.shape[0]
    lanes = stat_lanes(n_code)
    stats = [received[p, :, received.shape[2] - lanes :].astype(F32) for p in range(n_code)]
    top = functools.reduce(jnp.maximum, stats)
    scales = [roll_left(jnp.exp2(s - top), lanes // 2) for s in stats]
    pairs = [s + roll_left(s, 1) for s in stats]
    inners = [roll_left(s, 2) for s in pairs]
    total = sum(a * s for a, s in zip(scales, pairs))
    inner = sum(a * s for a, s in zip(scales, inners)) / total
    means = [i / s for i, s in zip(inners, pairs)]
    return [a / total for a in scales], means, inner


def merge_kernel(me, received, spread):
    n_code, rows, _ = received.shape
    dim = spread.shape[2] // 2
    scales, means, inner = merged_stats(received)
    lane = lax.broadcasted_iota(jnp.int32, inner.shape, 1)
    mine = lane == 4 * me[0]

    def column(value):
        return jnp.sum(jnp.where(mine, value, 0.0), axis=1, keepdims=True)

    quantized = jnp.zeros((rows, dim), F32)
    gradient = jnp.zeros((rows, dim), F32)
    for p in range(n_code):
        scale = column(scales[p])
        offset = column(scales[p] * (means[p] - inner))
        mix = received[p, :, :dim].astype(F32)
        quantized += scale * mix
        gradient += scale * received[p, :, dim : 2 * dim].astype(F32) + offset * mix
    quantized = quantized.astype(BF16)
    gradient = (gradient / SOFTMAX_HEAT).astype(BF16)
    for p in range(n_code):
        spread[p, :, :dim] = quantized
        spread[p, :, dim:] = gradient


def backward_kernel(prepared, where, *rest):
    if prepared:
        grad_out, codebook, codes, operands, inners, out, *rest = rest
    else:
        tokens, grad_out, codebook, codes, received, out, operands, inners, upper, lower, *rest = rest
    book, code_in, result, book_sem, code_sem, out_sem = rest
    tiles, width, dim = book.shape
    n_tokens = grad_out.shape[0]
    first = where[1] * tiles

    def fetch(t):
        at = pl.multiple_of((first + t) * width, width)
        return (
            pltpu.make_async_copy(codebook.at[pl.ds(at, width)], book.at[t], book_sem.at[t]),
            pltpu.make_async_copy(codes.at[first + t], code_in.at[t], code_sem.at[t]),
        )

    def start(t):
        for copy in fetch(t):
            copy.start()

    for t in range(min(AHEAD, tiles)):
        start(t)

    if not prepared:
        n_code, rows, _ = received.shape
        scales, _, inner = merged_stats(received)
        scale = jnp.zeros(inner.shape, F32)
        for p in range(n_code):
            scale = jnp.where(where[0] == p, scales[p], scale)
        for g in range(n_code):
            part = slice(g * rows, (g + 1) * rows)
            column = scale[:, 4 * g : 4 * g + 1]
            upper[part] = column * grad_out[part].astype(F32)
            lower[part] = column * (tokens[part].astype(F32) / SOFTMAX_HEAT)
            inners[part] = jnp.broadcast_to(inner[:, 4 * g : 4 * g + 1], (rows, 128))
        operands[0] = upper[...].T.astype(BF16)
        operands[1] = lower[...].T.astype(BF16)

    def send(t):
        return pltpu.make_async_copy(
            result.at[t], out.at[pl.ds(pl.multiple_of(t * width, width), width)], out_sem.at[t]
        )

    chunk = min(CHUNK, width)
    steps = [(t, slice(c, c + chunk)) for t in range(tiles) for c in range(0, width, chunk)]

    def gradient_of(step):
        t, c = step
        if c.start == 0:
            for copy in fetch(t):
                copy.wait()
            if t + AHEAD < tiles:
                start(t + AHEAD)
        return dot(grad_out[...], book[t, c], 1, 1)

    ahead = gradient_of(steps[0])
    for k, (t, c) in enumerate(steps):
        gradient = ahead
        if k + 1 < len(steps):
            ahead = gradient_of(steps[k + 1])
        code = code_in[t, :, c]
        inner = jnp.concatenate([inners[...]] * (chunk // 128), axis=1)
        score_gradient = (code.astype(F32) * (gradient - inner)).astype(BF16)
        value = dot(operands[0], code) + dot(operands[1], score_gradient)
        result[t, c] = value.astype(BF16).T
        if c.stop == width:
            send(t).start()
    for t in range(tiles):
        send(t).wait()


def add_kernel(n_parts, *refs):
    parts, out = refs[:n_parts], refs[n_parts]
    held, result, in_sem, out_sem = refs[n_parts + 1 :]
    steps, rows, _ = result.shape

    def fetch(i):
        at = pl.ds(i * rows, rows)
        return [
            pltpu.make_async_copy(part.at[at], held.at[j, i], in_sem.at[j, i])
            for j, part in enumerate(parts)
        ]

    def send(i):
        return pltpu.make_async_copy(result.at[i], out.at[pl.ds(i * rows, rows)], out_sem.at[i])

    for i in range(steps):
        for copy in fetch(i):
            copy.start()
    for i in range(steps):
        for copy in fetch(i):
            copy.wait()
        result[i] = sum(held[j, i].astype(F32) for j in range(n_parts))
        send(i).start()
    for i in range(steps):
        send(i).wait()


def unpack_kernel(gathered, quantized, gradient):
    n_code, rows, both = gathered.shape
    dim = both // 2
    for g in range(n_code):
        at = slice(g * rows, (g + 1) * rows)
        quantized[at] = gathered[g, :, :dim].astype(F32)
        gradient[at] = gathered[g, :, dim:].astype(F32)


def swap(value, axis, size, mask):
    return lax.ppermute(value, axis, [(i, i ^ mask) for i in range(size)])


def local(n_dp, n_code, tokens, codebook, noise, grad_out):
    n_tokens, dim = tokens.shape
    n_codes = codebook.shape[0]
    rows = n_tokens // n_code
    block = n_codes // n_dp
    width = min(1024, block)
    tiles = n_codes // width
    lanes = stat_lanes(n_code)
    products = 2 * n_tokens * n_codes * dim

    codes, sent = pl.pallas_call(
        functools.partial(forward_kernel, n_code),
        out_shape=(
            pltpu.HBM((tiles, n_tokens, width), BF16),
            jax.ShapeDtypeStruct((n_code, rows, 2 * dim + lanes), BF16),
        ),
        in_specs=[ANY, ANY, ANY, ANY],
        out_specs=(ANY, VMEM),
        scratch_shapes=[
            pltpu.VMEM((2 * n_tokens, dim), BF16),
            pltpu.VMEM((tiles, width, dim), BF16),
            pltpu.VMEM((tiles, n_tokens, width), BF16),
            pltpu.VMEM((2 * n_tokens, width), BF16),
            pltpu.VMEM((2 * n_tokens, width), BF16),
            pltpu.VMEM((n_tokens, 128), F32),
            pltpu.VMEM((n_tokens, 128), F32),
            pltpu.VMEM((2 * n_tokens, dim), F32),
            pltpu.SemaphoreType.DMA((2 * n_tokens // ROWS,)),
            pltpu.SemaphoreType.DMA((tiles,)),
            pltpu.SemaphoreType.DMA((tiles,)),
            pltpu.SemaphoreType.DMA((2,)),
        ],
        compiler_params=FULL,
        cost_estimate=pl.CostEstimate(
            flops=4 * products, bytes_accessed=24 * MIB, transcendentals=n_tokens * n_codes
        ),
        name="forward",
    )(tokens, grad_out, codebook, noise)

    received = lax.all_to_all(sent, "code", 0, 0, tiled=True)
    code_at = lax.axis_index("code")
    spread = pl.pallas_call(
        merge_kernel,
        out_shape=jax.ShapeDtypeStruct((n_code, rows, 2 * dim), BF16),
        in_specs=[SMEM, VMEM],
        out_specs=VMEM,
        compiler_params=FULL,
        name="merge",
    )(code_at[None], received)
    received, spread = lax.optimization_barrier((received, spread))
    gathered = lax.all_to_all(spread, "code", 0, 0, tiled=True)
    quantized, token_gradient = pl.pallas_call(
        unpack_kernel,
        out_shape=(jax.ShapeDtypeStruct((n_tokens, dim), F32),) * 2,
        in_specs=[VMEM],
        out_specs=(VMEM, VMEM),
        compiler_params=FULL,
        cost_estimate=pl.CostEstimate(flops=0, bytes_accessed=64 * MIB, transcendentals=0),
        name="unpack",
    )(gathered)

    block_tiles = block // width
    streams = [
        pltpu.VMEM((block_tiles, width, dim), BF16),
        pltpu.VMEM((block_tiles, n_tokens, width), BF16),
        pltpu.VMEM((block_tiles, width, dim), BF16),
        pltpu.SemaphoreType.DMA((block_tiles,)),
        pltpu.SemaphoreType.DMA((block_tiles,)),
        pltpu.SemaphoreType.DMA((block_tiles,)),
    ]
    block_shape = jax.ShapeDtypeStruct((block, dim), BF16)
    common = dict(
        compiler_params=FULL,
        cost_estimate=pl.CostEstimate(flops=1, bytes_accessed=1, transcendentals=0),
    )
    dp_at = lax.axis_index("dp")
    first, operands, inners = pl.pallas_call(
        functools.partial(backward_kernel, False),
        out_shape=(
            block_shape,
            jax.ShapeDtypeStruct((2, dim, n_tokens), BF16),
            jax.ShapeDtypeStruct((n_tokens, 128), F32),
        ),
        in_specs=[SMEM, VMEM, VMEM, ANY, ANY, VMEM],
        out_specs=(ANY, VMEM, VMEM),
        scratch_shapes=[
            pltpu.VMEM((n_tokens, dim), F32), pltpu.VMEM((n_tokens, dim), F32),
        ] + streams,
        name="backward_first",
        **common,
    )(jnp.stack([code_at, dp_at ^ (n_dp - 1)]), tokens, grad_out, codebook, codes, received)

    def backward(at):
        return pl.pallas_call(
            functools.partial(backward_kernel, True),
            out_shape=block_shape,
            in_specs=[SMEM, VMEM, ANY, ANY, VMEM, VMEM],
            out_specs=ANY,
            scratch_shapes=streams,
            name="backward",
            **common,
        )(jnp.stack([code_at, at]), grad_out, codebook, codes, operands, inners)

    blocks = [swap(first, "dp", n_dp, n_dp - 1)]
    blocks += [swap(backward(dp_at ^ d), "dp", n_dp, d) for d in range(1, n_dp - 1)]
    blocks.append(backward(dp_at))
    steps = max(block // 512, 1)
    own_rows = pl.pallas_call(
        functools.partial(add_kernel, n_dp),
        out_shape=jax.ShapeDtypeStruct((block, dim), F32),
        in_specs=[ANY] * n_dp,
        out_specs=ANY,
        scratch_shapes=[
            pltpu.VMEM((n_dp, steps, block // steps, dim), BF16),
            pltpu.VMEM((steps, block // steps, dim), F32),
            pltpu.SemaphoreType.DMA((n_dp, steps)),
            pltpu.SemaphoreType.DMA((steps,)),
        ],
        compiler_params=FULL,
        cost_estimate=pl.CostEstimate(
            flops=0, bytes_accessed=(2 * n_dp + 4) * block * dim, transcendentals=0
        ),
        name="add",
    )(*blocks)
    return quantized, token_gradient, own_rows[None]


def solution(mesh):
    n_dp, n_code = mesh.shape["dp"], mesh.shape["code"]
    in_specs = (P("dp", None), P("code", None), P("dp", "code"), P("dp", None))
    out_specs = (P("dp", None), P("dp", None), P("code", "dp", None))
    return jax.shard_map(
        functools.partial(local, n_dp, n_code),
        mesh=mesh, in_specs=in_specs, out_specs=out_specs, check_vma=False,
    )
```

```python
import functools
import math

import jax
import jax.numpy as jnp
from jax import lax
from jax.experimental import pallas as pl
from jax.experimental.pallas import tpu as pltpu
from jax.sharding import PartitionSpec as P

SOFTMAX_HEAT = 0.5
TO_LOG2 = math.log2(math.e) / SOFTMAX_HEAT
BF16 = jnp.bfloat16
F32 = jnp.float32
MIB = 1 << 20
CHUNK = 256
AHEAD = 3
PARTS = 4
ROWS = 64
LARGEST = 2.0**60
VMEM = pl.BlockSpec(memory_space=pltpu.VMEM)
SMEM = pl.BlockSpec(memory_space=pltpu.SMEM)
ANY = pl.BlockSpec(memory_space=pl.ANY)
FULL = pltpu.CompilerParams(vmem_limit_bytes=60 * MIB)
MOST = pltpu.CompilerParams(vmem_limit_bytes=56 * MIB)
SOME = pltpu.CompilerParams(vmem_limit_bytes=24 * MIB)


def dot(left, right, left_dim=1, right_dim=0):
    return lax.dot_general(
        left, right, (((left_dim,), (right_dim,)), ((), ())), preferred_element_type=F32
    )


def lane_groups(value):
    return [value[:, j : j + 128] for j in range(0, value.shape[1], 128)]


def stat_lanes(n_code):
    return max(8 * n_code, 128)


def high_low(value):
    high = value.astype(BF16).astype(F32)
    return high, (value - high).astype(BF16).astype(F32)


def forward_kernel(
    n_code, tokens, grad_out, codebook, noise, codes, sent,
    pair, book, noise_in, slot_a, slot_b, shifts, total, sums,
    pair_sem, book_sem, noise_sem, code_sem,
):
    tiles, n_tokens, width = codes.shape
    dim = tokens.shape[1]
    columns = [slice(c, c + CHUNK) for c in range(0, width, CHUNK)]
    slots = (slot_a, slot_b)

    def fetch(t):
        at = pl.multiple_of(t * width, width)
        return (
            pltpu.make_async_copy(codebook.at[pl.ds(at, width)], book.at[t], book_sem.at[t]),
            pltpu.make_async_copy(noise.at[:, pl.ds(at, width)], noise_in.at[t], noise_sem.at[t]),
        )

    def start(t):
        fetch(t)[0].start()
        at = pl.ds(pl.multiple_of(t * width, width), width)
        for r in range(0, n_tokens, n_tokens // PARTS):
            part = pl.ds(r, n_tokens // PARTS)
            pltpu.make_async_copy(
                noise.at[part, at], noise_in.at[t, part], noise_sem.at[t]
            ).start()

    def arrive(t):
        for copy in fetch(t):
            copy.wait()

    pair_copies = []
    for r in range(0, n_tokens, ROWS):
        for half, source in enumerate((tokens, grad_out)):
            pair_copies.append(
                pltpu.make_async_copy(
                    source.at[pl.ds(r, ROWS)],
                    pair.at[pl.ds(2 * r + half * ROWS, ROWS)],
                    pair_sem.at[len(pair_copies)],
                )
            )
    start(0)
    for copy in pair_copies:
        copy.start()
    for t in range(1, min(AHEAD + 1, tiles)):
        start(t)

    def raise_shift(t, some):
        for c in some:
            both = dot(pair[...], book[t, c], 1, 1)
            for r in range(0, n_tokens, ROWS):
                at = slice(r, r + ROWS)
                score = both[2 * r : 2 * r + ROWS] + noise_in[t, at, c].astype(F32)
                shifts[at] = functools.reduce(
                    jnp.maximum, lane_groups(score * TO_LOG2), shifts[at]
                )

    def store(t, s):
        return pltpu.make_async_copy(
            slots[s].at[pl.ds(0, n_tokens)], codes.at[t], code_sem.at[s]
        )

    def soften(t, s, fresh):
        if fresh is not None:
            @pl.when(fresh)
            def _():
                arrive(t)

                @pl.when(t + AHEAD < tiles)
                def _():
                    start(t + AHEAD)

        slot = slots[s]
        for c in columns:
            both = dot(pair[...], book[t, c], 1, 1)
            for r in range(0, n_tokens, ROWS):
                at = slice(r, r + ROWS)
                score = both[2 * r : 2 * r + ROWS] + noise_in[t, at, c].astype(F32)
                shift = jnp.concatenate([shifts[at]] * (CHUNK // 128), axis=1)
                weight = jnp.exp2(score * TO_LOG2 - shift)
                total[at] += sum(lane_groups(weight))
                slot[at, c] = weight.astype(BF16)
                gradient = both[2 * r + ROWS : 2 * r + 2 * ROWS]
                slot[n_tokens + r : n_tokens + r + ROWS, c] = (weight * gradient).astype(BF16)
        store(t, s).start()

    def accumulate(t, s):
        sums[...] += dot(slots[s][...], book[t])

    def attempt(state):
        again, _ = state
        fresh = again == 0
        shifts[...] = jnp.full(shifts.shape, -jnp.inf, F32)

        @pl.when(fresh)
        def _():
            raise_shift(0, columns[:2])

        @pl.when(jnp.logical_not(fresh))
        def _():
            def over(t, carry):
                raise_shift(t, columns)
                return carry

            lax.fori_loop(0, tiles, over, 0)

        shift = jnp.max(shifts[...], axis=1, keepdims=True).astype(BF16).astype(F32)
        shifts[...] = jnp.broadcast_to(shift, shifts.shape)
        total[...] = jnp.zeros(total.shape, F32)
        sums[...] = jnp.zeros(sums.shape, F32)
        soften(0, 0, None)

        def soften_pair(i, carry):
            @pl.when(i > 0)
            def _():
                store(2 * i - 1, 1).wait()

            soften(2 * i + 1, 1, fresh)
            accumulate(2 * i, 0)
            store(2 * i, 0).wait()
            soften(2 * i + 2, 0, fresh)
            accumulate(2 * i + 1, 1)
            return carry

        lax.fori_loop(0, tiles // 2 - 1, soften_pair, 0)
        if tiles > 2:
            store(tiles - 3, 1).wait()
        soften(tiles - 1, 1, fresh)
        accumulate(tiles - 2, 0)
        accumulate(tiles - 1, 1)
        store(tiles - 2, 0).wait()
        store(tiles - 1, 1).wait()
        fits = jnp.max(total[...]) < LARGEST
        return again + 1, jnp.logical_and(fresh, jnp.logical_not(fits))

    for copy in pair_copies:
        copy.wait()
    arrive(0)
    lax.while_loop(lambda state: state[1], attempt, (jnp.int32(0), jnp.bool_(True)))

    shift = shifts[:, :1]
    mix = sums[:n_tokens]
    pulled = sums[n_tokens:]
    own_total = jnp.sum(total[...], axis=1, keepdims=True)
    own_grad = jnp.concatenate(
        [pair[2 * r + ROWS : 2 * r + 2 * ROWS] for r in range(0, n_tokens, ROWS)], axis=0
    )
    own_inner = jnp.sum(own_grad.astype(F32) * mix, axis=1, keepdims=True)
    mean = own_inner / own_total
    rows = n_tokens // n_code
    lanes = stat_lanes(n_code)
    half = lanes // 2
    lane = lax.broadcasted_iota(jnp.int32, (rows, lanes), 1)
    stats = jnp.zeros((rows, lanes), F32)
    parts = high_low(own_total) + high_low(own_inner)
    for g in range(n_code):
        at = slice(g * rows, (g + 1) * rows)
        for i, part in enumerate(parts):
            stats = jnp.where(lane == 4 * g + i, part[at], stats)
        stats = jnp.where((lane - half) // 4 == g, shift[at], stats)
    stats = stats.astype(BF16)
    for g in range(n_code):
        at = slice(g * rows, (g + 1) * rows)
        sent[g, :, :dim] = mix[at].astype(BF16)
        sent[g, :, dim : 2 * dim] = (pulled[at] - mean[at] * mix[at]).astype(BF16)
        sent[g, :, 2 * dim :] = stats


def roll_left(value, by):
    return pltpu.roll(value, value.shape[1] - by, 1)


def merged_stats(received):
    n_code = received.shape[0]
    lanes = stat_lanes(n_code)
    stats = [received[p, :, received.shape[2] - lanes :].astype(F32) for p in range(n_code)]
    top = functools.reduce(jnp.maximum, stats)
    scales = [roll_left(jnp.exp2(s - top), lanes // 2) for s in stats]
    pairs = [s + roll_left(s, 1) for s in stats]
    inners = [roll_left(s, 2) for s in pairs]
    total = sum(a * s for a, s in zip(scales, pairs))
    inner = sum(a * s for a, s in zip(scales, inners)) / total
    means = [i / s for i, s in zip(inners, pairs)]
    return [a / total for a in scales], means, inner


def merge_kernel(me, received, spread):
    n_code, rows, _ = received.shape
    dim = spread.shape[2] // 2
    scales, means, inner = merged_stats(received)
    lane = lax.broadcasted_iota(jnp.int32, inner.shape, 1)
    mine = lane == 4 * me[0]

    def column(value):
        return jnp.sum(jnp.where(mine, value, 0.0), axis=1, keepdims=True)

    quantized = jnp.zeros((rows, dim), F32)
    gradient = jnp.zeros((rows, dim), F32)
    for p in range(n_code):
        scale = column(scales[p])
        offset = column(scales[p] * (means[p] - inner))
        mix = received[p, :, :dim].astype(F32)
        quantized += scale * mix
        gradient += scale * received[p, :, dim : 2 * dim].astype(F32) + offset * mix
    quantized = quantized.astype(BF16)
    gradient = (gradient / SOFTMAX_HEAT).astype(BF16)
    for p in range(n_code):
        spread[p, :, :dim] = quantized
        spread[p, :, dim:] = gradient


def backward_kernel(prepared, where, *rest):
    if prepared:
        grad_out, codebook, codes, operands, inners, out, *rest = rest
    else:
        tokens, grad_out, codebook, codes, received, out, operands, inners, upper, lower, *rest = rest
    book, code_in, result, book_sem, code_sem, out_sem = rest
    tiles, width, dim = book.shape
    n_tokens = grad_out.shape[0]
    first = where[1] * tiles

    def fetch(t):
        at = pl.multiple_of((first + t) * width, width)
        return (
            pltpu.make_async_copy(codebook.at[pl.ds(at, width)], book.at[t], book_sem.at[t]),
            pltpu.make_async_copy(codes.at[first + t], code_in.at[t], code_sem.at[t]),
        )

    def start(t):
        for copy in fetch(t):
            copy.start()

    for t in range(min(AHEAD, tiles)):
        start(t)

    if not prepared:
        n_code, rows, _ = received.shape
        scales, _, inner = merged_stats(received)
        scale = jnp.zeros(inner.shape, F32)
        for p in range(n_code):
            scale = jnp.where(where[0] == p, scales[p], scale)
        for g in range(n_code):
            part = slice(g * rows, (g + 1) * rows)
            column = scale[:, 4 * g : 4 * g + 1]
            upper[part] = column * grad_out[part].astype(F32)
            lower[part] = column * (tokens[part].astype(F32) / SOFTMAX_HEAT)
            inners[part] = jnp.broadcast_to(inner[:, 4 * g : 4 * g + 1], (rows, 128))
        operands[0] = upper[...].T.astype(BF16)
        operands[1] = lower[...].T.astype(BF16)

    def send(t):
        return pltpu.make_async_copy(
            result.at[t], out.at[pl.ds(pl.multiple_of(t * width, width), width)], out_sem.at[t]
        )

    chunk = min(CHUNK, width)
    steps = [(t, slice(c, c + chunk)) for t in range(tiles) for c in range(0, width, chunk)]

    def gradient_of(step):
        t, c = step
        if c.start == 0:
            for copy in fetch(t):
                copy.wait()
            if t + AHEAD < tiles:
                start(t + AHEAD)
        return dot(grad_out[...], book[t, c], 1, 1)

    ahead = gradient_of(steps[0])
    for k, (t, c) in enumerate(steps):
        gradient = ahead
        if k + 1 < len(steps):
            ahead = gradient_of(steps[k + 1])
        code = code_in[t, :, c]
        inner = jnp.concatenate([inners[...]] * (chunk // 128), axis=1)
        score_gradient = (code.astype(F32) * (gradient - inner)).astype(BF16)
        value = dot(operands[0], code) + dot(operands[1], score_gradient)
        result[t, c] = value.astype(BF16).T
        if c.stop == width:
            send(t).start()
    for t in range(tiles):
        send(t).wait()


def add_kernel(n_parts, *refs):
    parts, out = refs[:n_parts], refs[n_parts]
    held, result, in_sem, out_sem = refs[n_parts + 1 :]
    steps, rows, _ = result.shape

    def fetch(i):
        at = pl.ds(i * rows, rows)
        return [
            pltpu.make_async_copy(part.at[at], held.at[j, i], in_sem.at[j, i])
            for j, part in enumerate(parts)
        ]

    def send(i):
        return pltpu.make_async_copy(result.at[i], out.at[pl.ds(i * rows, rows)], out_sem.at[i])

    for i in range(steps):
        for copy in fetch(i):
            copy.start()
    for i in range(steps):
        for copy in fetch(i):
            copy.wait()
        result[i] = sum(held[j, i].astype(F32) for j in range(n_parts))
        send(i).start()
    for i in range(steps):
        send(i).wait()


def unpack_kernel(gathered, quantized, gradient):
    n_code, rows, both = gathered.shape
    dim = both // 2
    for g in range(n_code):
        at = slice(g * rows, (g + 1) * rows)
        quantized[at] = gathered[g, :, :dim].astype(F32)
        gradient[at] = gathered[g, :, dim:].astype(F32)


def swap(value, axis, size, mask):
    return lax.ppermute(value, axis, [(i, i ^ mask) for i in range(size)])


def local(n_dp, n_code, tokens, codebook, noise, grad_out):
    n_tokens, dim = tokens.shape
    n_codes = codebook.shape[0]
    rows = n_tokens // n_code
    block = n_codes // n_dp
    width = min(1024, block)
    tiles = n_codes // width
    lanes = stat_lanes(n_code)
    products = 2 * n_tokens * n_codes * dim

    codes, sent = pl.pallas_call(
        functools.partial(forward_kernel, n_code),
        out_shape=(
            pltpu.HBM((tiles, n_tokens, width), BF16),
            jax.ShapeDtypeStruct((n_code, rows, 2 * dim + lanes), BF16),
        ),
        in_specs=[ANY, ANY, ANY, ANY],
        out_specs=(ANY, VMEM),
        scratch_shapes=[
            pltpu.VMEM((2 * n_tokens, dim), BF16),
            pltpu.VMEM((tiles, width, dim), BF16),
            pltpu.VMEM((tiles, n_tokens, width), BF16),
            pltpu.VMEM((2 * n_tokens, width), BF16),
            pltpu.VMEM((2 * n_tokens, width), BF16),
            pltpu.VMEM((n_tokens, 128), F32),
            pltpu.VMEM((n_tokens, 128), F32),
            pltpu.VMEM((2 * n_tokens, dim), F32),
            pltpu.SemaphoreType.DMA((2 * n_tokens // ROWS,)),
            pltpu.SemaphoreType.DMA((tiles,)),
            pltpu.SemaphoreType.DMA((tiles,)),
            pltpu.SemaphoreType.DMA((2,)),
        ],
        compiler_params=FULL,
        cost_estimate=pl.CostEstimate(
            flops=4 * products, bytes_accessed=24 * MIB, transcendentals=n_tokens * n_codes
        ),
        name="forward",
    )(tokens, grad_out, codebook, noise)

    received = lax.all_to_all(sent, "code", 0, 0, tiled=True)
    code_at = lax.axis_index("code")
    spread = pl.pallas_call(
        merge_kernel,
        out_shape=jax.ShapeDtypeStruct((n_code, rows, 2 * dim), BF16),
        in_specs=[SMEM, VMEM],
        out_specs=VMEM,
        compiler_params=SOME,
        name="merge",
    )(code_at[None], received)
    received, spread = lax.optimization_barrier((received, spread))
    gathered = lax.all_to_all(spread, "code", 0, 0, tiled=True)
    quantized, token_gradient = pl.pallas_call(
        unpack_kernel,
        out_shape=(jax.ShapeDtypeStruct((n_tokens, dim), F32),) * 2,
        in_specs=[VMEM],
        out_specs=(VMEM, VMEM),
        compiler_params=SOME,
        cost_estimate=pl.CostEstimate(
            flops=100 * products, bytes_accessed=400 * MIB, transcendentals=0
        ),
        name="unpack",
    )(gathered)

    block_tiles = block // width
    streams = [
        pltpu.VMEM((block_tiles, width, dim), BF16),
        pltpu.VMEM((block_tiles, n_tokens, width), BF16),
        pltpu.VMEM((block_tiles, width, dim), BF16),
        pltpu.SemaphoreType.DMA((block_tiles,)),
        pltpu.SemaphoreType.DMA((block_tiles,)),
        pltpu.SemaphoreType.DMA((block_tiles,)),
    ]
    block_shape = jax.ShapeDtypeStruct((block, dim), BF16)
    common = dict(
        compiler_params=MOST,
        cost_estimate=pl.CostEstimate(flops=1, bytes_accessed=1, transcendentals=0),
    )
    dp_at = lax.axis_index("dp")
    first, operands, inners = pl.pallas_call(
        functools.partial(backward_kernel, False),
        out_shape=(
            block_shape,
            jax.ShapeDtypeStruct((2, dim, n_tokens), BF16),
            jax.ShapeDtypeStruct((n_tokens, 128), F32),
        ),
        in_specs=[SMEM, VMEM, VMEM, ANY, ANY, VMEM],
        out_specs=(ANY, VMEM, VMEM),
        scratch_shapes=[
            pltpu.VMEM((n_tokens, dim), F32), pltpu.VMEM((n_tokens, dim), F32),
        ] + streams,
        name="backward_first",
        **common,
    )(jnp.stack([code_at, dp_at ^ (n_dp - 1)]), tokens, grad_out, codebook, codes, received)

    def backward(at):
        return pl.pallas_call(
            functools.partial(backward_kernel, True),
            out_shape=block_shape,
            in_specs=[SMEM, VMEM, ANY, ANY, VMEM, VMEM],
            out_specs=ANY,
            scratch_shapes=streams,
            name="backward",
            **common,
        )(jnp.stack([code_at, at]), grad_out, codebook, codes, operands, inners)

    blocks = [swap(first, "dp", n_dp, n_dp - 1)]
    blocks += [swap(backward(dp_at ^ d), "dp", n_dp, d) for d in range(1, n_dp - 1)]
    blocks.append(backward(dp_at))
    steps = max(block // 512, 1)
    own_rows = pl.pallas_call(
        functools.partial(add_kernel, n_dp),
        out_shape=jax.ShapeDtypeStruct((block, dim), F32),
        in_specs=[ANY] * n_dp,
        out_specs=ANY,
        scratch_shapes=[
            pltpu.VMEM((n_dp, steps, block // steps, dim), BF16),
            pltpu.VMEM((steps, block // steps, dim), F32),
            pltpu.SemaphoreType.DMA((n_dp, steps)),
            pltpu.SemaphoreType.DMA((steps,)),
        ],
        compiler_params=SOME,
        cost_estimate=pl.CostEstimate(
            flops=0, bytes_accessed=(2 * n_dp + 4) * block * dim, transcendentals=0
        ),
        name="add",
    )(*blocks)
    return quantized, token_gradient, own_rows[None]


def solution(mesh):
    n_dp, n_code = mesh.shape["dp"], mesh.shape["code"]
    in_specs = (P("dp", None), P("code", None), P("dp", "code"), P("dp", None))
    out_specs = (P("dp", None), P("dp", None), P("code", "dp", None))
    return jax.shard_map(
        functools.partial(local, n_dp, n_code),
        mesh=mesh, in_specs=in_specs, out_specs=out_specs, check_vma=False,
    )
```

```python
import functools

import jax
import jax.numpy as jnp
from jax import lax
from jax.experimental import pallas as pl
from jax.experimental.pallas import tpu as pltpu
from jax.sharding import PartitionSpec as P

SOFTMAX_HEAT = 0.5
SHARPNESS = 1.0 / SOFTMAX_HEAT
BF16 = jnp.bfloat16
F32 = jnp.float32
MIB = 1 << 20
CHUNK = 256
HIGH = 512
AHEAD = 3
PARTS = 4
ROWS = 64
LARGEST = 2.0**60
VMEM = pl.BlockSpec(memory_space=pltpu.VMEM)
SMEM = pl.BlockSpec(memory_space=pltpu.SMEM)
ANY = pl.BlockSpec(memory_space=pl.ANY)
FULL = pltpu.CompilerParams(vmem_limit_bytes=60 * MIB)
MOST = pltpu.CompilerParams(vmem_limit_bytes=56 * MIB)
SOME = pltpu.CompilerParams(vmem_limit_bytes=24 * MIB)


def dot(left, right, left_dim=1, right_dim=0):
    return lax.dot_general(
        left, right, (((left_dim,), (right_dim,)), ((), ())), preferred_element_type=F32
    )


def lane_groups(value):
    return [value[:, j : j + 128] for j in range(0, value.shape[1], 128)]


def stat_lanes(n_code):
    return max(8 * n_code, 128)


def high_low(value):
    high = value.astype(BF16).astype(F32)
    return high, (value - high).astype(BF16).astype(F32)


def forward_kernel(
    n_code, tokens, grad_out, codebook, noise, codes, sent,
    pair, book, noise_in, slot_a, slot_b, shifts, total, sums,
    pair_sem, book_sem, noise_sem, code_sem,
):
    tiles, n_tokens, width = codes.shape
    dim = tokens.shape[1]
    columns = [slice(c, c + CHUNK) for c in range(0, width, CHUNK)]
    slots = (slot_a, slot_b)

    def fetch(t):
        at = pl.multiple_of(t * width, width)
        return (
            pltpu.make_async_copy(codebook.at[pl.ds(at, width)], book.at[t], book_sem.at[t]),
            pltpu.make_async_copy(noise.at[:, pl.ds(at, width)], noise_in.at[t], noise_sem.at[t]),
        )

    def start(t):
        fetch(t)[0].start()
        at = pl.ds(pl.multiple_of(t * width, width), width)
        for r in range(0, n_tokens, n_tokens // PARTS):
            part = pl.ds(r, n_tokens // PARTS)
            pltpu.make_async_copy(
                noise.at[part, at], noise_in.at[t, part], noise_sem.at[t]
            ).start()

    def arrive(t):
        for copy in fetch(t):
            copy.wait()

    pair_copies = []
    for r in range(0, n_tokens, ROWS):
        for half, source in enumerate((tokens, grad_out)):
            pair_copies.append(
                pltpu.make_async_copy(
                    source.at[pl.ds(r, ROWS)],
                    pair.at[pl.ds(2 * r + half * ROWS, ROWS)],
                    pair_sem.at[len(pair_copies)],
                )
            )
    start(0)
    for copy in pair_copies:
        copy.start()
    for t in range(1, min(AHEAD + 1, tiles)):
        start(t)

    def logits(both, t, r, c):
        noise_part = (noise_in[t, r : r + ROWS, c] * BF16(SHARPNESS)).astype(F32)
        return both[2 * r : 2 * r + ROWS] + noise_part

    def raise_shift(t, some):
        for c in some:
            both = dot(pair[...], book[t, c], 1, 1)
            for r in range(0, n_tokens, ROWS):
                at = slice(r, r + ROWS)
                shifts[at] = functools.reduce(
                    jnp.maximum, lane_groups(logits(both, t, r, c)), shifts[at]
                )

    def store(t, s):
        return pltpu.make_async_copy(
            slots[s].at[pl.ds(0, n_tokens)], codes.at[t], code_sem.at[s]
        )

    def soften(t, s, fresh, last=None):
        if fresh is not None:
            @pl.when(fresh)
            def _():
                arrive(t)

                @pl.when(t + AHEAD < tiles)
                def _():
                    start(t + AHEAD)

        slot = slots[s]
        ahead = dot(pair[...], book[t, columns[0]], 1, 1)
        for k, c in enumerate(columns):
            both = ahead
            if k + 1 < len(columns):
                ahead = dot(pair[...], book[t, columns[k + 1]], 1, 1)
            elif last is not None:
                last()
            for r in range(0, n_tokens, ROWS):
                at = slice(r, r + ROWS)
                shift = jnp.concatenate([shifts[at]] * (CHUNK // 128), axis=1)
                weight = jnp.exp(logits(both, t, r, c) - shift)
                total[at] += sum(lane_groups(weight))
                slot[at, c] = weight.astype(BF16)
                gradient = both[2 * r + ROWS : 2 * r + 2 * ROWS]
                slot[n_tokens + r : n_tokens + r + ROWS, c] = (weight * gradient).astype(BF16)
        store(t, s).start()

    def accumulate(t, s):
        sums[...] += dot(slots[s][...], book[t])

    def attempt(state):
        again, _ = state
        fresh = again == 0
        shifts[...] = jnp.full(shifts.shape, -jnp.inf, F32)

        @pl.when(fresh)
        def _():
            raise_shift(0, columns[:2])

        @pl.when(jnp.logical_not(fresh))
        def _():
            def over(t, carry):
                raise_shift(t, columns)
                return carry

            lax.fori_loop(0, tiles, over, 0)

        shift = jnp.max(shifts[...], axis=1, keepdims=True).astype(BF16).astype(F32)
        shifts[...] = jnp.broadcast_to(shift, shifts.shape)
        total[...] = jnp.zeros(total.shape, F32)
        sums[...] = jnp.zeros(sums.shape, F32)
        soften(0, 0, None)

        def soften_pair(i, carry):
            @pl.when(i > 0)
            def _():
                store(2 * i - 1, 1).wait()

            soften(2 * i + 1, 1, fresh, lambda: accumulate(2 * i, 0))
            store(2 * i, 0).wait()
            soften(2 * i + 2, 0, fresh, lambda: accumulate(2 * i + 1, 1))
            return carry

        lax.fori_loop(0, tiles // 2 - 1, soften_pair, 0)
        if tiles > 2:
            store(tiles - 3, 1).wait()
        soften(tiles - 1, 1, fresh, lambda: accumulate(tiles - 2, 0))
        accumulate(tiles - 1, 1)
        store(tiles - 2, 0).wait()
        store(tiles - 1, 1).wait()
        fits = jnp.max(total[...]) < LARGEST
        return again + 1, jnp.logical_and(fresh, jnp.logical_not(fits))

    for copy in pair_copies:
        copy.wait()
    for r in range(0, n_tokens, ROWS):
        pair[2 * r : 2 * r + ROWS] = pair[2 * r : 2 * r + ROWS] * BF16(SHARPNESS)
    arrive(0)
    lax.while_loop(lambda state: state[1], attempt, (jnp.int32(0), jnp.bool_(True)))

    shift = shifts[:, :1]
    mix = sums[:n_tokens]
    pulled = sums[n_tokens:]
    own_total = jnp.sum(total[...], axis=1, keepdims=True)
    own_grad = jnp.concatenate(
        [pair[2 * r + ROWS : 2 * r + 2 * ROWS] for r in range(0, n_tokens, ROWS)], axis=0
    )
    own_inner = jnp.sum(own_grad.astype(F32) * mix, axis=1, keepdims=True)
    mean = own_inner / own_total
    rows = n_tokens // n_code
    lanes = stat_lanes(n_code)
    half = lanes // 2
    lane = lax.broadcasted_iota(jnp.int32, (rows, lanes), 1)
    stats = jnp.zeros((rows, lanes), F32)
    parts = high_low(own_total) + high_low(own_inner)
    for g in range(n_code):
        at = slice(g * rows, (g + 1) * rows)
        for i, part in enumerate(parts):
            stats = jnp.where(lane == 4 * g + i, part[at], stats)
        stats = jnp.where((lane - half) // 4 == g, shift[at], stats)
    stats = stats.astype(BF16)
    for g in range(n_code):
        at = slice(g * rows, (g + 1) * rows)
        sent[g, :, :dim] = mix[at].astype(BF16)
        sent[g, :, dim : 2 * dim] = (pulled[at] - mean[at] * mix[at]).astype(BF16)
        sent[g, :, 2 * dim :] = stats


def roll_left(value, by):
    return pltpu.roll(value, value.shape[1] - by, 1)


def merged_stats(received):
    n_code = received.shape[0]
    lanes = stat_lanes(n_code)
    stats = [received[p, :, received.shape[2] - lanes :].astype(F32) for p in range(n_code)]
    top = functools.reduce(jnp.maximum, stats)
    scales = [roll_left(jnp.exp(s - top), lanes // 2) for s in stats]
    pairs = [s + roll_left(s, 1) for s in stats]
    inners = [roll_left(s, 2) for s in pairs]
    total = sum(a * s for a, s in zip(scales, pairs))
    inner = sum(a * s for a, s in zip(scales, inners)) / total
    means = [i / s for i, s in zip(inners, pairs)]
    return [a / total for a in scales], means, inner


def merge_kernel(me, received, spread):
    n_code, rows, _ = received.shape
    dim = spread.shape[2] // 2
    scales, means, inner = merged_stats(received)
    lane = lax.broadcasted_iota(jnp.int32, inner.shape, 1)
    mine = lane == 4 * me[0]

    def column(value):
        return jnp.sum(jnp.where(mine, value, 0.0), axis=1, keepdims=True)

    quantized = jnp.zeros((rows, dim), F32)
    gradient = jnp.zeros((rows, dim), F32)
    for p in range(n_code):
        scale = column(scales[p])
        offset = column(scales[p] * (means[p] - inner))
        mix = received[p, :, :dim].astype(F32)
        quantized += scale * mix
        gradient += scale * received[p, :, dim : 2 * dim].astype(F32) + offset * mix
    quantized = quantized.astype(BF16)
    gradient = (gradient / SOFTMAX_HEAT).astype(BF16)
    for p in range(n_code):
        spread[p, :, :dim] = quantized
        spread[p, :, dim:] = gradient


def turn_kernel(grad_out, codes, turned, turned_grad, held, result, in_sem, out_sem):
    tiles, _, width = held.shape

    def fetch(t):
        return pltpu.make_async_copy(codes.at[t], held.at[t], in_sem.at[t])

    def send(t):
        at = pl.ds(pl.multiple_of(t * width, width), width)
        return pltpu.make_async_copy(result.at[t], turned.at[at], out_sem.at[t])

    for t in range(tiles):
        fetch(t).start()
    turned_grad[...] = grad_out[...].T

    def turn(t, carry):
        fetch(t).wait()
        for c in range(0, width, CHUNK):
            result[t, c : c + CHUNK] = held[t, :, c : c + CHUNK].T
        send(t).start()
        return carry

    lax.fori_loop(0, tiles, turn, 0)
    for t in range(tiles):
        send(t).wait()


def backward_kernel(prepared, block, *rest):
    if prepared:
        turned_grad, codebook, turned, operands, inners, out, *rest = rest
    else:
        code_at, tokens, grad_out, turned_grad, codebook, turned, received, *rest = rest
        out, operands, inners, spread_inner, *rest = rest
    book, code_in, result, book_sem, code_sem, out_sem = rest
    tiles, width, dim = book.shape
    n_tokens = turned_grad.shape[1]

    def fetch(t):
        at = pl.ds(pl.multiple_of((block[0] * tiles + t) * width, width), width)
        return (
            pltpu.make_async_copy(codebook.at[at], book.at[t], book_sem.at[t]),
            pltpu.make_async_copy(turned.at[at], code_in.at[t], code_sem.at[t]),
        )

    def start(t):
        for copy in fetch(t):
            copy.start()

    for t in range(min(AHEAD, tiles)):
        start(t)

    if not prepared:
        n_code, rows, _ = received.shape
        scales, _, inner = merged_stats(received)
        scale = jnp.zeros(inner.shape, F32)
        for p in range(n_code):
            scale = jnp.where(code_at[0] == p, scales[p], scale)
        for g in range(n_code):
            part = slice(g * rows, (g + 1) * rows)
            column = scale[:, 4 * g : 4 * g + 1]
            operands[0, part] = (column * grad_out[part].astype(F32)).astype(BF16)
            operands[1, part] = (column * (tokens[part].astype(F32) / SOFTMAX_HEAT)).astype(BF16)
            spread_inner[part] = jnp.broadcast_to(inner[:, 4 * g : 4 * g + 1], (rows, 128))
        inners[...] = spread_inner[...].T[:8]

    def send(t):
        return pltpu.make_async_copy(
            result.at[t], out.at[pl.ds(pl.multiple_of(t * width, width), width)], out_sem.at[t]
        )

    high = min(HIGH, width)
    steps = [(t, slice(c, c + high)) for t in range(tiles) for c in range(0, width, high)]

    def gradient_of(step):
        t, c = step
        if c.start == 0:
            for copy in fetch(t):
                copy.wait()
            if t + AHEAD < tiles:
                start(t + AHEAD)
        return dot(book[t, c], turned_grad[...])

    ahead = gradient_of(steps[0])
    for k, (t, c) in enumerate(steps):
        gradient = ahead
        if k + 1 < len(steps):
            ahead = gradient_of(steps[k + 1])
        code = code_in[t, c]
        score_gradient = (code.astype(F32) * (gradient - inners[:1])).astype(BF16)
        value = dot(code, operands[0]) + dot(score_gradient, operands[1])
        result[t, c] = value.astype(BF16)
        if c.stop == width:
            send(t).start()
    for t in range(tiles):
        send(t).wait()


def add_kernel(n_parts, *refs):
    parts, out = refs[:n_parts], refs[n_parts]
    held, result, in_sem, out_sem = refs[n_parts + 1 :]
    steps, rows, _ = result.shape

    def fetch(i):
        at = pl.ds(i * rows, rows)
        return [
            pltpu.make_async_copy(part.at[at], held.at[j, i], in_sem.at[j, i])
            for j, part in enumerate(parts)
        ]

    def send(i):
        return pltpu.make_async_copy(result.at[i], out.at[pl.ds(i * rows, rows)], out_sem.at[i])

    for i in range(steps):
        for copy in fetch(i):
            copy.start()
    for i in range(steps):
        for copy in fetch(i):
            copy.wait()
        result[i] = sum(held[j, i].astype(F32) for j in range(n_parts))
        send(i).start()
    for i in range(steps):
        send(i).wait()


def unpack_kernel(gathered, quantized, gradient):
    n_code, rows, both = gathered.shape
    dim = both // 2
    for g in range(n_code):
        at = slice(g * rows, (g + 1) * rows)
        quantized[at] = gathered[g, :, :dim].astype(F32)
        gradient[at] = gathered[g, :, dim:].astype(F32)


def swap(value, axis, size, mask):
    return lax.ppermute(value, axis, [(i, i ^ mask) for i in range(size)])


def local(n_dp, n_code, tokens, codebook, noise, grad_out):
    n_tokens, dim = tokens.shape
    n_codes = codebook.shape[0]
    rows = n_tokens // n_code
    block = n_codes // n_dp
    width = min(1024, block)
    tiles = n_codes // width
    lanes = stat_lanes(n_code)
    products = 2 * n_tokens * n_codes * dim

    codes, sent = pl.pallas_call(
        functools.partial(forward_kernel, n_code),
        out_shape=(
            pltpu.HBM((tiles, n_tokens, width), BF16),
            jax.ShapeDtypeStruct((n_code, rows, 2 * dim + lanes), BF16),
        ),
        in_specs=[ANY, ANY, ANY, ANY],
        out_specs=(ANY, VMEM),
        scratch_shapes=[
            pltpu.VMEM((2 * n_tokens, dim), BF16),
            pltpu.VMEM((tiles, width, dim), BF16),
            pltpu.VMEM((tiles, n_tokens, width), BF16),
            pltpu.VMEM((2 * n_tokens, width), BF16),
            pltpu.VMEM((2 * n_tokens, width), BF16),
            pltpu.VMEM((n_tokens, 128), F32),
            pltpu.VMEM((n_tokens, 128), F32),
            pltpu.VMEM((2 * n_tokens, dim), F32),
            pltpu.SemaphoreType.DMA((2 * n_tokens // ROWS,)),
            pltpu.SemaphoreType.DMA((tiles,)),
            pltpu.SemaphoreType.DMA((tiles,)),
            pltpu.SemaphoreType.DMA((2,)),
        ],
        compiler_params=FULL,
        cost_estimate=pl.CostEstimate(
            flops=4 * products, bytes_accessed=24 * MIB, transcendentals=n_tokens * n_codes
        ),
        name="forward",
    )(tokens, grad_out, codebook, noise)

    received = lax.all_to_all(sent, "code", 0, 0, tiled=True)
    turned, turned_grad = pl.pallas_call(
        turn_kernel,
        out_shape=(
            pltpu.HBM((n_codes, n_tokens), BF16),
            jax.ShapeDtypeStruct((dim, n_tokens), BF16),
        ),
        in_specs=[VMEM, ANY],
        out_specs=(ANY, VMEM),
        scratch_shapes=[
            pltpu.VMEM((tiles, n_tokens, width), BF16),
            pltpu.VMEM((tiles, width, n_tokens), BF16),
            pltpu.SemaphoreType.DMA((tiles,)),
            pltpu.SemaphoreType.DMA((tiles,)),
        ],
        compiler_params=FULL,
        cost_estimate=pl.CostEstimate(
            flops=0, bytes_accessed=4 * n_tokens * n_codes, transcendentals=0
        ),
        name="turn",
    )(grad_out, codes)
    received, turned, turned_grad = lax.optimization_barrier((received, turned, turned_grad))
    code_at = lax.axis_index("code")
    spread = pl.pallas_call(
        merge_kernel,
        out_shape=jax.ShapeDtypeStruct((n_code, rows, 2 * dim), BF16),
        in_specs=[SMEM, VMEM],
        out_specs=VMEM,
        compiler_params=SOME,
        name="merge",
    )(code_at[None], received)
    received, spread = lax.optimization_barrier((received, spread))
    gathered = lax.all_to_all(spread, "code", 0, 0, tiled=True)
    quantized, token_gradient = pl.pallas_call(
        unpack_kernel,
        out_shape=(jax.ShapeDtypeStruct((n_tokens, dim), F32),) * 2,
        in_specs=[VMEM],
        out_specs=(VMEM, VMEM),
        compiler_params=SOME,
        cost_estimate=pl.CostEstimate(
            flops=100 * products, bytes_accessed=400 * MIB, transcendentals=0
        ),
        name="unpack",
    )(gathered)

    block_tiles = block // width
    streams = [
        pltpu.VMEM((block_tiles, width, dim), BF16),
        pltpu.VMEM((block_tiles, width, n_tokens), BF16),
        pltpu.VMEM((block_tiles, width, dim), BF16),
        pltpu.SemaphoreType.DMA((block_tiles,)),
        pltpu.SemaphoreType.DMA((block_tiles,)),
        pltpu.SemaphoreType.DMA((block_tiles,)),
    ]
    block_shape = jax.ShapeDtypeStruct((block, dim), BF16)
    common = dict(
        compiler_params=MOST,
        cost_estimate=pl.CostEstimate(flops=1, bytes_accessed=1, transcendentals=0),
    )
    dp_at = lax.axis_index("dp")
    first, operands, inners = pl.pallas_call(
        functools.partial(backward_kernel, False),
        out_shape=(
            block_shape,
            jax.ShapeDtypeStruct((2, n_tokens, dim), BF16),
            jax.ShapeDtypeStruct((8, n_tokens), F32),
        ),
        in_specs=[SMEM, SMEM, VMEM, VMEM, VMEM, ANY, ANY, VMEM],
        out_specs=(ANY, VMEM, VMEM),
        scratch_shapes=[pltpu.VMEM((n_tokens, 128), F32)] + streams,
        name="backward_first",
        **common,
    )(
        (dp_at ^ (n_dp - 1))[None], code_at[None], tokens, grad_out, turned_grad, codebook,
        turned, received,
    )

    def backward(at):
        return pl.pallas_call(
            functools.partial(backward_kernel, True),
            out_shape=block_shape,
            in_specs=[SMEM, VMEM, ANY, ANY, VMEM, VMEM],
            out_specs=ANY,
            scratch_shapes=streams,
            name="backward",
            **common,
        )(at[None], turned_grad, codebook, turned, operands, inners)

    blocks = [swap(first, "dp", n_dp, n_dp - 1)]
    blocks += [swap(backward(dp_at ^ d), "dp", n_dp, d) for d in range(1, n_dp - 1)]
    blocks.append(backward(dp_at))
    steps = max(block // 512, 1)
    own_rows = pl.pallas_call(
        functools.partial(add_kernel, n_dp),
        out_shape=jax.ShapeDtypeStruct((block, dim), F32),
        in_specs=[ANY] * n_dp,
        out_specs=ANY,
        scratch_shapes=[
            pltpu.VMEM((n_dp, steps, block // steps, dim), BF16),
            pltpu.VMEM((steps, block // steps, dim), F32),
            pltpu.SemaphoreType.DMA((n_dp, steps)),
            pltpu.SemaphoreType.DMA((steps,)),
        ],
        compiler_params=SOME,
        cost_estimate=pl.CostEstimate(
            flops=0, bytes_accessed=(2 * n_dp + 4) * block * dim, transcendentals=0
        ),
        name="add",
    )(*blocks)
    return quantized, token_gradient, own_rows[None]


def solution(mesh):
    n_dp, n_code = mesh.shape["dp"], mesh.shape["code"]
    in_specs = (P("dp", None), P("code", None), P("dp", "code"), P("dp", None))
    out_specs = (P("dp", None), P("dp", None), P("code", "dp", None))
    return jax.shard_map(
        functools.partial(local, n_dp, n_code),
        mesh=mesh, in_specs=in_specs, out_specs=out_specs, check_vma=False,
    )
```

```python
import functools

import jax
import jax.numpy as jnp
from jax import lax
from jax.experimental import pallas as pl
from jax.experimental.pallas import tpu as pltpu
from jax.sharding import PartitionSpec as P

SOFTMAX_HEAT = 0.5
SHARPNESS = 1.0 / SOFTMAX_HEAT
BF16 = jnp.bfloat16
F32 = jnp.float32
MIB = 1 << 20
CHUNK = 512
AHEAD = 3
ROWS = 64
LARGEST = 2.0**60
VMEM = pl.BlockSpec(memory_space=pltpu.VMEM)
SMEM = pl.BlockSpec(memory_space=pltpu.SMEM)
ANY = pl.BlockSpec(memory_space=pl.ANY)
FULL = pltpu.CompilerParams(vmem_limit_bytes=60 * MIB)
MOST = pltpu.CompilerParams(vmem_limit_bytes=56 * MIB)
SOME = pltpu.CompilerParams(vmem_limit_bytes=24 * MIB)


def dot(left, right, left_dim=1, right_dim=0):
    return lax.dot_general(
        left, right, (((left_dim,), (right_dim,)), ((), ())), preferred_element_type=F32
    )


def lane_groups(value):
    return [value[:, j : j + 128] for j in range(0, value.shape[1], 128)]


def stat_lanes(n_code):
    return max(8 * n_code, 128)


def high_low(value):
    high = value.astype(BF16).astype(F32)
    return high, (value - high).astype(BF16).astype(F32)


def forward_kernel(
    n_code, tokens, grad_out, codebook, noise, codes, sent, mix, mean,
    own_tokens, own_grad, book, noise_in, slot_a, slot_b, shifts, total,
    own_sem, book_sem, noise_sem, code_sem,
):
    tiles, n_tokens, width = codes.shape
    dim = tokens.shape[1]
    columns = [slice(c, c + CHUNK) for c in range(0, width, CHUNK)]
    slots = (slot_a, slot_b)

    def fetch(t):
        at = pl.multiple_of(t * width, width)
        return (
            pltpu.make_async_copy(codebook.at[pl.ds(at, width)], book.at[t], book_sem.at[t]),
            pltpu.make_async_copy(noise.at[:, pl.ds(at, width)], noise_in.at[t], noise_sem.at[t]),
        )

    def start(t):
        for copy in fetch(t):
            copy.start()

    def arrive(t):
        for copy in fetch(t):
            copy.wait()

    own_copies = (
        pltpu.make_async_copy(tokens, own_tokens, own_sem.at[0]),
        pltpu.make_async_copy(grad_out, own_grad, own_sem.at[1]),
    )
    own_copies[0].start()
    for t in range(min(AHEAD + 1, tiles)):
        start(t)
    own_copies[1].start()

    def score(t, c):
        return dot(own_tokens[...], book[t, c], 1, 1)

    def logits(scores, t, at, c):
        return scores[at] + (noise_in[t, at, c] * BF16(SHARPNESS)).astype(F32)

    row_parts = [slice(r, r + ROWS) for r in range(0, n_tokens, ROWS)]

    def raise_shift(t, some):
        for c in some:
            scores = score(t, c)
            for at in row_parts:
                shifts[at] = functools.reduce(
                    jnp.maximum, lane_groups(logits(scores, t, at, c)), shifts[at]
                )

    def store(t, s):
        return pltpu.make_async_copy(slots[s], codes.at[t], code_sem.at[s])

    def soften(t, s, fresh, last=None):
        if fresh is not None:
            @pl.when(fresh)
            def _():
                arrive(t)

                @pl.when(t + AHEAD < tiles)
                def _():
                    start(t + AHEAD)

        slot = slots[s]
        ahead = score(t, columns[0])
        for k, c in enumerate(columns):
            scores = ahead
            if k + 1 < len(columns):
                ahead = score(t, columns[k + 1])
            elif last is not None:
                last()
            for at in row_parts:
                shift = jnp.concatenate([shifts[at]] * (CHUNK // 128), axis=1)
                weight = jnp.exp(logits(scores, t, at, c) - shift)
                total[at] += sum(lane_groups(weight))
                slot[at, c] = weight.astype(BF16)
        store(t, s).start()

    def accumulate(t, s):
        mix[...] += dot(slots[s][...], book[t])

    def attempt(state):
        again, _ = state
        fresh = again == 0
        shifts[...] = jnp.full(shifts.shape, -jnp.inf, F32)

        @pl.when(fresh)
        def _():
            raise_shift(0, columns[:1])

        @pl.when(jnp.logical_not(fresh))
        def _():
            def over(t, carry):
                raise_shift(t, columns)
                return carry

            lax.fori_loop(0, tiles, over, 0)

        shift = jnp.max(shifts[...], axis=1, keepdims=True).astype(BF16).astype(F32)
        shifts[...] = jnp.broadcast_to(shift, shifts.shape)
        total[...] = jnp.zeros(total.shape, F32)
        mix[...] = jnp.zeros(mix.shape, F32)
        soften(0, 0, None)

        def soften_pair(i, carry):
            @pl.when(i > 0)
            def _():
                store(2 * i - 1, 1).wait()

            soften(2 * i + 1, 1, fresh, lambda: accumulate(2 * i, 0))
            store(2 * i, 0).wait()
            soften(2 * i + 2, 0, fresh, lambda: accumulate(2 * i + 1, 1))
            return carry

        lax.fori_loop(0, tiles // 2 - 1, soften_pair, 0)
        if tiles > 2:
            store(tiles - 3, 1).wait()
        soften(tiles - 1, 1, fresh, lambda: accumulate(tiles - 2, 0))
        accumulate(tiles - 1, 1)
        store(tiles - 2, 0).wait()
        store(tiles - 1, 1).wait()
        fits = jnp.max(total[...]) < LARGEST
        return again + 1, jnp.logical_and(fresh, jnp.logical_not(fits))

    own_copies[0].wait()
    own_tokens[...] = own_tokens[...] * BF16(SHARPNESS)
    arrive(0)
    lax.while_loop(lambda state: state[1], attempt, (jnp.int32(0), jnp.bool_(True)))

    own_copies[1].wait()
    shift = shifts[:, :1]
    own_total = jnp.sum(total[...], axis=1, keepdims=True)
    own_inner = jnp.sum(own_grad[...].astype(F32) * mix[...], axis=1, keepdims=True)
    mean[...] = jnp.broadcast_to(own_inner / own_total, mean.shape)
    rows = n_tokens // n_code
    lanes = stat_lanes(n_code)
    half = lanes // 2
    lane = lax.broadcasted_iota(jnp.int32, (rows, lanes), 1)
    stats = jnp.zeros((rows, lanes), F32)
    parts = high_low(own_total) + high_low(own_inner)
    for g in range(n_code):
        at = slice(g * rows, (g + 1) * rows)
        for i, part in enumerate(parts):
            stats = jnp.where(lane == 4 * g + i, part[at], stats)
        stats = jnp.where((lane - half) // 4 == g, shift[at], stats)
    stats = stats.astype(BF16)
    for g in range(n_code):
        sent[g, :, :dim] = mix[g * rows : (g + 1) * rows].astype(BF16)
        sent[g, :, dim:] = stats


def pull_kernel(
    grad_out, codebook, codes, mix, mean, sent,
    book, code_in, slot_a, slot_b, pulled, book_sem, code_sem,
):
    tiles, width, dim = book.shape
    n_code, rows, _ = sent.shape
    slots = (slot_a, slot_b)
    steps = [(t, slice(c, c + CHUNK)) for t in range(tiles) for c in range(0, width, CHUNK)]

    def fetch(t):
        at = pl.ds(t * width, width)
        return (
            pltpu.make_async_copy(codebook.at[at], book.at[t], book_sem.at[t]),
            pltpu.make_async_copy(codes.at[t], code_in.at[t], code_sem.at[t]),
        )

    def start(t):
        for copy in fetch(t):
            copy.start()

    def gradient_of(step):
        t, c = step
        if c.start == 0:
            for copy in fetch(t):
                copy.wait()
            if t + AHEAD < tiles:
                start(t + AHEAD)
        return dot(grad_out[...], book[t, c], 1, 1)

    for t in range(min(AHEAD, tiles)):
        start(t)
    pulled[...] = jnp.zeros(pulled.shape, F32)
    ahead = gradient_of(steps[0])
    for k, (t, c) in enumerate(steps):
        gradient = ahead
        if k + 1 < len(steps):
            ahead = gradient_of(steps[k + 1])
        if c.start == 0 and t > 0:
            pulled[...] += dot(slots[(t - 1) % 2][...], book[t - 1])
        slots[t % 2][:, c] = (code_in[t, :, c].astype(F32) * gradient).astype(BF16)
    pulled[...] += dot(slots[(tiles - 1) % 2][...], book[tiles - 1])
    for g in range(n_code):
        at = slice(g * rows, (g + 1) * rows)
        means = jnp.concatenate([mean[at]] * (dim // 128), axis=1)
        sent[g] = (pulled[at] - means * mix[at]).astype(BF16)


def roll_left(value, by):
    return pltpu.roll(value, value.shape[1] - by, 1)


def merged_stats(received):
    n_code = received.shape[0]
    lanes = stat_lanes(n_code)
    stats = [received[p, :, received.shape[2] - lanes :].astype(F32) for p in range(n_code)]
    top = functools.reduce(jnp.maximum, stats)
    scales = [roll_left(jnp.exp(s - top), lanes // 2) for s in stats]
    pairs = [s + roll_left(s, 1) for s in stats]
    inners = [roll_left(s, 2) for s in pairs]
    total = sum(a * s for a, s in zip(scales, pairs))
    inner = sum(a * s for a, s in zip(scales, inners)) / total
    means = [i / s for i, s in zip(inners, pairs)]
    return [a / total for a in scales], means, inner


def merge_kernel(me, received, received_pulled, spread):
    n_code, rows, _ = received.shape
    dim = spread.shape[2] // 2
    scales, means, inner = merged_stats(received)
    lane = lax.broadcasted_iota(jnp.int32, inner.shape, 1)
    mine = lane == 4 * me[0]

    def column(value):
        return jnp.sum(jnp.where(mine, value, 0.0), axis=1, keepdims=True)

    quantized = jnp.zeros((rows, dim), F32)
    gradient = jnp.zeros((rows, dim), F32)
    for p in range(n_code):
        scale = column(scales[p])
        offset = column(scales[p] * (means[p] - inner))
        mix = received[p, :, :dim].astype(F32)
        quantized += scale * mix
        gradient += scale * received_pulled[p].astype(F32) + offset * mix
    quantized = quantized.astype(BF16)
    gradient = (gradient / SOFTMAX_HEAT).astype(BF16)
    for p in range(n_code):
        spread[p, :, :dim] = quantized
        spread[p, :, dim:] = gradient


def backward_kernel(prepared, block, *rest):
    if prepared:
        grad_out, codebook, codes, operands, inners, out, *rest = rest
    else:
        code_at, tokens, grad_out, codebook, codes, received, out, operands, inners, upper, lower, *rest = rest
    book, code_in, result, book_sem, code_sem, out_sem = rest
    tiles, width, dim = book.shape
    n_tokens = grad_out.shape[0]
    first = block[0] * tiles

    def fetch(t):
        at = pl.multiple_of((first + t) * width, width)
        return (
            pltpu.make_async_copy(codebook.at[pl.ds(at, width)], book.at[t], book_sem.at[t]),
            pltpu.make_async_copy(codes.at[first + t], code_in.at[t], code_sem.at[t]),
        )

    def start(t):
        for copy in fetch(t):
            copy.start()

    for t in range(min(AHEAD, tiles)):
        start(t)

    if not prepared:
        n_code, rows, _ = received.shape
        scales, _, inner = merged_stats(received)
        scale = jnp.zeros(inner.shape, F32)
        for p in range(n_code):
            scale = jnp.where(code_at[0] == p, scales[p], scale)
        for g in range(n_code):
            part = slice(g * rows, (g + 1) * rows)
            column = scale[:, 4 * g : 4 * g + 1]
            upper[part] = column * grad_out[part].astype(F32)
            lower[part] = column * (tokens[part].astype(F32) / SOFTMAX_HEAT)
            inners[part] = jnp.broadcast_to(inner[:, 4 * g : 4 * g + 1], (rows, 128))
        operands[0] = upper[...].T.astype(BF16)
        operands[1] = lower[...].T.astype(BF16)

    def send(t):
        return pltpu.make_async_copy(
            result.at[t], out.at[pl.ds(pl.multiple_of(t * width, width), width)], out_sem.at[t]
        )

    chunk = min(CHUNK, width)
    steps = [(t, slice(c, c + chunk)) for t in range(tiles) for c in range(0, width, chunk)]

    def gradient_of(step):
        t, c = step
        if c.start == 0:
            for copy in fetch(t):
                copy.wait()
            if t + AHEAD < tiles:
                start(t + AHEAD)
        return dot(grad_out[...], book[t, c], 1, 1)

    ahead = gradient_of(steps[0])
    for k, (t, c) in enumerate(steps):
        gradient = ahead
        if k + 1 < len(steps):
            ahead = gradient_of(steps[k + 1])
        code = code_in[t, :, c]
        inner = jnp.concatenate([inners[...]] * (chunk // 128), axis=1)
        score_gradient = (code.astype(F32) * (gradient - inner)).astype(BF16)
        value = dot(operands[0], code) + dot(operands[1], score_gradient)
        result[t, c] = value.astype(BF16).T
        if c.stop == width:
            send(t).start()
    for t in range(tiles):
        send(t).wait()


def add_kernel(n_parts, *refs):
    parts, out = refs[:n_parts], refs[n_parts]
    held, result, in_sem, out_sem = refs[n_parts + 1 :]
    steps, rows, _ = result.shape

    def fetch(i):
        at = pl.ds(i * rows, rows)
        return [
            pltpu.make_async_copy(part.at[at], held.at[j, i], in_sem.at[j, i])
            for j, part in enumerate(parts)
        ]

    def send(i):
        return pltpu.make_async_copy(result.at[i], out.at[pl.ds(i * rows, rows)], out_sem.at[i])

    for i in range(steps):
        for copy in fetch(i):
            copy.start()
    for i in range(steps):
        for copy in fetch(i):
            copy.wait()
        result[i] = sum(held[j, i].astype(F32) for j in range(n_parts))
        send(i).start()
    for i in range(steps):
        send(i).wait()


def unpack_kernel(gathered, quantized, gradient):
    n_code, rows, both = gathered.shape
    dim = both // 2
    for g in range(n_code):
        at = slice(g * rows, (g + 1) * rows)
        quantized[at] = gathered[g, :, :dim].astype(F32)
        gradient[at] = gathered[g, :, dim:].astype(F32)


def swap(value, axis, size, mask):
    return lax.ppermute(value, axis, [(i, i ^ mask) for i in range(size)])


def local(n_dp, n_code, tokens, codebook, noise, grad_out):
    n_tokens, dim = tokens.shape
    n_codes = codebook.shape[0]
    rows = n_tokens // n_code
    block = n_codes // n_dp
    width = min(1024, block)
    tiles = n_codes // width
    lanes = stat_lanes(n_code)
    products = 2 * n_tokens * n_codes * dim

    codes, sent, mix, mean = pl.pallas_call(
        functools.partial(forward_kernel, n_code),
        out_shape=(
            pltpu.HBM((tiles, n_tokens, width), BF16),
            jax.ShapeDtypeStruct((n_code, rows, dim + lanes), BF16),
            jax.ShapeDtypeStruct((n_tokens, dim), F32),
            jax.ShapeDtypeStruct((n_tokens, 128), F32),
        ),
        in_specs=[ANY, ANY, ANY, ANY],
        out_specs=(ANY, VMEM, VMEM, VMEM),
        scratch_shapes=[
            pltpu.VMEM((n_tokens, dim), BF16),
            pltpu.VMEM((n_tokens, dim), BF16),
            pltpu.VMEM((tiles, width, dim), BF16),
            pltpu.VMEM((tiles, n_tokens, width), BF16),
            pltpu.VMEM((n_tokens, width), BF16),
            pltpu.VMEM((n_tokens, width), BF16),
            pltpu.VMEM((n_tokens, 128), F32),
            pltpu.VMEM((n_tokens, 128), F32),
            pltpu.SemaphoreType.DMA((2,)),
            pltpu.SemaphoreType.DMA((tiles,)),
            pltpu.SemaphoreType.DMA((tiles,)),
            pltpu.SemaphoreType.DMA((2,)),
        ],
        compiler_params=FULL,
        cost_estimate=pl.CostEstimate(
            flops=2 * products, bytes_accessed=20 * MIB, transcendentals=n_tokens * n_codes
        ),
        name="forward",
    )(tokens, grad_out, codebook, noise)
    received = lax.all_to_all(sent, "code", 0, 0, tiled=True)

    sent_pulled = pl.pallas_call(
        pull_kernel,
        out_shape=jax.ShapeDtypeStruct((n_code, rows, dim), BF16),
        in_specs=[VMEM, ANY, ANY, VMEM, VMEM],
        out_specs=VMEM,
        scratch_shapes=[
            pltpu.VMEM((tiles, width, dim), BF16),
            pltpu.VMEM((tiles, n_tokens, width), BF16),
            pltpu.VMEM((n_tokens, width), BF16),
            pltpu.VMEM((n_tokens, width), BF16),
            pltpu.VMEM((n_tokens, dim), F32),
            pltpu.SemaphoreType.DMA((tiles,)),
            pltpu.SemaphoreType.DMA((tiles,)),
        ],
        compiler_params=FULL,
        cost_estimate=pl.CostEstimate(
            flops=2 * products, bytes_accessed=12 * MIB, transcendentals=0
        ),
        name="pull",
    )(grad_out, codebook, codes, mix, mean)
    received_pulled = lax.all_to_all(sent_pulled, "code", 0, 0, tiled=True)

    code_at = lax.axis_index("code")
    dp_at = lax.axis_index("dp")
    block_tiles = block // width
    streams = [
        pltpu.VMEM((block_tiles, width, dim), BF16),
        pltpu.VMEM((block_tiles, n_tokens, width), BF16),
        pltpu.VMEM((block_tiles, width, dim), BF16),
        pltpu.SemaphoreType.DMA((block_tiles,)),
        pltpu.SemaphoreType.DMA((block_tiles,)),
        pltpu.SemaphoreType.DMA((block_tiles,)),
    ]
    block_shape = jax.ShapeDtypeStruct((block, dim), BF16)
    common = dict(
        compiler_params=MOST,
        cost_estimate=pl.CostEstimate(
            flops=3 * products // n_dp, bytes_accessed=16 * MIB // n_dp, transcendentals=0
        ),
    )
    first, operands, inners = pl.pallas_call(
        functools.partial(backward_kernel, False),
        out_shape=(
            block_shape,
            jax.ShapeDtypeStruct((2, dim, n_tokens), BF16),
            jax.ShapeDtypeStruct((n_tokens, 128), F32),
        ),
        in_specs=[SMEM, SMEM, VMEM, VMEM, ANY, ANY, VMEM],
        out_specs=(ANY, VMEM, VMEM),
        scratch_shapes=[
            pltpu.VMEM((n_tokens, dim), F32), pltpu.VMEM((n_tokens, dim), F32),
        ] + streams,
        name="backward_first",
        **common,
    )(
        (dp_at ^ (n_dp - 1))[None], code_at[None], tokens, grad_out, codebook, codes, received
    )
    received_pulled, operands = lax.optimization_barrier((received_pulled, operands))
    spread = pl.pallas_call(
        merge_kernel,
        out_shape=jax.ShapeDtypeStruct((n_code, rows, 2 * dim), BF16),
        in_specs=[SMEM, VMEM, VMEM],
        out_specs=VMEM,
        compiler_params=SOME,
        name="merge",
    )(code_at[None], received, received_pulled)
    spread, operands = lax.optimization_barrier((spread, operands))
    gathered = lax.all_to_all(spread, "code", 0, 0, tiled=True)

    def backward(at):
        return pl.pallas_call(
            functools.partial(backward_kernel, True),
            out_shape=block_shape,
            in_specs=[SMEM, VMEM, ANY, ANY, VMEM, VMEM],
            out_specs=ANY,
            scratch_shapes=streams,
            name="backward",
            **common,
        )(at[None], grad_out, codebook, codes, operands, inners)

    blocks = [swap(first, "dp", n_dp, n_dp - 1)]
    blocks += [swap(backward(dp_at ^ d), "dp", n_dp, d) for d in range(1, n_dp - 1)]
    blocks.append(backward(dp_at))
    steps = max(block // 512, 1)
    own_rows = pl.pallas_call(
        functools.partial(add_kernel, n_dp),
        out_shape=jax.ShapeDtypeStruct((block, dim), F32),
        in_specs=[ANY] * n_dp,
        out_specs=ANY,
        scratch_shapes=[
            pltpu.VMEM((n_dp, steps, block // steps, dim), BF16),
            pltpu.VMEM((steps, block // steps, dim), F32),
            pltpu.SemaphoreType.DMA((n_dp, steps)),
            pltpu.SemaphoreType.DMA((steps,)),
        ],
        compiler_params=SOME,
        cost_estimate=pl.CostEstimate(
            flops=0, bytes_accessed=(2 * n_dp + 4) * block * dim, transcendentals=0
        ),
        name="add",
    )(*blocks)
    gathered, own_rows = lax.optimization_barrier((gathered, own_rows))
    quantized, token_gradient = pl.pallas_call(
        unpack_kernel,
        out_shape=(jax.ShapeDtypeStruct((n_tokens, dim), F32),) * 2,
        in_specs=[VMEM],
        out_specs=(VMEM, VMEM),
        compiler_params=SOME,
        cost_estimate=pl.CostEstimate(
            flops=0, bytes_accessed=12 * n_tokens * dim, transcendentals=0
        ),
        name="unpack",
    )(gathered)
    return quantized, token_gradient, own_rows[None]


def solution(mesh):
    n_dp, n_code = mesh.shape["dp"], mesh.shape["code"]
    in_specs = (P("dp", None), P("code", None), P("dp", "code"), P("dp", None))
    out_specs = (P("dp", None), P("dp", None), P("code", "dp", None))
    return jax.shard_map(
        functools.partial(local, n_dp, n_code),
        mesh=mesh, in_specs=in_specs, out_specs=out_specs, check_vma=False,
    )
```

```python
import functools

import jax
import jax.numpy as jnp
from jax import lax
from jax.experimental import pallas as pl
from jax.experimental.pallas import tpu as pltpu
from jax.sharding import PartitionSpec as P

SOFTMAX_HEAT = 0.5
SHARPNESS = 1.0 / SOFTMAX_HEAT
BF16 = jnp.bfloat16
F32 = jnp.float32
MIB = 1 << 20
CHUNK = 256
WIDE = 512
AHEAD = 2
ROWS = 64
LARGEST = 2.0**60
VMEM = pl.BlockSpec(memory_space=pltpu.VMEM)
SMEM = pl.BlockSpec(memory_space=pltpu.SMEM)
ANY = pl.BlockSpec(memory_space=pl.ANY)
FULL = pltpu.CompilerParams(vmem_limit_bytes=60 * MIB)
MOST = pltpu.CompilerParams(vmem_limit_bytes=56 * MIB)
SOME = pltpu.CompilerParams(vmem_limit_bytes=24 * MIB)


def dot(left, right, left_dim=1, right_dim=0):
    return lax.dot_general(
        left, right, (((left_dim,), (right_dim,)), ((), ())), preferred_element_type=F32
    )


def lane_groups(value):
    return [value[:, j : j + 128] for j in range(0, value.shape[1], 128)]


def stat_lanes(n_code):
    return max(8 * n_code, 128)


def high_low(value):
    high = value.astype(BF16).astype(F32)
    return high, (value - high).astype(BF16).astype(F32)


def forward_kernel(
    n_code, tokens, grad_out, codebook, noise, codes, sent, means,
    pair, book, noise_in, slot_a, slot_b, shifts, total, sums,
    pair_sem, book_sem, noise_sem, code_sem,
):
    tiles, n_tokens, width = codes.shape
    dim = tokens.shape[1]
    columns = [slice(c, c + CHUNK) for c in range(0, width, CHUNK)]
    slots = (slot_a, slot_b)

    def fetch(t):
        at = pl.multiple_of(t * width, width)
        return (
            pltpu.make_async_copy(codebook.at[pl.ds(at, width)], book.at[t], book_sem.at[t]),
            pltpu.make_async_copy(noise.at[:, pl.ds(at, width)], noise_in.at[t], noise_sem.at[t]),
        )

    def start(t):
        for copy in fetch(t):
            copy.start()

    def arrive(t):
        for copy in fetch(t):
            copy.wait()

    pair_copies = []
    for r in range(0, n_tokens, ROWS):
        for half, source in enumerate((tokens, grad_out)):
            pair_copies.append(
                pltpu.make_async_copy(
                    source.at[pl.ds(r, ROWS)],
                    pair.at[pl.ds(2 * r + half * ROWS, ROWS)],
                    pair_sem.at[len(pair_copies)],
                )
            )
    start(0)
    for copy in pair_copies:
        copy.start()
    for t in range(1, min(AHEAD + 1, tiles)):
        start(t)

    def logits(both, t, r, c):
        noise_part = (noise_in[t, r : r + ROWS, c] * BF16(SHARPNESS)).astype(F32)
        return both[2 * r : 2 * r + ROWS] + noise_part

    def raise_shift(t, some):
        for c in some:
            both = dot(pair[...], book[t, c], 1, 1)
            for r in range(0, n_tokens, ROWS):
                at = slice(r, r + ROWS)
                shifts[at] = functools.reduce(
                    jnp.maximum, lane_groups(logits(both, t, r, c)), shifts[at]
                )

    def store(t, s):
        return pltpu.make_async_copy(
            slots[s].at[pl.ds(0, n_tokens)], codes.at[t], code_sem.at[s]
        )

    def soften(t, s, fresh, last=None):
        if fresh is not None:
            @pl.when(fresh)
            def _():
                arrive(t)

                @pl.when(t + AHEAD < tiles)
                def _():
                    start(t + AHEAD)

        slot = slots[s]
        ahead = dot(pair[...], book[t, columns[0]], 1, 1)
        for k, c in enumerate(columns):
            both = ahead
            if k + 1 < len(columns):
                ahead = dot(pair[...], book[t, columns[k + 1]], 1, 1)
            elif last is not None:
                last()
            for r in range(0, n_tokens, ROWS):
                at = slice(r, r + ROWS)
                shift = jnp.concatenate([shifts[at]] * (CHUNK // 128), axis=1)
                weight = jnp.exp(logits(both, t, r, c) - shift)
                total[at] += sum(lane_groups(weight))
                slot[at, c] = weight.astype(BF16)
                gradient = both[2 * r + ROWS : 2 * r + 2 * ROWS]
                slot[n_tokens + r : n_tokens + r + ROWS, c] = (weight * gradient).astype(BF16)
        store(t, s).start()

    def accumulate(t, s):
        sums[...] += dot(slots[s][...], book[t])

    def attempt(state):
        again, _ = state
        fresh = again == 0
        shifts[...] = jnp.full(shifts.shape, -jnp.inf, F32)

        @pl.when(fresh)
        def _():
            raise_shift(0, columns[:2])

        @pl.when(jnp.logical_not(fresh))
        def _():
            def over(t, carry):
                raise_shift(t, columns)
                return carry

            lax.fori_loop(0, tiles, over, 0)

        shift = jnp.max(shifts[...], axis=1, keepdims=True).astype(BF16).astype(F32)
        shifts[...] = jnp.broadcast_to(shift, shifts.shape)
        total[...] = jnp.zeros(total.shape, F32)
        sums[...] = jnp.zeros(sums.shape, F32)
        soften(0, 0, None)

        def soften_pair(i, carry):
            @pl.when(i > 0)
            def _():
                store(2 * i - 1, 1).wait()

            soften(2 * i + 1, 1, fresh, lambda: accumulate(2 * i, 0))
            store(2 * i, 0).wait()
            soften(2 * i + 2, 0, fresh, lambda: accumulate(2 * i + 1, 1))
            return carry

        lax.fori_loop(0, tiles // 2 - 1, soften_pair, 0)
        if tiles > 2:
            store(tiles - 3, 1).wait()
        soften(tiles - 1, 1, fresh, lambda: accumulate(tiles - 2, 0))
        accumulate(tiles - 1, 1)
        store(tiles - 2, 0).wait()
        store(tiles - 1, 1).wait()
        fits = jnp.max(total[...]) < LARGEST
        return again + 1, jnp.logical_and(fresh, jnp.logical_not(fits))

    for copy in pair_copies:
        copy.wait()
    for r in range(0, n_tokens, ROWS):
        pair[2 * r : 2 * r + ROWS] = pair[2 * r : 2 * r + ROWS] * BF16(SHARPNESS)
    arrive(0)
    lax.while_loop(lambda state: state[1], attempt, (jnp.int32(0), jnp.bool_(True)))

    shift = shifts[:, :1]
    mix = sums[:n_tokens]
    pulled = sums[n_tokens:]
    own_total = jnp.sum(total[...], axis=1, keepdims=True)
    own_grad = jnp.concatenate(
        [pair[2 * r + ROWS : 2 * r + 2 * ROWS] for r in range(0, n_tokens, ROWS)], axis=0
    )
    own_inner = jnp.sum(own_grad.astype(F32) * mix, axis=1, keepdims=True)
    mean = own_inner / own_total
    means[...] = jnp.broadcast_to(mean, means.shape)
    rows = n_tokens // n_code
    lanes = stat_lanes(n_code)
    half = lanes // 2
    lane = lax.broadcasted_iota(jnp.int32, (rows, lanes), 1)
    stats = jnp.zeros((rows, lanes), F32)
    parts = high_low(own_total) + high_low(own_inner)
    for g in range(n_code):
        at = slice(g * rows, (g + 1) * rows)
        for i, part in enumerate(parts):
            stats = jnp.where(lane == 4 * g + i, part[at], stats)
        stats = jnp.where((lane - half) // 4 == g, shift[at], stats)
    stats = stats.astype(BF16)
    for g in range(n_code):
        at = slice(g * rows, (g + 1) * rows)
        sent[g, :, :dim] = mix[at].astype(BF16)
        sent[g, :, dim : 2 * dim] = (pulled[at] - mean[at] * mix[at]).astype(BF16)
        sent[g, :, 2 * dim :] = stats


def roll_left(value, by):
    return pltpu.roll(value, value.shape[1] - by, 1)


def merged_stats(received):
    n_code = received.shape[0]
    lanes = stat_lanes(n_code)
    stats = [received[p, :, received.shape[2] - lanes :].astype(F32) for p in range(n_code)]
    top = functools.reduce(jnp.maximum, stats)
    scales = [roll_left(jnp.exp(s - top), lanes // 2) for s in stats]
    pairs = [s + roll_left(s, 1) for s in stats]
    inners = [roll_left(s, 2) for s in pairs]
    total = sum(a * s for a, s in zip(scales, pairs))
    inner = sum(a * s for a, s in zip(scales, inners)) / total
    means = [i / s for i, s in zip(inners, pairs)]
    return [a / total for a in scales], means, inner


def merge_kernel(me, received, spread):
    n_code, rows, _ = received.shape
    dim = spread.shape[2] // 2
    scales, means, inner = merged_stats(received)
    lane = lax.broadcasted_iota(jnp.int32, inner.shape, 1)
    mine = lane == 4 * me[0]

    def column(value):
        return jnp.sum(jnp.where(mine, value, 0.0), axis=1, keepdims=True)

    quantized = jnp.zeros((rows, dim), F32)
    gradient = jnp.zeros((rows, dim), F32)
    for p in range(n_code):
        scale = column(scales[p])
        offset = column(scales[p] * (means[p] - inner))
        mix = received[p, :, :dim].astype(F32)
        quantized += scale * mix
        gradient += scale * received[p, :, dim : 2 * dim].astype(F32) + offset * mix
    quantized = quantized.astype(BF16)
    gradient = (gradient / SOFTMAX_HEAT).astype(BF16)
    for p in range(n_code):
        spread[p, :, :dim] = quantized
        spread[p, :, dim:] = gradient


def weigh_kernel(
    grad_out, codebook, codes, means, weighed, book, code_in, result, book_sem, code_sem, out_sem
):
    tiles, width, _ = book.shape
    steps = [(t, slice(c, c + WIDE)) for t in range(tiles) for c in range(0, width, WIDE)]

    def fetch(t):
        at = pl.ds(t * width, width)
        return (
            pltpu.make_async_copy(codebook.at[at], book.at[t], book_sem.at[t]),
            pltpu.make_async_copy(codes.at[t], code_in.at[t], code_sem.at[t]),
        )

    def start(t):
        for copy in fetch(t):
            copy.start()

    def send(t):
        return pltpu.make_async_copy(result.at[t], weighed.at[t], out_sem.at[t])

    def gradient_of(step):
        t, c = step
        if c.start == 0:
            for copy in fetch(t):
                copy.wait()
            if t + AHEAD < tiles:
                start(t + AHEAD)
        return dot(grad_out[...], book[t, c], 1, 1)

    for t in range(min(AHEAD, tiles)):
        start(t)
    ahead = gradient_of(steps[0])
    for k, (t, c) in enumerate(steps):
        gradient = ahead
        if k + 1 < len(steps):
            ahead = gradient_of(steps[k + 1])
        mean = jnp.concatenate([means[...]] * (WIDE // 128), axis=1)
        result[t, :, c] = (code_in[t, :, c].astype(F32) * (gradient - mean)).astype(BF16)
        if c.stop == width:
            send(t).start()
    for t in range(tiles):
        send(t).wait()


def backward_kernel(prepared, block, *rest):
    if prepared:
        codes, weighed, operands, out, *rest = rest
    else:
        code_at, tokens, grad_out, codes, weighed, received, out, operands, *rest = rest
        upper, lower, *rest = rest
    both_in, result, in_sem, out_sem = rest
    tiles, width, dim = result.shape
    n_tokens = both_in.shape[1] // 2

    def fetch(t):
        return [
            pltpu.make_async_copy(
                source.at[block[0] * tiles + t],
                both_in.at[t, pl.ds(half * n_tokens, n_tokens)],
                in_sem.at[half, t],
            )
            for half, source in enumerate((codes, weighed))
        ]

    def start(t):
        for copy in fetch(t):
            copy.start()

    for t in range(min(AHEAD, tiles)):
        start(t)

    if not prepared:
        n_code, rows, _ = received.shape
        scales, means, inner = merged_stats(received)
        scale = jnp.zeros(inner.shape, F32)
        mean = jnp.zeros(inner.shape, F32)
        for p in range(n_code):
            scale = jnp.where(code_at[0] == p, scales[p], scale)
            mean = jnp.where(code_at[0] == p, means[p], mean)
        offset = mean - inner
        for g in range(n_code):
            part = slice(g * rows, (g + 1) * rows)
            at = slice(4 * g, 4 * g + 1)
            token = scale[:, at] * (tokens[part].astype(F32) / SOFTMAX_HEAT)
            upper[part] = scale[:, at] * grad_out[part].astype(F32) + offset[:, at] * token
            lower[part] = token
        operands[:, :n_tokens] = upper[...].T.astype(BF16)
        operands[:, n_tokens:] = lower[...].T.astype(BF16)

    def send(t):
        return pltpu.make_async_copy(
            result.at[t], out.at[pl.ds(t * width, width)], out_sem.at[t]
        )

    wide = min(WIDE, width)
    steps = [(t, slice(c, c + wide)) for t in range(tiles) for c in range(0, width, wide)]

    def product(step):
        t, c = step
        if c.start == 0:
            for copy in fetch(t):
                copy.wait()
            if t + AHEAD < tiles:
                start(t + AHEAD)
        return dot(operands[...], both_in[t, :, c])

    ahead = product(steps[0])
    for k, (t, c) in enumerate(steps):
        value = ahead
        if k + 1 < len(steps):
            ahead = product(steps[k + 1])
        result[t, c] = value.astype(BF16).T
        if c.stop == width:
            send(t).start()
    for t in range(tiles):
        send(t).wait()


def add_kernel(n_parts, *refs):
    parts, out = refs[:n_parts], refs[n_parts]
    held, result, in_sem, out_sem = refs[n_parts + 1 :]
    steps, rows, _ = result.shape

    def fetch(i):
        at = pl.ds(i * rows, rows)
        return [
            pltpu.make_async_copy(part.at[at], held.at[j, i], in_sem.at[j, i])
            for j, part in enumerate(parts)
        ]

    def send(i):
        return pltpu.make_async_copy(result.at[i], out.at[pl.ds(i * rows, rows)], out_sem.at[i])

    for i in range(steps):
        for copy in fetch(i):
            copy.start()
    for i in range(steps):
        for copy in fetch(i):
            copy.wait()
        result[i] = sum(held[j, i].astype(F32) for j in range(n_parts))
        send(i).start()
    for i in range(steps):
        send(i).wait()


def unpack_kernel(gathered, quantized, gradient):
    n_code, rows, both = gathered.shape
    dim = both // 2
    for g in range(n_code):
        at = slice(g * rows, (g + 1) * rows)
        quantized[at] = gathered[g, :, :dim].astype(F32)
        gradient[at] = gathered[g, :, dim:].astype(F32)


def swap(value, axis, size, mask):
    return lax.ppermute(value, axis, [(i, i ^ mask) for i in range(size)])


def local(n_dp, n_code, tokens, codebook, noise, grad_out):
    n_tokens, dim = tokens.shape
    n_codes = codebook.shape[0]
    rows = n_tokens // n_code
    block = n_codes // n_dp
    width = min(1024, block)
    tiles = n_codes // width
    lanes = stat_lanes(n_code)
    products = 2 * n_tokens * n_codes * dim

    codes, sent, means = pl.pallas_call(
        functools.partial(forward_kernel, n_code),
        out_shape=(
            pltpu.HBM((tiles, n_tokens, width), BF16),
            jax.ShapeDtypeStruct((n_code, rows, 2 * dim + lanes), BF16),
            jax.ShapeDtypeStruct((n_tokens, 128), F32),
        ),
        in_specs=[ANY, ANY, ANY, ANY],
        out_specs=(ANY, VMEM, VMEM),
        scratch_shapes=[
            pltpu.VMEM((2 * n_tokens, dim), BF16),
            pltpu.VMEM((tiles, width, dim), BF16),
            pltpu.VMEM((tiles, n_tokens, width), BF16),
            pltpu.VMEM((2 * n_tokens, width), BF16),
            pltpu.VMEM((2 * n_tokens, width), BF16),
            pltpu.VMEM((n_tokens, 128), F32),
            pltpu.VMEM((n_tokens, 128), F32),
            pltpu.VMEM((2 * n_tokens, dim), F32),
            pltpu.SemaphoreType.DMA((2 * n_tokens // ROWS,)),
            pltpu.SemaphoreType.DMA((tiles,)),
            pltpu.SemaphoreType.DMA((tiles,)),
            pltpu.SemaphoreType.DMA((2,)),
        ],
        compiler_params=FULL,
        cost_estimate=pl.CostEstimate(
            flops=4 * products, bytes_accessed=24 * MIB, transcendentals=n_tokens * n_codes
        ),
        name="forward",
    )(tokens, grad_out, codebook, noise)

    received = lax.all_to_all(sent, "code", 0, 0, tiled=True)
    weighed = pl.pallas_call(
        weigh_kernel,
        out_shape=pltpu.HBM((tiles, n_tokens, width), BF16),
        in_specs=[VMEM, ANY, ANY, VMEM],
        out_specs=ANY,
        scratch_shapes=[
            pltpu.VMEM((tiles, width, dim), BF16),
            pltpu.VMEM((tiles, n_tokens, width), BF16),
            pltpu.VMEM((tiles, n_tokens, width), BF16),
            pltpu.SemaphoreType.DMA((tiles,)),
            pltpu.SemaphoreType.DMA((tiles,)),
            pltpu.SemaphoreType.DMA((tiles,)),
        ],
        compiler_params=FULL,
        cost_estimate=pl.CostEstimate(
            flops=products, bytes_accessed=20 * MIB, transcendentals=0
        ),
        name="weigh",
    )(grad_out, codebook, codes, means)
    received, weighed = lax.optimization_barrier((received, weighed))
    code_at = lax.axis_index("code")
    spread = pl.pallas_call(
        merge_kernel,
        out_shape=jax.ShapeDtypeStruct((n_code, rows, 2 * dim), BF16),
        in_specs=[SMEM, VMEM],
        out_specs=VMEM,
        compiler_params=SOME,
        name="merge",
    )(code_at[None], received)
    received, spread = lax.optimization_barrier((received, spread))
    gathered = lax.all_to_all(spread, "code", 0, 0, tiled=True)
    quantized, token_gradient = pl.pallas_call(
        unpack_kernel,
        out_shape=(jax.ShapeDtypeStruct((n_tokens, dim), F32),) * 2,
        in_specs=[VMEM],
        out_specs=(VMEM, VMEM),
        compiler_params=SOME,
        cost_estimate=pl.CostEstimate(
            flops=100 * products, bytes_accessed=400 * MIB, transcendentals=0
        ),
        name="unpack",
    )(gathered)

    block_tiles = block // width
    streams = [
        pltpu.VMEM((block_tiles, 2 * n_tokens, width), BF16),
        pltpu.VMEM((block_tiles, width, dim), BF16),
        pltpu.SemaphoreType.DMA((2, block_tiles)),
        pltpu.SemaphoreType.DMA((block_tiles,)),
    ]
    block_shape = jax.ShapeDtypeStruct((block, dim), BF16)
    common = dict(
        compiler_params=MOST,
        cost_estimate=pl.CostEstimate(flops=1, bytes_accessed=1, transcendentals=0),
    )
    dp_at = lax.axis_index("dp")
    first, operands = pl.pallas_call(
        functools.partial(backward_kernel, False),
        out_shape=(block_shape, jax.ShapeDtypeStruct((dim, 2 * n_tokens), BF16)),
        in_specs=[SMEM, SMEM, VMEM, VMEM, ANY, ANY, VMEM],
        out_specs=(ANY, VMEM),
        scratch_shapes=[
            pltpu.VMEM((n_tokens, dim), F32), pltpu.VMEM((n_tokens, dim), F32),
        ] + streams,
        name="backward_first",
        **common,
    )(
        (dp_at ^ (n_dp - 1))[None], code_at[None], tokens, grad_out, codes, weighed, received
    )

    def backward(at):
        return pl.pallas_call(
            functools.partial(backward_kernel, True),
            out_shape=block_shape,
            in_specs=[SMEM, ANY, ANY, VMEM],
            out_specs=ANY,
            scratch_shapes=streams,
            name="backward",
            **common,
        )(at[None], codes, weighed, operands)

    blocks = [swap(first, "dp", n_dp, n_dp - 1)]
    blocks += [swap(backward(dp_at ^ d), "dp", n_dp, d) for d in range(1, n_dp - 1)]
    blocks.append(backward(dp_at))
    steps = max(block // 512, 1)
    own_rows = pl.pallas_call(
        functools.partial(add_kernel, n_dp),
        out_shape=jax.ShapeDtypeStruct((block, dim), F32),
        in_specs=[ANY] * n_dp,
        out_specs=ANY,
        scratch_shapes=[
            pltpu.VMEM((n_dp, steps, block // steps, dim), BF16),
            pltpu.VMEM((steps, block // steps, dim), F32),
            pltpu.SemaphoreType.DMA((n_dp, steps)),
            pltpu.SemaphoreType.DMA((steps,)),
        ],
        compiler_params=SOME,
        cost_estimate=pl.CostEstimate(
            flops=0, bytes_accessed=(2 * n_dp + 4) * block * dim, transcendentals=0
        ),
        name="add",
    )(*blocks)
    return quantized, token_gradient, own_rows[None]


def solution(mesh):
    n_dp, n_code = mesh.shape["dp"], mesh.shape["code"]
    in_specs = (P("dp", None), P("code", None), P("dp", "code"), P("dp", None))
    out_specs = (P("dp", None), P("dp", None), P("code", "dp", None))
    return jax.shard_map(
        functools.partial(local, n_dp, n_code),
        mesh=mesh, in_specs=in_specs, out_specs=out_specs, check_vma=False,
    )
```

```python
import functools

import jax
import jax.numpy as jnp
from jax import lax
from jax.experimental import pallas as pl
from jax.experimental.pallas import tpu as pltpu
from jax.sharding import PartitionSpec as P

SOFTMAX_HEAT = 0.5
SHARPNESS = 1.0 / SOFTMAX_HEAT
BF16 = jnp.bfloat16
F32 = jnp.float32
MIB = 1 << 20
CHUNK = 256
WIDE = 512
AHEAD = 2
NEAR = 3
ROWS = 64
LARGEST = 2.0**60
VMEM = pl.BlockSpec(memory_space=pltpu.VMEM)
SMEM = pl.BlockSpec(memory_space=pltpu.SMEM)
ANY = pl.BlockSpec(memory_space=pl.ANY)
FULL = pltpu.CompilerParams(vmem_limit_bytes=60 * MIB)
MOST = pltpu.CompilerParams(vmem_limit_bytes=56 * MIB)
SOME = pltpu.CompilerParams(vmem_limit_bytes=24 * MIB)


def dot(left, right, left_dim=1, right_dim=0):
    return lax.dot_general(
        left, right, (((left_dim,), (right_dim,)), ((), ())), preferred_element_type=F32
    )


def lane_groups(value):
    return [value[:, j : j + 128] for j in range(0, value.shape[1], 128)]


def stat_lanes(n_code):
    return max(8 * n_code, 128)


def high_low(value):
    high = value.astype(BF16).astype(F32)
    return high, (value - high).astype(BF16).astype(F32)


def forward_kernel(
    n_code, tokens, grad_out, codebook, noise, codes, sent, means,
    pair, book, noise_in, slot_a, slot_b, shifts, total, sums,
    pair_sem, book_sem, noise_sem, code_sem,
):
    tiles, width, dim = book.shape
    n_tokens = tokens.shape[0]
    wide = codes.shape[2]
    columns = [slice(c, c + CHUNK) for c in range(0, width, CHUNK)]
    slots = (slot_a, slot_b)

    def fetch(t):
        at = pl.multiple_of(t * width, width)
        return (
            pltpu.make_async_copy(codebook.at[pl.ds(at, width)], book.at[t], book_sem.at[t]),
            pltpu.make_async_copy(noise.at[:, pl.ds(at, width)], noise_in.at[t], noise_sem.at[t]),
        )

    def start(t):
        for copy in fetch(t):
            copy.start()

    def arrive(t):
        for copy in fetch(t):
            copy.wait()

    pair_copies = []
    for r in range(0, n_tokens, ROWS):
        for half, source in enumerate((tokens, grad_out)):
            pair_copies.append(
                pltpu.make_async_copy(
                    source.at[pl.ds(r, ROWS)],
                    pair.at[pl.ds(2 * r + half * ROWS, ROWS)],
                    pair_sem.at[len(pair_copies)],
                )
            )
    for copy in pair_copies:
        copy.start()
    start(0)

    def logits(both, t, r, c):
        noise_part = (noise_in[t, r : r + ROWS, c] * BF16(SHARPNESS)).astype(F32)
        return both[2 * r : 2 * r + ROWS] + noise_part

    def raise_shift(t, some):
        for c in some:
            both = dot(pair[...], book[t, c], 1, 1)
            for r in range(0, n_tokens, ROWS):
                at = slice(r, r + ROWS)
                shifts[at] = functools.reduce(
                    jnp.maximum, lane_groups(logits(both, t, r, c)), shifts[at]
                )

    def store(t, s):
        return [
            pltpu.make_async_copy(
                slots[s].at[pl.ds(0, n_tokens), pl.ds(j * wide, wide)],
                codes.at[t * (width // wide) + j],
                code_sem.at[s, j],
            )
            for j in range(width // wide)
        ]

    def stored(t, s):
        for copy in store(t, s):
            copy.wait()

    def soften(t, s, fresh, last=None):
        if fresh is not None:
            @pl.when(fresh)
            def _():
                arrive(t)

                @pl.when(t + AHEAD < tiles)
                def _():
                    start(t + AHEAD)

        slot = slots[s]
        ahead = dot(pair[...], book[t, columns[0]], 1, 1)
        for k, c in enumerate(columns):
            both = ahead
            if k + 1 < len(columns):
                ahead = dot(pair[...], book[t, columns[k + 1]], 1, 1)
            elif last is not None:
                last()
            for r in range(0, n_tokens, ROWS):
                at = slice(r, r + ROWS)
                shift = jnp.concatenate([shifts[at]] * (CHUNK // 128), axis=1)
                weight = jnp.exp(logits(both, t, r, c) - shift)
                total[at] += sum(lane_groups(weight))
                slot[at, c] = weight.astype(BF16)
                gradient = both[2 * r + ROWS : 2 * r + 2 * ROWS]
                slot[n_tokens + r : n_tokens + r + ROWS, c] = (weight * gradient).astype(BF16)
        for copy in store(t, s):
            copy.start()

    def accumulate(t, s):
        sums[...] += dot(slots[s][...], book[t])

    def attempt(state):
        again, _ = state
        fresh = again == 0
        shifts[...] = jnp.full(shifts.shape, -jnp.inf, F32)

        @pl.when(fresh)
        def _():
            raise_shift(0, columns[:1])

        @pl.when(jnp.logical_not(fresh))
        def _():
            stored(tiles - 2, 0)
            stored(tiles - 1, 1)

            def over(t, carry):
                raise_shift(t, columns)
                return carry

            lax.fori_loop(0, tiles, over, 0)

        shift = jnp.max(shifts[...], axis=1, keepdims=True).astype(BF16).astype(F32)
        shifts[...] = jnp.broadcast_to(shift, shifts.shape)
        total[...] = jnp.zeros(total.shape, F32)
        sums[...] = jnp.zeros(sums.shape, F32)
        soften(0, 0, None)

        def soften_pair(i, carry):
            @pl.when(i > 0)
            def _():
                stored(2 * i - 1, 1)

            soften(2 * i + 1, 1, fresh, lambda: accumulate(2 * i, 0))
            stored(2 * i, 0)
            soften(2 * i + 2, 0, fresh, lambda: accumulate(2 * i + 1, 1))
            return carry

        lax.fori_loop(0, tiles // 2 - 1, soften_pair, 0)
        if tiles > 2:
            stored(tiles - 3, 1)
        soften(tiles - 1, 1, fresh, lambda: accumulate(tiles - 2, 0))
        accumulate(tiles - 1, 1)
        fits = jnp.max(total[...]) < LARGEST
        return again + 1, jnp.logical_and(fresh, jnp.logical_not(fits))

    for copy in pair_copies:
        copy.wait()
    for r in range(0, n_tokens, ROWS):
        pair[2 * r : 2 * r + ROWS] = pair[2 * r : 2 * r + ROWS] * BF16(SHARPNESS)
    arrive(0)
    for t in range(1, min(AHEAD + 1, tiles)):
        start(t)
    lax.while_loop(lambda state: state[1], attempt, (jnp.int32(0), jnp.bool_(True)))

    shift = shifts[:, :1]
    mix = sums[:n_tokens]
    pulled = sums[n_tokens:]
    own_total = jnp.sum(total[...], axis=1, keepdims=True)
    own_grad = jnp.concatenate(
        [pair[2 * r + ROWS : 2 * r + 2 * ROWS] for r in range(0, n_tokens, ROWS)], axis=0
    )
    own_inner = jnp.sum(own_grad.astype(F32) * mix, axis=1, keepdims=True)
    mean = own_inner / own_total
    means[...] = jnp.broadcast_to(mean, means.shape)
    rows = n_tokens // n_code
    lanes = stat_lanes(n_code)
    half = lanes // 2
    lane = lax.broadcasted_iota(jnp.int32, (rows, lanes), 1)
    stats = jnp.zeros((rows, lanes), F32)
    parts = high_low(own_total) + high_low(own_inner)
    for g in range(n_code):
        at = slice(g * rows, (g + 1) * rows)
        for i, part in enumerate(parts):
            stats = jnp.where(lane == 4 * g + i, part[at], stats)
        stats = jnp.where((lane - half) // 4 == g, shift[at], stats)
    stats = stats.astype(BF16)
    for g in range(n_code):
        at = slice(g * rows, (g + 1) * rows)
        sent[g, :, :dim] = mix[at].astype(BF16)
        sent[g, :, dim : 2 * dim] = (pulled[at] - mean[at] * mix[at]).astype(BF16)
        sent[g, :, 2 * dim :] = stats
    stored(tiles - 2, 0)
    stored(tiles - 1, 1)


def roll_left(value, by):
    return pltpu.roll(value, value.shape[1] - by, 1)


def merged_stats(received):
    n_code = received.shape[0]
    lanes = stat_lanes(n_code)
    stats = [received[p, :, received.shape[2] - lanes :].astype(F32) for p in range(n_code)]
    top = functools.reduce(jnp.maximum, stats)
    scales = [roll_left(jnp.exp(s - top), lanes // 2) for s in stats]
    pairs = [s + roll_left(s, 1) for s in stats]
    inners = [roll_left(s, 2) for s in pairs]
    total = sum(a * s for a, s in zip(scales, pairs))
    inner = sum(a * s for a, s in zip(scales, inners)) / total
    means = [i / s for i, s in zip(inners, pairs)]
    return [a / total for a in scales], means, inner


def merge_kernel(me, received, spread):
    n_code, rows, _ = received.shape
    dim = spread.shape[2] // 2
    scales, means, inner = merged_stats(received)
    lane = lax.broadcasted_iota(jnp.int32, inner.shape, 1)
    mine = lane == 4 * me[0]

    def column(value):
        return jnp.sum(jnp.where(mine, value, 0.0), axis=1, keepdims=True)

    quantized = jnp.zeros((rows, dim), F32)
    gradient = jnp.zeros((rows, dim), F32)
    for p in range(n_code):
        scale = column(scales[p])
        offset = column(scales[p] * (means[p] - inner))
        mix = received[p, :, :dim].astype(F32)
        quantized += scale * mix
        gradient += scale * received[p, :, dim : 2 * dim].astype(F32) + offset * mix
    quantized = quantized.astype(BF16)
    gradient = (gradient / SOFTMAX_HEAT).astype(BF16)
    for p in range(n_code):
        spread[p, :, :dim] = quantized
        spread[p, :, dim:] = gradient


def weigh_kernel(
    grad_out, codebook, codes, means, weighed, book, code_in, result, book_sem, code_sem, out_sem
):
    tiles, width, _ = book.shape
    steps = [(t, slice(c, c + WIDE)) for t in range(tiles) for c in range(0, width, WIDE)]

    def fetch(t):
        at = pl.ds(t * width, width)
        return (
            pltpu.make_async_copy(codebook.at[at], book.at[t], book_sem.at[t]),
            pltpu.make_async_copy(codes.at[t], code_in.at[t], code_sem.at[t]),
        )

    def start(t):
        for copy in fetch(t):
            copy.start()

    def send(t):
        return pltpu.make_async_copy(result.at[t], weighed.at[t], out_sem.at[t])

    def gradient_of(step):
        t, c = step
        if c.start == 0:
            for copy in fetch(t):
                copy.wait()
            if t + NEAR < tiles:
                start(t + NEAR)
        return dot(grad_out[...], book[t, c], 1, 1)

    for t in range(min(NEAR, tiles)):
        start(t)
    ahead = gradient_of(steps[0])
    for k, (t, c) in enumerate(steps):
        gradient = ahead
        if k + 1 < len(steps):
            ahead = gradient_of(steps[k + 1])
        mean = jnp.concatenate([means[...]] * (WIDE // 128), axis=1)
        result[t, :, c] = (code_in[t, :, c].astype(F32) * (gradient - mean)).astype(BF16)
        if c.stop == width:
            send(t).start()
    for t in range(tiles):
        send(t).wait()


def backward_kernel(prepared, block, *rest):
    if prepared:
        codes, weighed, operands, out, *rest = rest
    else:
        code_at, tokens, grad_out, codes, weighed, received, out, operands, *rest = rest
        upper, lower, *rest = rest
    both_in, result, in_sem, out_sem = rest
    tiles, width, dim = result.shape
    n_tokens = both_in.shape[1] // 2

    def fetch(t):
        return [
            pltpu.make_async_copy(
                source.at[block[0] * tiles + t],
                both_in.at[t, pl.ds(half * n_tokens, n_tokens)],
                in_sem.at[half, t],
            )
            for half, source in enumerate((codes, weighed))
        ]

    def start(t):
        for copy in fetch(t):
            copy.start()

    for t in range(min(NEAR, tiles)):
        start(t)

    if not prepared:
        n_code, rows, _ = received.shape
        scales, means, inner = merged_stats(received)
        scale = jnp.zeros(inner.shape, F32)
        mean = jnp.zeros(inner.shape, F32)
        for p in range(n_code):
            scale = jnp.where(code_at[0] == p, scales[p], scale)
            mean = jnp.where(code_at[0] == p, means[p], mean)
        offset = mean - inner
        for g in range(n_code):
            part = slice(g * rows, (g + 1) * rows)
            at = slice(4 * g, 4 * g + 1)
            token = scale[:, at] * (tokens[part].astype(F32) / SOFTMAX_HEAT)
            upper[part] = scale[:, at] * grad_out[part].astype(F32) + offset[:, at] * token
            lower[part] = token
        operands[:, :n_tokens] = upper[...].T.astype(BF16)
        operands[:, n_tokens:] = lower[...].T.astype(BF16)

    def send(t):
        return pltpu.make_async_copy(
            result.at[t], out.at[pl.ds(t * width, width)], out_sem.at[t]
        )

    wide = min(WIDE, width)
    steps = [(t, slice(c, c + wide)) for t in range(tiles) for c in range(0, width, wide)]

    def product(step):
        t, c = step
        if c.start == 0:
            for copy in fetch(t):
                copy.wait()
            if t + NEAR < tiles:
                start(t + NEAR)
        return dot(operands[...], both_in[t, :, c])

    ahead = product(steps[0])
    for k, (t, c) in enumerate(steps):
        value = ahead
        if k + 1 < len(steps):
            ahead = product(steps[k + 1])
        result[t, c] = value.astype(BF16).T
        if c.stop == width:
            send(t).start()
    for t in range(tiles):
        send(t).wait()


def add_kernel(n_parts, *refs):
    parts, out = refs[:n_parts], refs[n_parts]
    held, result, in_sem, out_sem = refs[n_parts + 1 :]
    steps, rows, _ = result.shape

    def fetch(i):
        at = pl.ds(i * rows, rows)
        return [
            pltpu.make_async_copy(part.at[at], held.at[j, i], in_sem.at[j, i])
            for j, part in enumerate(parts)
        ]

    def send(i):
        return pltpu.make_async_copy(result.at[i], out.at[pl.ds(i * rows, rows)], out_sem.at[i])

    for i in range(steps):
        for copy in fetch(i):
            copy.start()
    for i in range(steps):
        for copy in fetch(i):
            copy.wait()
        result[i] = sum(held[j, i].astype(F32) for j in range(n_parts))
        send(i).start()
    for i in range(steps):
        send(i).wait()


def unpack_kernel(gathered, quantized, gradient):
    n_code, rows, both = gathered.shape
    dim = both // 2
    for g in range(n_code):
        at = slice(g * rows, (g + 1) * rows)
        quantized[at] = gathered[g, :, :dim].astype(F32)
        gradient[at] = gathered[g, :, dim:].astype(F32)


def swap(value, axis, size, mask):
    return lax.ppermute(value, axis, [(i, i ^ mask) for i in range(size)])


def local(n_dp, n_code, tokens, codebook, noise, grad_out):
    n_tokens, dim = tokens.shape
    n_codes = codebook.shape[0]
    rows = n_tokens // n_code
    block = n_codes // n_dp
    width = min(1024, block)
    wide = min(WIDE, width)
    tiles_in = n_codes // wide
    tiles = n_codes // width
    lanes = stat_lanes(n_code)
    products = 2 * n_tokens * n_codes * dim

    codes, sent, means = pl.pallas_call(
        functools.partial(forward_kernel, n_code),
        out_shape=(
            pltpu.HBM((n_codes // wide, n_tokens, wide), BF16),
            jax.ShapeDtypeStruct((n_code, rows, 2 * dim + lanes), BF16),
            jax.ShapeDtypeStruct((n_tokens, 128), F32),
        ),
        in_specs=[ANY, ANY, ANY, ANY],
        out_specs=(ANY, VMEM, VMEM),
        scratch_shapes=[
            pltpu.VMEM((2 * n_tokens, dim), BF16),
            pltpu.VMEM((tiles, width, dim), BF16),
            pltpu.VMEM((tiles, n_tokens, width), BF16),
            pltpu.VMEM((2 * n_tokens, width), BF16),
            pltpu.VMEM((2 * n_tokens, width), BF16),
            pltpu.VMEM((n_tokens, 128), F32),
            pltpu.VMEM((n_tokens, 128), F32),
            pltpu.VMEM((2 * n_tokens, dim), F32),
            pltpu.SemaphoreType.DMA((2 * n_tokens // ROWS,)),
            pltpu.SemaphoreType.DMA((tiles,)),
            pltpu.SemaphoreType.DMA((tiles,)),
            pltpu.SemaphoreType.DMA((2, width // wide)),
        ],
        compiler_params=FULL,
        cost_estimate=pl.CostEstimate(
            flops=4 * products, bytes_accessed=24 * MIB, transcendentals=n_tokens * n_codes
        ),
        name="forward",
    )(tokens, grad_out, codebook, noise)

    received = lax.all_to_all(sent, "code", 0, 0, tiled=True)
    weighed = pl.pallas_call(
        weigh_kernel,
        out_shape=pltpu.HBM((tiles_in, n_tokens, wide), BF16),
        in_specs=[VMEM, ANY, ANY, VMEM],
        out_specs=ANY,
        scratch_shapes=[
            pltpu.VMEM((tiles_in, wide, dim), BF16),
            pltpu.VMEM((tiles_in, n_tokens, wide), BF16),
            pltpu.VMEM((tiles_in, n_tokens, wide), BF16),
            pltpu.SemaphoreType.DMA((tiles_in,)),
            pltpu.SemaphoreType.DMA((tiles_in,)),
            pltpu.SemaphoreType.DMA((tiles_in,)),
        ],
        compiler_params=FULL,
        cost_estimate=pl.CostEstimate(
            flops=products, bytes_accessed=20 * MIB, transcendentals=0
        ),
        name="weigh",
    )(grad_out, codebook, codes, means)
    received, weighed = lax.optimization_barrier((received, weighed))
    code_at = lax.axis_index("code")
    spread = pl.pallas_call(
        merge_kernel,
        out_shape=jax.ShapeDtypeStruct((n_code, rows, 2 * dim), BF16),
        in_specs=[SMEM, VMEM],
        out_specs=VMEM,
        compiler_params=SOME,
        name="merge",
    )(code_at[None], received)
    received, spread = lax.optimization_barrier((received, spread))
    gathered = lax.all_to_all(spread, "code", 0, 0, tiled=True)
    quantized, token_gradient = pl.pallas_call(
        unpack_kernel,
        out_shape=(jax.ShapeDtypeStruct((n_tokens, dim), F32),) * 2,
        in_specs=[VMEM],
        out_specs=(VMEM, VMEM),
        compiler_params=SOME,
        cost_estimate=pl.CostEstimate(
            flops=100 * products, bytes_accessed=400 * MIB, transcendentals=0
        ),
        name="unpack",
    )(gathered)

    block_tiles = block // wide
    streams = [
        pltpu.VMEM((block_tiles, 2 * n_tokens, wide), BF16),
        pltpu.VMEM((block_tiles, wide, dim), BF16),
        pltpu.SemaphoreType.DMA((2, block_tiles)),
        pltpu.SemaphoreType.DMA((block_tiles,)),
    ]
    block_shape = jax.ShapeDtypeStruct((block, dim), BF16)
    common = dict(
        compiler_params=MOST,
        cost_estimate=pl.CostEstimate(flops=1, bytes_accessed=1, transcendentals=0),
    )
    dp_at = lax.axis_index("dp")
    first, operands = pl.pallas_call(
        functools.partial(backward_kernel, False),
        out_shape=(block_shape, jax.ShapeDtypeStruct((dim, 2 * n_tokens), BF16)),
        in_specs=[SMEM, SMEM, VMEM, VMEM, ANY, ANY, VMEM],
        out_specs=(ANY, VMEM),
        scratch_shapes=[
            pltpu.VMEM((n_tokens, dim), F32), pltpu.VMEM((n_tokens, dim), F32),
        ] + streams,
        name="backward_first",
        **common,
    )(
        (dp_at ^ (n_dp - 1))[None], code_at[None], tokens, grad_out, codes, weighed, received
    )

    def backward(at):
        return pl.pallas_call(
            functools.partial(backward_kernel, True),
            out_shape=block_shape,
            in_specs=[SMEM, ANY, ANY, VMEM],
            out_specs=ANY,
            scratch_shapes=streams,
            name="backward",
            **common,
        )(at[None], codes, weighed, operands)

    blocks = [swap(first, "dp", n_dp, n_dp - 1)]
    blocks += [swap(backward(dp_at ^ d), "dp", n_dp, d) for d in range(1, n_dp - 1)]
    blocks.append(backward(dp_at))
    steps = max(block // 512, 1)
    own_rows = pl.pallas_call(
        functools.partial(add_kernel, n_dp),
        out_shape=jax.ShapeDtypeStruct((block, dim), F32),
        in_specs=[ANY] * n_dp,
        out_specs=ANY,
        scratch_shapes=[
            pltpu.VMEM((n_dp, steps, block // steps, dim), BF16),
            pltpu.VMEM((steps, block // steps, dim), F32),
            pltpu.SemaphoreType.DMA((n_dp, steps)),
            pltpu.SemaphoreType.DMA((steps,)),
        ],
        compiler_params=SOME,
        cost_estimate=pl.CostEstimate(
            flops=0, bytes_accessed=(2 * n_dp + 4) * block * dim, transcendentals=0
        ),
        name="add",
    )(*blocks)
    return quantized, token_gradient, own_rows[None]


def solution(mesh):
    n_dp, n_code = mesh.shape["dp"], mesh.shape["code"]
    in_specs = (P("dp", None), P("code", None), P("dp", "code"), P("dp", None))
    out_specs = (P("dp", None), P("dp", None), P("code", "dp", None))
    return jax.shard_map(
        functools.partial(local, n_dp, n_code),
        mesh=mesh, in_specs=in_specs, out_specs=out_specs, check_vma=False,
    )
```

```python
import functools

import jax
import jax.numpy as jnp
from jax import lax
from jax.experimental import pallas as pl
from jax.experimental.pallas import tpu as pltpu
from jax.sharding import PartitionSpec as P

SOFTMAX_HEAT = 0.5
SHARPNESS = 1.0 / SOFTMAX_HEAT
BF16 = jnp.bfloat16
F32 = jnp.float32
MIB = 1 << 20
CHUNK = 256
WIDE = 512
AHEAD = 2
NEAR = 3
ROWS = 64
LARGEST = 2.0**60
VMEM = pl.BlockSpec(memory_space=pltpu.VMEM)
SMEM = pl.BlockSpec(memory_space=pltpu.SMEM)
ANY = pl.BlockSpec(memory_space=pl.ANY)
FULL = pltpu.CompilerParams(vmem_limit_bytes=60 * MIB)
MOST = pltpu.CompilerParams(vmem_limit_bytes=56 * MIB)
PART = pltpu.CompilerParams(vmem_limit_bytes=58 * MIB)
SOME = pltpu.CompilerParams(vmem_limit_bytes=24 * MIB)


def dot(left, right, left_dim=1, right_dim=0):
    return lax.dot_general(
        left, right, (((left_dim,), (right_dim,)), ((), ())), preferred_element_type=F32
    )


def lane_groups(value):
    return [value[:, j : j + 128] for j in range(0, value.shape[1], 128)]


def stat_lanes(n_code):
    return max(8 * n_code, 128)


def high_low(value):
    high = value.astype(BF16).astype(F32)
    return high, (value - high).astype(BF16).astype(F32)


def forward_kernel(
    n_code, tokens, grad_out, codebook, noise, sent, means, shifts,
    pair, book, noise_in, slot_a, slot_b, total, sums, pair_sem, book_sem, noise_sem,
):
    tiles, width, dim = book.shape
    n_tokens = tokens.shape[0]
    columns = [slice(c, c + CHUNK) for c in range(0, width, CHUNK)]
    slots = (slot_a, slot_b)

    def fetch(t):
        at = pl.multiple_of(t * width, width)
        return (
            pltpu.make_async_copy(codebook.at[pl.ds(at, width)], book.at[t], book_sem.at[t]),
            pltpu.make_async_copy(noise.at[:, pl.ds(at, width)], noise_in.at[t], noise_sem.at[t]),
        )

    def start(t):
        for copy in fetch(t):
            copy.start()

    def arrive(t):
        for copy in fetch(t):
            copy.wait()

    pair_copies = []
    for r in range(0, n_tokens, ROWS):
        for half, source in enumerate((tokens, grad_out)):
            pair_copies.append(
                pltpu.make_async_copy(
                    source.at[pl.ds(r, ROWS)],
                    pair.at[pl.ds(2 * r + half * ROWS, ROWS)],
                    pair_sem.at[len(pair_copies)],
                )
            )
    for copy in pair_copies:
        copy.start()
    start(0)

    def logits(both, t, r, c):
        noise_part = (noise_in[t, r : r + ROWS, c] * BF16(SHARPNESS)).astype(F32)
        return both[2 * r : 2 * r + ROWS] + noise_part

    def raise_shift(t, some):
        for c in some:
            both = dot(pair[...], book[t, c], 1, 1)
            for r in range(0, n_tokens, ROWS):
                at = slice(r, r + ROWS)
                shifts[at] = functools.reduce(
                    jnp.maximum, lane_groups(logits(both, t, r, c)), shifts[at]
                )

    def soften(t, s, fresh, last=None):
        if fresh is not None:
            @pl.when(fresh)
            def _():
                arrive(t)

                @pl.when(t + AHEAD < tiles)
                def _():
                    start(t + AHEAD)

        slot = slots[s]
        ahead = dot(pair[...], book[t, columns[0]], 1, 1)
        for k, c in enumerate(columns):
            both = ahead
            if k + 1 < len(columns):
                ahead = dot(pair[...], book[t, columns[k + 1]], 1, 1)
            elif last is not None:
                last()
            for r in range(0, n_tokens, ROWS):
                at = slice(r, r + ROWS)
                shift = jnp.concatenate([shifts[at]] * (CHUNK // 128), axis=1)
                weight = jnp.exp(logits(both, t, r, c) - shift)
                total[at] += sum(lane_groups(weight))
                slot[at, c] = weight.astype(BF16)
                gradient = both[2 * r + ROWS : 2 * r + 2 * ROWS]
                slot[n_tokens + r : n_tokens + r + ROWS, c] = (weight * gradient).astype(BF16)

    def accumulate(t, s):
        sums[...] += dot(slots[s][...], book[t])

    def attempt(state):
        again, _ = state
        fresh = again == 0
        shifts[...] = jnp.full(shifts.shape, -jnp.inf, F32)

        @pl.when(fresh)
        def _():
            raise_shift(0, columns[:1])

        @pl.when(jnp.logical_not(fresh))
        def _():
            def over(t, carry):
                raise_shift(t, columns)
                return carry

            lax.fori_loop(0, tiles, over, 0)

        shift = jnp.max(shifts[...], axis=1, keepdims=True).astype(BF16).astype(F32)
        shifts[...] = jnp.broadcast_to(shift, shifts.shape)
        total[...] = jnp.zeros(total.shape, F32)
        sums[...] = jnp.zeros(sums.shape, F32)
        soften(0, 0, None)

        def soften_pair(i, carry):
            soften(2 * i + 1, 1, fresh, lambda: accumulate(2 * i, 0))
            soften(2 * i + 2, 0, fresh, lambda: accumulate(2 * i + 1, 1))
            return carry

        lax.fori_loop(0, tiles // 2 - 1, soften_pair, 0)
        soften(tiles - 1, 1, fresh, lambda: accumulate(tiles - 2, 0))
        accumulate(tiles - 1, 1)
        fits = jnp.max(total[...]) < LARGEST
        return again + 1, jnp.logical_and(fresh, jnp.logical_not(fits))

    for copy in pair_copies:
        copy.wait()
    for r in range(0, n_tokens, ROWS):
        pair[2 * r : 2 * r + ROWS] = pair[2 * r : 2 * r + ROWS] * BF16(SHARPNESS)
    arrive(0)
    for t in range(1, min(AHEAD + 1, tiles)):
        start(t)
    lax.while_loop(lambda state: state[1], attempt, (jnp.int32(0), jnp.bool_(True)))

    shift = shifts[:, :1]
    mix = sums[:n_tokens]
    pulled = sums[n_tokens:]
    own_total = jnp.sum(total[...], axis=1, keepdims=True)
    own_grad = jnp.concatenate(
        [pair[2 * r + ROWS : 2 * r + 2 * ROWS] for r in range(0, n_tokens, ROWS)], axis=0
    )
    own_inner = jnp.sum(own_grad.astype(F32) * mix, axis=1, keepdims=True)
    mean = own_inner / own_total
    means[...] = jnp.broadcast_to(mean, means.shape)
    rows = n_tokens // n_code
    lanes = stat_lanes(n_code)
    half = lanes // 2
    lane = lax.broadcasted_iota(jnp.int32, (rows, lanes), 1)
    stats = jnp.zeros((rows, lanes), F32)
    parts = high_low(own_total) + high_low(own_inner)
    for g in range(n_code):
        at = slice(g * rows, (g + 1) * rows)
        for i, part in enumerate(parts):
            stats = jnp.where(lane == 4 * g + i, part[at], stats)
        stats = jnp.where((lane - half) // 4 == g, shift[at], stats)
    stats = stats.astype(BF16)
    for g in range(n_code):
        at = slice(g * rows, (g + 1) * rows)
        sent[g, :, :dim] = mix[at].astype(BF16)
        sent[g, :, dim : 2 * dim] = (pulled[at] - mean[at] * mix[at]).astype(BF16)
        sent[g, :, 2 * dim :] = stats


def roll_left(value, by):
    return pltpu.roll(value, value.shape[1] - by, 1)


def merged_stats(received):
    n_code = received.shape[0]
    lanes = stat_lanes(n_code)
    stats = [received[p, :, received.shape[2] - lanes :].astype(F32) for p in range(n_code)]
    top = functools.reduce(jnp.maximum, stats)
    scales = [roll_left(jnp.exp(s - top), lanes // 2) for s in stats]
    pairs = [s + roll_left(s, 1) for s in stats]
    inners = [roll_left(s, 2) for s in pairs]
    total = sum(a * s for a, s in zip(scales, pairs))
    inner = sum(a * s for a, s in zip(scales, inners)) / total
    means = [i / s for i, s in zip(inners, pairs)]
    return [a / total for a in scales], means, inner


def merge_kernel(me, received, spread):
    n_code, rows, _ = received.shape
    dim = spread.shape[2] // 2
    scales, means, inner = merged_stats(received)
    lane = lax.broadcasted_iota(jnp.int32, inner.shape, 1)
    mine = lane == 4 * me[0]

    def column(value):
        return jnp.sum(jnp.where(mine, value, 0.0), axis=1, keepdims=True)

    quantized = jnp.zeros((rows, dim), F32)
    gradient = jnp.zeros((rows, dim), F32)
    for p in range(n_code):
        scale = column(scales[p])
        offset = column(scales[p] * (means[p] - inner))
        mix = received[p, :, :dim].astype(F32)
        quantized += scale * mix
        gradient += scale * received[p, :, dim : 2 * dim].astype(F32) + offset * mix
    quantized = quantized.astype(BF16)
    gradient = (gradient / SOFTMAX_HEAT).astype(BF16)
    for p in range(n_code):
        spread[p, :, :dim] = quantized
        spread[p, :, dim:] = gradient


def weigh_kernel(
    tokens, grad_out, codebook, noise, means, shifts, codes, weighed,
    book, noise_in, code_out, weighed_out, sharp, book_sem, noise_sem, out_sem,
):
    tiles, width, _ = book.shape
    wide = codes.shape[2]
    steps = [(t, slice(c, c + wide)) for t in range(tiles) for c in range(0, width, wide)]

    def fetch(t):
        at = pl.ds(t * width, width)
        return (
            pltpu.make_async_copy(codebook.at[at], book.at[t], book_sem.at[t]),
            pltpu.make_async_copy(noise.at[:, at], noise_in.at[t], noise_sem.at[t]),
        )

    def start(t):
        for copy in fetch(t):
            copy.start()

    def send(k):
        return (
            pltpu.make_async_copy(code_out.at[k], codes.at[k], out_sem.at[0, k]),
            pltpu.make_async_copy(weighed_out.at[k], weighed.at[k], out_sem.at[1, k]),
        )

    def products_of(step):
        t, c = step
        if c.start == 0:
            for copy in fetch(t):
                copy.wait()
            if t + NEAR < tiles:
                start(t + NEAR)
        keys = book[t, c]
        return dot(sharp[...], keys, 1, 1), dot(grad_out[...], keys, 1, 1)

    for t in range(min(NEAR, tiles)):
        start(t)
    sharp[...] = tokens[...] * BF16(SHARPNESS)
    ahead = products_of(steps[0])
    for k, (t, c) in enumerate(steps):
        score, gradient = ahead
        if k + 1 < len(steps):
            ahead = products_of(steps[k + 1])
        shift = jnp.concatenate([shifts[...]] * (wide // 128), axis=1)
        mean = jnp.concatenate([means[...]] * (wide // 128), axis=1)
        noise_part = (noise_in[t, :, c] * BF16(SHARPNESS)).astype(F32)
        code = jnp.exp(score + noise_part - shift).astype(BF16)
        code_out[k] = code
        weighed_out[k] = (code.astype(F32) * (gradient - mean)).astype(BF16)
        for copy in send(k):
            copy.start()
    for k in range(len(steps)):
        for copy in send(k):
            copy.wait()


def backward_kernel(prepared, block, *rest):
    if prepared:
        codes, weighed, operands, out, *rest = rest
    else:
        code_at, tokens, grad_out, codes, weighed, received, out, operands, *rest = rest
        upper, lower, *rest = rest
    both_in, result, in_sem, out_sem = rest
    tiles, width, dim = result.shape
    n_tokens = both_in.shape[1] // 2

    def fetch(t):
        return [
            pltpu.make_async_copy(
                source.at[block[0] * tiles + t],
                both_in.at[t, pl.ds(half * n_tokens, n_tokens)],
                in_sem.at[half, t],
            )
            for half, source in enumerate((codes, weighed))
        ]

    def start(t):
        for copy in fetch(t):
            copy.start()

    for t in range(min(NEAR, tiles)):
        start(t)

    if not prepared:
        n_code, rows, _ = received.shape
        scales, means, inner = merged_stats(received)
        scale = jnp.zeros(inner.shape, F32)
        mean = jnp.zeros(inner.shape, F32)
        for p in range(n_code):
            scale = jnp.where(code_at[0] == p, scales[p], scale)
            mean = jnp.where(code_at[0] == p, means[p], mean)
        offset = mean - inner
        for g in range(n_code):
            part = slice(g * rows, (g + 1) * rows)
            at = slice(4 * g, 4 * g + 1)
            token = scale[:, at] * (tokens[part].astype(F32) / SOFTMAX_HEAT)
            upper[part] = scale[:, at] * grad_out[part].astype(F32) + offset[:, at] * token
            lower[part] = token
        operands[:, :n_tokens] = upper[...].T.astype(BF16)
        operands[:, n_tokens:] = lower[...].T.astype(BF16)

    def send(t):
        return pltpu.make_async_copy(
            result.at[t], out.at[pl.ds(t * width, width)], out_sem.at[t]
        )

    wide = min(WIDE, width)
    steps = [(t, slice(c, c + wide)) for t in range(tiles) for c in range(0, width, wide)]

    def product(step):
        t, c = step
        if c.start == 0:
            for copy in fetch(t):
                copy.wait()
            if t + NEAR < tiles:
                start(t + NEAR)
        return dot(operands[...], both_in[t, :, c])

    ahead = product(steps[0])
    for k, (t, c) in enumerate(steps):
        value = ahead
        if k + 1 < len(steps):
            ahead = product(steps[k + 1])
        result[t, c] = value.astype(BF16).T
        if c.stop == width:
            send(t).start()
    for t in range(tiles):
        send(t).wait()


def add_kernel(n_parts, *refs):
    parts, out = refs[:n_parts], refs[n_parts]
    held, result, in_sem, out_sem = refs[n_parts + 1 :]
    steps, rows, _ = result.shape

    def fetch(i):
        at = pl.ds(i * rows, rows)
        return [
            pltpu.make_async_copy(part.at[at], held.at[j, i], in_sem.at[j, i])
            for j, part in enumerate(parts)
        ]

    def send(i):
        return pltpu.make_async_copy(result.at[i], out.at[pl.ds(i * rows, rows)], out_sem.at[i])

    for i in range(steps):
        for copy in fetch(i):
            copy.start()
    for i in range(steps):
        for copy in fetch(i):
            copy.wait()
        result[i] = sum(held[j, i].astype(F32) for j in range(n_parts))
        send(i).start()
    for i in range(steps):
        send(i).wait()


def unpack_kernel(gathered, quantized, gradient):
    n_code, rows, both = gathered.shape
    dim = both // 2
    for g in range(n_code):
        at = slice(g * rows, (g + 1) * rows)
        quantized[at] = gathered[g, :, :dim].astype(F32)
        gradient[at] = gathered[g, :, dim:].astype(F32)


def swap(value, axis, size, mask):
    return lax.ppermute(value, axis, [(i, i ^ mask) for i in range(size)])


def local(n_dp, n_code, tokens, codebook, noise, grad_out):
    n_tokens, dim = tokens.shape
    n_codes = codebook.shape[0]
    rows = n_tokens // n_code
    block = n_codes // n_dp
    width = min(1024, block)
    wide = min(WIDE, width)
    tiles_in = n_codes // wide
    tiles = n_codes // width
    lanes = stat_lanes(n_code)
    products = 2 * n_tokens * n_codes * dim

    sent, means, shifts = pl.pallas_call(
        functools.partial(forward_kernel, n_code),
        out_shape=(
            jax.ShapeDtypeStruct((n_code, rows, 2 * dim + lanes), BF16),
            jax.ShapeDtypeStruct((n_tokens, 128), F32),
            jax.ShapeDtypeStruct((n_tokens, 128), F32),
        ),
        in_specs=[ANY, ANY, ANY, ANY],
        out_specs=(VMEM, VMEM, VMEM),
        scratch_shapes=[
            pltpu.VMEM((2 * n_tokens, dim), BF16),
            pltpu.VMEM((tiles, width, dim), BF16),
            pltpu.VMEM((tiles, n_tokens, width), BF16),
            pltpu.VMEM((2 * n_tokens, width), BF16),
            pltpu.VMEM((2 * n_tokens, width), BF16),
            pltpu.VMEM((n_tokens, 128), F32),
            pltpu.VMEM((2 * n_tokens, dim), F32),
            pltpu.SemaphoreType.DMA((2 * n_tokens // ROWS,)),
            pltpu.SemaphoreType.DMA((tiles,)),
            pltpu.SemaphoreType.DMA((tiles,)),
        ],
        compiler_params=FULL,
        cost_estimate=pl.CostEstimate(
            flops=4 * products, bytes_accessed=12 * MIB, transcendentals=n_tokens * n_codes
        ),
        name="forward",
    )(tokens, grad_out, codebook, noise)

    received = lax.all_to_all(sent, "code", 0, 0, tiled=True)
    codes, weighed = pl.pallas_call(
        weigh_kernel,
        out_shape=(pltpu.HBM((tiles_in, n_tokens, wide), BF16),) * 2,
        in_specs=[VMEM, VMEM, ANY, ANY, VMEM, VMEM],
        out_specs=(ANY, ANY),
        scratch_shapes=[
            pltpu.VMEM((tiles, width, dim), BF16),
            pltpu.VMEM((tiles, n_tokens, width), BF16),
            pltpu.VMEM((tiles_in, n_tokens, wide), BF16),
            pltpu.VMEM((tiles_in, n_tokens, wide), BF16),
            pltpu.VMEM((n_tokens, dim), BF16),
            pltpu.SemaphoreType.DMA((tiles,)),
            pltpu.SemaphoreType.DMA((tiles,)),
            pltpu.SemaphoreType.DMA((2, tiles_in)),
        ],
        compiler_params=FULL,
        cost_estimate=pl.CostEstimate(
            flops=2 * products, bytes_accessed=28 * MIB, transcendentals=n_tokens * n_codes
        ),
        name="weigh",
    )(tokens, grad_out, codebook, noise, means, shifts)
    received, weighed = lax.optimization_barrier((received, weighed))
    code_at = lax.axis_index("code")
    spread = pl.pallas_call(
        merge_kernel,
        out_shape=jax.ShapeDtypeStruct((n_code, rows, 2 * dim), BF16),
        in_specs=[SMEM, VMEM],
        out_specs=VMEM,
        compiler_params=SOME,
        name="merge",
    )(code_at[None], received)
    received, spread = lax.optimization_barrier((received, spread))
    gathered = lax.all_to_all(spread, "code", 0, 0, tiled=True)
    quantized, token_gradient = pl.pallas_call(
        unpack_kernel,
        out_shape=(jax.ShapeDtypeStruct((n_tokens, dim), F32),) * 2,
        in_specs=[VMEM],
        out_specs=(VMEM, VMEM),
        compiler_params=SOME,
        cost_estimate=pl.CostEstimate(
            flops=100 * products, bytes_accessed=400 * MIB, transcendentals=0
        ),
        name="unpack",
    )(gathered)

    block_tiles = block // wide
    streams = [
        pltpu.VMEM((block_tiles, 2 * n_tokens, wide), BF16),
        pltpu.VMEM((block_tiles, wide, dim), BF16),
        pltpu.SemaphoreType.DMA((2, block_tiles)),
        pltpu.SemaphoreType.DMA((block_tiles,)),
    ]
    block_shape = jax.ShapeDtypeStruct((block, dim), BF16)
    common = dict(
        compiler_params=MOST,
        cost_estimate=pl.CostEstimate(flops=1, bytes_accessed=1, transcendentals=0),
    )
    dp_at = lax.axis_index("dp")
    first, operands = pl.pallas_call(
        functools.partial(backward_kernel, False),
        out_shape=(block_shape, jax.ShapeDtypeStruct((dim, 2 * n_tokens), BF16)),
        in_specs=[SMEM, SMEM, VMEM, VMEM, ANY, ANY, VMEM],
        out_specs=(ANY, VMEM),
        scratch_shapes=[
            pltpu.VMEM((n_tokens, dim), F32), pltpu.VMEM((n_tokens, dim), F32),
        ] + streams,
        name="backward_first",
        **common,
    )(
        (dp_at ^ (n_dp - 1))[None], code_at[None], tokens, grad_out, codes, weighed, received
    )

    def backward(at):
        return pl.pallas_call(
            functools.partial(backward_kernel, True),
            out_shape=block_shape,
            in_specs=[SMEM, ANY, ANY, VMEM],
            out_specs=ANY,
            scratch_shapes=streams,
            name="backward",
            **common,
        )(at[None], codes, weighed, operands)

    blocks = [swap(first, "dp", n_dp, n_dp - 1)]
    blocks += [swap(backward(dp_at ^ d), "dp", n_dp, d) for d in range(1, n_dp - 1)]
    blocks.append(backward(dp_at))
    steps = max(block // 512, 1)
    own_rows = pl.pallas_call(
        functools.partial(add_kernel, n_dp),
        out_shape=jax.ShapeDtypeStruct((block, dim), F32),
        in_specs=[ANY] * n_dp,
        out_specs=ANY,
        scratch_shapes=[
            pltpu.VMEM((n_dp, steps, block // steps, dim), BF16),
            pltpu.VMEM((steps, block // steps, dim), F32),
            pltpu.SemaphoreType.DMA((n_dp, steps)),
            pltpu.SemaphoreType.DMA((steps,)),
        ],
        compiler_params=PART,
        cost_estimate=pl.CostEstimate(
            flops=0, bytes_accessed=(2 * n_dp + 4) * block * dim, transcendentals=0
        ),
        name="add",
    )(*blocks)
    return quantized, token_gradient, own_rows[None]


def solution(mesh):
    n_dp, n_code = mesh.shape["dp"], mesh.shape["code"]
    in_specs = (P("dp", None), P("code", None), P("dp", "code"), P("dp", None))
    out_specs = (P("dp", None), P("dp", None), P("code", "dp", None))
    return jax.shard_map(
        functools.partial(local, n_dp, n_code),
        mesh=mesh, in_specs=in_specs, out_specs=out_specs, check_vma=False,
    )
```

```python
import functools

import jax
import jax.numpy as jnp
from jax import lax
from jax.experimental import pallas as pl
from jax.experimental.pallas import tpu as pltpu
from jax.sharding import PartitionSpec as P

SOFTMAX_HEAT = 0.5
SHARPNESS = 1.0 / SOFTMAX_HEAT
BF16 = jnp.bfloat16
F32 = jnp.float32
MIB = 1 << 20
CHUNK = 512
WIDE = 512
AHEAD = 2
NEAR = 3
ROWS = 64
LARGEST = 2.0**60
VMEM = pl.BlockSpec(memory_space=pltpu.VMEM)
SMEM = pl.BlockSpec(memory_space=pltpu.SMEM)
ANY = pl.BlockSpec(memory_space=pl.ANY)
FULL = pltpu.CompilerParams(vmem_limit_bytes=60 * MIB)
MOST = pltpu.CompilerParams(vmem_limit_bytes=56 * MIB)
PART = pltpu.CompilerParams(vmem_limit_bytes=58 * MIB)
SOME = pltpu.CompilerParams(vmem_limit_bytes=24 * MIB)


def dot(left, right, left_dim=1, right_dim=0):
    return lax.dot_general(
        left, right, (((left_dim,), (right_dim,)), ((), ())), preferred_element_type=F32
    )


def lane_groups(value):
    return [value[:, j : j + 128] for j in range(0, value.shape[1], 128)]


def stat_lanes(n_code):
    return max(8 * n_code, 128)


def high_low(value):
    high = value.astype(BF16).astype(F32)
    return high, (value - high).astype(BF16).astype(F32)


def forward_kernel(
    n_code, tokens, grad_out, codebook, noise, sent, means, shifts,
    pair, book, noise_in, slot_a, slot_b, total, sums, pair_sem, book_sem, noise_sem,
):
    tiles, width, dim = book.shape
    n_tokens = tokens.shape[0]
    columns = [slice(c, c + CHUNK) for c in range(0, width, CHUNK)]
    slots = (slot_a, slot_b)

    def fetch(t):
        at = pl.multiple_of(t * width, width)
        return (
            pltpu.make_async_copy(codebook.at[pl.ds(at, width)], book.at[t], book_sem.at[t]),
            pltpu.make_async_copy(noise.at[:, pl.ds(at, width)], noise_in.at[t], noise_sem.at[t]),
        )

    def start(t):
        for copy in fetch(t):
            copy.start()

    def arrive(t):
        for copy in fetch(t):
            copy.wait()

    pair_copies = []
    for r in range(0, n_tokens, ROWS):
        for half, source in enumerate((tokens, grad_out)):
            pair_copies.append(
                pltpu.make_async_copy(
                    source.at[pl.ds(r, ROWS)],
                    pair.at[pl.ds(2 * r + half * ROWS, ROWS)],
                    pair_sem.at[len(pair_copies)],
                )
            )
    for copy in pair_copies:
        copy.start()
    start(0)

    def logits(both, t, r, c):
        noise_part = (noise_in[t, r : r + ROWS, c] * BF16(SHARPNESS)).astype(F32)
        return both[2 * r : 2 * r + ROWS] + noise_part

    def raise_shift(t, some):
        for c in some:
            both = dot(pair[...], book[t, c], 1, 1)
            for r in range(0, n_tokens, ROWS):
                at = slice(r, r + ROWS)
                shifts[at] = functools.reduce(
                    jnp.maximum, lane_groups(logits(both, t, r, c)), shifts[at]
                )

    def soften(t, s, fresh, last=None):
        if fresh is not None:
            @pl.when(fresh)
            def _():
                arrive(t)

                @pl.when(t + AHEAD < tiles)
                def _():
                    start(t + AHEAD)

        slot = slots[s]
        ahead = dot(pair[...], book[t, columns[0]], 1, 1)
        for k, c in enumerate(columns):
            both = ahead
            if k + 1 < len(columns):
                ahead = dot(pair[...], book[t, columns[k + 1]], 1, 1)
            elif last is not None:
                last()
            for r in range(0, n_tokens, ROWS):
                at = slice(r, r + ROWS)
                shift = jnp.concatenate([shifts[at]] * (CHUNK // 128), axis=1)
                weight = jnp.exp(logits(both, t, r, c) - shift)
                total[at] += sum(lane_groups(weight))
                slot[at, c] = weight.astype(BF16)
                gradient = both[2 * r + ROWS : 2 * r + 2 * ROWS]
                slot[n_tokens + r : n_tokens + r + ROWS, c] = (weight * gradient).astype(BF16)

    def accumulate(t, s):
        for half in (slice(0, n_tokens), slice(n_tokens, 2 * n_tokens)):
            sums[half] += dot(slots[s][half], book[t])

    def attempt(state):
        again, _ = state
        fresh = again == 0
        shifts[...] = jnp.full(shifts.shape, -jnp.inf, F32)

        @pl.when(fresh)
        def _():
            raise_shift(0, columns[:1])

        @pl.when(jnp.logical_not(fresh))
        def _():
            def over(t, carry):
                raise_shift(t, columns)
                return carry

            lax.fori_loop(0, tiles, over, 0)

        shift = jnp.max(shifts[...], axis=1, keepdims=True).astype(BF16).astype(F32)
        shifts[...] = jnp.broadcast_to(shift, shifts.shape)
        total[...] = jnp.zeros(total.shape, F32)
        sums[...] = jnp.zeros(sums.shape, F32)
        soften(0, 0, None)

        def soften_pair(i, carry):
            soften(2 * i + 1, 1, fresh, lambda: accumulate(2 * i, 0))
            soften(2 * i + 2, 0, fresh, lambda: accumulate(2 * i + 1, 1))
            return carry

        lax.fori_loop(0, tiles // 2 - 1, soften_pair, 0)
        soften(tiles - 1, 1, fresh, lambda: accumulate(tiles - 2, 0))
        accumulate(tiles - 1, 1)
        fits = jnp.max(total[...]) < LARGEST
        return again + 1, jnp.logical_and(fresh, jnp.logical_not(fits))

    for copy in pair_copies:
        copy.wait()
    for r in range(0, n_tokens, ROWS):
        pair[2 * r : 2 * r + ROWS] = pair[2 * r : 2 * r + ROWS] * BF16(SHARPNESS)
    arrive(0)
    for t in range(1, min(AHEAD + 1, tiles)):
        start(t)
    lax.while_loop(lambda state: state[1], attempt, (jnp.int32(0), jnp.bool_(True)))

    shift = shifts[:, :1]
    mix = sums[:n_tokens]
    pulled = sums[n_tokens:]
    own_total = jnp.sum(total[...], axis=1, keepdims=True)
    own_grad = jnp.concatenate(
        [pair[2 * r + ROWS : 2 * r + 2 * ROWS] for r in range(0, n_tokens, ROWS)], axis=0
    )
    own_inner = jnp.sum(own_grad.astype(F32) * mix, axis=1, keepdims=True)
    mean = own_inner / own_total
    means[...] = jnp.broadcast_to(mean, means.shape)
    rows = n_tokens // n_code
    lanes = stat_lanes(n_code)
    half = lanes // 2
    lane = lax.broadcasted_iota(jnp.int32, (rows, lanes), 1)
    stats = jnp.zeros((rows, lanes), F32)
    parts = high_low(own_total) + high_low(own_inner)
    for g in range(n_code):
        at = slice(g * rows, (g + 1) * rows)
        for i, part in enumerate(parts):
            stats = jnp.where(lane == 4 * g + i, part[at], stats)
        stats = jnp.where((lane - half) // 4 == g, shift[at], stats)
    stats = stats.astype(BF16)
    for g in range(n_code):
        at = slice(g * rows, (g + 1) * rows)
        sent[g, :, :dim] = mix[at].astype(BF16)
        sent[g, :, dim : 2 * dim] = (pulled[at] - mean[at] * mix[at]).astype(BF16)
        sent[g, :, 2 * dim :] = stats


def roll_left(value, by):
    return pltpu.roll(value, value.shape[1] - by, 1)


def merged_stats(received):
    n_code = received.shape[0]
    lanes = stat_lanes(n_code)
    stats = [received[p, :, received.shape[2] - lanes :].astype(F32) for p in range(n_code)]
    top = functools.reduce(jnp.maximum, stats)
    scales = [roll_left(jnp.exp(s - top), lanes // 2) for s in stats]
    pairs = [s + roll_left(s, 1) for s in stats]
    inners = [roll_left(s, 2) for s in pairs]
    total = sum(a * s for a, s in zip(scales, pairs))
    inner = sum(a * s for a, s in zip(scales, inners)) / total
    means = [i / s for i, s in zip(inners, pairs)]
    return [a / total for a in scales], means, inner


def merge_kernel(me, received, spread):
    n_code, rows, _ = received.shape
    dim = spread.shape[2] // 2
    scales, means, inner = merged_stats(received)
    lane = lax.broadcasted_iota(jnp.int32, inner.shape, 1)
    mine = lane == 4 * me[0]

    def column(value):
        return jnp.sum(jnp.where(mine, value, 0.0), axis=1, keepdims=True)

    quantized = jnp.zeros((rows, dim), F32)
    gradient = jnp.zeros((rows, dim), F32)
    for p in range(n_code):
        scale = column(scales[p])
        offset = column(scales[p] * (means[p] - inner))
        mix = received[p, :, :dim].astype(F32)
        quantized += scale * mix
        gradient += scale * received[p, :, dim : 2 * dim].astype(F32) + offset * mix
    quantized = quantized.astype(BF16)
    gradient = (gradient / SOFTMAX_HEAT).astype(BF16)
    for p in range(n_code):
        spread[p, :, :dim] = quantized
        spread[p, :, dim:] = gradient


def weigh_kernel(
    tokens, grad_out, codebook, noise, means, shifts, codes, weighed,
    book, noise_in, code_out, weighed_out, sharp, book_sem, noise_sem, out_sem,
):
    tiles, width, _ = book.shape
    wide = codes.shape[2]
    steps = [(t, slice(c, c + wide)) for t in range(tiles) for c in range(0, width, wide)]

    def fetch(t):
        at = pl.ds(t * width, width)
        return (
            pltpu.make_async_copy(codebook.at[at], book.at[t], book_sem.at[t]),
            pltpu.make_async_copy(noise.at[:, at], noise_in.at[t], noise_sem.at[t]),
        )

    def start(t):
        for copy in fetch(t):
            copy.start()

    def send(k):
        return (
            pltpu.make_async_copy(code_out.at[k], codes.at[k], out_sem.at[0, k]),
            pltpu.make_async_copy(weighed_out.at[k], weighed.at[k], out_sem.at[1, k]),
        )

    def products_of(step):
        t, c = step
        if c.start == 0:
            for copy in fetch(t):
                copy.wait()
            if t + NEAR < tiles:
                start(t + NEAR)
        keys = book[t, c]
        return dot(sharp[...], keys, 1, 1), dot(grad_out[...], keys, 1, 1)

    for t in range(min(NEAR, tiles)):
        start(t)
    sharp[...] = tokens[...] * BF16(SHARPNESS)
    ahead = products_of(steps[0])
    for k, (t, c) in enumerate(steps):
        score, gradient = ahead
        if k + 1 < len(steps):
            ahead = products_of(steps[k + 1])
        shift = jnp.concatenate([shifts[...]] * (wide // 128), axis=1)
        mean = jnp.concatenate([means[...]] * (wide // 128), axis=1)
        noise_part = (noise_in[t, :, c] * BF16(SHARPNESS)).astype(F32)
        code = jnp.exp(score + noise_part - shift).astype(BF16)
        code_out[k] = code
        weighed_out[k] = (code.astype(F32) * (gradient - mean)).astype(BF16)
        for copy in send(k):
            copy.start()
    for k in range(len(steps)):
        for copy in send(k):
            copy.wait()


def backward_kernel(prepared, block, *rest):
    if prepared:
        codes, weighed, operands, out, *rest = rest
    else:
        code_at, tokens, grad_out, codes, weighed, received, out, operands, *rest = rest
        upper, lower, *rest = rest
    both_in, result, in_sem, out_sem = rest
    tiles, width, dim = result.shape
    n_tokens = both_in.shape[1] // 2

    def fetch(t):
        return [
            pltpu.make_async_copy(
                source.at[block[0] * tiles + t],
                both_in.at[t, pl.ds(half * n_tokens, n_tokens)],
                in_sem.at[half, t],
            )
            for half, source in enumerate((codes, weighed))
        ]

    def start(t):
        for copy in fetch(t):
            copy.start()

    for t in range(tiles):
        start(t)

    if not prepared:
        n_code, rows, _ = received.shape
        scales, means, inner = merged_stats(received)
        scale = jnp.zeros(inner.shape, F32)
        mean = jnp.zeros(inner.shape, F32)
        for p in range(n_code):
            scale = jnp.where(code_at[0] == p, scales[p], scale)
            mean = jnp.where(code_at[0] == p, means[p], mean)
        offset = mean - inner
        for g in range(n_code):
            part = slice(g * rows, (g + 1) * rows)
            at = slice(4 * g, 4 * g + 1)
            token = scale[:, at] * (tokens[part].astype(F32) / SOFTMAX_HEAT)
            upper[part] = scale[:, at] * grad_out[part].astype(F32) + offset[:, at] * token
            lower[part] = token
        operands[:, :n_tokens] = upper[...].T.astype(BF16)
        operands[:, n_tokens:] = lower[...].T.astype(BF16)

    def send(t):
        return pltpu.make_async_copy(
            result.at[t], out.at[pl.ds(t * width, width)], out_sem.at[t]
        )

    wide = min(WIDE, width)
    steps = [(t, slice(c, c + wide)) for t in range(tiles) for c in range(0, width, wide)]

    def product(step):
        t, c = step
        if c.start == 0:
            for copy in fetch(t):
                copy.wait()
        return dot(operands[...], both_in[t, :, c])

    ahead = product(steps[0])
    for k, (t, c) in enumerate(steps):
        value = ahead
        if k + 1 < len(steps):
            ahead = product(steps[k + 1])
        result[t, c] = value.astype(BF16).T
        if c.stop == width:
            send(t).start()
    for t in range(tiles):
        send(t).wait()


def add_kernel(n_parts, *refs):
    parts, out = refs[:n_parts], refs[n_parts]
    held, result, in_sem, out_sem = refs[n_parts + 1 :]
    steps, rows, _ = result.shape

    def fetch(i):
        at = pl.ds(i * rows, rows)
        return [
            pltpu.make_async_copy(part.at[at], held.at[j, i], in_sem.at[j, i])
            for j, part in enumerate(parts)
        ]

    def send(i):
        return pltpu.make_async_copy(result.at[i], out.at[pl.ds(i * rows, rows)], out_sem.at[i])

    for i in range(steps):
        for copy in fetch(i):
            copy.start()
    for i in range(steps):
        for copy in fetch(i):
            copy.wait()
        result[i] = sum(held[j, i].astype(F32) for j in range(n_parts))
        send(i).start()
    for i in range(steps):
        send(i).wait()


def unpack_kernel(gathered, quantized, gradient):
    n_code, rows, both = gathered.shape
    dim = both // 2
    for g in range(n_code):
        at = slice(g * rows, (g + 1) * rows)
        quantized[at] = gathered[g, :, :dim].astype(F32)
        gradient[at] = gathered[g, :, dim:].astype(F32)


def swap(value, axis, size, mask):
    return lax.ppermute(value, axis, [(i, i ^ mask) for i in range(size)])


def local(n_dp, n_code, tokens, codebook, noise, grad_out):
    n_tokens, dim = tokens.shape
    n_codes = codebook.shape[0]
    rows = n_tokens // n_code
    block = n_codes // n_dp
    width = min(1024, block)
    wide = min(WIDE, width)
    tiles_in = n_codes // wide
    tiles = n_codes // width
    lanes = stat_lanes(n_code)
    products = 2 * n_tokens * n_codes * dim

    sent, means, shifts = pl.pallas_call(
        functools.partial(forward_kernel, n_code),
        out_shape=(
            jax.ShapeDtypeStruct((n_code, rows, 2 * dim + lanes), BF16),
            jax.ShapeDtypeStruct((n_tokens, 128), F32),
            jax.ShapeDtypeStruct((n_tokens, 128), F32),
        ),
        in_specs=[ANY, ANY, ANY, ANY],
        out_specs=(VMEM, VMEM, VMEM),
        scratch_shapes=[
            pltpu.VMEM((2 * n_tokens, dim), BF16),
            pltpu.VMEM((tiles, width, dim), BF16),
            pltpu.VMEM((tiles, n_tokens, width), BF16),
            pltpu.VMEM((2 * n_tokens, width), BF16),
            pltpu.VMEM((2 * n_tokens, width), BF16),
            pltpu.VMEM((n_tokens, 128), F32),
            pltpu.VMEM((2 * n_tokens, dim), F32),
            pltpu.SemaphoreType.DMA((2 * n_tokens // ROWS,)),
            pltpu.SemaphoreType.DMA((tiles,)),
            pltpu.SemaphoreType.DMA((tiles,)),
        ],
        compiler_params=FULL,
        cost_estimate=pl.CostEstimate(
            flops=4 * products, bytes_accessed=12 * MIB, transcendentals=n_tokens * n_codes
        ),
        name="forward",
    )(tokens, grad_out, codebook, noise)

    received = lax.all_to_all(sent, "code", 0, 0, tiled=True)
    codes, weighed = pl.pallas_call(
        weigh_kernel,
        out_shape=(pltpu.HBM((tiles_in, n_tokens, wide), BF16),) * 2,
        in_specs=[VMEM, VMEM, ANY, ANY, VMEM, VMEM],
        out_specs=(ANY, ANY),
        scratch_shapes=[
            pltpu.VMEM((tiles, width, dim), BF16),
            pltpu.VMEM((tiles, n_tokens, width), BF16),
            pltpu.VMEM((tiles_in, n_tokens, wide), BF16),
            pltpu.VMEM((tiles_in, n_tokens, wide), BF16),
            pltpu.VMEM((n_tokens, dim), BF16),
            pltpu.SemaphoreType.DMA((tiles,)),
            pltpu.SemaphoreType.DMA((tiles,)),
            pltpu.SemaphoreType.DMA((2, tiles_in)),
        ],
        compiler_params=FULL,
        cost_estimate=pl.CostEstimate(
            flops=2 * products, bytes_accessed=28 * MIB, transcendentals=n_tokens * n_codes
        ),
        name="weigh",
    )(tokens, grad_out, codebook, noise, means, shifts)
    received, weighed = lax.optimization_barrier((received, weighed))
    code_at = lax.axis_index("code")
    spread = pl.pallas_call(
        merge_kernel,
        out_shape=jax.ShapeDtypeStruct((n_code, rows, 2 * dim), BF16),
        in_specs=[SMEM, VMEM],
        out_specs=VMEM,
        compiler_params=SOME,
        name="merge",
    )(code_at[None], received)
    received, spread = lax.optimization_barrier((received, spread))
    gathered = lax.all_to_all(spread, "code", 0, 0, tiled=True)
    quantized, token_gradient = pl.pallas_call(
        unpack_kernel,
        out_shape=(jax.ShapeDtypeStruct((n_tokens, dim), F32),) * 2,
        in_specs=[VMEM],
        out_specs=(VMEM, VMEM),
        compiler_params=SOME,
        cost_estimate=pl.CostEstimate(
            flops=100 * products, bytes_accessed=400 * MIB, transcendentals=0
        ),
        name="unpack",
    )(gathered)

    block_tiles = block // wide
    streams = [
        pltpu.VMEM((block_tiles, 2 * n_tokens, wide), BF16),
        pltpu.VMEM((block_tiles, wide, dim), BF16),
        pltpu.SemaphoreType.DMA((2, block_tiles)),
        pltpu.SemaphoreType.DMA((block_tiles,)),
    ]
    block_shape = jax.ShapeDtypeStruct((block, dim), BF16)
    common = dict(
        compiler_params=MOST,
        cost_estimate=pl.CostEstimate(flops=1, bytes_accessed=1, transcendentals=0),
    )
    dp_at = lax.axis_index("dp")
    first, operands = pl.pallas_call(
        functools.partial(backward_kernel, False),
        out_shape=(block_shape, jax.ShapeDtypeStruct((dim, 2 * n_tokens), BF16)),
        in_specs=[SMEM, SMEM, VMEM, VMEM, ANY, ANY, VMEM],
        out_specs=(ANY, VMEM),
        scratch_shapes=[
            pltpu.VMEM((n_tokens, dim), F32), pltpu.VMEM((n_tokens, dim), F32),
        ] + streams,
        name="backward_first",
        **common,
    )(
        (dp_at ^ (n_dp - 1))[None], code_at[None], tokens, grad_out, codes, weighed, received
    )

    def backward(at):
        return pl.pallas_call(
            functools.partial(backward_kernel, True),
            out_shape=block_shape,
            in_specs=[SMEM, ANY, ANY, VMEM],
            out_specs=ANY,
            scratch_shapes=streams,
            name="backward",
            **common,
        )(at[None], codes, weighed, operands)

    blocks = [swap(first, "dp", n_dp, n_dp - 1)]
    blocks += [swap(backward(dp_at ^ d), "dp", n_dp, d) for d in range(1, n_dp - 1)]
    blocks.append(backward(dp_at))
    steps = max(block // 512, 1)
    own_rows = pl.pallas_call(
        functools.partial(add_kernel, n_dp),
        out_shape=jax.ShapeDtypeStruct((block, dim), F32),
        in_specs=[ANY] * n_dp,
        out_specs=ANY,
        scratch_shapes=[
            pltpu.VMEM((n_dp, steps, block // steps, dim), BF16),
            pltpu.VMEM((steps, block // steps, dim), F32),
            pltpu.SemaphoreType.DMA((n_dp, steps)),
            pltpu.SemaphoreType.DMA((steps,)),
        ],
        compiler_params=PART,
        cost_estimate=pl.CostEstimate(
            flops=0, bytes_accessed=(2 * n_dp + 4) * block * dim, transcendentals=0
        ),
        name="add",
    )(*blocks)
    return quantized, token_gradient, own_rows[None]


def solution(mesh):
    n_dp, n_code = mesh.shape["dp"], mesh.shape["code"]
    in_specs = (P("dp", None), P("code", None), P("dp", "code"), P("dp", None))
    out_specs = (P("dp", None), P("dp", None), P("code", "dp", None))
    return jax.shard_map(
        functools.partial(local, n_dp, n_code),
        mesh=mesh, in_specs=in_specs, out_specs=out_specs, check_vma=False,
    )
```

```python
import functools

import jax
import jax.numpy as jnp
from jax import lax
from jax.experimental import pallas as pl
from jax.experimental.pallas import tpu as pltpu
from jax.sharding import PartitionSpec as P

SOFTMAX_HEAT = 0.5
SHARPNESS = 1.0 / SOFTMAX_HEAT
BF16 = jnp.bfloat16
F32 = jnp.float32
MIB = 1 << 20
CHUNK = 256
WIDE = 512
AHEAD = 2
NEAR = 3
ROWS = 64
LARGEST = 2.0**60
VMEM = pl.BlockSpec(memory_space=pltpu.VMEM)
SMEM = pl.BlockSpec(memory_space=pltpu.SMEM)
ANY = pl.BlockSpec(memory_space=pl.ANY)
FULL = pltpu.CompilerParams(vmem_limit_bytes=60 * MIB)
MOST = pltpu.CompilerParams(vmem_limit_bytes=56 * MIB)
PART = pltpu.CompilerParams(vmem_limit_bytes=58 * MIB)
SOME = pltpu.CompilerParams(vmem_limit_bytes=24 * MIB)


def dot(left, right, left_dim=1, right_dim=0):
    return lax.dot_general(
        left, right, (((left_dim,), (right_dim,)), ((), ())), preferred_element_type=F32
    )


def lane_groups(value):
    return [value[:, j : j + 128] for j in range(0, value.shape[1], 128)]


def stat_lanes(n_code):
    return max(8 * n_code, 128)


def high_low(value):
    high = value.astype(BF16).astype(F32)
    return high, (value - high).astype(BF16).astype(F32)


def forward_kernel(
    n_code, tokens, grad_out, codebook, noise, sent, sides,
    pair, book, noise_in, slot_a, slot_b, shifts, total, sums, sent_out, sides_out,
    pair_sem, book_sem, noise_sem, first_sem, out_sem,
):
    tiles, width, dim = book.shape
    n_tokens = tokens.shape[0]
    columns = [slice(c, c + CHUNK) for c in range(0, width, CHUNK)]
    slots = (slot_a, slot_b)

    def fetch(t):
        at = pl.multiple_of(t * width, width)
        return (
            pltpu.make_async_copy(codebook.at[pl.ds(at, width)], book.at[t], book_sem.at[t]),
            pltpu.make_async_copy(noise.at[:, pl.ds(at, width)], noise_in.at[t], noise_sem.at[t]),
        )

    def start(t):
        for copy in fetch(t):
            copy.start()

    def arrive(t):
        for copy in fetch(t):
            copy.wait()

    pair_copies = []
    for r in range(0, n_tokens, ROWS):
        for half, source in enumerate((tokens, grad_out)):
            pair_copies.append(
                pltpu.make_async_copy(
                    source.at[pl.ds(r, ROWS)],
                    pair.at[pl.ds(2 * r + half * ROWS, ROWS)],
                    pair_sem.at[len(pair_copies)],
                )
            )
    halves = []
    for h in range(2):
        at = pl.ds(h * (width // 2), width // 2)
        halves.append((
            pltpu.make_async_copy(codebook.at[at], book.at[0, at], first_sem.at[h, 0]),
            pltpu.make_async_copy(noise.at[:, at], noise_in.at[0, :, at], first_sem.at[h, 1]),
        ))
    halves[0][0].start()
    for copy in pair_copies:
        copy.start()
    halves[0][1].start()
    for copy in halves[1]:
        copy.start()

    def logits(both, t, r, c):
        noise_part = (noise_in[t, r : r + ROWS, c] * BF16(SHARPNESS)).astype(F32)
        return both[2 * r : 2 * r + ROWS] + noise_part

    def raise_shift(t, some):
        for c in some:
            both = dot(pair[...], book[t, c], 1, 1)
            for r in range(0, n_tokens, ROWS):
                at = slice(r, r + ROWS)
                shifts[at] = functools.reduce(
                    jnp.maximum, lane_groups(logits(both, t, r, c)), shifts[at]
                )

    def soften(t, s, fresh, last=None):
        if fresh is not None:
            @pl.when(fresh)
            def _():
                arrive(t)

                @pl.when(t + AHEAD < tiles)
                def _():
                    start(t + AHEAD)

        slot = slots[s]
        ahead = dot(pair[...], book[t, columns[0]], 1, 1)
        for k, c in enumerate(columns):
            both = ahead
            if k + 1 < len(columns):
                ahead = dot(pair[...], book[t, columns[k + 1]], 1, 1)
            elif last is not None:
                last()
            for r in range(0, n_tokens, ROWS):
                at = slice(r, r + ROWS)
                shift = jnp.concatenate([shifts[at]] * (CHUNK // 128), axis=1)
                weight = jnp.exp(logits(both, t, r, c) - shift)
                total[at] += sum(lane_groups(weight))
                slot[at, c] = weight.astype(BF16)
                gradient = both[2 * r + ROWS : 2 * r + 2 * ROWS]
                slot[n_tokens + r : n_tokens + r + ROWS, c] = (weight * gradient).astype(BF16)

    def accumulate(t, s):
        sums[...] += dot(slots[s][...], book[t])

    def attempt(state):
        again, _ = state
        fresh = again == 0
        shifts[...] = jnp.full(shifts.shape, -jnp.inf, F32)

        @pl.when(fresh)
        def _():
            raise_shift(0, columns[:1])

        @pl.when(jnp.logical_not(fresh))
        def _():
            def over(t, carry):
                raise_shift(t, columns)
                return carry

            lax.fori_loop(0, tiles, over, 0)

        shift = jnp.max(shifts[...], axis=1, keepdims=True).astype(BF16).astype(F32)
        shifts[...] = jnp.broadcast_to(shift, shifts.shape)
        total[...] = jnp.zeros(total.shape, F32)
        sums[...] = jnp.zeros(sums.shape, F32)

        @pl.when(fresh)
        def _():
            for copy in halves[1]:
                copy.wait()

        soften(0, 0, None)

        def soften_pair(i, carry):
            soften(2 * i + 1, 1, fresh, lambda: accumulate(2 * i, 0))
            soften(2 * i + 2, 0, fresh, lambda: accumulate(2 * i + 1, 1))
            return carry

        lax.fori_loop(0, tiles // 2 - 1, soften_pair, 0)
        soften(tiles - 1, 1, fresh, lambda: accumulate(tiles - 2, 0))
        accumulate(tiles - 1, 1)
        fits = jnp.max(total[...]) < LARGEST
        return again + 1, jnp.logical_and(fresh, jnp.logical_not(fits))

    for copy in pair_copies:
        copy.wait()
    for r in range(0, n_tokens, ROWS):
        pair[2 * r : 2 * r + ROWS] = pair[2 * r : 2 * r + ROWS] * BF16(SHARPNESS)
    for copy in halves[0]:
        copy.wait()
    for t in range(1, min(AHEAD + 1, tiles)):
        start(t)
    lax.while_loop(lambda state: state[1], attempt, (jnp.int32(0), jnp.bool_(True)))

    shift = shifts[:, :1]
    mix = sums[:n_tokens]
    pulled = sums[n_tokens:]
    own_total = jnp.sum(total[...], axis=1, keepdims=True)
    own_grad = jnp.concatenate(
        [pair[2 * r + ROWS : 2 * r + 2 * ROWS] for r in range(0, n_tokens, ROWS)], axis=0
    )
    own_inner = jnp.sum(own_grad.astype(F32) * mix, axis=1, keepdims=True)
    mean = own_inner / own_total
    side = lax.broadcasted_iota(jnp.int32, sides_out.shape, 1)
    sides_out[...] = jnp.where(side < 64, mean, shift)
    copies = [pltpu.make_async_copy(sides_out, sides, out_sem.at[0])]
    copies[0].start()
    rows = n_tokens // n_code
    lanes = stat_lanes(n_code)
    half = lanes // 2
    lane = lax.broadcasted_iota(jnp.int32, (rows, lanes), 1)
    stats = jnp.zeros((rows, lanes), F32)
    parts = high_low(own_total) + high_low(own_inner)
    for g in range(n_code):
        at = slice(g * rows, (g + 1) * rows)
        for i, part in enumerate(parts):
            stats = jnp.where(lane == 4 * g + i, part[at], stats)
        stats = jnp.where((lane - half) // 4 == g, shift[at], stats)
    stats = stats.astype(BF16)
    group = n_code // min(n_code, 4)
    for g in range(n_code):
        at = slice(g * rows, (g + 1) * rows)
        sent_out[g, :, :dim] = mix[at].astype(BF16)
        sent_out[g, :, dim : 2 * dim] = (pulled[at] - mean[at] * mix[at]).astype(BF16)
        sent_out[g, :, 2 * dim :] = stats
        if (g + 1) % group == 0:
            part = pl.ds(g + 1 - group, group)
            copies.append(
                pltpu.make_async_copy(sent_out.at[part], sent.at[part], out_sem.at[len(copies)])
            )
            copies[-1].start()
    for copy in copies:
        copy.wait()


def roll_left(value, by):
    return pltpu.roll(value, value.shape[1] - by, 1)


def merged_stats(received):
    n_code = received.shape[0]
    lanes = stat_lanes(n_code)
    stats = [received[p, :, received.shape[2] - lanes :].astype(F32) for p in range(n_code)]
    top = functools.reduce(jnp.maximum, stats)
    scales = [roll_left(jnp.exp(s - top), lanes // 2) for s in stats]
    pairs = [s + roll_left(s, 1) for s in stats]
    inners = [roll_left(s, 2) for s in pairs]
    total = sum(a * s for a, s in zip(scales, pairs))
    inner = sum(a * s for a, s in zip(scales, inners)) / total
    means = [i / s for i, s in zip(inners, pairs)]
    return [a / total for a in scales], means, inner


def merge_kernel(me, received, spread):
    n_code, rows, _ = received.shape
    dim = spread.shape[2] // 2
    scales, means, inner = merged_stats(received)
    lane = lax.broadcasted_iota(jnp.int32, inner.shape, 1)
    mine = lane == 4 * me[0]

    def column(value):
        return jnp.sum(jnp.where(mine, value, 0.0), axis=1, keepdims=True)

    quantized = jnp.zeros((rows, dim), F32)
    gradient = jnp.zeros((rows, dim), F32)
    for p in range(n_code):
        scale = column(scales[p])
        offset = column(scales[p] * (means[p] - inner))
        mix = received[p, :, :dim].astype(F32)
        quantized += scale * mix
        gradient += scale * received[p, :, dim : 2 * dim].astype(F32) + offset * mix
    quantized = quantized.astype(BF16)
    gradient = (gradient / SOFTMAX_HEAT).astype(BF16)
    for p in range(n_code):
        spread[p, :, :dim] = quantized
        spread[p, :, dim:] = gradient


def weigh_kernel(
    tokens, grad_out, codebook, noise, sides, codes, weighed,
    book, noise_in, code_out, weighed_out, sharp, means, shifts, book_sem, noise_sem, out_sem,
):
    tiles, width, _ = book.shape
    wide = codes.shape[2]
    steps = [(t, slice(c, c + wide)) for t in range(tiles) for c in range(0, width, wide)]

    def fetch(t):
        at = pl.ds(t * width, width)
        return (
            pltpu.make_async_copy(codebook.at[at], book.at[t], book_sem.at[t]),
            pltpu.make_async_copy(noise.at[:, at], noise_in.at[t], noise_sem.at[t]),
        )

    def start(t):
        for copy in fetch(t):
            copy.start()

    def send(k):
        return (
            pltpu.make_async_copy(code_out.at[k], codes.at[k], out_sem.at[0, k]),
            pltpu.make_async_copy(weighed_out.at[k], weighed.at[k], out_sem.at[1, k]),
        )

    def products_of(step):
        t, c = step
        if c.start == 0:
            for copy in fetch(t):
                copy.wait()
            if t + NEAR < tiles:
                start(t + NEAR)
        keys = book[t, c]
        return dot(sharp[...], keys, 1, 1), dot(grad_out[...], keys, 1, 1)

    for t in range(min(NEAR, tiles)):
        start(t)
    sharp[...] = tokens[...] * BF16(SHARPNESS)
    means[...] = jnp.broadcast_to(sides[:, :1], means.shape)
    shifts[...] = jnp.broadcast_to(sides[:, 64:65], shifts.shape)
    ahead = products_of(steps[0])
    for k, (t, c) in enumerate(steps):
        score, gradient = ahead
        if k + 1 < len(steps):
            ahead = products_of(steps[k + 1])
        shift = jnp.concatenate([shifts[...]] * (wide // 128), axis=1)
        mean = jnp.concatenate([means[...]] * (wide // 128), axis=1)
        noise_part = (noise_in[t, :, c] * BF16(SHARPNESS)).astype(F32)
        code = jnp.exp(score + noise_part - shift).astype(BF16)
        code_out[k] = code
        weighed_out[k] = (code.astype(F32) * (gradient - mean)).astype(BF16)
        for copy in send(k):
            copy.start()
    for k in range(len(steps)):
        for copy in send(k):
            copy.wait()


def backward_kernel(prepared, block, *rest):
    if prepared:
        codes, weighed, given, out, *rest = rest
    else:
        code_at, tokens, grad_out, codes, weighed, received, out, kept, *rest = rest
        own, upper, lower, *rest = rest
    both_in, result, operands, in_sem, out_sem, own_sem = rest
    tiles, width, dim = result.shape
    n_tokens = both_in.shape[1] // 2

    def fetch(t):
        return [
            pltpu.make_async_copy(
                source.at[block[0] * tiles + t],
                both_in.at[t, pl.ds(half * n_tokens, n_tokens)],
                in_sem.at[half, t],
            )
            for half, source in enumerate((codes, weighed))
        ]

    def start(t):
        for copy in fetch(t):
            copy.start()

    start(0)
    if prepared:
        own_copies = [pltpu.make_async_copy(given, operands, own_sem.at[0])]
    else:
        own_copies = [
            pltpu.make_async_copy(tokens, own.at[0], own_sem.at[0]),
            pltpu.make_async_copy(grad_out, own.at[1], own_sem.at[1]),
        ]
    for copy in own_copies:
        copy.start()
    for t in range(1, min(NEAR, tiles)):
        start(t)

    if prepared:
        own_copies[0].wait()
    else:
        n_code, rows, _ = received.shape
        scales, means, inner = merged_stats(received)
        scale = jnp.zeros(inner.shape, F32)
        mean = jnp.zeros(inner.shape, F32)
        for p in range(n_code):
            scale = jnp.where(code_at[0] == p, scales[p], scale)
            mean = jnp.where(code_at[0] == p, means[p], mean)
        offset = mean - inner
        for copy in own_copies:
            copy.wait()
        for g in range(n_code):
            part = slice(g * rows, (g + 1) * rows)
            at = slice(4 * g, 4 * g + 1)
            token = scale[:, at] * (own[0, part].astype(F32) / SOFTMAX_HEAT)
            upper[part] = scale[:, at] * own[1, part].astype(F32) + offset[:, at] * token
            lower[part] = token
        operands[:, :n_tokens] = upper[...].T.astype(BF16)
        operands[:, n_tokens:] = lower[...].T.astype(BF16)
        keep = pltpu.make_async_copy(operands, kept, own_sem.at[0])
        keep.start()

    def send(t):
        return pltpu.make_async_copy(
            result.at[t], out.at[pl.ds(t * width, width)], out_sem.at[t]
        )

    wide = min(WIDE, width)
    steps = [(t, slice(c, c + wide)) for t in range(tiles) for c in range(0, width, wide)]

    def product(step):
        t, c = step
        if c.start == 0:
            for copy in fetch(t):
                copy.wait()
            if t + NEAR < tiles:
                start(t + NEAR)
        return dot(operands[...], both_in[t, :, c])

    ahead = product(steps[0])
    for k, (t, c) in enumerate(steps):
        value = ahead
        if k + 1 < len(steps):
            ahead = product(steps[k + 1])
        result[t, c] = value.astype(BF16).T
        if c.stop == width:
            send(t).start()
    for t in range(tiles):
        send(t).wait()
    if not prepared:
        keep.wait()


def add_kernel(n_parts, *refs):
    parts, out = refs[:n_parts], refs[n_parts]
    held, result, in_sem, out_sem = refs[n_parts + 1 :]
    steps, rows, _ = result.shape

    def fetch(i):
        at = pl.ds(i * rows, rows)
        return [
            pltpu.make_async_copy(part.at[at], held.at[j, i], in_sem.at[j, i])
            for j, part in enumerate(parts)
        ]

    def send(i):
        return pltpu.make_async_copy(result.at[i], out.at[pl.ds(i * rows, rows)], out_sem.at[i])

    for i in range(steps):
        for copy in fetch(i):
            copy.start()
    for i in range(steps):
        for copy in fetch(i):
            copy.wait()
        result[i] = sum(held[j, i].astype(F32) for j in range(n_parts))
        send(i).start()
    for i in range(steps):
        send(i).wait()


def unpack_kernel(gathered, quantized, gradient):
    n_code, rows, both = gathered.shape
    dim = both // 2
    for g in range(n_code):
        at = slice(g * rows, (g + 1) * rows)
        quantized[at] = gathered[g, :, :dim].astype(F32)
        gradient[at] = gathered[g, :, dim:].astype(F32)


def swap(value, axis, size, mask):
    return lax.ppermute(value, axis, [(i, i ^ mask) for i in range(size)])


def local(n_dp, n_code, tokens, codebook, noise, grad_out):
    n_tokens, dim = tokens.shape
    n_codes = codebook.shape[0]
    rows = n_tokens // n_code
    block = n_codes // n_dp
    width = min(1024, block)
    wide = min(WIDE, width)
    tiles_in = n_codes // wide
    tiles = n_codes // width
    lanes = stat_lanes(n_code)
    products = 2 * n_tokens * n_codes * dim

    sent, sides = pl.pallas_call(
        functools.partial(forward_kernel, n_code),
        out_shape=(
            jax.ShapeDtypeStruct((n_code, rows, 2 * dim + lanes), BF16),
            jax.ShapeDtypeStruct((n_tokens, 128), F32),
        ),
        in_specs=[ANY, ANY, ANY, ANY],
        out_specs=(ANY, ANY),
        scratch_shapes=[
            pltpu.VMEM((2 * n_tokens, dim), BF16),
            pltpu.VMEM((tiles, width, dim), BF16),
            pltpu.VMEM((tiles, n_tokens, width), BF16),
            pltpu.VMEM((2 * n_tokens, width), BF16),
            pltpu.VMEM((2 * n_tokens, width), BF16),
            pltpu.VMEM((n_tokens, 128), F32),
            pltpu.VMEM((n_tokens, 128), F32),
            pltpu.VMEM((2 * n_tokens, dim), F32),
            pltpu.VMEM((n_code, rows, 2 * dim + lanes), BF16),
            pltpu.VMEM((n_tokens, 128), F32),
            pltpu.SemaphoreType.DMA((2 * n_tokens // ROWS,)),
            pltpu.SemaphoreType.DMA((tiles,)),
            pltpu.SemaphoreType.DMA((tiles,)),
            pltpu.SemaphoreType.DMA((2, 2)),
            pltpu.SemaphoreType.DMA((1 + min(n_code, 4),)),
        ],
        compiler_params=FULL,
        cost_estimate=pl.CostEstimate(
            flops=4 * products, bytes_accessed=12 * MIB, transcendentals=n_tokens * n_codes
        ),
        name="forward",
    )(tokens, grad_out, codebook, noise)

    received = lax.all_to_all(sent, "code", 0, 0, tiled=True)
    codes, weighed = pl.pallas_call(
        weigh_kernel,
        out_shape=(pltpu.HBM((tiles_in, n_tokens, wide), BF16),) * 2,
        in_specs=[VMEM, VMEM, ANY, ANY, VMEM],
        out_specs=(ANY, ANY),
        scratch_shapes=[
            pltpu.VMEM((tiles, width, dim), BF16),
            pltpu.VMEM((tiles, n_tokens, width), BF16),
            pltpu.VMEM((tiles_in, n_tokens, wide), BF16),
            pltpu.VMEM((tiles_in, n_tokens, wide), BF16),
            pltpu.VMEM((n_tokens, dim), BF16),
            pltpu.VMEM((n_tokens, 128), F32),
            pltpu.VMEM((n_tokens, 128), F32),
            pltpu.SemaphoreType.DMA((tiles,)),
            pltpu.SemaphoreType.DMA((tiles,)),
            pltpu.SemaphoreType.DMA((2, tiles_in)),
        ],
        compiler_params=FULL,
        cost_estimate=pl.CostEstimate(
            flops=2 * products, bytes_accessed=28 * MIB, transcendentals=n_tokens * n_codes
        ),
        name="weigh",
    )(tokens, grad_out, codebook, noise, sides)
    received, weighed = lax.optimization_barrier((received, weighed))
    code_at = lax.axis_index("code")
    spread = pl.pallas_call(
        merge_kernel,
        out_shape=jax.ShapeDtypeStruct((n_code, rows, 2 * dim), BF16),
        in_specs=[SMEM, VMEM],
        out_specs=VMEM,
        compiler_params=SOME,
        name="merge",
    )(code_at[None], received)
    received, spread = lax.optimization_barrier((received, spread))
    gathered = lax.all_to_all(spread, "code", 0, 0, tiled=True)
    quantized, token_gradient = pl.pallas_call(
        unpack_kernel,
        out_shape=(jax.ShapeDtypeStruct((n_tokens, dim), F32),) * 2,
        in_specs=[VMEM],
        out_specs=(VMEM, VMEM),
        compiler_params=SOME,
        cost_estimate=pl.CostEstimate(
            flops=100 * products, bytes_accessed=400 * MIB, transcendentals=0
        ),
        name="unpack",
    )(gathered)

    block_tiles = block // wide
    streams = [
        pltpu.VMEM((block_tiles, 2 * n_tokens, wide), BF16),
        pltpu.VMEM((block_tiles, wide, dim), BF16),
        pltpu.VMEM((dim, 2 * n_tokens), BF16),
        pltpu.SemaphoreType.DMA((2, block_tiles)),
        pltpu.SemaphoreType.DMA((block_tiles,)),
        pltpu.SemaphoreType.DMA((2,)),
    ]
    block_shape = jax.ShapeDtypeStruct((block, dim), BF16)
    common = dict(
        compiler_params=MOST,
        cost_estimate=pl.CostEstimate(flops=1, bytes_accessed=1, transcendentals=0),
    )
    dp_at = lax.axis_index("dp")
    first, operands = pl.pallas_call(
        functools.partial(backward_kernel, False),
        out_shape=(block_shape, jax.ShapeDtypeStruct((dim, 2 * n_tokens), BF16)),
        in_specs=[SMEM, SMEM, ANY, ANY, ANY, ANY, VMEM],
        out_specs=(ANY, ANY),
        scratch_shapes=[
            pltpu.VMEM((2, n_tokens, dim), BF16),
            pltpu.VMEM((n_tokens, dim), F32),
            pltpu.VMEM((n_tokens, dim), F32),
        ] + streams,
        name="backward_first",
        **common,
    )(
        (dp_at ^ (n_dp - 1))[None], code_at[None], tokens, grad_out, codes, weighed, received
    )

    def backward(at):
        return pl.pallas_call(
            functools.partial(backward_kernel, True),
            out_shape=block_shape,
            in_specs=[SMEM, ANY, ANY, ANY],
            out_specs=ANY,
            scratch_shapes=streams,
            name="backward",
            **common,
        )(at[None], codes, weighed, operands)

    blocks = [swap(first, "dp", n_dp, n_dp - 1)]
    blocks += [swap(backward(dp_at ^ d), "dp", n_dp, d) for d in range(1, n_dp - 1)]
    blocks.append(backward(dp_at))
    steps = max(block // 512, 1)
    own_rows = pl.pallas_call(
        functools.partial(add_kernel, n_dp),
        out_shape=jax.ShapeDtypeStruct((block, dim), F32),
        in_specs=[ANY] * n_dp,
        out_specs=ANY,
        scratch_shapes=[
            pltpu.VMEM((n_dp, steps, block // steps, dim), BF16),
            pltpu.VMEM((steps, block // steps, dim), F32),
            pltpu.SemaphoreType.DMA((n_dp, steps)),
            pltpu.SemaphoreType.DMA((steps,)),
        ],
        compiler_params=PART,
        cost_estimate=pl.CostEstimate(
            flops=0, bytes_accessed=(2 * n_dp + 4) * block * dim, transcendentals=0
        ),
        name="add",
    )(*blocks)
    return quantized, token_gradient, own_rows[None]


def solution(mesh):
    n_dp, n_code = mesh.shape["dp"], mesh.shape["code"]
    in_specs = (P("dp", None), P("code", None), P("dp", "code"), P("dp", None))
    out_specs = (P("dp", None), P("dp", None), P("code", "dp", None))
    return jax.shard_map(
        functools.partial(local, n_dp, n_code),
        mesh=mesh, in_specs=in_specs, out_specs=out_specs, check_vma=False,
    )
```

```python
import functools

import jax
import jax.numpy as jnp
from jax import lax
from jax.experimental import pallas as pl
from jax.experimental.pallas import tpu as pltpu
from jax.sharding import PartitionSpec as P

SOFTMAX_HEAT = 0.5
SHARPNESS = 1.0 / SOFTMAX_HEAT
BF16 = jnp.bfloat16
F32 = jnp.float32
MIB = 1 << 20
CHUNK = 256
WIDE = 512
AHEAD = 2
NEAR = 3
ROWS = 64
LARGEST = 2.0**60
VMEM = pl.BlockSpec(memory_space=pltpu.VMEM)
SMEM = pl.BlockSpec(memory_space=pltpu.SMEM)
ANY = pl.BlockSpec(memory_space=pl.ANY)
FULL = pltpu.CompilerParams(vmem_limit_bytes=60 * MIB)
MOST = pltpu.CompilerParams(vmem_limit_bytes=56 * MIB)
PART = pltpu.CompilerParams(vmem_limit_bytes=58 * MIB)
SOME = pltpu.CompilerParams(vmem_limit_bytes=24 * MIB)


def dot(left, right, left_dim=1, right_dim=0):
    return lax.dot_general(
        left, right, (((left_dim,), (right_dim,)), ((), ())), preferred_element_type=F32
    )


def lane_groups(value):
    return [value[:, j : j + 128] for j in range(0, value.shape[1], 128)]


def stat_lanes(n_code):
    return max(8 * n_code, 128)


def high_low(value):
    high = value.astype(BF16).astype(F32)
    return high, (value - high).astype(BF16).astype(F32)


def forward_kernel(
    n_code, tokens, grad_out, codebook, noise, sent, sides,
    pair, book, noise_in, slot_a, slot_b, shifts, total, sums, sent_out, sides_out,
    pair_sem, book_sem, noise_sem, first_sem, out_sem,
):
    tiles, width, dim = book.shape
    n_tokens = tokens.shape[0]
    columns = [slice(c, c + CHUNK) for c in range(0, width, CHUNK)]
    slots = (slot_a, slot_b)

    def fetch(t):
        at = pl.multiple_of(t * width, width)
        return (
            pltpu.make_async_copy(codebook.at[pl.ds(at, width)], book.at[t], book_sem.at[t]),
            pltpu.make_async_copy(noise.at[:, pl.ds(at, width)], noise_in.at[t], noise_sem.at[t]),
        )

    def start(t):
        for copy in fetch(t):
            copy.start()

    def arrive(t):
        for copy in fetch(t):
            copy.wait()

    pair_copies = []
    for r in range(0, n_tokens, ROWS):
        for half, source in enumerate((tokens, grad_out)):
            pair_copies.append(
                pltpu.make_async_copy(
                    source.at[pl.ds(r, ROWS)],
                    pair.at[pl.ds(2 * r + half * ROWS, ROWS)],
                    pair_sem.at[len(pair_copies)],
                )
            )
    halves = []
    for h in range(2):
        at = pl.ds(h * (width // 2), width // 2)
        halves.append((
            pltpu.make_async_copy(codebook.at[at], book.at[0, at], first_sem.at[h, 0]),
            pltpu.make_async_copy(noise.at[:, at], noise_in.at[0, :, at], first_sem.at[h, 1]),
        ))
    halves[0][0].start()
    for copy in pair_copies:
        copy.start()
    halves[0][1].start()
    for copy in halves[1]:
        copy.start()

    def logits(both, t, r, c):
        noise_part = (noise_in[t, r : r + ROWS, c] * BF16(SHARPNESS)).astype(F32)
        return both[2 * r : 2 * r + ROWS] + noise_part

    def raise_shift(t, some):
        for c in some:
            both = dot(pair[...], book[t, c], 1, 1)
            for r in range(0, n_tokens, ROWS):
                at = slice(r, r + ROWS)
                shifts[at] = functools.reduce(
                    jnp.maximum, lane_groups(logits(both, t, r, c)), shifts[at]
                )

    def soften(t, s, fresh, last=None):
        if fresh is not None:
            @pl.when(fresh)
            def _():
                arrive(t)

                @pl.when(t + AHEAD < tiles)
                def _():
                    start(t + AHEAD)

        slot = slots[s]
        ahead = dot(pair[...], book[t, columns[0]], 1, 1)
        for k, c in enumerate(columns):
            both = ahead
            if k + 1 < len(columns):
                ahead = dot(pair[...], book[t, columns[k + 1]], 1, 1)
            elif last is not None:
                last()
            for r in range(0, n_tokens, ROWS):
                at = slice(r, r + ROWS)
                shift = jnp.concatenate([shifts[at]] * (CHUNK // 128), axis=1)
                weight = jnp.exp(logits(both, t, r, c) - shift)
                total[at] += sum(lane_groups(weight))
                slot[at, c] = weight.astype(BF16)
                gradient = both[2 * r + ROWS : 2 * r + 2 * ROWS]
                slot[n_tokens + r : n_tokens + r + ROWS, c] = (weight * gradient).astype(BF16)

    def accumulate(t, s):
        sums[...] += dot(slots[s][...], book[t])

    def attempt(state):
        again, _ = state
        fresh = again == 0
        shifts[...] = jnp.full(shifts.shape, -jnp.inf, F32)

        @pl.when(fresh)
        def _():
            raise_shift(0, columns[:1])

        @pl.when(jnp.logical_not(fresh))
        def _():
            def over(t, carry):
                raise_shift(t, columns)
                return carry

            lax.fori_loop(0, tiles, over, 0)

        shift = jnp.max(shifts[...], axis=1, keepdims=True).astype(BF16).astype(F32)
        shifts[...] = jnp.broadcast_to(shift, shifts.shape)
        total[...] = jnp.zeros(total.shape, F32)
        sums[...] = jnp.zeros(sums.shape, F32)

        @pl.when(fresh)
        def _():
            for copy in halves[1]:
                copy.wait()

        soften(0, 0, None)

        def soften_pair(i, carry):
            soften(2 * i + 1, 1, fresh, lambda: accumulate(2 * i, 0))
            soften(2 * i + 2, 0, fresh, lambda: accumulate(2 * i + 1, 1))
            return carry

        lax.fori_loop(0, tiles // 2 - 1, soften_pair, 0)
        soften(tiles - 1, 1, fresh, lambda: accumulate(tiles - 2, 0))
        accumulate(tiles - 1, 1)
        fits = jnp.max(total[...]) < LARGEST
        return again + 1, jnp.logical_and(fresh, jnp.logical_not(fits))

    for copy in pair_copies:
        copy.wait()
    for r in range(0, n_tokens, ROWS):
        pair[2 * r : 2 * r + ROWS] = pair[2 * r : 2 * r + ROWS] * BF16(SHARPNESS)
    for copy in halves[0]:
        copy.wait()
    for t in range(1, min(AHEAD + 1, tiles)):
        start(t)
    lax.while_loop(lambda state: state[1], attempt, (jnp.int32(0), jnp.bool_(True)))

    shift = shifts[:, :1]
    mix = sums[:n_tokens]
    pulled = sums[n_tokens:]
    own_total = jnp.sum(total[...], axis=1, keepdims=True)
    own_grad = jnp.concatenate(
        [pair[2 * r + ROWS : 2 * r + 2 * ROWS] for r in range(0, n_tokens, ROWS)], axis=0
    )
    own_inner = jnp.sum(own_grad.astype(F32) * mix, axis=1, keepdims=True)
    mean = own_inner / own_total
    side = lax.broadcasted_iota(jnp.int32, sides_out.shape, 1)
    sides_out[...] = jnp.where(side < 64, mean, shift)
    copies = [pltpu.make_async_copy(sides_out, sides, out_sem.at[0])]
    copies[0].start()
    rows = n_tokens // n_code
    lanes = stat_lanes(n_code)
    half = lanes // 2
    lane = lax.broadcasted_iota(jnp.int32, (rows, lanes), 1)
    stats = jnp.zeros((rows, lanes), F32)
    parts = high_low(own_total) + high_low(own_inner)
    for g in range(n_code):
        at = slice(g * rows, (g + 1) * rows)
        for i, part in enumerate(parts):
            stats = jnp.where(lane == 4 * g + i, part[at], stats)
        stats = jnp.where((lane - half) // 4 == g, shift[at], stats)
    stats = stats.astype(BF16)
    group = n_code // min(n_code, 4)
    for g in range(n_code):
        at = slice(g * rows, (g + 1) * rows)
        sent_out[g, :, :dim] = mix[at].astype(BF16)
        sent_out[g, :, dim : 2 * dim] = (pulled[at] - mean[at] * mix[at]).astype(BF16)
        sent_out[g, :, 2 * dim :] = stats
        if (g + 1) % group == 0:
            part = pl.ds(g + 1 - group, group)
            copies.append(
                pltpu.make_async_copy(sent_out.at[part], sent.at[part], out_sem.at[len(copies)])
            )
            copies[-1].start()
    for copy in copies:
        copy.wait()


def roll_left(value, by):
    return pltpu.roll(value, value.shape[1] - by, 1)


def pair_sums(value):
    both = value + roll_left(value, 1)
    return both, roll_left(both, 2)


def merged_stats(received):
    n_code = received.shape[0]
    lanes = stat_lanes(n_code)
    stats = [received[p, :, received.shape[2] - lanes :].astype(F32) for p in range(n_code)]
    top = functools.reduce(jnp.maximum, stats)
    factors = [roll_left(jnp.exp(s - top), lanes // 2) for s in stats]
    total, inner = pair_sums(sum(f * s for f, s in zip(factors, stats)))
    return stats, factors, top, total, inner / total


def merge_kernel(me, received, spread):
    n_code, rows, _ = received.shape
    dim = spread.shape[2] // 2
    stats, factors, _, total, inner = merged_stats(received)
    lane = lax.broadcasted_iota(jnp.int32, inner.shape, 1)
    mine = lane == 4 * me[0]

    def column(value):
        return jnp.sum(jnp.where(mine, value, 0.0), axis=1, keepdims=True)

    quantized = jnp.zeros((rows, dim), F32)
    gradient = jnp.zeros((rows, dim), F32)
    for p in range(n_code):
        own_total, own_inner = pair_sums(stats[p])
        factor = column(factors[p])
        offset = column(factors[p] * (own_inner / own_total - inner))
        mix = received[p, :, :dim].astype(F32)
        quantized += factor * mix
        gradient += factor * received[p, :, dim : 2 * dim].astype(F32) + offset * mix
    scale = 1.0 / column(total)
    quantized = (quantized * scale).astype(BF16)
    gradient = (gradient * (scale / SOFTMAX_HEAT)).astype(BF16)
    for p in range(n_code):
        spread[p, :, :dim] = quantized
        spread[p, :, dim:] = gradient


def weigh_kernel(
    tokens, grad_out, codebook, noise, sides, codes, weighed, turned,
    book, noise_in, code_out, weighed_out, sharp, means, shifts, turned_out,
    book_sem, noise_sem, out_sem, turned_sem,
):
    tiles, width, _ = book.shape
    wide = codes.shape[2]
    steps = [(t, slice(c, c + wide)) for t in range(tiles) for c in range(0, width, wide)]

    def fetch(t):
        at = pl.ds(t * width, width)
        return (
            pltpu.make_async_copy(codebook.at[at], book.at[t], book_sem.at[t]),
            pltpu.make_async_copy(noise.at[:, at], noise_in.at[t], noise_sem.at[t]),
        )

    def start(t):
        for copy in fetch(t):
            copy.start()

    def send(k):
        return (
            pltpu.make_async_copy(code_out.at[k], codes.at[k], out_sem.at[0, k]),
            pltpu.make_async_copy(weighed_out.at[k], weighed.at[k], out_sem.at[1, k]),
        )

    def products_of(step):
        t, c = step
        if c.start == 0:
            for copy in fetch(t):
                copy.wait()
            if t + NEAR < tiles:
                start(t + NEAR)
        keys = book[t, c]
        return dot(sharp[...], keys, 1, 1), dot(grad_out[...], keys, 1, 1)

    for t in range(min(NEAR, tiles)):
        start(t)
    sharp[...] = tokens[...] * BF16(SHARPNESS)
    means[...] = jnp.broadcast_to(sides[:, :1], means.shape)
    shifts[...] = jnp.broadcast_to(sides[:, 64:65], shifts.shape)
    turned_out[0] = grad_out[...].T
    turned_out[1] = sharp[...].T
    turned_copy = pltpu.make_async_copy(turned_out, turned, turned_sem)
    turned_copy.start()
    ahead = products_of(steps[0])
    for k, (t, c) in enumerate(steps):
        score, gradient = ahead
        if k + 1 < len(steps):
            ahead = products_of(steps[k + 1])
        shift = jnp.concatenate([shifts[...]] * (wide // 128), axis=1)
        mean = jnp.concatenate([means[...]] * (wide // 128), axis=1)
        noise_part = (noise_in[t, :, c] * BF16(SHARPNESS)).astype(F32)
        code = jnp.exp(score + noise_part - shift).astype(BF16)
        code_out[k] = code
        weighed_out[k] = (code.astype(F32) * (gradient - mean)).astype(BF16)
        for copy in send(k):
            copy.start()
    for k in range(len(steps)):
        for copy in send(k):
            copy.wait()
    turned_copy.wait()


def backward_kernel(prepared, block, *rest):
    if prepared:
        codes, weighed, given, out, *rest = rest
    else:
        code_at, turned, codes, weighed, received, out, kept, own, spread, *rest = rest
    both_in, result, operands, in_sem, out_sem, own_sem = rest
    tiles, width, dim = result.shape
    n_tokens = both_in.shape[1] // 2

    def fetch(t):
        return [
            pltpu.make_async_copy(
                source.at[block[0] * tiles + t],
                both_in.at[t, pl.ds(half * n_tokens, n_tokens)],
                in_sem.at[half, t],
            )
            for half, source in enumerate((codes, weighed))
        ]

    def start(t):
        for copy in fetch(t):
            copy.start()

    start(0)
    if prepared:
        own_copies = [pltpu.make_async_copy(given, operands, own_sem.at[0])]
    else:
        own_copies = [pltpu.make_async_copy(turned, own, own_sem.at[0])]
    for copy in own_copies:
        copy.start()
    for t in range(1, min(NEAR, tiles)):
        start(t)

    if prepared:
        own_copies[0].wait()
    else:
        n_code, rows, _ = received.shape
        _, _, top, total, inner = merged_stats(received)
        lanes = top.shape[1]
        stats = received[code_at[0], :, received.shape[2] - lanes :].astype(F32)
        own_total, own_inner = pair_sums(stats)
        scale = roll_left(jnp.exp(stats - top), lanes // 2) / total
        offset = scale * (own_inner / own_total - inner)
        lane = lax.broadcasted_iota(jnp.int32, (rows, 128), 1)
        for g in range(n_code):
            at = slice(4 * g, 4 * g + 1)
            spread[g * rows : (g + 1) * rows] = jnp.where(lane < 64, scale[:, at], offset[:, at])
        factors = spread[...].T
        scale, offset = factors[:1], factors[64:65]
        own_copies[0].wait()
        grad, token = own[0].astype(F32), own[1].astype(F32)
        operands[:, :n_tokens] = (scale * grad + offset * token).astype(BF16)
        operands[:, n_tokens:] = (scale * token).astype(BF16)
        keep = pltpu.make_async_copy(operands, kept, own_sem.at[0])
        keep.start()

    def send(t):
        return pltpu.make_async_copy(
            result.at[t], out.at[pl.ds(t * width, width)], out_sem.at[t]
        )

    wide = min(WIDE, width)
    steps = [(t, slice(c, c + wide)) for t in range(tiles) for c in range(0, width, wide)]

    def product(step):
        t, c = step
        if c.start == 0:
            for copy in fetch(t):
                copy.wait()
            if t + NEAR < tiles:
                start(t + NEAR)
        return dot(operands[...], both_in[t, :, c])

    ahead = product(steps[0])
    for k, (t, c) in enumerate(steps):
        value = ahead
        if k + 1 < len(steps):
            ahead = product(steps[k + 1])
        result[t, c] = value.astype(BF16).T
        if c.stop == width:
            send(t).start()
    for t in range(tiles):
        send(t).wait()
    if not prepared:
        keep.wait()


def add_kernel(n_parts, *refs):
    parts, out = refs[:n_parts], refs[n_parts]
    held, result, in_sem, out_sem = refs[n_parts + 1 :]
    steps, rows, _ = result.shape

    def fetch(i):
        at = pl.ds(i * rows, rows)
        return [
            pltpu.make_async_copy(part.at[at], held.at[j, i], in_sem.at[j, i])
            for j, part in enumerate(parts)
        ]

    def send(i):
        return pltpu.make_async_copy(result.at[i], out.at[pl.ds(i * rows, rows)], out_sem.at[i])

    for i in range(steps):
        for copy in fetch(i):
            copy.start()
    for i in range(steps):
        for copy in fetch(i):
            copy.wait()
        result[i] = sum(held[j, i].astype(F32) for j in range(n_parts))
        send(i).start()
    for i in range(steps):
        send(i).wait()


def unpack_kernel(gathered, quantized, gradient):
    n_code, rows, both = gathered.shape
    dim = both // 2
    for g in range(n_code):
        at = slice(g * rows, (g + 1) * rows)
        quantized[at] = gathered[g, :, :dim].astype(F32)
        gradient[at] = gathered[g, :, dim:].astype(F32)


def swap(value, axis, size, mask):
    return lax.ppermute(value, axis, [(i, i ^ mask) for i in range(size)])


def local(n_dp, n_code, tokens, codebook, noise, grad_out):
    n_tokens, dim = tokens.shape
    n_codes = codebook.shape[0]
    rows = n_tokens // n_code
    block = n_codes // n_dp
    width = min(1024, block)
    wide = min(WIDE, width)
    tiles_in = n_codes // wide
    tiles = n_codes // width
    lanes = stat_lanes(n_code)
    products = 2 * n_tokens * n_codes * dim

    sent, sides = pl.pallas_call(
        functools.partial(forward_kernel, n_code),
        out_shape=(
            jax.ShapeDtypeStruct((n_code, rows, 2 * dim + lanes), BF16),
            jax.ShapeDtypeStruct((n_tokens, 128), F32),
        ),
        in_specs=[ANY, ANY, ANY, ANY],
        out_specs=(ANY, ANY),
        scratch_shapes=[
            pltpu.VMEM((2 * n_tokens, dim), BF16),
            pltpu.VMEM((tiles, width, dim), BF16),
            pltpu.VMEM((tiles, n_tokens, width), BF16),
            pltpu.VMEM((2 * n_tokens, width), BF16),
            pltpu.VMEM((2 * n_tokens, width), BF16),
            pltpu.VMEM((n_tokens, 128), F32),
            pltpu.VMEM((n_tokens, 128), F32),
            pltpu.VMEM((2 * n_tokens, dim), F32),
            pltpu.VMEM((n_code, rows, 2 * dim + lanes), BF16),
            pltpu.VMEM((n_tokens, 128), F32),
            pltpu.SemaphoreType.DMA((2 * n_tokens // ROWS,)),
            pltpu.SemaphoreType.DMA((tiles,)),
            pltpu.SemaphoreType.DMA((tiles,)),
            pltpu.SemaphoreType.DMA((2, 2)),
            pltpu.SemaphoreType.DMA((1 + min(n_code, 4),)),
        ],
        compiler_params=FULL,
        cost_estimate=pl.CostEstimate(
            flops=4 * products, bytes_accessed=12 * MIB, transcendentals=n_tokens * n_codes
        ),
        name="forward",
    )(tokens, grad_out, codebook, noise)

    received = lax.all_to_all(sent, "code", 0, 0, tiled=True)
    codes, weighed, turned = pl.pallas_call(
        weigh_kernel,
        out_shape=(pltpu.HBM((tiles_in, n_tokens, wide), BF16),) * 2
        + (jax.ShapeDtypeStruct((2, dim, n_tokens), BF16),),
        in_specs=[VMEM, VMEM, ANY, ANY, VMEM],
        out_specs=(ANY, ANY, ANY),
        scratch_shapes=[
            pltpu.VMEM((tiles, width, dim), BF16),
            pltpu.VMEM((tiles, n_tokens, width), BF16),
            pltpu.VMEM((tiles_in, n_tokens, wide), BF16),
            pltpu.VMEM((tiles_in, n_tokens, wide), BF16),
            pltpu.VMEM((n_tokens, dim), BF16),
            pltpu.VMEM((n_tokens, 128), F32),
            pltpu.VMEM((n_tokens, 128), F32),
            pltpu.VMEM((2, dim, n_tokens), BF16),
            pltpu.SemaphoreType.DMA((tiles,)),
            pltpu.SemaphoreType.DMA((tiles,)),
            pltpu.SemaphoreType.DMA((2, tiles_in)),
            pltpu.SemaphoreType.DMA,
        ],
        compiler_params=FULL,
        cost_estimate=pl.CostEstimate(
            flops=2 * products, bytes_accessed=28 * MIB, transcendentals=n_tokens * n_codes
        ),
        name="weigh",
    )(tokens, grad_out, codebook, noise, sides)
    received, weighed = lax.optimization_barrier((received, weighed))
    code_at = lax.axis_index("code")
    spread = pl.pallas_call(
        merge_kernel,
        out_shape=jax.ShapeDtypeStruct((n_code, rows, 2 * dim), BF16),
        in_specs=[SMEM, VMEM],
        out_specs=VMEM,
        compiler_params=SOME,
        name="merge",
    )(code_at[None], received)
    received, spread = lax.optimization_barrier((received, spread))
    gathered = lax.all_to_all(spread, "code", 0, 0, tiled=True)
    quantized, token_gradient = pl.pallas_call(
        unpack_kernel,
        out_shape=(jax.ShapeDtypeStruct((n_tokens, dim), F32),) * 2,
        in_specs=[VMEM],
        out_specs=(VMEM, VMEM),
        compiler_params=SOME,
        cost_estimate=pl.CostEstimate(
            flops=100 * products, bytes_accessed=400 * MIB, transcendentals=0
        ),
        name="unpack",
    )(gathered)

    block_tiles = block // wide
    streams = [
        pltpu.VMEM((block_tiles, 2 * n_tokens, wide), BF16),
        pltpu.VMEM((block_tiles, wide, dim), BF16),
        pltpu.VMEM((dim, 2 * n_tokens), BF16),
        pltpu.SemaphoreType.DMA((2, block_tiles)),
        pltpu.SemaphoreType.DMA((block_tiles,)),
        pltpu.SemaphoreType.DMA((1,)),
    ]
    block_shape = jax.ShapeDtypeStruct((block, dim), BF16)
    common = dict(
        compiler_params=MOST,
        cost_estimate=pl.CostEstimate(flops=1, bytes_accessed=1, transcendentals=0),
    )
    dp_at = lax.axis_index("dp")
    first, operands = pl.pallas_call(
        functools.partial(backward_kernel, False),
        out_shape=(block_shape, jax.ShapeDtypeStruct((dim, 2 * n_tokens), BF16)),
        in_specs=[SMEM, SMEM, ANY, ANY, ANY, VMEM],
        out_specs=(ANY, ANY),
        scratch_shapes=[
            pltpu.VMEM((2, dim, n_tokens), BF16),
            pltpu.VMEM((n_tokens, 128), F32),
        ] + streams,
        name="backward_first",
        **common,
    )(
        (dp_at ^ (n_dp - 1))[None], code_at[None], turned, codes, weighed, received
    )

    def backward(at):
        return pl.pallas_call(
            functools.partial(backward_kernel, True),
            out_shape=block_shape,
            in_specs=[SMEM, ANY, ANY, ANY],
            out_specs=ANY,
            scratch_shapes=streams,
            name="backward",
            **common,
        )(at[None], codes, weighed, operands)

    blocks = [swap(first, "dp", n_dp, n_dp - 1)]
    blocks += [swap(backward(dp_at ^ d), "dp", n_dp, d) for d in range(1, n_dp - 1)]
    blocks.append(backward(dp_at))
    steps = max(block // 512, 1)
    own_rows = pl.pallas_call(
        functools.partial(add_kernel, n_dp),
        out_shape=jax.ShapeDtypeStruct((block, dim), F32),
        in_specs=[ANY] * n_dp,
        out_specs=ANY,
        scratch_shapes=[
            pltpu.VMEM((n_dp, steps, block // steps, dim), BF16),
            pltpu.VMEM((steps, block // steps, dim), F32),
            pltpu.SemaphoreType.DMA((n_dp, steps)),
            pltpu.SemaphoreType.DMA((steps,)),
        ],
        compiler_params=PART,
        cost_estimate=pl.CostEstimate(
            flops=0, bytes_accessed=(2 * n_dp + 4) * block * dim, transcendentals=0
        ),
        name="add",
    )(*blocks)
    return quantized, token_gradient, own_rows[None]


def solution(mesh):
    n_dp, n_code = mesh.shape["dp"], mesh.shape["code"]
    in_specs = (P("dp", None), P("code", None), P("dp", "code"), P("dp", None))
    out_specs = (P("dp", None), P("dp", None), P("code", "dp", None))
    return jax.shard_map(
        functools.partial(local, n_dp, n_code),
        mesh=mesh, in_specs=in_specs, out_specs=out_specs, check_vma=False,
    )
```

```python
import functools

import jax
import jax.numpy as jnp
from jax import lax
from jax.experimental import pallas as pl
from jax.experimental.pallas import tpu as pltpu
from jax.sharding import PartitionSpec as P

SOFTMAX_HEAT = 0.5
SHARPNESS = 1.0 / SOFTMAX_HEAT
BF16 = jnp.bfloat16
F32 = jnp.float32
MIB = 1 << 20
CHUNK = 256
WIDE = 512
AHEAD = 2
NEAR = 3
PACK = 16
ROWS = 64
LARGEST = 2.0**60
VMEM = pl.BlockSpec(memory_space=pltpu.VMEM)
SMEM = pl.BlockSpec(memory_space=pltpu.SMEM)
ANY = pl.BlockSpec(memory_space=pl.ANY)
FULL = pltpu.CompilerParams(vmem_limit_bytes=60 * MIB)
MOST = pltpu.CompilerParams(vmem_limit_bytes=56 * MIB)
PART = pltpu.CompilerParams(vmem_limit_bytes=58 * MIB)
SOME = pltpu.CompilerParams(vmem_limit_bytes=24 * MIB)


def dot(left, right, left_dim=1, right_dim=0):
    return lax.dot_general(
        left, right, (((left_dim,), (right_dim,)), ((), ())), preferred_element_type=F32
    )


def lane_groups(value):
    return [value[:, j : j + 128] for j in range(0, value.shape[1], 128)]


def stat_lanes(n_tokens):
    return max(n_tokens // PACK * 4, 128)


def high_low(value):
    high = value.astype(BF16).astype(F32)
    return high, (value - high).astype(BF16).astype(F32)


def forward_kernel(
    n_code, tokens, grad_out, codebook, noise, sent, sides,
    own, pair, book, noise_in, slot_a, slot_b, shifts, total, sums, sent_out, sides_out,
    own_sem, book_sem, noise_sem, first_sem, out_sem,
):
    tiles, width, dim = book.shape
    n_tokens = tokens.shape[0]
    columns = [slice(c, c + CHUNK) for c in range(0, width, CHUNK)]
    slots = (slot_a, slot_b)

    def fetch(t):
        at = pl.multiple_of(t * width, width)
        return (
            pltpu.make_async_copy(codebook.at[pl.ds(at, width)], book.at[t], book_sem.at[t]),
            pltpu.make_async_copy(noise.at[:, pl.ds(at, width)], noise_in.at[t], noise_sem.at[t]),
        )

    def start(t):
        for copy in fetch(t):
            copy.start()

    def arrive(t):
        for copy in fetch(t):
            copy.wait()

    own_copies = (
        pltpu.make_async_copy(tokens, own.at[0], own_sem.at[0]),
        pltpu.make_async_copy(grad_out, own.at[1], own_sem.at[1]),
    )
    halves = []
    for h in range(2):
        at = pl.ds(h * (width // 2), width // 2)
        halves.append((
            pltpu.make_async_copy(codebook.at[at], book.at[0, at], first_sem.at[h, 0]),
            pltpu.make_async_copy(noise.at[:, at], noise_in.at[0, :, at], first_sem.at[h, 1]),
        ))
    for copy in own_copies + halves[0]:
        copy.start()
    for copy in halves[1]:
        copy.start()

    def logits(both, t, r, c):
        noise_part = (noise_in[t, r : r + ROWS, c] * BF16(SHARPNESS)).astype(F32)
        return both[2 * r : 2 * r + ROWS] + noise_part

    def raise_shift(t, some):
        for c in some:
            both = dot(pair[...], book[t, c], 1, 1)
            for r in range(0, n_tokens, ROWS):
                at = slice(r, r + ROWS)
                shifts[at] = functools.reduce(
                    jnp.maximum, lane_groups(logits(both, t, r, c)), shifts[at]
                )

    def soften(t, s, fresh, last=None):
        if fresh is not None:
            @pl.when(fresh)
            def _():
                arrive(t)

                @pl.when(t + AHEAD < tiles)
                def _():
                    start(t + AHEAD)

        slot = slots[s]
        ahead = dot(pair[...], book[t, columns[0]], 1, 1)
        for k, c in enumerate(columns):
            both = ahead
            if k + 1 < len(columns):
                ahead = dot(pair[...], book[t, columns[k + 1]], 1, 1)
            elif last is not None:
                last()
            for r in range(0, n_tokens, ROWS):
                at = slice(r, r + ROWS)
                shift = jnp.concatenate([shifts[at]] * (CHUNK // 128), axis=1)
                weight = jnp.exp(logits(both, t, r, c) - shift)
                total[at] += sum(lane_groups(weight))
                slot[at, c] = weight.astype(BF16)
                gradient = both[2 * r + ROWS : 2 * r + 2 * ROWS]
                slot[n_tokens + r : n_tokens + r + ROWS, c] = (weight * gradient).astype(BF16)

    def accumulate(t, s):
        sums[...] += dot(slots[s][...], book[t])

    def attempt(state):
        again, _ = state
        fresh = again == 0
        shifts[...] = jnp.full(shifts.shape, -jnp.inf, F32)

        @pl.when(fresh)
        def _():
            raise_shift(0, columns[:1])

        @pl.when(jnp.logical_not(fresh))
        def _():
            def over(t, carry):
                raise_shift(t, columns)
                return carry

            lax.fori_loop(0, tiles, over, 0)

        shift = jnp.max(shifts[...], axis=1, keepdims=True).astype(BF16).astype(F32)
        shifts[...] = jnp.broadcast_to(shift, shifts.shape)
        total[...] = jnp.zeros(total.shape, F32)
        sums[...] = jnp.zeros(sums.shape, F32)

        @pl.when(fresh)
        def _():
            for copy in halves[1]:
                copy.wait()

        soften(0, 0, None)

        def soften_pair(i, carry):
            soften(2 * i + 1, 1, fresh, lambda: accumulate(2 * i, 0))
            soften(2 * i + 2, 0, fresh, lambda: accumulate(2 * i + 1, 1))
            return carry

        lax.fori_loop(0, tiles // 2 - 1, soften_pair, 0)
        soften(tiles - 1, 1, fresh, lambda: accumulate(tiles - 2, 0))
        accumulate(tiles - 1, 1)
        fits = jnp.max(total[...]) < LARGEST
        return again + 1, jnp.logical_and(fresh, jnp.logical_not(fits))

    for copy in own_copies:
        copy.wait()
    for r in range(0, n_tokens, ROWS):
        pair[2 * r : 2 * r + ROWS] = own[0, r : r + ROWS] * BF16(SHARPNESS)
        pair[2 * r + ROWS : 2 * r + 2 * ROWS] = own[1, r : r + ROWS]
    for copy in halves[0]:
        copy.wait()
    for t in range(1, min(AHEAD + 1, tiles)):
        start(t)
    lax.while_loop(lambda state: state[1], attempt, (jnp.int32(0), jnp.bool_(True)))

    shift = shifts[:, :1]
    mix = sums[:n_tokens]
    pulled = sums[n_tokens:]
    own_total = jnp.sum(total[...], axis=1, keepdims=True)
    own_inner = jnp.sum(own[1].astype(F32) * mix, axis=1, keepdims=True)
    mean = own_inner / own_total
    side = lax.broadcasted_iota(jnp.int32, sides_out.shape, 1)
    sides_out[...] = jnp.where(side < 64, mean, shift)
    copies = [pltpu.make_async_copy(sides_out, sides, out_sem.at[0])]
    copies[0].start()
    rows = n_tokens // n_code
    lanes = stat_lanes(n_tokens)
    lane = lax.broadcasted_iota(jnp.int32, (PACK, lanes), 1)
    stats = jnp.zeros((PACK, lanes), F32)
    parts = (own_total,) + high_low(mean) + (shift,)
    for q in range(n_tokens // PACK):
        for i, part in enumerate(parts):
            stats = jnp.where(lane == 4 * q + i, part[q * PACK : (q + 1) * PACK], stats)
    stats = [stats[:, j : j + 128].astype(BF16) for j in range(0, lanes, 128)]
    group = n_code // min(n_code, 4)
    for g in range(n_code):
        at = slice(g * rows, (g + 1) * rows)
        data = lane_groups(mix[at]) + lane_groups(pulled[at] - mean[at] * mix[at])
        for j, value in enumerate(data):
            sent_out[g, j * rows : (j + 1) * rows] = value.astype(BF16)
        for j, value in enumerate(stats):
            first = len(data) * rows + j * PACK
            sent_out[g, first : first + PACK] = value
        if (g + 1) % group == 0:
            part = pl.ds(g + 1 - group, group)
            copies.append(
                pltpu.make_async_copy(sent_out.at[part], sent.at[part], out_sem.at[len(copies)])
            )
            copies[-1].start()
    for copy in copies:
        copy.wait()


def roll_left(value, by):
    return pltpu.roll(value, value.shape[1] - by, 1)


def stats_of(received, p, n_tokens):
    first = received.shape[1] - stat_lanes(n_tokens) // 128 * PACK
    blocks = [received[p, r : r + PACK] for r in range(first, received.shape[1], PACK)]
    return jnp.concatenate(blocks, axis=1).astype(F32)


def factor_of(stats, top):
    return roll_left(jnp.exp(stats - top), 3)


def mean_of(stats):
    return roll_left(stats, 1) + roll_left(stats, 2)


def merged_stats(received, n_tokens):
    stats = [stats_of(received, p, n_tokens) for p in range(received.shape[0])]
    top = functools.reduce(jnp.maximum, stats)
    factors = [factor_of(s, top) * s for s in stats]
    means = [mean_of(s) for s in stats]
    total = sum(factors)
    inner = sum(f * m for f, m in zip(factors, means)) / total
    scales = [factor_of(s, top) / total for s in stats]
    return scales, means, top, total, inner


def merge_kernel(me, received, spread):
    n_code, rows, both = spread.shape
    dim = both // 2
    scales, means, _, _, inner = merged_stats(received, n_code * rows)
    lane = lax.broadcasted_iota(jnp.int32, inner.shape, 1)
    groups = rows // PACK
    mine = [lane == 4 * (me[0] * groups + h) for h in range(groups)]

    def column(value):
        columns = [jnp.sum(jnp.where(m, value, 0.0), axis=1, keepdims=True) for m in mine]
        return jnp.concatenate(columns, axis=0)

    count = dim // 128
    quantized = [jnp.zeros((rows, 128), F32)] * count
    gradient = [jnp.zeros((rows, 128), F32)] * count
    for p in range(n_code):
        scale = column(scales[p])
        offset = column(scales[p] * (means[p] - inner))
        for j in range(count):
            mix = received[p, j * rows : (j + 1) * rows].astype(F32)
            pulled = received[p, (count + j) * rows : (count + j + 1) * rows].astype(F32)
            quantized[j] += scale * mix
            gradient[j] += scale * pulled + offset * mix
    for j in range(count):
        results = (quantized[j].astype(BF16), (gradient[j] / SOFTMAX_HEAT).astype(BF16))
        for p in range(n_code):
            for i, result in enumerate(results):
                spread[p, :, i * dim + j * 128 : i * dim + (j + 1) * 128] = result


def weigh_kernel(
    tokens, grad_out, codebook, noise, sides, codes, weighed, turned,
    book, noise_in, code_out, weighed_out, sharp, means, shifts, turned_out,
    book_sem, noise_sem, out_sem, turned_sem,
):
    tiles, width, _ = book.shape
    wide = codes.shape[2]
    steps = [(t, slice(c, c + wide)) for t in range(tiles) for c in range(0, width, wide)]

    def fetch(t):
        at = pl.ds(t * width, width)
        return (
            pltpu.make_async_copy(codebook.at[at], book.at[t], book_sem.at[t]),
            pltpu.make_async_copy(noise.at[:, at], noise_in.at[t], noise_sem.at[t]),
        )

    def start(t):
        for copy in fetch(t):
            copy.start()

    def send(k):
        return (
            pltpu.make_async_copy(code_out.at[k], codes.at[k], out_sem.at[0, k]),
            pltpu.make_async_copy(weighed_out.at[k], weighed.at[k], out_sem.at[1, k]),
        )

    def products_of(step):
        t, c = step
        if c.start == 0:
            for copy in fetch(t):
                copy.wait()
            if t + NEAR < tiles:
                start(t + NEAR)
        keys = book[t, c]
        return dot(sharp[...], keys, 1, 1), dot(grad_out[...], keys, 1, 1)

    for t in range(min(NEAR, tiles)):
        start(t)
    sharp[...] = tokens[...] * BF16(SHARPNESS)
    means[...] = jnp.broadcast_to(sides[:, :1], means.shape)
    shifts[...] = jnp.broadcast_to(sides[:, 64:65], shifts.shape)
    turned_out[0] = grad_out[...].T
    turned_out[1] = sharp[...].T
    turned_copy = pltpu.make_async_copy(turned_out, turned, turned_sem)
    turned_copy.start()
    ahead = products_of(steps[0])
    for k, (t, c) in enumerate(steps):
        score, gradient = ahead
        if k + 1 < len(steps):
            ahead = products_of(steps[k + 1])
        shift = jnp.concatenate([shifts[...]] * (wide // 128), axis=1)
        mean = jnp.concatenate([means[...]] * (wide // 128), axis=1)
        noise_part = (noise_in[t, :, c] * BF16(SHARPNESS)).astype(F32)
        code = jnp.exp(score + noise_part - shift).astype(BF16)
        code_out[k] = code
        weighed_out[k] = (code.astype(F32) * (gradient - mean)).astype(BF16)
        for copy in send(k):
            copy.start()
    for k in range(len(steps)):
        for copy in send(k):
            copy.wait()
    turned_copy.wait()


def backward_kernel(prepared, block, *rest):
    if prepared:
        codes, weighed, given, out, *rest = rest
    else:
        code_at, turned, codes, weighed, received, out, kept, own, spread, *rest = rest
    both_in, result, operands, in_sem, out_sem, own_sem = rest
    tiles, width, dim = result.shape
    n_tokens = both_in.shape[1] // 2

    def fetch(t):
        return [
            pltpu.make_async_copy(
                source.at[block[0] * tiles + t],
                both_in.at[t, pl.ds(half * n_tokens, n_tokens)],
                in_sem.at[half, t],
            )
            for half, source in enumerate((codes, weighed))
        ]

    def start(t):
        for copy in fetch(t):
            copy.start()

    start(0)
    if prepared:
        own_copies = [pltpu.make_async_copy(given, operands, own_sem.at[0])]
    else:
        own_copies = [pltpu.make_async_copy(turned, own, own_sem.at[0])]
    for copy in own_copies:
        copy.start()
    for t in range(1, min(NEAR, tiles)):
        start(t)

    if prepared:
        own_copies[0].wait()
    else:
        _, _, top, total, inner = merged_stats(received, n_tokens)
        stats = stats_of(received, code_at[0], n_tokens)
        scale = factor_of(stats, top) / total
        offset = scale * (mean_of(stats) - inner)
        lane = lax.broadcasted_iota(jnp.int32, (PACK, 128), 1)
        for q in range(n_tokens // PACK):
            at = slice(4 * q, 4 * q + 1)
            spread[q * PACK : (q + 1) * PACK] = jnp.where(
                lane < 64, scale[:, at], offset[:, at]
            )
        factors = spread[...].T
        scale, offset = factors[:1], factors[64:65]
        own_copies[0].wait()
        grad, token = own[0].astype(F32), own[1].astype(F32)
        operands[:, :n_tokens] = (scale * grad + offset * token).astype(BF16)
        operands[:, n_tokens:] = (scale * token).astype(BF16)
        keep = pltpu.make_async_copy(operands, kept, own_sem.at[0])
        keep.start()

    def send(t):
        return pltpu.make_async_copy(
            result.at[t], out.at[pl.ds(t * width, width)], out_sem.at[t]
        )

    wide = min(WIDE, width)
    steps = [(t, slice(c, c + wide)) for t in range(tiles) for c in range(0, width, wide)]

    def product(step):
        t, c = step
        if c.start == 0:
            for copy in fetch(t):
                copy.wait()
            if t + NEAR < tiles:
                start(t + NEAR)
        return dot(operands[...], both_in[t, :, c])

    ahead = product(steps[0])
    for k, (t, c) in enumerate(steps):
        value = ahead
        if k + 1 < len(steps):
            ahead = product(steps[k + 1])
        result[t, c] = value.astype(BF16).T
        if c.stop == width:
            send(t).start()
    for t in range(tiles):
        send(t).wait()
    if not prepared:
        keep.wait()


def add_kernel(n_parts, *refs):
    parts, out = refs[:n_parts], refs[n_parts]
    held, result, in_sem, out_sem = refs[n_parts + 1 :]
    steps, rows, _ = result.shape

    def fetch(i):
        at = pl.ds(i * rows, rows)
        return [
            pltpu.make_async_copy(part.at[at], held.at[j, i], in_sem.at[j, i])
            for j, part in enumerate(parts)
        ]

    def send(i):
        return pltpu.make_async_copy(result.at[i], out.at[pl.ds(i * rows, rows)], out_sem.at[i])

    for i in range(steps):
        for copy in fetch(i):
            copy.start()
    for i in range(steps):
        for copy in fetch(i):
            copy.wait()
        result[i] = sum(held[j, i].astype(F32) for j in range(n_parts))
        send(i).start()
    for i in range(steps):
        send(i).wait()


def unpack_kernel(gathered, quantized, gradient):
    n_code, rows, both = gathered.shape
    dim = both // 2
    for g in range(n_code):
        at = slice(g * rows, (g + 1) * rows)
        quantized[at] = gathered[g, :, :dim].astype(F32)
        gradient[at] = gathered[g, :, dim:].astype(F32)


def swap(value, axis, size, mask):
    return lax.ppermute(value, axis, [(i, i ^ mask) for i in range(size)])


def local(n_dp, n_code, tokens, codebook, noise, grad_out):
    n_tokens, dim = tokens.shape
    n_codes = codebook.shape[0]
    rows = n_tokens // n_code
    block = n_codes // n_dp
    width = min(1024, block)
    wide = min(WIDE, width)
    tiles_in = n_codes // wide
    tiles = n_codes // width
    piece = rows * (2 * dim // 128) + stat_lanes(n_tokens) // 128 * PACK
    products = 2 * n_tokens * n_codes * dim

    sent, sides = pl.pallas_call(
        functools.partial(forward_kernel, n_code),
        out_shape=(
            jax.ShapeDtypeStruct((n_code, piece, 128), BF16),
            jax.ShapeDtypeStruct((n_tokens, 128), F32),
        ),
        in_specs=[ANY, ANY, ANY, ANY],
        out_specs=(ANY, ANY),
        scratch_shapes=[
            pltpu.VMEM((2, n_tokens, dim), BF16),
            pltpu.VMEM((2 * n_tokens, dim), BF16),
            pltpu.VMEM((tiles, width, dim), BF16),
            pltpu.VMEM((tiles, n_tokens, width), BF16),
            pltpu.VMEM((2 * n_tokens, width), BF16),
            pltpu.VMEM((2 * n_tokens, width), BF16),
            pltpu.VMEM((n_tokens, 128), F32),
            pltpu.VMEM((n_tokens, 128), F32),
            pltpu.VMEM((2 * n_tokens, dim), F32),
            pltpu.VMEM((n_code, piece, 128), BF16),
            pltpu.VMEM((n_tokens, 128), F32),
            pltpu.SemaphoreType.DMA((2,)),
            pltpu.SemaphoreType.DMA((tiles,)),
            pltpu.SemaphoreType.DMA((tiles,)),
            pltpu.SemaphoreType.DMA((2, 2)),
            pltpu.SemaphoreType.DMA((1 + min(n_code, 4),)),
        ],
        compiler_params=FULL,
        cost_estimate=pl.CostEstimate(
            flops=4 * products, bytes_accessed=12 * MIB, transcendentals=n_tokens * n_codes
        ),
        name="forward",
    )(tokens, grad_out, codebook, noise)

    received = lax.all_to_all(sent, "code", 0, 0, tiled=True)
    codes, weighed, turned = pl.pallas_call(
        weigh_kernel,
        out_shape=(pltpu.HBM((tiles_in, n_tokens, wide), BF16),) * 2
        + (jax.ShapeDtypeStruct((2, dim, n_tokens), BF16),),
        in_specs=[VMEM, VMEM, ANY, ANY, VMEM],
        out_specs=(ANY, ANY, ANY),
        scratch_shapes=[
            pltpu.VMEM((tiles, width, dim), BF16),
            pltpu.VMEM((tiles, n_tokens, width), BF16),
            pltpu.VMEM((tiles_in, n_tokens, wide), BF16),
            pltpu.VMEM((tiles_in, n_tokens, wide), BF16),
            pltpu.VMEM((n_tokens, dim), BF16),
            pltpu.VMEM((n_tokens, 128), F32),
            pltpu.VMEM((n_tokens, 128), F32),
            pltpu.VMEM((2, dim, n_tokens), BF16),
            pltpu.SemaphoreType.DMA((tiles,)),
            pltpu.SemaphoreType.DMA((tiles,)),
            pltpu.SemaphoreType.DMA((2, tiles_in)),
            pltpu.SemaphoreType.DMA,
        ],
        compiler_params=FULL,
        cost_estimate=pl.CostEstimate(
            flops=2 * products, bytes_accessed=28 * MIB, transcendentals=n_tokens * n_codes
        ),
        name="weigh",
    )(tokens, grad_out, codebook, noise, sides)
    received, weighed = lax.optimization_barrier((received, weighed))
    code_at = lax.axis_index("code")
    spread = pl.pallas_call(
        merge_kernel,
        out_shape=jax.ShapeDtypeStruct((n_code, rows, 2 * dim), BF16),
        in_specs=[SMEM, VMEM],
        out_specs=VMEM,
        compiler_params=SOME,
        name="merge",
    )(code_at[None], received)
    received, spread = lax.optimization_barrier((received, spread))
    gathered = lax.all_to_all(spread, "code", 0, 0, tiled=True)
    quantized, token_gradient = pl.pallas_call(
        unpack_kernel,
        out_shape=(jax.ShapeDtypeStruct((n_tokens, dim), F32),) * 2,
        in_specs=[VMEM],
        out_specs=(VMEM, VMEM),
        compiler_params=SOME,
        cost_estimate=pl.CostEstimate(
            flops=100 * products, bytes_accessed=400 * MIB, transcendentals=0
        ),
        name="unpack",
    )(gathered)

    block_tiles = block // wide
    streams = [
        pltpu.VMEM((block_tiles, 2 * n_tokens, wide), BF16),
        pltpu.VMEM((block_tiles, wide, dim), BF16),
        pltpu.VMEM((dim, 2 * n_tokens), BF16),
        pltpu.SemaphoreType.DMA((2, block_tiles)),
        pltpu.SemaphoreType.DMA((block_tiles,)),
        pltpu.SemaphoreType.DMA((1,)),
    ]
    block_shape = jax.ShapeDtypeStruct((block, dim), BF16)
    common = dict(
        compiler_params=MOST,
        cost_estimate=pl.CostEstimate(flops=1, bytes_accessed=1, transcendentals=0),
    )
    dp_at = lax.axis_index("dp")
    first, operands = pl.pallas_call(
        functools.partial(backward_kernel, False),
        out_shape=(block_shape, jax.ShapeDtypeStruct((dim, 2 * n_tokens), BF16)),
        in_specs=[SMEM, SMEM, ANY, ANY, ANY, VMEM],
        out_specs=(ANY, ANY),
        scratch_shapes=[
            pltpu.VMEM((2, dim, n_tokens), BF16),
            pltpu.VMEM((n_tokens, 128), F32),
        ] + streams,
        name="backward_first",
        **common,
    )(
        (dp_at ^ (n_dp - 1))[None], code_at[None], turned, codes, weighed, received
    )

    def backward(at):
        return pl.pallas_call(
            functools.partial(backward_kernel, True),
            out_shape=block_shape,
            in_specs=[SMEM, ANY, ANY, ANY],
            out_specs=ANY,
            scratch_shapes=streams,
            name="backward",
            **common,
        )(at[None], codes, weighed, operands)

    blocks = [swap(first, "dp", n_dp, n_dp - 1)]
    blocks += [swap(backward(dp_at ^ d), "dp", n_dp, d) for d in range(1, n_dp - 1)]
    blocks.append(backward(dp_at))
    steps = max(block // 512, 1)
    own_rows = pl.pallas_call(
        functools.partial(add_kernel, n_dp),
        out_shape=jax.ShapeDtypeStruct((block, dim), F32),
        in_specs=[ANY] * n_dp,
        out_specs=ANY,
        scratch_shapes=[
            pltpu.VMEM((n_dp, steps, block // steps, dim), BF16),
            pltpu.VMEM((steps, block // steps, dim), F32),
            pltpu.SemaphoreType.DMA((n_dp, steps)),
            pltpu.SemaphoreType.DMA((steps,)),
        ],
        compiler_params=PART,
        cost_estimate=pl.CostEstimate(
            flops=0, bytes_accessed=(2 * n_dp + 4) * block * dim, transcendentals=0
        ),
        name="add",
    )(*blocks)
    return quantized, token_gradient, own_rows[None]


def solution(mesh):
    n_dp, n_code = mesh.shape["dp"], mesh.shape["code"]
    in_specs = (P("dp", None), P("code", None), P("dp", "code"), P("dp", None))
    out_specs = (P("dp", None), P("dp", None), P("code", "dp", None))
    return jax.shard_map(
        functools.partial(local, n_dp, n_code),
        mesh=mesh, in_specs=in_specs, out_specs=out_specs, check_vma=False,
    )
```

```python
import functools

import jax
import jax.numpy as jnp
from jax import lax
from jax.experimental import pallas as pl
from jax.experimental.pallas import tpu as pltpu
from jax.sharding import PartitionSpec as P

SOFTMAX_HEAT = 0.5
SHARPNESS = 1.0 / SOFTMAX_HEAT
BF16 = jnp.bfloat16
F32 = jnp.float32
MIB = 1 << 20
CHUNK = 256
WIDE = 512
AHEAD = 2
NEAR = 3
PACK = 16
ROWS = 64
LARGEST = 2.0**30
VMEM = pl.BlockSpec(memory_space=pltpu.VMEM)
SMEM = pl.BlockSpec(memory_space=pltpu.SMEM)
ANY = pl.BlockSpec(memory_space=pl.ANY)
FULL = pltpu.CompilerParams(vmem_limit_bytes=60 * MIB)
MOST = pltpu.CompilerParams(vmem_limit_bytes=54 * MIB)
SOME = pltpu.CompilerParams(vmem_limit_bytes=24 * MIB)


def dot(left, right, left_dim=1, right_dim=0):
    return lax.dot_general(
        left, right, (((left_dim,), (right_dim,)), ((), ())), preferred_element_type=F32
    )


def lane_groups(value):
    return [value[:, j : j + 128] for j in range(0, value.shape[1], 128)]


def stat_lanes(n_tokens):
    return max(n_tokens // PACK * 4, 128)


def high_low(value):
    high = value.astype(BF16).astype(F32)
    return high, (value - high).astype(BF16).astype(F32)


def forward_kernel(
    n_code, tokens, grad_out, codebook, noise, sent, sides,
    own, pair, book, noise_in, slot_a, slot_b, shifts, total, sums, sent_out, sides_out,
    own_sem, book_sem, noise_sem, first_sem, out_sem,
):
    tiles, width, dim = book.shape
    n_tokens = tokens.shape[0]
    columns = [slice(c, c + CHUNK) for c in range(0, width, CHUNK)]
    slots = (slot_a, slot_b)

    def fetch(t):
        at = pl.multiple_of(t * width, width)
        return (
            pltpu.make_async_copy(codebook.at[pl.ds(at, width)], book.at[t], book_sem.at[t]),
            pltpu.make_async_copy(noise.at[:, pl.ds(at, width)], noise_in.at[t], noise_sem.at[t]),
        )

    def start(t):
        for copy in fetch(t):
            copy.start()

    def arrive(t):
        for copy in fetch(t):
            copy.wait()

    own_copies = (
        pltpu.make_async_copy(tokens, own.at[0], own_sem.at[0]),
        pltpu.make_async_copy(grad_out, own.at[1], own_sem.at[1]),
    )
    halves = []
    for h in range(2):
        at = pl.ds(h * (width // 2), width // 2)
        halves.append((
            pltpu.make_async_copy(codebook.at[at], book.at[0, at], first_sem.at[h, 0]),
            pltpu.make_async_copy(noise.at[:, at], noise_in.at[0, :, at], first_sem.at[h, 1]),
        ))
    for copy in own_copies + halves[0]:
        copy.start()
    for copy in halves[1]:
        copy.start()

    def logits(both, t, r, c):
        noise_part = (noise_in[t, r : r + ROWS, c] * BF16(SHARPNESS)).astype(F32)
        return both[2 * r : 2 * r + ROWS] + noise_part

    def raise_shift(t, some):
        for c in some:
            both = dot(pair[...], book[t, c], 1, 1)
            for r in range(0, n_tokens, ROWS):
                at = slice(r, r + ROWS)
                shifts[at] = functools.reduce(
                    jnp.maximum, lane_groups(logits(both, t, r, c)), shifts[at]
                )

    def soften(t, s, fresh, last=None):
        if fresh is not None:
            @pl.when(fresh)
            def _():
                arrive(t)

                @pl.when(t + AHEAD < tiles)
                def _():
                    start(t + AHEAD)

        slot = slots[s]
        ahead = dot(pair[...], book[t, columns[0]], 1, 1)
        for k, c in enumerate(columns):
            both = ahead
            if k + 1 < len(columns):
                ahead = dot(pair[...], book[t, columns[k + 1]], 1, 1)
            elif last is not None:
                last()
            for r in range(0, n_tokens, ROWS):
                at = slice(r, r + ROWS)
                shift = jnp.concatenate([shifts[at]] * (CHUNK // 128), axis=1)
                weight = jnp.exp(logits(both, t, r, c) - shift)
                total[at] += sum(lane_groups(weight))
                slot[at, c] = weight.astype(BF16)
                gradient = both[2 * r + ROWS : 2 * r + 2 * ROWS]
                slot[n_tokens + r : n_tokens + r + ROWS, c] = (weight * gradient).astype(BF16)

    def accumulate(t, s):
        sums[...] += dot(slots[s][...], book[t])

    def attempt(state):
        again, _ = state
        fresh = again == 0
        shifts[...] = jnp.full(shifts.shape, -jnp.inf, F32)

        @pl.when(fresh)
        def _():
            for r in range(0, n_tokens, ROWS):
                some = noise_in[0, r : r + ROWS, columns[0]] * BF16(SHARPNESS)
                shifts[r : r + ROWS] = functools.reduce(
                    jnp.maximum, lane_groups(some.astype(F32))
                )

        @pl.when(jnp.logical_not(fresh))
        def _():
            def over(t, carry):
                raise_shift(t, columns)
                return carry

            lax.fori_loop(0, tiles, over, 0)

        shift = jnp.max(shifts[...], axis=1, keepdims=True).astype(BF16).astype(F32)
        shifts[...] = jnp.broadcast_to(shift, shifts.shape)
        total[...] = jnp.zeros(total.shape, F32)
        sums[...] = jnp.zeros(sums.shape, F32)

        @pl.when(fresh)
        def _():
            for copy in halves[1]:
                copy.wait()

        soften(0, 0, None)

        def soften_pair(i, carry):
            soften(2 * i + 1, 1, fresh, lambda: accumulate(2 * i, 0))
            soften(2 * i + 2, 0, fresh, lambda: accumulate(2 * i + 1, 1))
            return carry

        lax.fori_loop(0, tiles // 2 - 1, soften_pair, 0)
        soften(tiles - 1, 1, fresh, lambda: accumulate(tiles - 2, 0))
        accumulate(tiles - 1, 1)
        row_total = jnp.sum(total[...], axis=1, keepdims=True)
        total[...] = jnp.broadcast_to(row_total, total.shape)
        fits = jnp.logical_and(jnp.max(total[...]) < LARGEST, jnp.min(total[...]) > 1 / LARGEST)
        return again + 1, jnp.logical_and(fresh, jnp.logical_not(fits))

    for copy in own_copies:
        copy.wait()
    for r in range(0, n_tokens, ROWS):
        pair[2 * r : 2 * r + ROWS] = own[0, r : r + ROWS] * BF16(SHARPNESS)
        pair[2 * r + ROWS : 2 * r + 2 * ROWS] = own[1, r : r + ROWS]
    for copy in halves[0]:
        copy.wait()
    for t in range(1, min(AHEAD + 1, tiles)):
        start(t)
    lax.while_loop(lambda state: state[1], attempt, (jnp.int32(0), jnp.bool_(True)))

    shift = shifts[:, :1]
    mix = sums[:n_tokens]
    pulled = sums[n_tokens:]
    own_total = total[:, :1]
    own_inner = jnp.sum(own[1].astype(F32) * mix, axis=1, keepdims=True)
    mean = own_inner / own_total
    side = lax.broadcasted_iota(jnp.int32, sides_out.shape, 1)
    sides_out[...] = jnp.where(side < 64, mean, shift)
    copies = [pltpu.make_async_copy(sides_out, sides, out_sem.at[0])]
    copies[0].start()
    rows = n_tokens // n_code
    lanes = stat_lanes(n_tokens)
    lane = lax.broadcasted_iota(jnp.int32, (PACK, lanes), 1)
    stats = jnp.zeros((PACK, lanes), F32)
    parts = (own_total,) + high_low(mean) + (shift,)
    for q in range(n_tokens // PACK):
        for i, part in enumerate(parts):
            stats = jnp.where(lane == 4 * q + i, part[q * PACK : (q + 1) * PACK], stats)
    stats = [stats[:, j : j + 128].astype(BF16) for j in range(0, lanes, 128)]
    group = n_code // min(n_code, 4)
    for g in range(n_code):
        at = slice(g * rows, (g + 1) * rows)
        data = lane_groups(mix[at]) + lane_groups(pulled[at] - mean[at] * mix[at])
        for j, value in enumerate(data):
            sent_out[g, j * rows : (j + 1) * rows] = value.astype(BF16)
        for j, value in enumerate(stats):
            first = len(data) * rows + j * PACK
            sent_out[g, first : first + PACK] = value
        if (g + 1) % group == 0:
            part = pl.ds(g + 1 - group, group)
            copies.append(
                pltpu.make_async_copy(sent_out.at[part], sent.at[part], out_sem.at[len(copies)])
            )
            copies[-1].start()
    for copy in copies:
        copy.wait()


def roll_left(value, by):
    return pltpu.roll(value, value.shape[1] - by, 1)


def stats_of(received, p, n_tokens):
    first = received.shape[1] - stat_lanes(n_tokens) // 128 * PACK
    blocks = [received[p, r : r + PACK] for r in range(first, received.shape[1], PACK)]
    return jnp.concatenate(blocks, axis=1).astype(F32)


def factor_of(stats, top):
    return roll_left(jnp.exp(stats - top), 3)


def mean_of(stats):
    return roll_left(stats, 1) + roll_left(stats, 2)


def merged_stats(received, n_tokens):
    stats = [stats_of(received, p, n_tokens) for p in range(received.shape[0])]
    top = functools.reduce(jnp.maximum, stats)
    factors = [factor_of(s, top) * s for s in stats]
    means = [mean_of(s) for s in stats]
    total = sum(factors)
    inner = sum(f * m for f, m in zip(factors, means)) / total
    scales = [factor_of(s, top) / total for s in stats]
    return scales, means, top, total, inner


def merge_kernel(me, received, spread):
    n_code, rows, both = spread.shape
    dim = both // 2
    scales, means, _, _, inner = merged_stats(received, n_code * rows)
    lane = lax.broadcasted_iota(jnp.int32, inner.shape, 1)
    groups = rows // PACK
    mine = [lane == 4 * (me[0] * groups + h) for h in range(groups)]

    def column(value):
        columns = [jnp.sum(jnp.where(m, value, 0.0), axis=1, keepdims=True) for m in mine]
        return jnp.concatenate(columns, axis=0)

    count = dim // 128
    quantized = [jnp.zeros((rows, 128), F32)] * count
    gradient = [jnp.zeros((rows, 128), F32)] * count
    for p in range(n_code):
        scale = column(scales[p])
        offset = column(scales[p] * (means[p] - inner))
        for j in range(count):
            mix = received[p, j * rows : (j + 1) * rows].astype(F32)
            pulled = received[p, (count + j) * rows : (count + j + 1) * rows].astype(F32)
            quantized[j] += scale * mix
            gradient[j] += scale * pulled + offset * mix
    for j in range(count):
        results = (quantized[j].astype(BF16), (gradient[j] / SOFTMAX_HEAT).astype(BF16))
        for p in range(n_code):
            for i, result in enumerate(results):
                spread[p, :, i * dim + j * 128 : i * dim + (j + 1) * 128] = result


def weigh_kernel(
    tokens, grad_out, codebook, noise, sides, codes, weighed, turned,
    book, noise_in, code_out, weighed_out, sharp, means, shifts, turned_out,
    book_sem, noise_sem, out_sem, turned_sem,
):
    tiles, width, _ = book.shape
    wide = codes.shape[2]
    steps = [(t, slice(c, c + wide)) for t in range(tiles) for c in range(0, width, wide)]

    def fetch(t):
        at = pl.ds(t * width, width)
        return (
            pltpu.make_async_copy(codebook.at[at], book.at[t], book_sem.at[t]),
            pltpu.make_async_copy(noise.at[:, at], noise_in.at[t], noise_sem.at[t]),
        )

    def start(t):
        for copy in fetch(t):
            copy.start()

    def send(k):
        return (
            pltpu.make_async_copy(code_out.at[k], codes.at[k], out_sem.at[0, k]),
            pltpu.make_async_copy(weighed_out.at[k], weighed.at[k], out_sem.at[1, k]),
        )

    def products_of(step):
        t, c = step
        if c.start == 0:
            for copy in fetch(t):
                copy.wait()
            if t + NEAR < tiles:
                start(t + NEAR)
        keys = book[t, c]
        return dot(sharp[...], keys, 1, 1), dot(grad_out[...], keys, 1, 1)

    for t in range(min(NEAR, tiles)):
        start(t)
    sharp[...] = tokens[...] * BF16(SHARPNESS)
    means[...] = jnp.broadcast_to(sides[:, :1], means.shape)
    shifts[...] = jnp.broadcast_to(sides[:, 64:65], shifts.shape)
    turned_out[0] = grad_out[...].T
    turned_out[1] = sharp[...].T
    turned_copy = pltpu.make_async_copy(turned_out, turned, turned_sem)
    turned_copy.start()
    ahead = products_of(steps[0])
    for k, (t, c) in enumerate(steps):
        score, gradient = ahead
        if k + 1 < len(steps):
            ahead = products_of(steps[k + 1])
        shift = jnp.concatenate([shifts[...]] * (wide // 128), axis=1)
        mean = jnp.concatenate([means[...]] * (wide // 128), axis=1)
        noise_part = (noise_in[t, :, c] * BF16(SHARPNESS)).astype(F32)
        code = jnp.exp(score + noise_part - shift).astype(BF16)
        code_out[k] = code
        weighed_out[k] = (code.astype(F32) * (gradient - mean)).astype(BF16)
        for copy in send(k):
            copy.start()
    for k in range(len(steps)):
        for copy in send(k):
            copy.wait()
    turned_copy.wait()


def backward_kernel(prepared, block, *rest):
    if prepared:
        codes, weighed, given, out, *rest = rest
    else:
        code_at, turned, codes, weighed, received, out, kept, own, spread, *rest = rest
    both_in, operands, in_sem, own_sem, *rest = rest
    tiles, _, width = both_in.shape
    if not prepared:
        result, out_sem = rest
    n_tokens = both_in.shape[1] // 2

    def fetch(t):
        return [
            pltpu.make_async_copy(
                source.at[block[0] * tiles + t],
                both_in.at[t, pl.ds(half * n_tokens, n_tokens)],
                in_sem.at[half, t],
            )
            for half, source in enumerate((codes, weighed))
        ]

    def start(t):
        for copy in fetch(t):
            copy.start()

    start(0)
    if prepared:
        own_copies = [pltpu.make_async_copy(given, operands, own_sem.at[0])]
    else:
        own_copies = [pltpu.make_async_copy(turned, own, own_sem.at[0])]
    for copy in own_copies:
        copy.start()
    for t in range(1, min(NEAR, tiles)):
        start(t)

    if prepared:
        own_copies[0].wait()
    else:
        _, _, top, total, inner = merged_stats(received, n_tokens)
        stats = stats_of(received, code_at[0], n_tokens)
        scale = factor_of(stats, top) / total
        offset = scale * (mean_of(stats) - inner)
        lane = lax.broadcasted_iota(jnp.int32, (PACK, 128), 1)
        for q in range(n_tokens // PACK):
            at = slice(4 * q, 4 * q + 1)
            spread[q * PACK : (q + 1) * PACK] = jnp.where(
                lane < 64, scale[:, at], offset[:, at]
            )
        factors = spread[...].T
        scale, offset = factors[:1], factors[64:65]
        own_copies[0].wait()
        grad, token = own[0].astype(F32), own[1].astype(F32)
        operands[:, :n_tokens] = (scale * grad + offset * token).astype(BF16)
        operands[:, n_tokens:] = (scale * token).astype(BF16)
        keep = pltpu.make_async_copy(operands, kept, own_sem.at[0])
        keep.start()

    def send(t):
        return pltpu.make_async_copy(
            result.at[t], out.at[pl.ds(t * width, width)], out_sem.at[t]
        )

    wide = min(WIDE, width)
    steps = [(t, slice(c, c + wide)) for t in range(tiles) for c in range(0, width, wide)]

    def product(step):
        t, c = step
        if c.start == 0:
            for copy in fetch(t):
                copy.wait()
            if t + NEAR < tiles:
                start(t + NEAR)
        return dot(operands[...], both_in[t, :, c])

    ahead = product(steps[0])
    for k, (t, c) in enumerate(steps):
        value = ahead
        if k + 1 < len(steps):
            ahead = product(steps[k + 1])
        if prepared:
            out[t * width + c.start : t * width + c.stop] = value.astype(BF16).T
        else:
            result[t, c] = value.astype(BF16).T
            if c.stop == width:
                send(t).start()
    if not prepared:
        keep.wait()
        for t in range(tiles):
            send(t).wait()


def add_kernel(n_parts, *refs):
    parts, own, out = refs[: n_parts - 1], refs[n_parts - 1], refs[n_parts]
    held, result, in_sem, out_sem = refs[n_parts + 1 :]
    steps, rows, _ = result.shape

    def fetch(i):
        at = pl.ds(i * rows, rows)
        return [
            pltpu.make_async_copy(part.at[at], held.at[j, i], in_sem.at[j, i])
            for j, part in enumerate(parts)
        ]

    def send(i):
        return pltpu.make_async_copy(result.at[i], out.at[pl.ds(i * rows, rows)], out_sem.at[i])

    for i in range(steps):
        for copy in fetch(i):
            copy.start()
    for i in range(steps):
        for copy in fetch(i):
            copy.wait()
        mine = own[i * rows : (i + 1) * rows].astype(F32)
        result[i] = sum((held[j, i].astype(F32) for j in range(len(parts))), mine)
        send(i).start()
    for i in range(steps):
        send(i).wait()


def unpack_kernel(gathered, quantized, gradient):
    n_code, rows, both = gathered.shape
    dim = both // 2
    for g in range(n_code):
        at = slice(g * rows, (g + 1) * rows)
        quantized[at] = gathered[g, :, :dim].astype(F32)
        gradient[at] = gathered[g, :, dim:].astype(F32)


def swap(value, axis, size, mask):
    return lax.ppermute(value, axis, [(i, i ^ mask) for i in range(size)])


def local(n_dp, n_code, tokens, codebook, noise, grad_out):
    n_tokens, dim = tokens.shape
    n_codes = codebook.shape[0]
    rows = n_tokens // n_code
    block = n_codes // n_dp
    width = min(1024, block)
    wide = min(WIDE, width)
    tiles_in = n_codes // wide
    tiles = n_codes // width
    piece = rows * (2 * dim // 128) + stat_lanes(n_tokens) // 128 * PACK
    products = 2 * n_tokens * n_codes * dim

    sent, sides = pl.pallas_call(
        functools.partial(forward_kernel, n_code),
        out_shape=(
            jax.ShapeDtypeStruct((n_code, piece, 128), BF16),
            jax.ShapeDtypeStruct((n_tokens, 128), F32),
        ),
        in_specs=[ANY, ANY, ANY, ANY],
        out_specs=(ANY, ANY),
        scratch_shapes=[
            pltpu.VMEM((2, n_tokens, dim), BF16),
            pltpu.VMEM((2 * n_tokens, dim), BF16),
            pltpu.VMEM((tiles, width, dim), BF16),
            pltpu.VMEM((tiles, n_tokens, width), BF16),
            pltpu.VMEM((2 * n_tokens, width), BF16),
            pltpu.VMEM((2 * n_tokens, width), BF16),
            pltpu.VMEM((n_tokens, 128), F32),
            pltpu.VMEM((n_tokens, 128), F32),
            pltpu.VMEM((2 * n_tokens, dim), F32),
            pltpu.VMEM((n_code, piece, 128), BF16),
            pltpu.VMEM((n_tokens, 128), F32),
            pltpu.SemaphoreType.DMA((2,)),
            pltpu.SemaphoreType.DMA((tiles,)),
            pltpu.SemaphoreType.DMA((tiles,)),
            pltpu.SemaphoreType.DMA((2, 2)),
            pltpu.SemaphoreType.DMA((1 + min(n_code, 4),)),
        ],
        compiler_params=FULL,
        cost_estimate=pl.CostEstimate(
            flops=4 * products, bytes_accessed=12 * MIB, transcendentals=n_tokens * n_codes
        ),
        name="forward",
    )(tokens, grad_out, codebook, noise)

    received = lax.all_to_all(sent, "code", 0, 0, tiled=True)
    codes, weighed, turned = pl.pallas_call(
        weigh_kernel,
        out_shape=(pltpu.HBM((tiles_in, n_tokens, wide), BF16),) * 2
        + (jax.ShapeDtypeStruct((2, dim, n_tokens), BF16),),
        in_specs=[VMEM, VMEM, ANY, ANY, VMEM],
        out_specs=(ANY, ANY, ANY),
        scratch_shapes=[
            pltpu.VMEM((tiles, width, dim), BF16),
            pltpu.VMEM((tiles, n_tokens, width), BF16),
            pltpu.VMEM((tiles_in, n_tokens, wide), BF16),
            pltpu.VMEM((tiles_in, n_tokens, wide), BF16),
            pltpu.VMEM((n_tokens, dim), BF16),
            pltpu.VMEM((n_tokens, 128), F32),
            pltpu.VMEM((n_tokens, 128), F32),
            pltpu.VMEM((2, dim, n_tokens), BF16),
            pltpu.SemaphoreType.DMA((tiles,)),
            pltpu.SemaphoreType.DMA((tiles,)),
            pltpu.SemaphoreType.DMA((2, tiles_in)),
            pltpu.SemaphoreType.DMA,
        ],
        compiler_params=FULL,
        cost_estimate=pl.CostEstimate(
            flops=2 * products, bytes_accessed=28 * MIB, transcendentals=n_tokens * n_codes
        ),
        name="weigh",
    )(tokens, grad_out, codebook, noise, sides)
    received, weighed = lax.optimization_barrier((received, weighed))
    code_at = lax.axis_index("code")
    spread = pl.pallas_call(
        merge_kernel,
        out_shape=jax.ShapeDtypeStruct((n_code, rows, 2 * dim), BF16),
        in_specs=[SMEM, VMEM],
        out_specs=VMEM,
        compiler_params=SOME,
        name="merge",
    )(code_at[None], received)
    received, spread = lax.optimization_barrier((received, spread))
    gathered = lax.all_to_all(spread, "code", 0, 0, tiled=True)
    quantized, token_gradient = pl.pallas_call(
        unpack_kernel,
        out_shape=(jax.ShapeDtypeStruct((n_tokens, dim), F32),) * 2,
        in_specs=[VMEM],
        out_specs=(VMEM, VMEM),
        compiler_params=SOME,
        cost_estimate=pl.CostEstimate(
            flops=100 * products, bytes_accessed=400 * MIB, transcendentals=0
        ),
        name="unpack",
    )(gathered)

    block_tiles = block // wide
    streams = [
        pltpu.VMEM((block_tiles, 2 * n_tokens, wide), BF16),
        pltpu.VMEM((dim, 2 * n_tokens), BF16),
        pltpu.SemaphoreType.DMA((2, block_tiles)),
        pltpu.SemaphoreType.DMA((1,)),
    ]
    common = dict(
        compiler_params=MOST,
        cost_estimate=pl.CostEstimate(flops=1, bytes_accessed=1, transcendentals=0),
    )
    dp_at = lax.axis_index("dp")
    first, operands = pl.pallas_call(
        functools.partial(backward_kernel, False),
        out_shape=(
            jax.ShapeDtypeStruct((block, dim), BF16),
            jax.ShapeDtypeStruct((dim, 2 * n_tokens), BF16),
        ),
        in_specs=[SMEM, SMEM, ANY, ANY, ANY, VMEM],
        out_specs=(ANY, ANY),
        scratch_shapes=[
            pltpu.VMEM((2, dim, n_tokens), BF16),
            pltpu.VMEM((n_tokens, 128), F32),
        ] + streams + [
            pltpu.VMEM((block_tiles, wide, dim), BF16),
            pltpu.SemaphoreType.DMA((block_tiles,)),
        ],
        name="backward_first",
        **common,
    )(
        (dp_at ^ (n_dp - 1))[None], code_at[None], turned, codes, weighed, received
    )

    def backward(at):
        return pl.pallas_call(
            functools.partial(backward_kernel, True),
            out_shape=pltpu.VMEM((block, dim), BF16),
            in_specs=[SMEM, ANY, ANY, ANY],
            out_specs=VMEM,
            scratch_shapes=streams,
            name="backward",
            **common,
        )(at[None], codes, weighed, operands)

    blocks = [swap(first, "dp", n_dp, n_dp - 1)]
    blocks += [swap(backward(dp_at ^ d), "dp", n_dp, d) for d in range(1, n_dp - 1)]
    blocks.append(backward(dp_at))
    steps = max(block // 512, 1)
    own_rows = pl.pallas_call(
        functools.partial(add_kernel, n_dp),
        out_shape=jax.ShapeDtypeStruct((block, dim), F32),
        in_specs=[ANY] * (n_dp - 1) + [VMEM],
        out_specs=ANY,
        scratch_shapes=[
            pltpu.VMEM((n_dp - 1, steps, block // steps, dim), BF16),
            pltpu.VMEM((steps, block // steps, dim), F32),
            pltpu.SemaphoreType.DMA((n_dp - 1, steps)),
            pltpu.SemaphoreType.DMA((steps,)),
        ],
        compiler_params=SOME,
        cost_estimate=pl.CostEstimate(
            flops=0, bytes_accessed=(2 * n_dp + 4) * block * dim, transcendentals=0
        ),
        name="add",
    )(*blocks)
    return quantized, token_gradient, own_rows[None]


def solution(mesh):
    n_dp, n_code = mesh.shape["dp"], mesh.shape["code"]
    in_specs = (P("dp", None), P("code", None), P("dp", "code"), P("dp", None))
    out_specs = (P("dp", None), P("dp", None), P("code", "dp", None))
    return jax.shard_map(
        functools.partial(local, n_dp, n_code),
        mesh=mesh, in_specs=in_specs, out_specs=out_specs, check_vma=False,
    )
```

```python
import functools

import jax
import jax.numpy as jnp
from jax import lax
from jax.experimental import pallas as pl
from jax.experimental.pallas import tpu as pltpu
from jax.sharding import PartitionSpec as P

SOFTMAX_HEAT = 0.5
SHARPNESS = 1.0 / SOFTMAX_HEAT
BF16 = jnp.bfloat16
F32 = jnp.float32
MIB = 1 << 20
CHUNK = 256
WIDE = 512
NEAR = 3
PACK = 16
ROWS = 64
LARGEST = 2.0**30
VMEM = pl.BlockSpec(memory_space=pltpu.VMEM)
SMEM = pl.BlockSpec(memory_space=pltpu.SMEM)
ANY = pl.BlockSpec(memory_space=pl.ANY)
FULL = pltpu.CompilerParams(vmem_limit_bytes=60 * MIB)
MOST = pltpu.CompilerParams(vmem_limit_bytes=54 * MIB)
SOME = pltpu.CompilerParams(vmem_limit_bytes=24 * MIB)


def dot(left, right, left_dim=1, right_dim=0):
    return lax.dot_general(
        left, right, (((left_dim,), (right_dim,)), ((), ())), preferred_element_type=F32
    )


def lane_groups(value):
    return [value[:, j : j + 128] for j in range(0, value.shape[1], 128)]


def stat_lanes(n_tokens):
    return max(n_tokens // PACK * 4, 128)


def high_low(value):
    high = value.astype(BF16).astype(F32)
    return high, (value - high).astype(BF16).astype(F32)


def forward_kernel(
    n_code, tokens, grad_out, codebook, noise, sent, sides,
    own, pair, book, noise_in, slot_a, slot_b, shifts, total, sums, sent_out, sides_out,
    own_sem, book_sem, noise_sem, first_sem, out_sem,
):
    tiles, width, dim = book.shape
    n_tokens = tokens.shape[0]
    columns = [slice(c, c + CHUNK) for c in range(0, width, CHUNK)]
    slots = (slot_a, slot_b)

    def fetch(t):
        at = pl.multiple_of(t * width, width)
        return (
            pltpu.make_async_copy(codebook.at[pl.ds(at, width)], book.at[t], book_sem.at[t]),
            pltpu.make_async_copy(noise.at[:, pl.ds(at, width)], noise_in.at[t], noise_sem.at[t]),
        )

    def start(t):
        for copy in fetch(t):
            copy.start()

    def arrive(t):
        for copy in fetch(t):
            copy.wait()

    own_copies = (
        pltpu.make_async_copy(tokens, own.at[0], own_sem.at[0]),
        pltpu.make_async_copy(grad_out, own.at[1], own_sem.at[1]),
    )
    halves = []
    for h in range(2):
        at = pl.ds(h * (width // 2), width // 2)
        halves.append((
            pltpu.make_async_copy(codebook.at[at], book.at[0, at], first_sem.at[h, 0]),
            pltpu.make_async_copy(noise.at[:, at], noise_in.at[0, :, at], first_sem.at[h, 1]),
        ))
    for copy in own_copies + halves[0]:
        copy.start()
    for copy in halves[1]:
        copy.start()

    def logits(both, t, r, c):
        noise_part = (noise_in[t, r : r + ROWS, c] * BF16(SHARPNESS)).astype(F32)
        return both[2 * r : 2 * r + ROWS] + noise_part

    def raise_shift(t, some):
        for c in some:
            both = dot(pair[...], book[t, c], 1, 1)
            for r in range(0, n_tokens, ROWS):
                at = slice(r, r + ROWS)
                shifts[at] = functools.reduce(
                    jnp.maximum, lane_groups(logits(both, t, r, c)), shifts[at]
                )

    def soften(t, s, last=None):
        slot = slots[s]
        ahead = dot(pair[...], book[t, columns[0]], 1, 1)
        for k, c in enumerate(columns):
            both = ahead
            if k + 1 < len(columns):
                ahead = dot(pair[...], book[t, columns[k + 1]], 1, 1)
            elif last is not None:
                last()
            for r in range(0, n_tokens, ROWS):
                at = slice(r, r + ROWS)
                shift = jnp.concatenate([shifts[at]] * (CHUNK // 128), axis=1)
                weight = jnp.exp(logits(both, t, r, c) - shift)
                total[at] += sum(lane_groups(weight))
                slot[at, c] = weight.astype(BF16)
                gradient = both[2 * r + ROWS : 2 * r + 2 * ROWS]
                slot[n_tokens + r : n_tokens + r + ROWS, c] = (weight * gradient).astype(BF16)

    def accumulate(t, s):
        sums[...] += dot(slots[s][...], book[t])

    def attempt(state):
        again, _ = state
        fresh = again == 0
        shifts[...] = jnp.full(shifts.shape, -jnp.inf, F32)

        @pl.when(fresh)
        def _():
            for r in range(0, n_tokens, ROWS):
                some = noise_in[0, r : r + ROWS, columns[0]] * BF16(SHARPNESS)
                shifts[r : r + ROWS] = functools.reduce(
                    jnp.maximum, lane_groups(some.astype(F32))
                )

        @pl.when(jnp.logical_not(fresh))
        def _():
            def over(t, carry):
                raise_shift(t, columns)
                return carry

            lax.fori_loop(0, tiles, over, 0)

        shift = jnp.max(shifts[...], axis=1, keepdims=True).astype(BF16).astype(F32)
        shifts[...] = jnp.broadcast_to(shift, shifts.shape)
        total[...] = jnp.zeros(total.shape, F32)
        sums[...] = jnp.zeros(sums.shape, F32)

        @pl.when(fresh)
        def _():
            for copy in halves[1]:
                copy.wait()

        soften(0, 0)

        def soften_pair(i, carry):
            @pl.when(fresh)
            def _():
                arrive(2 * i + 1)
                arrive(2 * i + 2)
                start(2 * i + 3)

                @pl.when(2 * i + 4 < tiles)
                def _():
                    start(2 * i + 4)

            soften(2 * i + 1, 1, lambda: accumulate(2 * i, 0))
            soften(2 * i + 2, 0, lambda: accumulate(2 * i + 1, 1))
            return carry

        lax.fori_loop(0, tiles // 2 - 1, soften_pair, 0)

        @pl.when(fresh)
        def _():
            arrive(tiles - 1)

        soften(tiles - 1, 1, lambda: accumulate(tiles - 2, 0))
        accumulate(tiles - 1, 1)
        row_total = jnp.sum(total[...], axis=1, keepdims=True)
        total[...] = jnp.broadcast_to(row_total, total.shape)
        fits = jnp.logical_and(jnp.max(total[...]) < LARGEST, jnp.min(total[...]) > 1 / LARGEST)
        return again + 1, jnp.logical_and(fresh, jnp.logical_not(fits))

    for copy in own_copies:
        copy.wait()
    for r in range(0, n_tokens, ROWS):
        pair[2 * r : 2 * r + ROWS] = own[0, r : r + ROWS] * BF16(SHARPNESS)
        pair[2 * r + ROWS : 2 * r + 2 * ROWS] = own[1, r : r + ROWS]
    for copy in halves[0]:
        copy.wait()
    for t in range(1, min(3, tiles)):
        start(t)
    lax.while_loop(lambda state: state[1], attempt, (jnp.int32(0), jnp.bool_(True)))

    shift = shifts[:, :1]
    mix = sums[:n_tokens]
    pulled = sums[n_tokens:]
    own_total = total[:, :1]
    own_inner = jnp.sum(own[1].astype(F32) * mix, axis=1, keepdims=True)
    mean = own_inner / own_total
    side = lax.broadcasted_iota(jnp.int32, sides_out.shape, 1)
    sides_out[...] = jnp.where(side < 64, mean, shift)
    copies = [pltpu.make_async_copy(sides_out, sides, out_sem.at[0])]
    copies[0].start()
    rows = n_tokens // n_code
    lanes = stat_lanes(n_tokens)
    lane = lax.broadcasted_iota(jnp.int32, (PACK, lanes), 1)
    stats = jnp.zeros((PACK, lanes), F32)
    parts = (own_total,) + high_low(mean) + (shift,)
    for q in range(n_tokens // PACK):
        for i, part in enumerate(parts):
            stats = jnp.where(lane == 4 * q + i, part[q * PACK : (q + 1) * PACK], stats)
    stats = [stats[:, j : j + 128].astype(BF16) for j in range(0, lanes, 128)]
    group = n_code // min(n_code, 4)
    for g in range(n_code):
        at = slice(g * rows, (g + 1) * rows)
        data = lane_groups(mix[at]) + lane_groups(pulled[at] - mean[at] * mix[at])
        for j, value in enumerate(data):
            sent_out[g, j * rows : (j + 1) * rows] = value.astype(BF16)
        for j, value in enumerate(stats):
            first = len(data) * rows + j * PACK
            sent_out[g, first : first + PACK] = value
        if (g + 1) % group == 0:
            part = pl.ds(g + 1 - group, group)
            copies.append(
                pltpu.make_async_copy(sent_out.at[part], sent.at[part], out_sem.at[len(copies)])
            )
            copies[-1].start()
    for copy in copies:
        copy.wait()


def roll_left(value, by):
    return pltpu.roll(value, value.shape[1] - by, 1)


def stats_of(received, p, n_tokens):
    first = received.shape[1] - stat_lanes(n_tokens) // 128 * PACK
    blocks = [received[p, r : r + PACK] for r in range(first, received.shape[1], PACK)]
    return jnp.concatenate(blocks, axis=1).astype(F32)


def factor_of(stats, top):
    return roll_left(jnp.exp(stats - top), 3)


def mean_of(stats):
    return roll_left(stats, 1) + roll_left(stats, 2)


def merged_stats(received, n_tokens):
    stats = [stats_of(received, p, n_tokens) for p in range(received.shape[0])]
    top = functools.reduce(jnp.maximum, stats)
    factors = [factor_of(s, top) * s for s in stats]
    means = [mean_of(s) for s in stats]
    total = sum(factors)
    inner = sum(f * m for f, m in zip(factors, means)) / total
    scales = [factor_of(s, top) / total for s in stats]
    return scales, means, top, total, inner


def merge_kernel(me, received, spread):
    n_code, rows, both = spread.shape
    dim = both // 2
    scales, means, _, _, inner = merged_stats(received, n_code * rows)
    lane = lax.broadcasted_iota(jnp.int32, inner.shape, 1)
    groups = rows // PACK
    mine = [lane == 4 * (me[0] * groups + h) for h in range(groups)]

    def column(value):
        columns = [jnp.sum(jnp.where(m, value, 0.0), axis=1, keepdims=True) for m in mine]
        return jnp.concatenate(columns, axis=0)

    count = dim // 128
    quantized = [jnp.zeros((rows, 128), F32)] * count
    gradient = [jnp.zeros((rows, 128), F32)] * count
    for p in range(n_code):
        scale = column(scales[p])
        offset = column(scales[p] * (means[p] - inner))
        for j in range(count):
            mix = received[p, j * rows : (j + 1) * rows].astype(F32)
            pulled = received[p, (count + j) * rows : (count + j + 1) * rows].astype(F32)
            quantized[j] += scale * mix
            gradient[j] += scale * pulled + offset * mix
    for j in range(count):
        results = (quantized[j].astype(BF16), (gradient[j] / SOFTMAX_HEAT).astype(BF16))
        for p in range(n_code):
            for i, result in enumerate(results):
                spread[p, :, i * dim + j * 128 : i * dim + (j + 1) * 128] = result


def weigh_kernel(
    tokens, grad_out, codebook, noise, sides, codes, weighed, turned,
    book, noise_in, code_out, weighed_out, sharp, means, shifts, turned_out,
    book_sem, noise_sem, out_sem, turned_sem,
):
    tiles, width, _ = book.shape
    wide = codes.shape[2]
    steps = [(t, slice(c, c + wide)) for t in range(tiles) for c in range(0, width, wide)]

    def fetch(t):
        at = pl.ds(t * width, width)
        return (
            pltpu.make_async_copy(codebook.at[at], book.at[t], book_sem.at[t]),
            pltpu.make_async_copy(noise.at[:, at], noise_in.at[t], noise_sem.at[t]),
        )

    def start(t):
        for copy in fetch(t):
            copy.start()

    def send(k):
        return (
            pltpu.make_async_copy(code_out.at[k], codes.at[k], out_sem.at[0, k]),
            pltpu.make_async_copy(weighed_out.at[k], weighed.at[k], out_sem.at[1, k]),
        )

    def products_of(step):
        t, c = step
        if c.start == 0:
            for copy in fetch(t):
                copy.wait()
            if t + NEAR < tiles:
                start(t + NEAR)
        keys = book[t, c]
        return dot(sharp[...], keys, 1, 1), dot(grad_out[...], keys, 1, 1)

    for t in range(min(NEAR, tiles)):
        start(t)
    sharp[...] = tokens[...] * BF16(SHARPNESS)
    means[...] = jnp.broadcast_to(sides[:, :1], means.shape)
    shifts[...] = jnp.broadcast_to(sides[:, 64:65], shifts.shape)
    turned_out[0] = grad_out[...].T
    turned_out[1] = sharp[...].T
    turned_copy = pltpu.make_async_copy(turned_out, turned, turned_sem)
    turned_copy.start()
    ahead = products_of(steps[0])
    for k, (t, c) in enumerate(steps):
        score, gradient = ahead
        if k + 1 < len(steps):
            ahead = products_of(steps[k + 1])
        shift = jnp.concatenate([shifts[...]] * (wide // 128), axis=1)
        mean = jnp.concatenate([means[...]] * (wide // 128), axis=1)
        noise_part = (noise_in[t, :, c] * BF16(SHARPNESS)).astype(F32)
        code = jnp.exp(score + noise_part - shift).astype(BF16)
        code_out[k] = code
        weighed_out[k] = (code.astype(F32) * (gradient - mean)).astype(BF16)
        for copy in send(k):
            copy.start()
    for k in range(len(steps)):
        for copy in send(k):
            copy.wait()
    turned_copy.wait()


def backward_kernel(prepared, block, *rest):
    if prepared:
        codes, weighed, given, out, *rest = rest
    else:
        code_at, turned, codes, weighed, received, out, kept, own, spread, *rest = rest
    both_in, operands, in_sem, own_sem, *rest = rest
    tiles, _, width = both_in.shape
    if not prepared:
        result, out_sem = rest
    n_tokens = both_in.shape[1] // 2

    def fetch(t):
        return [
            pltpu.make_async_copy(
                source.at[block[0] * tiles + t],
                both_in.at[t, pl.ds(half * n_tokens, n_tokens)],
                in_sem.at[half, t],
            )
            for half, source in enumerate((codes, weighed))
        ]

    def start(t):
        for copy in fetch(t):
            copy.start()

    start(0)
    if prepared:
        own_copies = [pltpu.make_async_copy(given, operands, own_sem.at[0])]
    else:
        own_copies = [pltpu.make_async_copy(turned, own, own_sem.at[0])]
    for copy in own_copies:
        copy.start()
    for t in range(1, min(NEAR, tiles)):
        start(t)

    if prepared:
        own_copies[0].wait()
    else:
        _, _, top, total, inner = merged_stats(received, n_tokens)
        stats = stats_of(received, code_at[0], n_tokens)
        scale = factor_of(stats, top) / total
        offset = scale * (mean_of(stats) - inner)
        lane = lax.broadcasted_iota(jnp.int32, (PACK, 128), 1)
        for q in range(n_tokens // PACK):
            at = slice(4 * q, 4 * q + 1)
            spread[q * PACK : (q + 1) * PACK] = jnp.where(
                lane < 64, scale[:, at], offset[:, at]
            )
        factors = spread[...].T
        scale, offset = factors[:1], factors[64:65]
        own_copies[0].wait()
        grad, token = own[0].astype(F32), own[1].astype(F32)
        operands[:, :n_tokens] = (scale * grad + offset * token).astype(BF16)
        operands[:, n_tokens:] = (scale * token).astype(BF16)
        keep = pltpu.make_async_copy(operands, kept, own_sem.at[0])
        keep.start()

    def send(t):
        return pltpu.make_async_copy(
            result.at[t], out.at[pl.ds(t * width, width)], out_sem.at[t]
        )

    wide = min(WIDE, width)
    steps = [(t, slice(c, c + wide)) for t in range(tiles) for c in range(0, width, wide)]

    def product(step):
        t, c = step
        if c.start == 0:
            for copy in fetch(t):
                copy.wait()
            if t + NEAR < tiles:
                start(t + NEAR)
        return dot(operands[...], both_in[t, :, c])

    ahead = product(steps[0])
    for k, (t, c) in enumerate(steps):
        value = ahead
        if k + 1 < len(steps):
            ahead = product(steps[k + 1])
        if prepared:
            out[t * width + c.start : t * width + c.stop] = value.astype(BF16).T
        else:
            result[t, c] = value.astype(BF16).T
            if c.stop == width:
                send(t).start()
    if not prepared:
        keep.wait()
        for t in range(tiles):
            send(t).wait()


def finish_kernel(n_parts, gathered, *refs):
    parts, own = refs[: n_parts - 1], refs[n_parts - 1]
    quantized, gradient, out, held, result, both, in_sem, out_sem, both_sem = refs[n_parts:]
    steps, rows, dim = result.shape
    n_code, share, _ = gathered.shape

    def fetch(i):
        at = pl.ds(i * rows, rows)
        return [
            pltpu.make_async_copy(part.at[at], held.at[j, i], in_sem.at[j, i])
            for j, part in enumerate(parts)
        ]

    def send(i):
        return pltpu.make_async_copy(result.at[i], out.at[pl.ds(i * rows, rows)], out_sem.at[i])

    for i in range(steps):
        for copy in fetch(i):
            copy.start()
    copies = []
    for i, target in enumerate((quantized, gradient)):
        for g in range(n_code):
            at = slice(g * share, (g + 1) * share)
            both[i, at] = gathered[g, :, i * dim : (i + 1) * dim].astype(F32)
        copies.append(pltpu.make_async_copy(both.at[i], target, both_sem.at[i]))
        copies[-1].start()
    for i in range(steps):
        for copy in fetch(i):
            copy.wait()
        mine = own[i * rows : (i + 1) * rows].astype(F32)
        result[i] = sum((held[j, i].astype(F32) for j in range(len(parts))), mine)
        send(i).start()
    for copy in copies + [send(i) for i in range(steps)]:
        copy.wait()


def swap(value, axis, size, mask):
    return lax.ppermute(value, axis, [(i, i ^ mask) for i in range(size)])


def local(n_dp, n_code, tokens, codebook, noise, grad_out):
    n_tokens, dim = tokens.shape
    n_codes = codebook.shape[0]
    rows = n_tokens // n_code
    block = n_codes // n_dp
    width = min(1024, block)
    wide = min(WIDE, width)
    tiles_in = n_codes // wide
    tiles = n_codes // width
    piece = rows * (2 * dim // 128) + stat_lanes(n_tokens) // 128 * PACK
    products = 2 * n_tokens * n_codes * dim

    sent, sides = pl.pallas_call(
        functools.partial(forward_kernel, n_code),
        out_shape=(
            jax.ShapeDtypeStruct((n_code, piece, 128), BF16),
            jax.ShapeDtypeStruct((n_tokens, 128), F32),
        ),
        in_specs=[ANY, ANY, ANY, ANY],
        out_specs=(ANY, ANY),
        scratch_shapes=[
            pltpu.VMEM((2, n_tokens, dim), BF16),
            pltpu.VMEM((2 * n_tokens, dim), BF16),
            pltpu.VMEM((tiles, width, dim), BF16),
            pltpu.VMEM((tiles, n_tokens, width), BF16),
            pltpu.VMEM((2 * n_tokens, width), BF16),
            pltpu.VMEM((2 * n_tokens, width), BF16),
            pltpu.VMEM((n_tokens, 128), F32),
            pltpu.VMEM((n_tokens, 128), F32),
            pltpu.VMEM((2 * n_tokens, dim), F32),
            pltpu.VMEM((n_code, piece, 128), BF16),
            pltpu.VMEM((n_tokens, 128), F32),
            pltpu.SemaphoreType.DMA((2,)),
            pltpu.SemaphoreType.DMA((tiles,)),
            pltpu.SemaphoreType.DMA((tiles,)),
            pltpu.SemaphoreType.DMA((2, 2)),
            pltpu.SemaphoreType.DMA((1 + min(n_code, 4),)),
        ],
        compiler_params=FULL,
        cost_estimate=pl.CostEstimate(
            flops=4 * products, bytes_accessed=12 * MIB, transcendentals=n_tokens * n_codes
        ),
        name="forward",
    )(tokens, grad_out, codebook, noise)

    received = lax.all_to_all(sent, "code", 0, 0, tiled=True)
    codes, weighed, turned = pl.pallas_call(
        weigh_kernel,
        out_shape=(pltpu.HBM((tiles_in, n_tokens, wide), BF16),) * 2
        + (jax.ShapeDtypeStruct((2, dim, n_tokens), BF16),),
        in_specs=[VMEM, VMEM, ANY, ANY, VMEM],
        out_specs=(ANY, ANY, ANY),
        scratch_shapes=[
            pltpu.VMEM((tiles, width, dim), BF16),
            pltpu.VMEM((tiles, n_tokens, width), BF16),
            pltpu.VMEM((tiles_in, n_tokens, wide), BF16),
            pltpu.VMEM((tiles_in, n_tokens, wide), BF16),
            pltpu.VMEM((n_tokens, dim), BF16),
            pltpu.VMEM((n_tokens, 128), F32),
            pltpu.VMEM((n_tokens, 128), F32),
            pltpu.VMEM((2, dim, n_tokens), BF16),
            pltpu.SemaphoreType.DMA((tiles,)),
            pltpu.SemaphoreType.DMA((tiles,)),
            pltpu.SemaphoreType.DMA((2, tiles_in)),
            pltpu.SemaphoreType.DMA,
        ],
        compiler_params=FULL,
        cost_estimate=pl.CostEstimate(
            flops=2 * products, bytes_accessed=28 * MIB, transcendentals=n_tokens * n_codes
        ),
        name="weigh",
    )(tokens, grad_out, codebook, noise, sides)
    received, weighed = lax.optimization_barrier((received, weighed))
    code_at = lax.axis_index("code")
    spread = pl.pallas_call(
        merge_kernel,
        out_shape=jax.ShapeDtypeStruct((n_code, rows, 2 * dim), BF16),
        in_specs=[SMEM, VMEM],
        out_specs=VMEM,
        compiler_params=SOME,
        name="merge",
    )(code_at[None], received)
    received, spread = lax.optimization_barrier((received, spread))
    gathered = lax.all_to_all(spread, "code", 0, 0, tiled=True)
    block_tiles = block // wide
    streams = [
        pltpu.VMEM((block_tiles, 2 * n_tokens, wide), BF16),
        pltpu.VMEM((dim, 2 * n_tokens), BF16),
        pltpu.SemaphoreType.DMA((2, block_tiles)),
        pltpu.SemaphoreType.DMA((1,)),
    ]
    common = dict(
        compiler_params=MOST,
        cost_estimate=pl.CostEstimate(flops=1, bytes_accessed=1, transcendentals=0),
    )
    dp_at = lax.axis_index("dp")
    first, operands = pl.pallas_call(
        functools.partial(backward_kernel, False),
        out_shape=(
            jax.ShapeDtypeStruct((block, dim), BF16),
            jax.ShapeDtypeStruct((dim, 2 * n_tokens), BF16),
        ),
        in_specs=[SMEM, SMEM, ANY, ANY, ANY, VMEM],
        out_specs=(ANY, ANY),
        scratch_shapes=[
            pltpu.VMEM((2, dim, n_tokens), BF16),
            pltpu.VMEM((n_tokens, 128), F32),
        ] + streams + [
            pltpu.VMEM((block_tiles, wide, dim), BF16),
            pltpu.SemaphoreType.DMA((block_tiles,)),
        ],
        name="backward_first",
        **common,
    )(
        (dp_at ^ (n_dp - 1))[None], code_at[None], turned, codes, weighed, received
    )

    def backward(at):
        return pl.pallas_call(
            functools.partial(backward_kernel, True),
            out_shape=pltpu.VMEM((block, dim), BF16),
            in_specs=[SMEM, ANY, ANY, ANY],
            out_specs=VMEM,
            scratch_shapes=streams,
            name="backward",
            compiler_params=MOST,
            cost_estimate=pl.CostEstimate(
                flops=100 * products, bytes_accessed=400 * MIB, transcendentals=0
            ),
        )(at[None], codes, weighed, operands)

    blocks = [swap(first, "dp", n_dp, n_dp - 1)]
    blocks += [swap(backward(dp_at ^ d), "dp", n_dp, d) for d in range(1, n_dp - 1)]
    blocks.append(backward(dp_at))
    steps = max(block // 512, 1)
    quantized, token_gradient, own_rows = pl.pallas_call(
        functools.partial(finish_kernel, n_dp),
        out_shape=(
            jax.ShapeDtypeStruct((n_tokens, dim), F32),
            jax.ShapeDtypeStruct((n_tokens, dim), F32),
            jax.ShapeDtypeStruct((block, dim), F32),
        ),
        in_specs=[VMEM] + [ANY] * (n_dp - 1) + [VMEM],
        out_specs=(ANY, ANY, ANY),
        scratch_shapes=[
            pltpu.VMEM((n_dp - 1, steps, block // steps, dim), BF16),
            pltpu.VMEM((steps, block // steps, dim), F32),
            pltpu.VMEM((2, n_tokens, dim), F32),
            pltpu.SemaphoreType.DMA((n_dp - 1, steps)),
            pltpu.SemaphoreType.DMA((steps,)),
            pltpu.SemaphoreType.DMA((2,)),
        ],
        compiler_params=SOME,
        cost_estimate=pl.CostEstimate(
            flops=0, bytes_accessed=(2 * n_dp + 4) * block * dim, transcendentals=0
        ),
        name="finish",
    )(gathered, *blocks)
    return quantized, token_gradient, own_rows[None]


def solution(mesh):
    n_dp, n_code = mesh.shape["dp"], mesh.shape["code"]
    in_specs = (P("dp", None), P("code", None), P("dp", "code"), P("dp", None))
    out_specs = (P("dp", None), P("dp", None), P("code", "dp", None))
    return jax.shard_map(
        functools.partial(local, n_dp, n_code),
        mesh=mesh, in_specs=in_specs, out_specs=out_specs, check_vma=False,
    )
```

```python
import functools

import jax
import jax.numpy as jnp
from jax import lax
from jax.experimental import pallas as pl
from jax.experimental.pallas import tpu as pltpu
from jax.sharding import PartitionSpec as P

SOFTMAX_HEAT = 0.5
SHARPNESS = 1.0 / SOFTMAX_HEAT
BF16 = jnp.bfloat16
F32 = jnp.float32
MIB = 1 << 20
CHUNK = 256
WIDE = 512
AHEAD = 2
NEAR = 3
PACK = 16
ROWS = 64
LARGEST = 2.0**30
VMEM = pl.BlockSpec(memory_space=pltpu.VMEM)
SMEM = pl.BlockSpec(memory_space=pltpu.SMEM)
ANY = pl.BlockSpec(memory_space=pl.ANY)
FULL = pltpu.CompilerParams(vmem_limit_bytes=60 * MIB)
MOST = pltpu.CompilerParams(vmem_limit_bytes=54 * MIB)
SOME = pltpu.CompilerParams(vmem_limit_bytes=24 * MIB)


def dot(left, right, left_dim=1, right_dim=0):
    return lax.dot_general(
        left, right, (((left_dim,), (right_dim,)), ((), ())), preferred_element_type=F32
    )


def lane_groups(value):
    return [value[:, j : j + 128] for j in range(0, value.shape[1], 128)]


def stat_lanes(n_tokens):
    return max(n_tokens // PACK * 4, 128)


def high_low(value):
    high = value.astype(BF16).astype(F32)
    return high, (value - high).astype(BF16).astype(F32)


def forward_kernel(
    n_code, tokens, grad_out, codebook, noise, sent, sides,
    own, pair, book, noise_in, slot_a, slot_b, shifts, total, sums, sent_out, sides_out,
    own_sem, book_sem, noise_sem, first_sem, out_sem,
):
    tiles, width, dim = book.shape
    n_tokens = tokens.shape[0]
    columns = [slice(c, c + CHUNK) for c in range(0, width, CHUNK)]
    slots = (slot_a, slot_b)

    def fetch(t):
        at = pl.multiple_of(t * width, width)
        return (
            pltpu.make_async_copy(codebook.at[pl.ds(at, width)], book.at[t], book_sem.at[t]),
            pltpu.make_async_copy(noise.at[:, pl.ds(at, width)], noise_in.at[t], noise_sem.at[t]),
        )

    def start(t):
        for copy in fetch(t):
            copy.start()

    def arrive(t):
        for copy in fetch(t):
            copy.wait()

    own_copies = (
        pltpu.make_async_copy(tokens, own.at[0], own_sem.at[0]),
        pltpu.make_async_copy(grad_out, own.at[1], own_sem.at[1]),
    )
    halves = []
    for h in range(2):
        at = pl.ds(h * (width // 2), width // 2)
        halves.append((
            pltpu.make_async_copy(codebook.at[at], book.at[0, at], first_sem.at[h, 0]),
            pltpu.make_async_copy(noise.at[:, at], noise_in.at[0, :, at], first_sem.at[h, 1]),
        ))
    for copy in own_copies + halves[0]:
        copy.start()
    for copy in halves[1]:
        copy.start()

    def logits(both, t, r, c):
        noise_part = (noise_in[t, r : r + ROWS, c] * BF16(SHARPNESS)).astype(F32)
        return both[2 * r : 2 * r + ROWS] + noise_part

    def raise_shift(t, some):
        for c in some:
            both = dot(pair[...], book[t, c], 1, 1)
            for r in range(0, n_tokens, ROWS):
                at = slice(r, r + ROWS)
                shifts[at] = functools.reduce(
                    jnp.maximum, lane_groups(logits(both, t, r, c)), shifts[at]
                )

    def soften(t, s, fresh, last=None):
        if fresh is not None:
            @pl.when(fresh)
            def _():
                arrive(t)

                @pl.when(t + AHEAD < tiles)
                def _():
                    start(t + AHEAD)

        slot = slots[s]
        ahead = dot(pair[...], book[t, columns[0]], 1, 1)
        for k, c in enumerate(columns):
            both = ahead
            if k + 1 < len(columns):
                ahead = dot(pair[...], book[t, columns[k + 1]], 1, 1)
            elif last is not None:
                last()
            for r in range(0, n_tokens, ROWS):
                at = slice(r, r + ROWS)
                shift = jnp.concatenate([shifts[at]] * (CHUNK // 128), axis=1)
                weight = jnp.exp(logits(both, t, r, c) - shift)
                total[at] += sum(lane_groups(weight))
                slot[at, c] = weight.astype(BF16)
                gradient = both[2 * r + ROWS : 2 * r + 2 * ROWS]
                slot[n_tokens + r : n_tokens + r + ROWS, c] = (weight * gradient).astype(BF16)

    def accumulate(t, s):
        sums[...] += dot(slots[s][...], book[t])

    def attempt(state):
        again, _ = state
        fresh = again == 0
        shifts[...] = jnp.full(shifts.shape, -jnp.inf, F32)

        @pl.when(fresh)
        def _():
            for r in range(0, n_tokens, ROWS):
                some = noise_in[0, r : r + ROWS, columns[0]] * BF16(SHARPNESS)
                shifts[r : r + ROWS] = functools.reduce(
                    jnp.maximum, lane_groups(some.astype(F32))
                )

        @pl.when(jnp.logical_not(fresh))
        def _():
            def over(t, carry):
                raise_shift(t, columns)
                return carry

            lax.fori_loop(0, tiles, over, 0)

        shift = jnp.max(shifts[...], axis=1, keepdims=True).astype(BF16).astype(F32)
        shifts[...] = jnp.broadcast_to(shift, shifts.shape)
        total[...] = jnp.zeros(total.shape, F32)
        sums[...] = jnp.zeros(sums.shape, F32)

        @pl.when(fresh)
        def _():
            for copy in halves[1]:
                copy.wait()

        soften(0, 0, None)

        def soften_pair(i, carry):
            soften(2 * i + 1, 1, fresh, lambda: accumulate(2 * i, 0))
            soften(2 * i + 2, 0, fresh, lambda: accumulate(2 * i + 1, 1))
            return carry

        lax.fori_loop(0, tiles // 2 - 1, soften_pair, 0)
        soften(tiles - 1, 1, fresh, lambda: accumulate(tiles - 2, 0))
        accumulate(tiles - 1, 1)
        row_total = jnp.sum(total[...], axis=1, keepdims=True)
        total[...] = jnp.broadcast_to(row_total, total.shape)
        fits = jnp.logical_and(jnp.max(total[...]) < LARGEST, jnp.min(total[...]) > 1 / LARGEST)
        return again + 1, jnp.logical_and(fresh, jnp.logical_not(fits))

    for copy in own_copies:
        copy.wait()
    for r in range(0, n_tokens, ROWS):
        pair[2 * r : 2 * r + ROWS] = own[0, r : r + ROWS] * BF16(SHARPNESS)
        pair[2 * r + ROWS : 2 * r + 2 * ROWS] = own[1, r : r + ROWS]
    for copy in halves[0]:
        copy.wait()
    for t in range(1, min(AHEAD + 1, tiles)):
        start(t)
    lax.while_loop(lambda state: state[1], attempt, (jnp.int32(0), jnp.bool_(True)))

    shift = shifts[:, :1]
    mix = sums[:n_tokens]
    pulled = sums[n_tokens:]
    own_total = total[:, :1]
    own_inner = jnp.sum(own[1].astype(F32) * mix, axis=1, keepdims=True)
    mean = own_inner / own_total
    side = lax.broadcasted_iota(jnp.int32, sides_out.shape, 1)
    sides_out[...] = jnp.where(side < 64, mean, shift)
    copies = [pltpu.make_async_copy(sides_out, sides, out_sem.at[0])]
    copies[0].start()
    rows = n_tokens // n_code
    lanes = stat_lanes(n_tokens)
    lane = lax.broadcasted_iota(jnp.int32, (PACK, lanes), 1)
    stats = jnp.zeros((PACK, lanes), F32)
    parts = (own_total,) + high_low(mean) + (shift,)
    for q in range(n_tokens // PACK):
        for i, part in enumerate(parts):
            stats = jnp.where(lane == 4 * q + i, part[q * PACK : (q + 1) * PACK], stats)
    stats = [stats[:, j : j + 128].astype(BF16) for j in range(0, lanes, 128)]
    group = n_code // min(n_code, 4)
    for g in range(n_code):
        at = slice(g * rows, (g + 1) * rows)
        data = lane_groups(mix[at]) + lane_groups(pulled[at] - mean[at] * mix[at])
        for j, value in enumerate(data):
            sent_out[g, j * rows : (j + 1) * rows] = value.astype(BF16)
        for j, value in enumerate(stats):
            first = len(data) * rows + j * PACK
            sent_out[g, first : first + PACK] = value
        if (g + 1) % group == 0:
            part = pl.ds(g + 1 - group, group)
            copies.append(
                pltpu.make_async_copy(sent_out.at[part], sent.at[part], out_sem.at[len(copies)])
            )
            copies[-1].start()
    for copy in copies:
        copy.wait()


def roll_left(value, by):
    return pltpu.roll(value, value.shape[1] - by, 1)


def stats_of(received, p, n_tokens):
    first = received.shape[1] - stat_lanes(n_tokens) // 128 * PACK
    blocks = [received[p, r : r + PACK] for r in range(first, received.shape[1], PACK)]
    return jnp.concatenate(blocks, axis=1).astype(F32)


def factor_of(stats, top):
    return roll_left(jnp.exp(stats - top), 3)


def mean_of(stats):
    return roll_left(stats, 1) + roll_left(stats, 2)


def merged_stats(received, n_tokens):
    stats = [stats_of(received, p, n_tokens) for p in range(received.shape[0])]
    top = functools.reduce(jnp.maximum, stats)
    factors = [factor_of(s, top) * s for s in stats]
    means = [mean_of(s) for s in stats]
    total = sum(factors)
    inner = sum(f * m for f, m in zip(factors, means)) / total
    scales = [factor_of(s, top) / total for s in stats]
    return scales, means, top, total, inner


def merge_kernel(me, received, spread, factors, columns):
    n_code, rows, both = spread.shape
    dim = both // 2
    n_tokens = n_code * rows
    scales, means, top, total, inner = merged_stats(received, n_tokens)
    own = stats_of(received, me[0], n_tokens)
    own_scale = factor_of(own, top) / total
    own_offset = own_scale * (mean_of(own) - inner)
    left = lax.broadcasted_iota(jnp.int32, (PACK, 128), 1) < 64
    for q in range(n_tokens // PACK):
        at = slice(4 * q, 4 * q + 1)
        columns[q * PACK : (q + 1) * PACK] = jnp.where(left, own_scale[:, at], own_offset[:, at])
    turned = columns[...].T
    factors[:8] = turned[:8]
    factors[8:] = turned[64:72]
    lane = lax.broadcasted_iota(jnp.int32, inner.shape, 1)
    groups = rows // PACK
    mine = [lane == 4 * (me[0] * groups + h) for h in range(groups)]

    def column(value):
        columns = [jnp.sum(jnp.where(m, value, 0.0), axis=1, keepdims=True) for m in mine]
        return jnp.concatenate(columns, axis=0)

    count = dim // 128
    quantized = [jnp.zeros((rows, 128), F32)] * count
    gradient = [jnp.zeros((rows, 128), F32)] * count
    for p in range(n_code):
        scale = column(scales[p])
        offset = column(scales[p] * (means[p] - inner))
        for j in range(count):
            mix = received[p, j * rows : (j + 1) * rows].astype(F32)
            pulled = received[p, (count + j) * rows : (count + j + 1) * rows].astype(F32)
            quantized[j] += scale * mix
            gradient[j] += scale * pulled + offset * mix
    for j in range(count):
        results = (quantized[j].astype(BF16), (gradient[j] / SOFTMAX_HEAT).astype(BF16))
        for p in range(n_code):
            for i, result in enumerate(results):
                spread[p, :, i * dim + j * 128 : i * dim + (j + 1) * 128] = result


def weigh_kernel(
    tokens, grad_out, codebook, noise, sides, codes, weighed, turned,
    book, noise_in, code_out, weighed_out, sharp, means, shifts, turned_out,
    book_sem, noise_sem, out_sem, turned_sem,
):
    tiles, width, _ = book.shape
    wide = codes.shape[2]
    steps = [(t, slice(c, c + wide)) for t in range(tiles) for c in range(0, width, wide)]

    def fetch(t):
        at = pl.ds(t * width, width)
        return (
            pltpu.make_async_copy(codebook.at[at], book.at[t], book_sem.at[t]),
            pltpu.make_async_copy(noise.at[:, at], noise_in.at[t], noise_sem.at[t]),
        )

    def start(t):
        for copy in fetch(t):
            copy.start()

    def send(k):
        return (
            pltpu.make_async_copy(code_out.at[k], codes.at[k], out_sem.at[0, k]),
            pltpu.make_async_copy(weighed_out.at[k], weighed.at[k], out_sem.at[1, k]),
        )

    def products_of(step):
        t, c = step
        if c.start == 0:
            for copy in fetch(t):
                copy.wait()
            if t + NEAR < tiles:
                start(t + NEAR)
        keys = book[t, c]
        return dot(sharp[...], keys, 1, 1), dot(grad_out[...], keys, 1, 1)

    for t in range(min(NEAR, tiles)):
        start(t)
    sharp[...] = tokens[...] * BF16(SHARPNESS)
    means[...] = jnp.broadcast_to(sides[:, :1], means.shape)
    shifts[...] = jnp.broadcast_to(sides[:, 64:65], shifts.shape)
    turned_out[0] = grad_out[...].T
    turned_out[1] = sharp[...].T
    turned_copy = pltpu.make_async_copy(turned_out, turned, turned_sem)
    turned_copy.start()
    ahead = products_of(steps[0])
    for k, (t, c) in enumerate(steps):
        score, gradient = ahead
        if k + 1 < len(steps):
            ahead = products_of(steps[k + 1])
        shift = jnp.concatenate([shifts[...]] * (wide // 128), axis=1)
        mean = jnp.concatenate([means[...]] * (wide // 128), axis=1)
        noise_part = (noise_in[t, :, c] * BF16(SHARPNESS)).astype(F32)
        code = jnp.exp(score + noise_part - shift).astype(BF16)
        code_out[k] = code
        weighed_out[k] = (code.astype(F32) * (gradient - mean)).astype(BF16)
        for copy in send(k):
            copy.start()
    for k in range(len(steps)):
        for copy in send(k):
            copy.wait()
    turned_copy.wait()


def backward_kernel(prepared, block, *rest):
    if prepared:
        codes, weighed, given, out, *rest = rest
    else:
        turned, codes, weighed, factors, out, kept, own, *rest = rest
    both_in, operands, in_sem, own_sem, *rest = rest
    tiles, _, width = both_in.shape
    if not prepared:
        result, out_sem = rest
    n_tokens = both_in.shape[1] // 2

    def fetch(t):
        return [
            pltpu.make_async_copy(
                source.at[block[0] * tiles + t],
                both_in.at[t, pl.ds(half * n_tokens, n_tokens)],
                in_sem.at[half, t],
            )
            for half, source in enumerate((codes, weighed))
        ]

    def start(t):
        for copy in fetch(t):
            copy.start()

    start(0)
    if prepared:
        own_copies = [pltpu.make_async_copy(given, operands, own_sem.at[0])]
    else:
        own_copies = [pltpu.make_async_copy(turned, own, own_sem.at[0])]
    for copy in own_copies:
        copy.start()
    for t in range(1, min(NEAR, tiles)):
        start(t)

    if prepared:
        own_copies[0].wait()
    else:
        scale, offset = factors[:1], factors[8:9]
        own_copies[0].wait()
        grad, token = own[0].astype(F32), own[1].astype(F32)
        operands[:, :n_tokens] = (scale * grad + offset * token).astype(BF16)
        operands[:, n_tokens:] = (scale * token).astype(BF16)
        keep = pltpu.make_async_copy(operands, kept, own_sem.at[0])
        keep.start()

    def send(t):
        return pltpu.make_async_copy(
            result.at[t], out.at[pl.ds(t * width, width)], out_sem.at[t]
        )

    wide = min(WIDE, width)
    steps = [(t, slice(c, c + wide)) for t in range(tiles) for c in range(0, width, wide)]

    def product(step):
        t, c = step
        if c.start == 0:
            for copy in fetch(t):
                copy.wait()
            if t + NEAR < tiles:
                start(t + NEAR)
        return dot(operands[...], both_in[t, :, c])

    ahead = product(steps[0])
    for k, (t, c) in enumerate(steps):
        value = ahead
        if k + 1 < len(steps):
            ahead = product(steps[k + 1])
        if prepared:
            out[t * width + c.start : t * width + c.stop] = value.astype(BF16).T
        else:
            result[t, c] = value.astype(BF16).T
            if c.stop == width:
                send(t).start()
    if not prepared:
        keep.wait()
        for t in range(tiles):
            send(t).wait()


def add_kernel(n_parts, *refs):
    parts, own, out = refs[: n_parts - 1], refs[n_parts - 1], refs[n_parts]
    held, result, in_sem, out_sem = refs[n_parts + 1 :]
    steps, rows, _ = result.shape

    def fetch(i):
        at = pl.ds(i * rows, rows)
        return [
            pltpu.make_async_copy(part.at[at], held.at[j, i], in_sem.at[j, i])
            for j, part in enumerate(parts)
        ]

    def send(i):
        return pltpu.make_async_copy(result.at[i], out.at[pl.ds(i * rows, rows)], out_sem.at[i])

    for i in range(steps):
        for copy in fetch(i):
            copy.start()
    for i in range(steps):
        for copy in fetch(i):
            copy.wait()
        mine = own[i * rows : (i + 1) * rows].astype(F32)
        result[i] = sum((held[j, i].astype(F32) for j in range(len(parts))), mine)
        send(i).start()
    for i in range(steps):
        send(i).wait()


def unpack_kernel(gathered, quantized, gradient):
    n_code, rows, both = gathered.shape
    dim = both // 2
    for g in range(n_code):
        at = slice(g * rows, (g + 1) * rows)
        quantized[at] = gathered[g, :, :dim].astype(F32)
        gradient[at] = gathered[g, :, dim:].astype(F32)


def swap(value, axis, size, mask):
    return lax.ppermute(value, axis, [(i, i ^ mask) for i in range(size)])


def local(n_dp, n_code, tokens, codebook, noise, grad_out):
    n_tokens, dim = tokens.shape
    n_codes = codebook.shape[0]
    rows = n_tokens // n_code
    block = n_codes // n_dp
    width = min(1024, block)
    wide = min(WIDE, width)
    tiles_in = n_codes // wide
    tiles = n_codes // width
    piece = rows * (2 * dim // 128) + stat_lanes(n_tokens) // 128 * PACK
    products = 2 * n_tokens * n_codes * dim

    sent, sides = pl.pallas_call(
        functools.partial(forward_kernel, n_code),
        out_shape=(
            jax.ShapeDtypeStruct((n_code, piece, 128), BF16),
            jax.ShapeDtypeStruct((n_tokens, 128), F32),
        ),
        in_specs=[ANY, ANY, ANY, ANY],
        out_specs=(ANY, ANY),
        scratch_shapes=[
            pltpu.VMEM((2, n_tokens, dim), BF16),
            pltpu.VMEM((2 * n_tokens, dim), BF16),
            pltpu.VMEM((tiles, width, dim), BF16),
            pltpu.VMEM((tiles, n_tokens, width), BF16),
            pltpu.VMEM((2 * n_tokens, width), BF16),
            pltpu.VMEM((2 * n_tokens, width), BF16),
            pltpu.VMEM((n_tokens, 128), F32),
            pltpu.VMEM((n_tokens, 128), F32),
            pltpu.VMEM((2 * n_tokens, dim), F32),
            pltpu.VMEM((n_code, piece, 128), BF16),
            pltpu.VMEM((n_tokens, 128), F32),
            pltpu.SemaphoreType.DMA((2,)),
            pltpu.SemaphoreType.DMA((tiles,)),
            pltpu.SemaphoreType.DMA((tiles,)),
            pltpu.SemaphoreType.DMA((2, 2)),
            pltpu.SemaphoreType.DMA((1 + min(n_code, 4),)),
        ],
        compiler_params=FULL,
        cost_estimate=pl.CostEstimate(
            flops=4 * products, bytes_accessed=12 * MIB, transcendentals=n_tokens * n_codes
        ),
        name="forward",
    )(tokens, grad_out, codebook, noise)

    received = lax.all_to_all(sent, "code", 0, 0, tiled=True)
    codes, weighed, turned = pl.pallas_call(
        weigh_kernel,
        out_shape=(pltpu.HBM((tiles_in, n_tokens, wide), BF16),) * 2
        + (jax.ShapeDtypeStruct((2, dim, n_tokens), BF16),),
        in_specs=[VMEM, VMEM, ANY, ANY, VMEM],
        out_specs=(ANY, ANY, ANY),
        scratch_shapes=[
            pltpu.VMEM((tiles, width, dim), BF16),
            pltpu.VMEM((tiles, n_tokens, width), BF16),
            pltpu.VMEM((tiles_in, n_tokens, wide), BF16),
            pltpu.VMEM((tiles_in, n_tokens, wide), BF16),
            pltpu.VMEM((n_tokens, dim), BF16),
            pltpu.VMEM((n_tokens, 128), F32),
            pltpu.VMEM((n_tokens, 128), F32),
            pltpu.VMEM((2, dim, n_tokens), BF16),
            pltpu.SemaphoreType.DMA((tiles,)),
            pltpu.SemaphoreType.DMA((tiles,)),
            pltpu.SemaphoreType.DMA((2, tiles_in)),
            pltpu.SemaphoreType.DMA,
        ],
        compiler_params=FULL,
        cost_estimate=pl.CostEstimate(
            flops=2 * products, bytes_accessed=28 * MIB, transcendentals=n_tokens * n_codes
        ),
        name="weigh",
    )(tokens, grad_out, codebook, noise, sides)
    received, weighed = lax.optimization_barrier((received, weighed))
    code_at = lax.axis_index("code")
    spread, factors = pl.pallas_call(
        merge_kernel,
        out_shape=(
            jax.ShapeDtypeStruct((n_code, rows, 2 * dim), BF16),
            jax.ShapeDtypeStruct((16, n_tokens), F32),
        ),
        in_specs=[SMEM, VMEM],
        out_specs=(VMEM, VMEM),
        scratch_shapes=[pltpu.VMEM((n_tokens, 128), F32)],
        compiler_params=SOME,
        name="merge",
    )(code_at[None], received)
    spread, factors = lax.optimization_barrier((spread, factors))
    gathered = lax.all_to_all(spread, "code", 0, 0, tiled=True)
    block_tiles = block // wide
    streams = [
        pltpu.VMEM((block_tiles, 2 * n_tokens, wide), BF16),
        pltpu.VMEM((dim, 2 * n_tokens), BF16),
        pltpu.SemaphoreType.DMA((2, block_tiles)),
        pltpu.SemaphoreType.DMA((1,)),
    ]
    common = dict(
        compiler_params=MOST,
        cost_estimate=pl.CostEstimate(flops=1, bytes_accessed=1, transcendentals=0),
    )
    dp_at = lax.axis_index("dp")
    first, operands = pl.pallas_call(
        functools.partial(backward_kernel, False),
        out_shape=(
            jax.ShapeDtypeStruct((block, dim), BF16),
            jax.ShapeDtypeStruct((dim, 2 * n_tokens), BF16),
        ),
        in_specs=[SMEM, ANY, ANY, ANY, VMEM],
        out_specs=(ANY, ANY),
        scratch_shapes=[
            pltpu.VMEM((2, dim, n_tokens), BF16),
        ] + streams + [
            pltpu.VMEM((block_tiles, wide, dim), BF16),
            pltpu.SemaphoreType.DMA((block_tiles,)),
        ],
        name="backward_first",
        **common,
    )((dp_at ^ (n_dp - 1))[None], turned, codes, weighed, factors)

    def backward(at):
        return pl.pallas_call(
            functools.partial(backward_kernel, True),
            out_shape=pltpu.VMEM((block, dim), BF16),
            in_specs=[SMEM, ANY, ANY, ANY],
            out_specs=VMEM,
            scratch_shapes=streams,
            name="backward",
            compiler_params=MOST,
            cost_estimate=pl.CostEstimate(
                flops=100 * products, bytes_accessed=400 * MIB, transcendentals=0
            ),
        )(at[None], codes, weighed, operands)

    blocks = [swap(first, "dp", n_dp, n_dp - 1)]
    blocks += [swap(backward(dp_at ^ d), "dp", n_dp, d) for d in range(1, n_dp - 1)]
    blocks.append(backward(dp_at))
    steps = max(block // 512, 1)
    own_rows = pl.pallas_call(
        functools.partial(add_kernel, n_dp),
        out_shape=jax.ShapeDtypeStruct((block, dim), F32),
        in_specs=[ANY] * (n_dp - 1) + [VMEM],
        out_specs=ANY,
        scratch_shapes=[
            pltpu.VMEM((n_dp - 1, steps, block // steps, dim), BF16),
            pltpu.VMEM((steps, block // steps, dim), F32),
            pltpu.SemaphoreType.DMA((n_dp - 1, steps)),
            pltpu.SemaphoreType.DMA((steps,)),
        ],
        compiler_params=SOME,
        cost_estimate=pl.CostEstimate(
            flops=0, bytes_accessed=(2 * n_dp + 4) * block * dim, transcendentals=0
        ),
        name="add",
    )(*blocks)
    gathered, own_rows = lax.optimization_barrier((gathered, own_rows))
    quantized, token_gradient = pl.pallas_call(
        unpack_kernel,
        out_shape=(jax.ShapeDtypeStruct((n_tokens, dim), F32),) * 2,
        in_specs=[VMEM],
        out_specs=(VMEM, VMEM),
        compiler_params=SOME,
        cost_estimate=pl.CostEstimate(
            flops=0, bytes_accessed=12 * n_tokens * dim, transcendentals=0
        ),
        name="unpack",
    )(gathered)
    return quantized, token_gradient, own_rows[None]


def solution(mesh):
    n_dp, n_code = mesh.shape["dp"], mesh.shape["code"]
    in_specs = (P("dp", None), P("code", None), P("dp", "code"), P("dp", None))
    out_specs = (P("dp", None), P("dp", None), P("code", "dp", None))
    return jax.shard_map(
        functools.partial(local, n_dp, n_code),
        mesh=mesh, in_specs=in_specs, out_specs=out_specs, check_vma=False,
    )
```

```python
import functools

import jax
import jax.numpy as jnp
from jax import lax
from jax.experimental import pallas as pl
from jax.experimental.pallas import tpu as pltpu
from jax.sharding import PartitionSpec as P

SOFTMAX_HEAT = 0.5
SHARPNESS = 1.0 / SOFTMAX_HEAT
BF16 = jnp.bfloat16
F32 = jnp.float32
MIB = 1 << 20
CHUNK = 256
WIDE = 512
AHEAD = 2
NEAR = 3
PACK = 16
ROWS = 64
LARGEST = 2.0**30
VMEM = pl.BlockSpec(memory_space=pltpu.VMEM)
SMEM = pl.BlockSpec(memory_space=pltpu.SMEM)
ANY = pl.BlockSpec(memory_space=pl.ANY)
FULL = pltpu.CompilerParams(vmem_limit_bytes=60 * MIB)
MOST = pltpu.CompilerParams(vmem_limit_bytes=54 * MIB)
SOME = pltpu.CompilerParams(vmem_limit_bytes=24 * MIB)


def dot(left, right, left_dim=1, right_dim=0):
    return lax.dot_general(
        left, right, (((left_dim,), (right_dim,)), ((), ())), preferred_element_type=F32
    )


def lane_groups(value):
    return [value[:, j : j + 128] for j in range(0, value.shape[1], 128)]


def stat_lanes(n_tokens):
    return max(n_tokens // PACK * 4, 128)


def high_low(value):
    high = value.astype(BF16).astype(F32)
    return high, (value - high).astype(BF16).astype(F32)


def forward_kernel(
    n_code, tokens, grad_out, codebook, noise, sent, sides,
    own, pair, book, noise_in, slot_a, slot_b, shifts, total, sums, sent_out, sides_out,
    own_sem, book_sem, noise_sem, first_sem, out_sem,
):
    tiles, width, dim = book.shape
    n_tokens = tokens.shape[0]
    columns = [slice(c, c + CHUNK) for c in range(0, width, CHUNK)]
    slots = (slot_a, slot_b)

    def fetch(t):
        at = pl.multiple_of(t * width, width)
        return (
            pltpu.make_async_copy(codebook.at[pl.ds(at, width)], book.at[t], book_sem.at[t]),
            pltpu.make_async_copy(noise.at[:, pl.ds(at, width)], noise_in.at[t], noise_sem.at[t]),
        )

    def start(t):
        for copy in fetch(t):
            copy.start()

    def arrive(t):
        for copy in fetch(t):
            copy.wait()

    own_copies = (
        pltpu.make_async_copy(tokens, own.at[0], own_sem.at[0]),
        pltpu.make_async_copy(grad_out, own.at[1], own_sem.at[1]),
    )
    halves = []
    for h in range(2):
        at = pl.ds(h * (width // 2), width // 2)
        halves.append((
            pltpu.make_async_copy(codebook.at[at], book.at[0, at], first_sem.at[h, 0]),
            pltpu.make_async_copy(noise.at[:, at], noise_in.at[0, :, at], first_sem.at[h, 1]),
        ))
    for copy in own_copies + halves[0]:
        copy.start()
    for copy in halves[1]:
        copy.start()

    def logits(both, t, r, c):
        noise_part = (noise_in[t, r : r + ROWS, c] * BF16(SHARPNESS)).astype(F32)
        return both[2 * r : 2 * r + ROWS] + noise_part

    def raise_shift(t, some):
        for c in some:
            both = dot(pair[...], book[t, c], 1, 1)
            for r in range(0, n_tokens, ROWS):
                at = slice(r, r + ROWS)
                shifts[at] = functools.reduce(
                    jnp.maximum, lane_groups(logits(both, t, r, c)), shifts[at]
                )

    def soften(t, s, fresh, last=None):
        if fresh is not None:
            @pl.when(fresh)
            def _():
                arrive(t)

                @pl.when(t + AHEAD < tiles)
                def _():
                    start(t + AHEAD)

        slot = slots[s]
        ahead = dot(pair[...], book[t, columns[0]], 1, 1)
        for k, c in enumerate(columns):
            both = ahead
            if k + 1 < len(columns):
                ahead = dot(pair[...], book[t, columns[k + 1]], 1, 1)
            elif last is not None:
                last()
            for r in range(0, n_tokens, ROWS):
                at = slice(r, r + ROWS)
                shift = jnp.concatenate([shifts[at]] * (CHUNK // 128), axis=1)
                weight = jnp.exp(logits(both, t, r, c) - shift)
                total[at] += sum(lane_groups(weight))
                slot[at, c] = weight.astype(BF16)
                gradient = both[2 * r + ROWS : 2 * r + 2 * ROWS]
                slot[n_tokens + r : n_tokens + r + ROWS, c] = (weight * gradient).astype(BF16)

    def accumulate(t, s):
        sums[...] += dot(slots[s][...], book[t])

    def attempt(state):
        again, _ = state
        fresh = again == 0
        shifts[...] = jnp.full(shifts.shape, -jnp.inf, F32)

        @pl.when(fresh)
        def _():
            for r in range(0, n_tokens, ROWS):
                some = noise_in[0, r : r + ROWS, columns[0]] * BF16(SHARPNESS)
                shifts[r : r + ROWS] = functools.reduce(
                    jnp.maximum, lane_groups(some.astype(F32))
                )

        @pl.when(jnp.logical_not(fresh))
        def _():
            def over(t, carry):
                raise_shift(t, columns)
                return carry

            lax.fori_loop(0, tiles, over, 0)

        shift = jnp.max(shifts[...], axis=1, keepdims=True).astype(BF16).astype(F32)
        shifts[...] = jnp.broadcast_to(shift, shifts.shape)
        total[...] = jnp.zeros(total.shape, F32)
        sums[...] = jnp.zeros(sums.shape, F32)

        @pl.when(fresh)
        def _():
            for copy in halves[1]:
                copy.wait()

        soften(0, 0, None)

        def soften_pair(i, carry):
            soften(2 * i + 1, 1, fresh, lambda: accumulate(2 * i, 0))
            soften(2 * i + 2, 0, fresh, lambda: accumulate(2 * i + 1, 1))
            return carry

        lax.fori_loop(0, tiles // 2 - 1, soften_pair, 0)
        soften(tiles - 1, 1, fresh, lambda: accumulate(tiles - 2, 0))
        accumulate(tiles - 1, 1)
        row_total = jnp.sum(total[...], axis=1, keepdims=True)
        total[...] = jnp.broadcast_to(row_total, total.shape)
        fits = jnp.logical_and(jnp.max(total[...]) < LARGEST, jnp.min(total[...]) > 1 / LARGEST)
        return again + 1, jnp.logical_and(fresh, jnp.logical_not(fits))

    for copy in own_copies:
        copy.wait()
    for r in range(0, n_tokens, ROWS):
        pair[2 * r : 2 * r + ROWS] = own[0, r : r + ROWS] * BF16(SHARPNESS)
        pair[2 * r + ROWS : 2 * r + 2 * ROWS] = own[1, r : r + ROWS]
    for copy in halves[0]:
        copy.wait()
    for t in range(1, min(AHEAD + 1, tiles)):
        start(t)
    lax.while_loop(lambda state: state[1], attempt, (jnp.int32(0), jnp.bool_(True)))

    shift = shifts[:, :1]
    mix = sums[:n_tokens]
    pulled = sums[n_tokens:]
    own_total = total[:, :1]
    own_inner = jnp.sum(own[1].astype(F32) * mix, axis=1, keepdims=True)
    mean = own_inner / own_total
    side = lax.broadcasted_iota(jnp.int32, sides_out.shape, 1)
    sides_out[...] = jnp.where(side < 64, mean, shift)
    copies = [pltpu.make_async_copy(sides_out, sides, out_sem.at[0])]
    copies[0].start()
    rows = n_tokens // n_code
    lanes = stat_lanes(n_tokens)
    lane = lax.broadcasted_iota(jnp.int32, (PACK, lanes), 1)
    stats = jnp.zeros((PACK, lanes), F32)
    parts = (own_total,) + high_low(mean) + (shift,)
    for q in range(n_tokens // PACK):
        for i, part in enumerate(parts):
            stats = jnp.where(lane == 4 * q + i, part[q * PACK : (q + 1) * PACK], stats)
    stats = [stats[:, j : j + 128].astype(BF16) for j in range(0, lanes, 128)]
    group = n_code // min(n_code, 4)
    for g in range(n_code):
        at = slice(g * rows, (g + 1) * rows)
        data = lane_groups(mix[at]) + lane_groups(pulled[at] - mean[at] * mix[at])
        for j, value in enumerate(data):
            sent_out[g, j * rows : (j + 1) * rows] = value.astype(BF16)
        for j, value in enumerate(stats):
            first = len(data) * rows + j * PACK
            sent_out[g, first : first + PACK] = value
        if (g + 1) % group == 0:
            part = pl.ds(g + 1 - group, group)
            copies.append(
                pltpu.make_async_copy(sent_out.at[part], sent.at[part], out_sem.at[len(copies)])
            )
            copies[-1].start()
    for copy in copies:
        copy.wait()


def roll_left(value, by):
    return pltpu.roll(value, value.shape[1] - by, 1)


def stats_of(received, p, n_tokens):
    first = received.shape[1] - stat_lanes(n_tokens) // 128 * PACK
    blocks = [received[p, r : r + PACK] for r in range(first, received.shape[1], PACK)]
    return jnp.concatenate(blocks, axis=1).astype(F32)


def factor_of(stats, top):
    return roll_left(jnp.exp(stats - top), 3)


def mean_of(stats):
    return roll_left(stats, 1) + roll_left(stats, 2)


def merged_stats(received, n_tokens):
    stats = [stats_of(received, p, n_tokens) for p in range(received.shape[0])]
    top = functools.reduce(jnp.maximum, stats)
    factors = [factor_of(s, top) * s for s in stats]
    means = [mean_of(s) for s in stats]
    total = sum(factors)
    inner = sum(f * m for f, m in zip(factors, means)) / total
    scales = [factor_of(s, top) / total for s in stats]
    return scales, means, top, total, inner


def merge_kernel(me, received, spread, factors, columns, factors_out, factors_sem):
    n_code, rows, both = spread.shape
    dim = both // 2
    n_tokens = n_code * rows
    scales, means, top, total, inner = merged_stats(received, n_tokens)
    own = stats_of(received, me[0], n_tokens)
    own_scale = factor_of(own, top) / total
    own_offset = own_scale * (mean_of(own) - inner)
    left = lax.broadcasted_iota(jnp.int32, (PACK, 128), 1) < 64
    for q in range(n_tokens // PACK):
        at = slice(4 * q, 4 * q + 1)
        columns[q * PACK : (q + 1) * PACK] = jnp.where(left, own_scale[:, at], own_offset[:, at])
    turned = columns[...].T
    factors_out[:8] = turned[:8]
    factors_out[8:] = turned[64:72]
    factors_copy = pltpu.make_async_copy(factors_out, factors, factors_sem)
    factors_copy.start()
    lane = lax.broadcasted_iota(jnp.int32, inner.shape, 1)
    groups = rows // PACK
    mine = [lane == 4 * (me[0] * groups + h) for h in range(groups)]

    def column(value):
        columns = [jnp.sum(jnp.where(m, value, 0.0), axis=1, keepdims=True) for m in mine]
        return jnp.concatenate(columns, axis=0)

    count = dim // 128
    quantized = [jnp.zeros((rows, 128), F32)] * count
    gradient = [jnp.zeros((rows, 128), F32)] * count
    for p in range(n_code):
        scale = column(scales[p])
        offset = column(scales[p] * (means[p] - inner))
        for j in range(count):
            mix = received[p, j * rows : (j + 1) * rows].astype(F32)
            pulled = received[p, (count + j) * rows : (count + j + 1) * rows].astype(F32)
            quantized[j] += scale * mix
            gradient[j] += scale * pulled + offset * mix
    for j in range(count):
        results = (quantized[j].astype(BF16), (gradient[j] / SOFTMAX_HEAT).astype(BF16))
        for p in range(n_code):
            for i, result in enumerate(results):
                spread[p, :, i * dim + j * 128 : i * dim + (j + 1) * 128] = result
    factors_copy.wait()


def weigh_kernel(
    tokens, grad_out, codebook, noise, sides, codes, weighed, turned,
    book, noise_in, code_out, weighed_out, sharp, means, shifts, turned_out,
    book_sem, noise_sem, out_sem, turned_sem,
):
    tiles, width, _ = book.shape
    wide = codes.shape[2]
    steps = [(t, slice(c, c + wide)) for t in range(tiles) for c in range(0, width, wide)]

    def fetch(t):
        at = pl.ds(t * width, width)
        return (
            pltpu.make_async_copy(codebook.at[at], book.at[t], book_sem.at[t]),
            pltpu.make_async_copy(noise.at[:, at], noise_in.at[t], noise_sem.at[t]),
        )

    def start(t):
        for copy in fetch(t):
            copy.start()

    def send(k):
        return (
            pltpu.make_async_copy(code_out.at[k], codes.at[k], out_sem.at[0, k]),
            pltpu.make_async_copy(weighed_out.at[k], weighed.at[k], out_sem.at[1, k]),
        )

    def products_of(step):
        t, c = step
        if c.start == 0:
            for copy in fetch(t):
                copy.wait()
            if t + NEAR < tiles:
                start(t + NEAR)
        keys = book[t, c]
        return dot(sharp[...], keys, 1, 1), dot(grad_out[...], keys, 1, 1)

    for t in range(min(NEAR, tiles)):
        start(t)
    sharp[...] = tokens[...] * BF16(SHARPNESS)
    means[...] = jnp.broadcast_to(sides[:, :1], means.shape)
    shifts[...] = jnp.broadcast_to(sides[:, 64:65], shifts.shape)
    turned_out[0] = grad_out[...].T
    turned_out[1] = sharp[...].T
    turned_copy = pltpu.make_async_copy(turned_out, turned, turned_sem)
    turned_copy.start()
    ahead = products_of(steps[0])
    for k, (t, c) in enumerate(steps):
        score, gradient = ahead
        if k + 1 < len(steps):
            ahead = products_of(steps[k + 1])
        shift = jnp.concatenate([shifts[...]] * (wide // 128), axis=1)
        mean = jnp.concatenate([means[...]] * (wide // 128), axis=1)
        noise_part = (noise_in[t, :, c] * BF16(SHARPNESS)).astype(F32)
        code = jnp.exp(score + noise_part - shift).astype(BF16)
        code_out[k] = code
        weighed_out[k] = (code.astype(F32) * (gradient - mean)).astype(BF16)
        for copy in send(k):
            copy.start()
    for k in range(len(steps)):
        for copy in send(k):
            copy.wait()
    turned_copy.wait()


def backward_kernel(prepared, block, *rest):
    if prepared:
        codes, weighed, given, out, *rest = rest
    else:
        turned, codes, weighed, given, out, kept, own, factors, *rest = rest
    both_in, operands, in_sem, own_sem, *rest = rest
    tiles, _, width = both_in.shape
    if not prepared:
        result, out_sem = rest
    n_tokens = both_in.shape[1] // 2

    def fetch(t):
        return [
            pltpu.make_async_copy(
                source.at[block[0] * tiles + t],
                both_in.at[t, pl.ds(half * n_tokens, n_tokens)],
                in_sem.at[half, t],
            )
            for half, source in enumerate((codes, weighed))
        ]

    def start(t):
        for copy in fetch(t):
            copy.start()

    start(0)
    if prepared:
        own_copies = [pltpu.make_async_copy(given, operands, own_sem.at[0])]
    else:
        own_copies = [
            pltpu.make_async_copy(turned, own, own_sem.at[0]),
            pltpu.make_async_copy(given, factors, own_sem.at[1]),
        ]
    for copy in own_copies:
        copy.start()
    for t in range(1, min(NEAR, tiles)):
        start(t)

    if prepared:
        own_copies[0].wait()
    else:
        for copy in own_copies:
            copy.wait()
        scale, offset = factors[:1], factors[8:9]
        grad, token = own[0].astype(F32), own[1].astype(F32)
        operands[:, :n_tokens] = (scale * grad + offset * token).astype(BF16)
        operands[:, n_tokens:] = (scale * token).astype(BF16)
        keep = pltpu.make_async_copy(operands, kept, own_sem.at[0])
        keep.start()

    def send(t):
        return pltpu.make_async_copy(
            result.at[t], out.at[pl.ds(t * width, width)], out_sem.at[t]
        )

    wide = min(WIDE, width)
    steps = [(t, slice(c, c + wide)) for t in range(tiles) for c in range(0, width, wide)]

    def product(step):
        t, c = step
        if c.start == 0:
            for copy in fetch(t):
                copy.wait()
            if t + NEAR < tiles:
                start(t + NEAR)
        return dot(operands[...], both_in[t, :, c])

    ahead = product(steps[0])
    for k, (t, c) in enumerate(steps):
        value = ahead
        if k + 1 < len(steps):
            ahead = product(steps[k + 1])
        if prepared:
            out[t * width + c.start : t * width + c.stop] = value.astype(BF16).T
        else:
            result[t, c] = value.astype(BF16).T
            if c.stop == width:
                send(t).start()
    if not prepared:
        keep.wait()
        for t in range(tiles):
            send(t).wait()


def add_kernel(n_parts, *refs):
    parts, own, out = refs[: n_parts - 1], refs[n_parts - 1], refs[n_parts]
    held, result, in_sem, out_sem = refs[n_parts + 1 :]
    steps, rows, _ = result.shape

    def fetch(i):
        at = pl.ds(i * rows, rows)
        return [
            pltpu.make_async_copy(part.at[at], held.at[j, i], in_sem.at[j, i])
            for j, part in enumerate(parts)
        ]

    def send(i):
        return pltpu.make_async_copy(result.at[i], out.at[pl.ds(i * rows, rows)], out_sem.at[i])

    for i in range(steps):
        for copy in fetch(i):
            copy.start()
    for i in range(steps):
        for copy in fetch(i):
            copy.wait()
        mine = own[i * rows : (i + 1) * rows].astype(F32)
        result[i] = sum((held[j, i].astype(F32) for j in range(len(parts))), mine)
        send(i).start()
    for i in range(steps):
        send(i).wait()


def unpack_kernel(gathered, _, quantized, gradient):
    n_code, rows, both = gathered.shape
    dim = both // 2
    for g in range(n_code):
        at = slice(g * rows, (g + 1) * rows)
        quantized[at] = gathered[g, :, :dim].astype(F32)
        gradient[at] = gathered[g, :, dim:].astype(F32)


def swap(value, axis, size, mask):
    return lax.ppermute(value, axis, [(i, i ^ mask) for i in range(size)])


def local(n_dp, n_code, tokens, codebook, noise, grad_out):
    n_tokens, dim = tokens.shape
    n_codes = codebook.shape[0]
    rows = n_tokens // n_code
    block = n_codes // n_dp
    width = min(1024, block)
    wide = min(WIDE, width)
    tiles_in = n_codes // wide
    tiles = n_codes // width
    piece = rows * (2 * dim // 128) + stat_lanes(n_tokens) // 128 * PACK
    products = 2 * n_tokens * n_codes * dim

    sent, sides = pl.pallas_call(
        functools.partial(forward_kernel, n_code),
        out_shape=(
            jax.ShapeDtypeStruct((n_code, piece, 128), BF16),
            jax.ShapeDtypeStruct((n_tokens, 128), F32),
        ),
        in_specs=[ANY, ANY, ANY, ANY],
        out_specs=(ANY, ANY),
        scratch_shapes=[
            pltpu.VMEM((2, n_tokens, dim), BF16),
            pltpu.VMEM((2 * n_tokens, dim), BF16),
            pltpu.VMEM((tiles, width, dim), BF16),
            pltpu.VMEM((tiles, n_tokens, width), BF16),
            pltpu.VMEM((2 * n_tokens, width), BF16),
            pltpu.VMEM((2 * n_tokens, width), BF16),
            pltpu.VMEM((n_tokens, 128), F32),
            pltpu.VMEM((n_tokens, 128), F32),
            pltpu.VMEM((2 * n_tokens, dim), F32),
            pltpu.VMEM((n_code, piece, 128), BF16),
            pltpu.VMEM((n_tokens, 128), F32),
            pltpu.SemaphoreType.DMA((2,)),
            pltpu.SemaphoreType.DMA((tiles,)),
            pltpu.SemaphoreType.DMA((tiles,)),
            pltpu.SemaphoreType.DMA((2, 2)),
            pltpu.SemaphoreType.DMA((1 + min(n_code, 4),)),
        ],
        compiler_params=FULL,
        cost_estimate=pl.CostEstimate(
            flops=4 * products, bytes_accessed=12 * MIB, transcendentals=n_tokens * n_codes
        ),
        name="forward",
    )(tokens, grad_out, codebook, noise)

    received = lax.all_to_all(sent, "code", 0, 0, tiled=True)
    codes, weighed, turned = pl.pallas_call(
        weigh_kernel,
        out_shape=(pltpu.HBM((tiles_in, n_tokens, wide), BF16),) * 2
        + (jax.ShapeDtypeStruct((2, dim, n_tokens), BF16),),
        in_specs=[VMEM, VMEM, ANY, ANY, VMEM],
        out_specs=(ANY, ANY, ANY),
        scratch_shapes=[
            pltpu.VMEM((tiles, width, dim), BF16),
            pltpu.VMEM((tiles, n_tokens, width), BF16),
            pltpu.VMEM((tiles_in, n_tokens, wide), BF16),
            pltpu.VMEM((tiles_in, n_tokens, wide), BF16),
            pltpu.VMEM((n_tokens, dim), BF16),
            pltpu.VMEM((n_tokens, 128), F32),
            pltpu.VMEM((n_tokens, 128), F32),
            pltpu.VMEM((2, dim, n_tokens), BF16),
            pltpu.SemaphoreType.DMA((tiles,)),
            pltpu.SemaphoreType.DMA((tiles,)),
            pltpu.SemaphoreType.DMA((2, tiles_in)),
            pltpu.SemaphoreType.DMA,
        ],
        compiler_params=FULL,
        cost_estimate=pl.CostEstimate(
            flops=2 * products, bytes_accessed=28 * MIB, transcendentals=n_tokens * n_codes
        ),
        name="weigh",
    )(tokens, grad_out, codebook, noise, sides)
    received, weighed = lax.optimization_barrier((received, weighed))
    code_at = lax.axis_index("code")
    spread, factors = pl.pallas_call(
        merge_kernel,
        out_shape=(
            jax.ShapeDtypeStruct((n_code, rows, 2 * dim), BF16),
            pltpu.HBM((16, n_tokens), F32),
        ),
        in_specs=[SMEM, VMEM],
        out_specs=(VMEM, ANY),
        scratch_shapes=[
            pltpu.VMEM((n_tokens, 128), F32),
            pltpu.VMEM((16, n_tokens), F32),
            pltpu.SemaphoreType.DMA,
        ],
        compiler_params=SOME,
        name="merge",
    )(code_at[None], received)
    spread, factors = lax.optimization_barrier((spread, factors))
    gathered = lax.all_to_all(spread, "code", 0, 0, tiled=True)
    block_tiles = block // wide
    streams = [
        pltpu.VMEM((block_tiles, 2 * n_tokens, wide), BF16),
        pltpu.VMEM((dim, 2 * n_tokens), BF16),
        pltpu.SemaphoreType.DMA((2, block_tiles)),
        pltpu.SemaphoreType.DMA((2,)),
    ]
    common = dict(
        compiler_params=MOST,
        cost_estimate=pl.CostEstimate(flops=1, bytes_accessed=1, transcendentals=0),
    )
    dp_at = lax.axis_index("dp")
    first, operands = pl.pallas_call(
        functools.partial(backward_kernel, False),
        out_shape=(
            jax.ShapeDtypeStruct((block, dim), BF16),
            jax.ShapeDtypeStruct((dim, 2 * n_tokens), BF16),
        ),
        in_specs=[SMEM, ANY, ANY, ANY, ANY],
        out_specs=(ANY, ANY),
        scratch_shapes=[
            pltpu.VMEM((2, dim, n_tokens), BF16),
            pltpu.VMEM((16, n_tokens), F32),
        ] + streams + [
            pltpu.VMEM((block_tiles, wide, dim), BF16),
            pltpu.SemaphoreType.DMA((block_tiles,)),
        ],
        name="backward_first",
        **common,
    )((dp_at ^ (n_dp - 1))[None], turned, codes, weighed, factors)

    def backward(at):
        return pl.pallas_call(
            functools.partial(backward_kernel, True),
            out_shape=pltpu.VMEM((block, dim), BF16),
            in_specs=[SMEM, ANY, ANY, ANY],
            out_specs=VMEM,
            scratch_shapes=streams,
            name="backward",
            compiler_params=MOST,
            cost_estimate=pl.CostEstimate(
                flops=100 * products, bytes_accessed=400 * MIB, transcendentals=0
            ),
        )(at[None], codes, weighed, operands)

    blocks = [swap(first, "dp", n_dp, n_dp - 1)]
    blocks += [swap(backward(dp_at ^ d), "dp", n_dp, d) for d in range(1, n_dp - 1)]
    blocks.append(backward(dp_at))
    steps = max(block // 512, 1)
    own_rows = pl.pallas_call(
        functools.partial(add_kernel, n_dp),
        out_shape=jax.ShapeDtypeStruct((block, dim), F32),
        in_specs=[ANY] * (n_dp - 1) + [VMEM],
        out_specs=ANY,
        scratch_shapes=[
            pltpu.VMEM((n_dp - 1, steps, block // steps, dim), BF16),
            pltpu.VMEM((steps, block // steps, dim), F32),
            pltpu.SemaphoreType.DMA((n_dp - 1, steps)),
            pltpu.SemaphoreType.DMA((steps,)),
        ],
        compiler_params=SOME,
        cost_estimate=pl.CostEstimate(
            flops=0, bytes_accessed=(2 * n_dp + 4) * block * dim, transcendentals=0
        ),
        name="add",
    )(*blocks)
    quantized, token_gradient = pl.pallas_call(
        unpack_kernel,
        out_shape=(jax.ShapeDtypeStruct((n_tokens, dim), F32),) * 2,
        in_specs=[VMEM, ANY],
        out_specs=(VMEM, VMEM),
        compiler_params=SOME,
        cost_estimate=pl.CostEstimate(
            flops=0, bytes_accessed=12 * n_tokens * dim, transcendentals=0
        ),
        name="unpack",
    )(gathered, own_rows)
    return quantized, token_gradient, own_rows[None]


def solution(mesh):
    n_dp, n_code = mesh.shape["dp"], mesh.shape["code"]
    in_specs = (P("dp", None), P("code", None), P("dp", "code"), P("dp", None))
    out_specs = (P("dp", None), P("dp", None), P("code", "dp", None))
    return jax.shard_map(
        functools.partial(local, n_dp, n_code),
        mesh=mesh, in_specs=in_specs, out_specs=out_specs, check_vma=False,
    )
```

```python
import functools

import jax
import jax.numpy as jnp
from jax import lax
from jax.experimental import pallas as pl
from jax.experimental.pallas import tpu as pltpu
from jax.sharding import PartitionSpec as P

SOFTMAX_HEAT = 0.5
SHARPNESS = 1.0 / SOFTMAX_HEAT
BF16 = jnp.bfloat16
F32 = jnp.float32
MIB = 1 << 20
CHUNK = 256
WIDE = 512
AHEAD = 2
NEAR = 3
PACK = 16
ROWS = 64
LARGEST = 2.0**30
VMEM = pl.BlockSpec(memory_space=pltpu.VMEM)
SMEM = pl.BlockSpec(memory_space=pltpu.SMEM)
ANY = pl.BlockSpec(memory_space=pl.ANY)
FULL = pltpu.CompilerParams(vmem_limit_bytes=60 * MIB)
MOST = pltpu.CompilerParams(vmem_limit_bytes=54 * MIB)
SOME = pltpu.CompilerParams(vmem_limit_bytes=24 * MIB)


def dot(left, right, left_dim=1, right_dim=0):
    return lax.dot_general(
        left, right, (((left_dim,), (right_dim,)), ((), ())), preferred_element_type=F32
    )


def lane_groups(value):
    return [value[:, j : j + 128] for j in range(0, value.shape[1], 128)]


def stat_lanes(n_tokens):
    return max(n_tokens // PACK * 4, 128)


def high_low(value):
    high = value.astype(BF16).astype(F32)
    return high, (value - high).astype(BF16).astype(F32)


def forward_kernel(
    n_code, tokens, grad_out, codebook, noise, sent, sides,
    own, pair, book, noise_in, slot_a, slot_b, shifts, total, sums, sent_out, sides_out,
    own_sem, book_sem, noise_sem, first_sem, out_sem,
):
    tiles, width, dim = book.shape
    n_tokens = tokens.shape[0]
    columns = [slice(c, c + CHUNK) for c in range(0, width, CHUNK)]
    slots = (slot_a, slot_b)

    def fetch(t):
        at = pl.multiple_of(t * width, width)
        return (
            pltpu.make_async_copy(codebook.at[pl.ds(at, width)], book.at[t], book_sem.at[t]),
            pltpu.make_async_copy(noise.at[:, pl.ds(at, width)], noise_in.at[t], noise_sem.at[t]),
        )

    def start(t):
        for copy in fetch(t):
            copy.start()

    def arrive(t):
        for copy in fetch(t):
            copy.wait()

    own_copies = (
        pltpu.make_async_copy(tokens, own.at[0], own_sem.at[0]),
        pltpu.make_async_copy(grad_out, own.at[1], own_sem.at[1]),
    )
    halves = []
    for h in range(2):
        at = pl.ds(h * (width // 2), width // 2)
        halves.append((
            pltpu.make_async_copy(codebook.at[at], book.at[0, at], first_sem.at[h, 0]),
            pltpu.make_async_copy(noise.at[:, at], noise_in.at[0, :, at], first_sem.at[h, 1]),
        ))
    for copy in own_copies + halves[0]:
        copy.start()
    for copy in halves[1]:
        copy.start()

    def logits(both, t, r, c):
        noise_part = (noise_in[t, r : r + ROWS, c] * BF16(SHARPNESS)).astype(F32)
        return both[2 * r : 2 * r + ROWS] + noise_part

    def raise_shift(t, some):
        for c in some:
            both = dot(pair[...], book[t, c], 1, 1)
            for r in range(0, n_tokens, ROWS):
                at = slice(r, r + ROWS)
                shifts[at] = functools.reduce(
                    jnp.maximum, lane_groups(logits(both, t, r, c)), shifts[at]
                )

    def soften(t, s, fresh, last=None):
        if fresh is not None:
            @pl.when(fresh)
            def _():
                arrive(t)

                @pl.when(t + AHEAD < tiles)
                def _():
                    start(t + AHEAD)

        slot = slots[s]
        ahead = dot(pair[...], book[t, columns[0]], 1, 1)
        for k, c in enumerate(columns):
            both = ahead
            if k + 1 < len(columns):
                ahead = dot(pair[...], book[t, columns[k + 1]], 1, 1)
            elif last is not None:
                last()
            for r in range(0, n_tokens, ROWS):
                at = slice(r, r + ROWS)
                shift = jnp.concatenate([shifts[at]] * (CHUNK // 128), axis=1)
                weight = jnp.exp(logits(both, t, r, c) - shift)
                total[at] += sum(lane_groups(weight))
                slot[at, c] = weight.astype(BF16)
                gradient = both[2 * r + ROWS : 2 * r + 2 * ROWS]
                slot[n_tokens + r : n_tokens + r + ROWS, c] = (weight * gradient).astype(BF16)

    def accumulate(t, s):
        sums[...] += dot(slots[s][...], book[t])

    def attempt(state):
        again, _ = state
        fresh = again == 0
        shifts[...] = jnp.full(shifts.shape, -jnp.inf, F32)

        @pl.when(fresh)
        def _():
            for r in range(0, n_tokens, ROWS):
                some = noise_in[0, r : r + ROWS, columns[0]] * BF16(SHARPNESS)
                shifts[r : r + ROWS] = functools.reduce(
                    jnp.maximum, lane_groups(some.astype(F32))
                )

        @pl.when(jnp.logical_not(fresh))
        def _():
            def over(t, carry):
                raise_shift(t, columns)
                return carry

            lax.fori_loop(0, tiles, over, 0)

        shift = jnp.max(shifts[...], axis=1, keepdims=True).astype(BF16).astype(F32)
        shifts[...] = jnp.broadcast_to(shift, shifts.shape)
        total[...] = jnp.zeros(total.shape, F32)
        sums[...] = jnp.zeros(sums.shape, F32)

        @pl.when(fresh)
        def _():
            for copy in halves[1]:
                copy.wait()

        soften(0, 0, None)

        def soften_pair(i, carry):
            soften(2 * i + 1, 1, fresh, lambda: accumulate(2 * i, 0))
            soften(2 * i + 2, 0, fresh, lambda: accumulate(2 * i + 1, 1))
            return carry

        lax.fori_loop(0, tiles // 2 - 1, soften_pair, 0)
        soften(tiles - 1, 1, fresh, lambda: accumulate(tiles - 2, 0))
        accumulate(tiles - 1, 1)
        row_total = jnp.sum(total[...], axis=1, keepdims=True)
        total[...] = jnp.broadcast_to(row_total, total.shape)
        fits = jnp.logical_and(jnp.max(total[...]) < LARGEST, jnp.min(total[...]) > 1 / LARGEST)
        return again + 1, jnp.logical_and(fresh, jnp.logical_not(fits))

    for copy in own_copies:
        copy.wait()
    for r in range(0, n_tokens, ROWS):
        pair[2 * r : 2 * r + ROWS] = own[0, r : r + ROWS] * BF16(SHARPNESS)
        pair[2 * r + ROWS : 2 * r + 2 * ROWS] = own[1, r : r + ROWS]
    for copy in halves[0]:
        copy.wait()
    for t in range(1, min(AHEAD + 1, tiles)):
        start(t)
    lax.while_loop(lambda state: state[1], attempt, (jnp.int32(0), jnp.bool_(True)))

    shift = shifts[:, :1]
    mix = sums[:n_tokens]
    pulled = sums[n_tokens:]
    own_total = total[:, :1]
    own_inner = jnp.sum(own[1].astype(F32) * mix, axis=1, keepdims=True)
    mean = own_inner / own_total
    side = lax.broadcasted_iota(jnp.int32, sides_out.shape, 1)
    sides_out[...] = jnp.where(side < 64, mean, shift)
    copies = [pltpu.make_async_copy(sides_out, sides, out_sem.at[0])]
    copies[0].start()
    rows = n_tokens // n_code
    lanes = stat_lanes(n_tokens)
    lane = lax.broadcasted_iota(jnp.int32, (PACK, lanes), 1)
    stats = jnp.zeros((PACK, lanes), F32)
    parts = (own_total,) + high_low(mean) + (shift,)
    for q in range(n_tokens // PACK):
        for i, part in enumerate(parts):
            stats = jnp.where(lane == 4 * q + i, part[q * PACK : (q + 1) * PACK], stats)
    stats = [stats[:, j : j + 128].astype(BF16) for j in range(0, lanes, 128)]
    group = n_code // min(n_code, 4)
    for g in range(n_code):
        at = slice(g * rows, (g + 1) * rows)
        data = lane_groups(mix[at]) + lane_groups(pulled[at] - mean[at] * mix[at])
        for j, value in enumerate(data):
            sent_out[g, j * rows : (j + 1) * rows] = value.astype(BF16)
        for j, value in enumerate(stats):
            first = len(data) * rows + j * PACK
            sent_out[g, first : first + PACK] = value
        if (g + 1) % group == 0:
            part = pl.ds(g + 1 - group, group)
            copies.append(
                pltpu.make_async_copy(sent_out.at[part], sent.at[part], out_sem.at[len(copies)])
            )
            copies[-1].start()
    for copy in copies:
        copy.wait()


def roll_left(value, by):
    return pltpu.roll(value, value.shape[1] - by, 1)


def stats_of(received, p, n_tokens):
    first = received.shape[1] - stat_lanes(n_tokens) // 128 * PACK
    blocks = [received[p, r : r + PACK] for r in range(first, received.shape[1], PACK)]
    return jnp.concatenate(blocks, axis=1).astype(F32)


def factor_of(stats, top):
    return roll_left(jnp.exp(stats - top), 3)


def mean_of(stats):
    return roll_left(stats, 1) + roll_left(stats, 2)


def merged_stats(received, n_tokens):
    stats = [stats_of(received, p, n_tokens) for p in range(received.shape[0])]
    top = functools.reduce(jnp.maximum, stats)
    factors = [factor_of(s, top) * s for s in stats]
    means = [mean_of(s) for s in stats]
    total = sum(factors)
    inner = sum(f * m for f, m in zip(factors, means)) / total
    scales = [factor_of(s, top) / total for s in stats]
    return scales, means, top, total, inner


def merge_kernel(me, received, spread, factors, columns, factors_out, factors_sem):
    n_code, rows, both = spread.shape
    dim = both // 2
    n_tokens = n_code * rows
    scales, means, top, total, inner = merged_stats(received, n_tokens)
    own = stats_of(received, me[0], n_tokens)
    own_scale = factor_of(own, top) / total
    own_offset = own_scale * (mean_of(own) - inner)
    left = lax.broadcasted_iota(jnp.int32, (PACK, 128), 1) < 64
    for q in range(n_tokens // PACK):
        at = slice(4 * q, 4 * q + 1)
        columns[q * PACK : (q + 1) * PACK] = jnp.where(left, own_scale[:, at], own_offset[:, at])
    turned = columns[...].T
    factors_out[:8] = turned[:8]
    factors_out[8:] = turned[64:72]
    factors_copy = pltpu.make_async_copy(factors_out, factors, factors_sem)
    factors_copy.start()
    lane = lax.broadcasted_iota(jnp.int32, inner.shape, 1)
    groups = rows // PACK
    mine = [lane == 4 * (me[0] * groups + h) for h in range(groups)]

    def column(value):
        columns = [jnp.sum(jnp.where(m, value, 0.0), axis=1, keepdims=True) for m in mine]
        return jnp.concatenate(columns, axis=0)

    count = dim // 128
    quantized = [jnp.zeros((rows, 128), F32)] * count
    gradient = [jnp.zeros((rows, 128), F32)] * count
    for p in range(n_code):
        scale = column(scales[p])
        offset = column(scales[p] * (means[p] - inner))
        for j in range(count):
            mix = received[p, j * rows : (j + 1) * rows].astype(F32)
            pulled = received[p, (count + j) * rows : (count + j + 1) * rows].astype(F32)
            quantized[j] += scale * mix
            gradient[j] += scale * pulled + offset * mix
    for j in range(count):
        results = (quantized[j].astype(BF16), (gradient[j] / SOFTMAX_HEAT).astype(BF16))
        for p in range(n_code):
            for i, result in enumerate(results):
                spread[p, :, i * dim + j * 128 : i * dim + (j + 1) * 128] = result
    factors_copy.wait()


def weigh_kernel(
    tokens, grad_out, codebook, noise, sides, codes, weighed, turned,
    book, noise_in, code_out, weighed_out, sharp, means, shifts, turned_out,
    book_sem, noise_sem, out_sem, turned_sem,
):
    tiles, width, _ = book.shape
    wide = codes.shape[2]
    steps = [(t, slice(c, c + wide)) for t in range(tiles) for c in range(0, width, wide)]

    def fetch(t):
        at = pl.ds(t * width, width)
        return (
            pltpu.make_async_copy(codebook.at[at], book.at[t], book_sem.at[t]),
            pltpu.make_async_copy(noise.at[:, at], noise_in.at[t], noise_sem.at[t]),
        )

    def start(t):
        for copy in fetch(t):
            copy.start()

    def send(k):
        return (
            pltpu.make_async_copy(code_out.at[k], codes.at[k], out_sem.at[0, k]),
            pltpu.make_async_copy(weighed_out.at[k], weighed.at[k], out_sem.at[1, k]),
        )

    def products_of(step):
        t, c = step
        if c.start == 0:
            for copy in fetch(t):
                copy.wait()
            if t + NEAR < tiles:
                start(t + NEAR)
        keys = book[t, c]
        return dot(sharp[...], keys, 1, 1), dot(grad_out[...], keys, 1, 1)

    for t in range(min(NEAR, tiles)):
        start(t)
    sharp[...] = tokens[...] * BF16(SHARPNESS)
    means[...] = jnp.broadcast_to(sides[:, :1], means.shape)
    shifts[...] = jnp.broadcast_to(sides[:, 64:65], shifts.shape)
    turned_out[0] = grad_out[...].T
    turned_out[1] = sharp[...].T
    turned_copy = pltpu.make_async_copy(turned_out, turned, turned_sem)
    turned_copy.start()
    ahead = products_of(steps[0])
    for k, (t, c) in enumerate(steps):
        score, gradient = ahead
        if k + 1 < len(steps):
            ahead = products_of(steps[k + 1])
        shift = jnp.concatenate([shifts[...]] * (wide // 128), axis=1)
        mean = jnp.concatenate([means[...]] * (wide // 128), axis=1)
        noise_part = (noise_in[t, :, c] * BF16(SHARPNESS)).astype(F32)
        code = jnp.exp(score + noise_part - shift).astype(BF16)
        code_out[k] = code
        weighed_out[k] = (code.astype(F32) * (gradient - mean)).astype(BF16)
        for copy in send(k):
            copy.start()
    for k in range(len(steps)):
        for copy in send(k):
            copy.wait()
    turned_copy.wait()


def backward_kernel(prepared, block, *rest):
    if prepared:
        codes, weighed, given, out, *rest = rest
    else:
        turned, codes, weighed, given, out, kept, own, factors, *rest = rest
    both_in, operands, in_sem, own_sem, *rest = rest
    tiles, _, width = both_in.shape
    if not prepared:
        result, out_sem = rest
    n_tokens = both_in.shape[1] // 2

    def fetch(t):
        return [
            pltpu.make_async_copy(
                source.at[block[0] * tiles + t],
                both_in.at[t, pl.ds(half * n_tokens, n_tokens)],
                in_sem.at[half, t],
            )
            for half, source in enumerate((codes, weighed))
        ]

    def start(t):
        for copy in fetch(t):
            copy.start()

    start(0)
    if prepared:
        own_copies = [pltpu.make_async_copy(given, operands, own_sem.at[0])]
    else:
        own_copies = [
            pltpu.make_async_copy(turned, own, own_sem.at[0]),
            pltpu.make_async_copy(given, factors, own_sem.at[1]),
        ]
    for copy in own_copies:
        copy.start()
    for t in range(1, min(NEAR, tiles)):
        start(t)

    if prepared:
        own_copies[0].wait()
    else:
        for copy in own_copies:
            copy.wait()
        scale, offset = factors[:1], factors[8:9]
        grad, token = own[0].astype(F32), own[1].astype(F32)
        operands[:, :n_tokens] = (scale * grad + offset * token).astype(BF16)
        operands[:, n_tokens:] = (scale * token).astype(BF16)
        keep = pltpu.make_async_copy(operands, kept, own_sem.at[0])
        keep.start()

    def send(t):
        return pltpu.make_async_copy(
            result.at[t], out.at[pl.ds(t * width, width)], out_sem.at[t]
        )

    wide = min(WIDE, width)
    steps = [(t, slice(c, c + wide)) for t in range(tiles) for c in range(0, width, wide)]

    def product(step):
        t, c = step
        if c.start == 0:
            for copy in fetch(t):
                copy.wait()
            if t + NEAR < tiles:
                start(t + NEAR)
        return dot(operands[...], both_in[t, :, c])

    ahead = product(steps[0])
    for k, (t, c) in enumerate(steps):
        value = ahead
        if k + 1 < len(steps):
            ahead = product(steps[k + 1])
        if prepared:
            out[t * width + c.start : t * width + c.stop] = value.astype(BF16).T
        else:
            result[t, c] = value.astype(BF16).T
            if c.stop == width:
                send(t).start()
    if not prepared:
        keep.wait()
        for t in range(tiles):
            send(t).wait()


def add_kernel(n_parts, *refs):
    parts, own, out, mark = refs[: n_parts - 1], refs[n_parts - 1], refs[n_parts], refs[n_parts + 1]
    held, result, in_sem, out_sem = refs[n_parts + 2 :]
    mark[...] = jnp.zeros(mark.shape, F32)
    steps, rows, _ = result.shape

    def fetch(i):
        at = pl.ds(i * rows, rows)
        return [
            pltpu.make_async_copy(part.at[at], held.at[j, i], in_sem.at[j, i])
            for j, part in enumerate(parts)
        ]

    def send(i):
        return pltpu.make_async_copy(result.at[i], out.at[pl.ds(i * rows, rows)], out_sem.at[i])

    for i in range(steps):
        for copy in fetch(i):
            copy.start()
    for i in range(steps):
        for copy in fetch(i):
            copy.wait()
        mine = own[i * rows : (i + 1) * rows].astype(F32)
        result[i] = sum((held[j, i].astype(F32) for j in range(len(parts))), mine)
        send(i).start()
    for i in range(steps):
        send(i).wait()


def unpack_kernel(gathered, _, quantized, gradient, held, both, in_sem, out_sem):
    n_code, rows, width = gathered.shape
    dim = width // 2
    steps = min(n_code, 4)
    group = n_code // steps

    def fetch(i):
        at = pl.ds(i * group, group)
        return pltpu.make_async_copy(gathered.at[at], held.at[at], in_sem.at[i])

    def send(i):
        at = pl.ds(i * group * rows, group * rows)
        return [
            pltpu.make_async_copy(both.at[k, at], target.at[at], out_sem.at[k, i])
            for k, target in enumerate((quantized, gradient))
        ]

    for i in range(steps):
        fetch(i).start()
    for i in range(steps):
        fetch(i).wait()
        for g in range(i * group, (i + 1) * group):
            at = slice(g * rows, (g + 1) * rows)
            both[0, at] = held[g, :, :dim].astype(F32)
            both[1, at] = held[g, :, dim:].astype(F32)
        for copy in send(i):
            copy.start()
    for i in range(steps):
        for copy in send(i):
            copy.wait()


def swap(value, axis, size, mask):
    return lax.ppermute(value, axis, [(i, i ^ mask) for i in range(size)])


def local(n_dp, n_code, tokens, codebook, noise, grad_out):
    n_tokens, dim = tokens.shape
    n_codes = codebook.shape[0]
    rows = n_tokens // n_code
    block = n_codes // n_dp
    width = min(1024, block)
    wide = min(WIDE, width)
    tiles_in = n_codes // wide
    tiles = n_codes // width
    piece = rows * (2 * dim // 128) + stat_lanes(n_tokens) // 128 * PACK
    products = 2 * n_tokens * n_codes * dim

    sent, sides = pl.pallas_call(
        functools.partial(forward_kernel, n_code),
        out_shape=(
            jax.ShapeDtypeStruct((n_code, piece, 128), BF16),
            jax.ShapeDtypeStruct((n_tokens, 128), F32),
        ),
        in_specs=[ANY, ANY, ANY, ANY],
        out_specs=(ANY, ANY),
        scratch_shapes=[
            pltpu.VMEM((2, n_tokens, dim), BF16),
            pltpu.VMEM((2 * n_tokens, dim), BF16),
            pltpu.VMEM((tiles, width, dim), BF16),
            pltpu.VMEM((tiles, n_tokens, width), BF16),
            pltpu.VMEM((2 * n_tokens, width), BF16),
            pltpu.VMEM((2 * n_tokens, width), BF16),
            pltpu.VMEM((n_tokens, 128), F32),
            pltpu.VMEM((n_tokens, 128), F32),
            pltpu.VMEM((2 * n_tokens, dim), F32),
            pltpu.VMEM((n_code, piece, 128), BF16),
            pltpu.VMEM((n_tokens, 128), F32),
            pltpu.SemaphoreType.DMA((2,)),
            pltpu.SemaphoreType.DMA((tiles,)),
            pltpu.SemaphoreType.DMA((tiles,)),
            pltpu.SemaphoreType.DMA((2, 2)),
            pltpu.SemaphoreType.DMA((1 + min(n_code, 4),)),
        ],
        compiler_params=FULL,
        cost_estimate=pl.CostEstimate(
            flops=4 * products, bytes_accessed=12 * MIB, transcendentals=n_tokens * n_codes
        ),
        name="forward",
    )(tokens, grad_out, codebook, noise)

    received = lax.all_to_all(sent, "code", 0, 0, tiled=True)
    codes, weighed, turned = pl.pallas_call(
        weigh_kernel,
        out_shape=(pltpu.HBM((tiles_in, n_tokens, wide), BF16),) * 2
        + (jax.ShapeDtypeStruct((2, dim, n_tokens), BF16),),
        in_specs=[VMEM, VMEM, ANY, ANY, VMEM],
        out_specs=(ANY, ANY, ANY),
        scratch_shapes=[
            pltpu.VMEM((tiles, width, dim), BF16),
            pltpu.VMEM((tiles, n_tokens, width), BF16),
            pltpu.VMEM((tiles_in, n_tokens, wide), BF16),
            pltpu.VMEM((tiles_in, n_tokens, wide), BF16),
            pltpu.VMEM((n_tokens, dim), BF16),
            pltpu.VMEM((n_tokens, 128), F32),
            pltpu.VMEM((n_tokens, 128), F32),
            pltpu.VMEM((2, dim, n_tokens), BF16),
            pltpu.SemaphoreType.DMA((tiles,)),
            pltpu.SemaphoreType.DMA((tiles,)),
            pltpu.SemaphoreType.DMA((2, tiles_in)),
            pltpu.SemaphoreType.DMA,
        ],
        compiler_params=FULL,
        cost_estimate=pl.CostEstimate(
            flops=2 * products, bytes_accessed=28 * MIB, transcendentals=n_tokens * n_codes
        ),
        name="weigh",
    )(tokens, grad_out, codebook, noise, sides)
    received, weighed = lax.optimization_barrier((received, weighed))
    code_at = lax.axis_index("code")
    spread, factors = pl.pallas_call(
        merge_kernel,
        out_shape=(
            jax.ShapeDtypeStruct((n_code, rows, 2 * dim), BF16),
            pltpu.HBM((16, n_tokens), F32),
        ),
        in_specs=[SMEM, VMEM],
        out_specs=(VMEM, ANY),
        scratch_shapes=[
            pltpu.VMEM((n_tokens, 128), F32),
            pltpu.VMEM((16, n_tokens), F32),
            pltpu.SemaphoreType.DMA,
        ],
        compiler_params=SOME,
        name="merge",
    )(code_at[None], received)
    spread, factors = lax.optimization_barrier((spread, factors))
    gathered = lax.all_to_all(spread, "code", 0, 0, tiled=True)
    block_tiles = block // wide
    streams = [
        pltpu.VMEM((block_tiles, 2 * n_tokens, wide), BF16),
        pltpu.VMEM((dim, 2 * n_tokens), BF16),
        pltpu.SemaphoreType.DMA((2, block_tiles)),
        pltpu.SemaphoreType.DMA((2,)),
    ]
    common = dict(
        compiler_params=MOST,
        cost_estimate=pl.CostEstimate(flops=1, bytes_accessed=1, transcendentals=0),
    )
    dp_at = lax.axis_index("dp")
    first, operands = pl.pallas_call(
        functools.partial(backward_kernel, False),
        out_shape=(
            jax.ShapeDtypeStruct((block, dim), BF16),
            jax.ShapeDtypeStruct((dim, 2 * n_tokens), BF16),
        ),
        in_specs=[SMEM, ANY, ANY, ANY, ANY],
        out_specs=(ANY, ANY),
        scratch_shapes=[
            pltpu.VMEM((2, dim, n_tokens), BF16),
            pltpu.VMEM((16, n_tokens), F32),
        ] + streams + [
            pltpu.VMEM((block_tiles, wide, dim), BF16),
            pltpu.SemaphoreType.DMA((block_tiles,)),
        ],
        name="backward_first",
        **common,
    )((dp_at ^ (n_dp - 1))[None], turned, codes, weighed, factors)

    def backward(at):
        return pl.pallas_call(
            functools.partial(backward_kernel, True),
            out_shape=pltpu.VMEM((block, dim), BF16),
            in_specs=[SMEM, ANY, ANY, ANY],
            out_specs=VMEM,
            scratch_shapes=streams,
            name="backward",
            compiler_params=MOST,
            cost_estimate=pl.CostEstimate(
                flops=100 * products, bytes_accessed=400 * MIB, transcendentals=0
            ),
        )(at[None], codes, weighed, operands)

    blocks = [swap(first, "dp", n_dp, n_dp - 1)]
    blocks += [swap(backward(dp_at ^ d), "dp", n_dp, d) for d in range(1, n_dp - 1)]
    blocks.append(backward(dp_at))
    steps = max(block // 512, 1)
    own_rows, mark = pl.pallas_call(
        functools.partial(add_kernel, n_dp),
        out_shape=(
            jax.ShapeDtypeStruct((block, dim), F32),
            jax.ShapeDtypeStruct((8, 128), F32),
        ),
        in_specs=[ANY] * (n_dp - 1) + [VMEM],
        out_specs=(ANY, VMEM),
        scratch_shapes=[
            pltpu.VMEM((n_dp - 1, steps, block // steps, dim), BF16),
            pltpu.VMEM((steps, block // steps, dim), F32),
            pltpu.SemaphoreType.DMA((n_dp - 1, steps)),
            pltpu.SemaphoreType.DMA((steps,)),
        ],
        compiler_params=SOME,
        cost_estimate=pl.CostEstimate(
            flops=0, bytes_accessed=(2 * n_dp + 4) * block * dim, transcendentals=0
        ),
        name="add",
    )(*blocks)
    quantized, token_gradient = pl.pallas_call(
        unpack_kernel,
        out_shape=(jax.ShapeDtypeStruct((n_tokens, dim), F32),) * 2,
        in_specs=[ANY, VMEM],
        out_specs=(ANY, ANY),
        scratch_shapes=[
            pltpu.VMEM((n_code, rows, 2 * dim), BF16),
            pltpu.VMEM((2, n_tokens, dim), F32),
            pltpu.SemaphoreType.DMA((min(n_code, 4),)),
            pltpu.SemaphoreType.DMA((2, min(n_code, 4))),
        ],
        compiler_params=SOME,
        cost_estimate=pl.CostEstimate(
            flops=0, bytes_accessed=12 * n_tokens * dim, transcendentals=0
        ),
        name="unpack",
    )(gathered, mark)
    return quantized, token_gradient, own_rows[None]


def solution(mesh):
    n_dp, n_code = mesh.shape["dp"], mesh.shape["code"]
    in_specs = (P("dp", None), P("code", None), P("dp", "code"), P("dp", None))
    out_specs = (P("dp", None), P("dp", None), P("code", "dp", None))
    return jax.shard_map(
        functools.partial(local, n_dp, n_code),
        mesh=mesh, in_specs=in_specs, out_specs=out_specs, check_vma=False,
    )
```

```python
import functools

import jax
import jax.numpy as jnp
from jax import lax
from jax.experimental import pallas as pl
from jax.experimental.pallas import tpu as pltpu
from jax.sharding import PartitionSpec as P

SOFTMAX_HEAT = 0.5
SHARPNESS = 1.0 / SOFTMAX_HEAT
BF16 = jnp.bfloat16
F32 = jnp.float32
MIB = 1 << 20
CHUNK = 256
WIDE = 512
AHEAD = 2
NEAR = 3
PACK = 16
ROWS = 64
LARGEST = 2.0**30
VMEM = pl.BlockSpec(memory_space=pltpu.VMEM)
SMEM = pl.BlockSpec(memory_space=pltpu.SMEM)
ANY = pl.BlockSpec(memory_space=pl.ANY)
FULL = pltpu.CompilerParams(vmem_limit_bytes=60 * MIB)
MOST = pltpu.CompilerParams(vmem_limit_bytes=52 * MIB)
SOME = pltpu.CompilerParams(vmem_limit_bytes=16 * MIB)


def dot(left, right, left_dim=1, right_dim=0):
    return lax.dot_general(
        left, right, (((left_dim,), (right_dim,)), ((), ())), preferred_element_type=F32
    )


def lane_groups(value):
    return [value[:, j : j + 128] for j in range(0, value.shape[1], 128)]


def stat_lanes(n_tokens):
    return max(n_tokens // PACK * 4, 128)


def high_low(value):
    high = value.astype(BF16).astype(F32)
    return high, (value - high).astype(BF16).astype(F32)


def forward_kernel(
    n_code, tokens, grad_out, codebook, noise, sent, sides,
    own, pair, book, noise_in, slot_a, slot_b, shifts, total, sums, sent_out, sides_out,
    own_sem, book_sem, noise_sem, first_sem, out_sem,
):
    tiles, width, dim = book.shape
    n_tokens = tokens.shape[0]
    columns = [slice(c, c + CHUNK) for c in range(0, width, CHUNK)]
    slots = (slot_a, slot_b)

    def fetch(t):
        at = pl.multiple_of(t * width, width)
        return (
            pltpu.make_async_copy(codebook.at[pl.ds(at, width)], book.at[t], book_sem.at[t]),
            pltpu.make_async_copy(noise.at[:, pl.ds(at, width)], noise_in.at[t], noise_sem.at[t]),
        )

    def start(t):
        for copy in fetch(t):
            copy.start()

    def arrive(t):
        for copy in fetch(t):
            copy.wait()

    own_copies = (
        pltpu.make_async_copy(tokens, own.at[0], own_sem.at[0]),
        pltpu.make_async_copy(grad_out, own.at[1], own_sem.at[1]),
    )
    halves = []
    for h in range(2):
        at = pl.ds(h * (width // 2), width // 2)
        halves.append((
            pltpu.make_async_copy(codebook.at[at], book.at[0, at], first_sem.at[h, 0]),
            pltpu.make_async_copy(noise.at[:, at], noise_in.at[0, :, at], first_sem.at[h, 1]),
        ))
    for copy in own_copies + halves[0]:
        copy.start()
    for copy in halves[1]:
        copy.start()

    def logits(both, t, r, c):
        noise_part = (noise_in[t, r : r + ROWS, c] * BF16(SHARPNESS)).astype(F32)
        return both[2 * r : 2 * r + ROWS] + noise_part

    def raise_shift(t, some):
        for c in some:
            both = dot(pair[...], book[t, c], 1, 1)
            for r in range(0, n_tokens, ROWS):
                at = slice(r, r + ROWS)
                shifts[at] = functools.reduce(
                    jnp.maximum, lane_groups(logits(both, t, r, c)), shifts[at]
                )

    def soften(t, s, fresh, last=None):
        if fresh is not None:
            @pl.when(fresh)
            def _():
                arrive(t)

                @pl.when(t + AHEAD < tiles)
                def _():
                    start(t + AHEAD)

        slot = slots[s]
        ahead = dot(pair[...], book[t, columns[0]], 1, 1)
        for k, c in enumerate(columns):
            both = ahead
            if k + 1 < len(columns):
                ahead = dot(pair[...], book[t, columns[k + 1]], 1, 1)
            elif last is not None:
                last()
            for r in range(0, n_tokens, ROWS):
                at = slice(r, r + ROWS)
                shift = jnp.concatenate([shifts[at]] * (CHUNK // 128), axis=1)
                weight = jnp.exp(logits(both, t, r, c) - shift)
                total[at] += sum(lane_groups(weight))
                slot[at, c] = weight.astype(BF16)
                gradient = both[2 * r + ROWS : 2 * r + 2 * ROWS]
                slot[n_tokens + r : n_tokens + r + ROWS, c] = (weight * gradient).astype(BF16)

    def accumulate(t, s):
        sums[...] += dot(slots[s][...], book[t])

    def attempt(state):
        again, _ = state
        fresh = again == 0
        shifts[...] = jnp.full(shifts.shape, -jnp.inf, F32)

        @pl.when(fresh)
        def _():
            for r in range(0, n_tokens, ROWS):
                some = noise_in[0, r : r + ROWS, columns[0]] * BF16(SHARPNESS)
                shifts[r : r + ROWS] = functools.reduce(
                    jnp.maximum, lane_groups(some.astype(F32))
                )

        @pl.when(jnp.logical_not(fresh))
        def _():
            def over(t, carry):
                raise_shift(t, columns)
                return carry

            lax.fori_loop(0, tiles, over, 0)

        shift = jnp.max(shifts[...], axis=1, keepdims=True).astype(BF16).astype(F32)
        shifts[...] = jnp.broadcast_to(shift, shifts.shape)
        total[...] = jnp.zeros(total.shape, F32)
        sums[...] = jnp.zeros(sums.shape, F32)

        @pl.when(fresh)
        def _():
            for copy in halves[1]:
                copy.wait()

        soften(0, 0, None)

        def soften_pair(i, carry):
            soften(2 * i + 1, 1, fresh, lambda: accumulate(2 * i, 0))
            soften(2 * i + 2, 0, fresh, lambda: accumulate(2 * i + 1, 1))
            return carry

        lax.fori_loop(0, tiles // 2 - 1, soften_pair, 0)
        soften(tiles - 1, 1, fresh, lambda: accumulate(tiles - 2, 0))
        accumulate(tiles - 1, 1)
        row_total = jnp.sum(total[...], axis=1, keepdims=True)
        total[...] = jnp.broadcast_to(row_total, total.shape)
        fits = jnp.logical_and(jnp.max(total[...]) < LARGEST, jnp.min(total[...]) > 1 / LARGEST)
        return again + 1, jnp.logical_and(fresh, jnp.logical_not(fits))

    for copy in own_copies:
        copy.wait()
    for r in range(0, n_tokens, ROWS):
        pair[2 * r : 2 * r + ROWS] = own[0, r : r + ROWS] * BF16(SHARPNESS)
        pair[2 * r + ROWS : 2 * r + 2 * ROWS] = own[1, r : r + ROWS]
    for copy in halves[0]:
        copy.wait()
    for t in range(1, min(AHEAD + 1, tiles)):
        start(t)
    lax.while_loop(lambda state: state[1], attempt, (jnp.int32(0), jnp.bool_(True)))

    shift = shifts[:, :1]
    mix = sums[:n_tokens]
    pulled = sums[n_tokens:]
    own_total = total[:, :1]
    own_inner = jnp.sum(own[1].astype(F32) * mix, axis=1, keepdims=True)
    mean = own_inner / own_total
    side = lax.broadcasted_iota(jnp.int32, sides_out.shape, 1)
    sides_out[...] = jnp.where(side < 64, mean, shift)
    copies = [pltpu.make_async_copy(sides_out, sides, out_sem.at[0])]
    copies[0].start()
    rows = n_tokens // n_code
    lanes = stat_lanes(n_tokens)
    lane = lax.broadcasted_iota(jnp.int32, (PACK, lanes), 1)
    stats = jnp.zeros((PACK, lanes), F32)
    parts = (own_total,) + high_low(mean) + (shift,)
    for q in range(n_tokens // PACK):
        for i, part in enumerate(parts):
            stats = jnp.where(lane == 4 * q + i, part[q * PACK : (q + 1) * PACK], stats)
    stats = [stats[:, j : j + 128].astype(BF16) for j in range(0, lanes, 128)]
    group = n_code // min(n_code, 4)
    for g in range(n_code):
        at = slice(g * rows, (g + 1) * rows)
        data = lane_groups(mix[at]) + lane_groups(pulled[at] - mean[at] * mix[at])
        for j, value in enumerate(data):
            sent_out[g, j * rows : (j + 1) * rows] = value.astype(BF16)
        for j, value in enumerate(stats):
            first = len(data) * rows + j * PACK
            sent_out[g, first : first + PACK] = value
        if (g + 1) % group == 0:
            part = pl.ds(g + 1 - group, group)
            copies.append(
                pltpu.make_async_copy(sent_out.at[part], sent.at[part], out_sem.at[len(copies)])
            )
            copies[-1].start()
    for copy in copies:
        copy.wait()


def roll_left(value, by):
    return pltpu.roll(value, value.shape[1] - by, 1)


def stats_of(received, p, n_tokens):
    first = received.shape[1] - stat_lanes(n_tokens) // 128 * PACK
    blocks = [received[p, r : r + PACK] for r in range(first, received.shape[1], PACK)]
    return jnp.concatenate(blocks, axis=1).astype(F32)


def factor_of(stats, top):
    return roll_left(jnp.exp(stats - top), 3)


def mean_of(stats):
    return roll_left(stats, 1) + roll_left(stats, 2)


def merged_stats(received, n_tokens):
    stats = [stats_of(received, p, n_tokens) for p in range(received.shape[0])]
    top = functools.reduce(jnp.maximum, stats)
    factors = [factor_of(s, top) * s for s in stats]
    means = [mean_of(s) for s in stats]
    total = sum(factors)
    inner = sum(f * m for f, m in zip(factors, means)) / total
    scales = [factor_of(s, top) / total for s in stats]
    return scales, means, top, total, inner


def merge_kernel(me, received, spread, factors, columns, factors_out, factors_sem):
    n_code, rows, both = spread.shape
    dim = both // 2
    n_tokens = n_code * rows
    scales, means, top, total, inner = merged_stats(received, n_tokens)
    own = stats_of(received, me[0], n_tokens)
    own_scale = factor_of(own, top) / total
    own_offset = own_scale * (mean_of(own) - inner)
    left = lax.broadcasted_iota(jnp.int32, (PACK, 128), 1) < 64
    for q in range(n_tokens // PACK):
        at = slice(4 * q, 4 * q + 1)
        columns[q * PACK : (q + 1) * PACK] = jnp.where(left, own_scale[:, at], own_offset[:, at])
    turned = columns[...].T
    factors_out[:8] = turned[:8]
    factors_out[8:] = turned[64:72]
    factors_copy = pltpu.make_async_copy(factors_out, factors, factors_sem)
    factors_copy.start()
    lane = lax.broadcasted_iota(jnp.int32, inner.shape, 1)
    groups = rows // PACK
    mine = [lane == 4 * (me[0] * groups + h) for h in range(groups)]

    def column(value):
        columns = [jnp.sum(jnp.where(m, value, 0.0), axis=1, keepdims=True) for m in mine]
        return jnp.concatenate(columns, axis=0)

    count = dim // 128
    quantized = [jnp.zeros((rows, 128), F32)] * count
    gradient = [jnp.zeros((rows, 128), F32)] * count
    for p in range(n_code):
        scale = column(scales[p])
        offset = column(scales[p] * (means[p] - inner))
        for j in range(count):
            mix = received[p, j * rows : (j + 1) * rows].astype(F32)
            pulled = received[p, (count + j) * rows : (count + j + 1) * rows].astype(F32)
            quantized[j] += scale * mix
            gradient[j] += scale * pulled + offset * mix
    for j in range(count):
        results = (quantized[j].astype(BF16), (gradient[j] / SOFTMAX_HEAT).astype(BF16))
        for p in range(n_code):
            for i, result in enumerate(results):
                spread[p, :, i * dim + j * 128 : i * dim + (j + 1) * 128] = result
    factors_copy.wait()


def weigh_kernel(
    tokens, grad_out, codebook, noise, sides, codes, weighed, turned,
    book, noise_in, code_out, weighed_out, sharp, means, shifts, turned_out,
    book_sem, noise_sem, out_sem, turned_sem,
):
    tiles, width, _ = book.shape
    wide = codes.shape[2]
    steps = [(t, slice(c, c + wide)) for t in range(tiles) for c in range(0, width, wide)]

    def fetch(t):
        at = pl.ds(t * width, width)
        return (
            pltpu.make_async_copy(codebook.at[at], book.at[t], book_sem.at[t]),
            pltpu.make_async_copy(noise.at[:, at], noise_in.at[t], noise_sem.at[t]),
        )

    def start(t):
        for copy in fetch(t):
            copy.start()

    def send(k):
        return (
            pltpu.make_async_copy(code_out.at[k], codes.at[k], out_sem.at[0, k]),
            pltpu.make_async_copy(weighed_out.at[k], weighed.at[k], out_sem.at[1, k]),
        )

    def products_of(step):
        t, c = step
        if c.start == 0:
            for copy in fetch(t):
                copy.wait()
            if t + NEAR < tiles:
                start(t + NEAR)
        keys = book[t, c]
        return dot(sharp[...], keys, 1, 1), dot(grad_out[...], keys, 1, 1)

    for t in range(min(NEAR, tiles)):
        start(t)
    sharp[...] = tokens[...] * BF16(SHARPNESS)
    means[...] = jnp.broadcast_to(sides[:, :1], means.shape)
    shifts[...] = jnp.broadcast_to(sides[:, 64:65], shifts.shape)
    turned_out[0] = grad_out[...].T
    turned_out[1] = sharp[...].T
    turned_copy = pltpu.make_async_copy(turned_out, turned, turned_sem)
    turned_copy.start()
    ahead = products_of(steps[0])
    for k, (t, c) in enumerate(steps):
        score, gradient = ahead
        if k + 1 < len(steps):
            ahead = products_of(steps[k + 1])
        shift = jnp.concatenate([shifts[...]] * (wide // 128), axis=1)
        mean = jnp.concatenate([means[...]] * (wide // 128), axis=1)
        noise_part = (noise_in[t, :, c] * BF16(SHARPNESS)).astype(F32)
        code = jnp.exp(score + noise_part - shift).astype(BF16)
        code_out[k] = code
        weighed_out[k] = (code.astype(F32) * (gradient - mean)).astype(BF16)
        for copy in send(k):
            copy.start()
    for k in range(len(steps)):
        for copy in send(k):
            copy.wait()
    turned_copy.wait()


def backward_kernel(prepared, block, *rest):
    if prepared:
        codes, weighed, given, out, *rest = rest
    else:
        turned, codes, weighed, given, out, kept, own, factors, *rest = rest
    both_in, operands, in_sem, own_sem, *rest = rest
    tiles, _, width = both_in.shape
    if not prepared:
        result, out_sem = rest
    n_tokens = both_in.shape[1] // 2

    def fetch(t):
        return [
            pltpu.make_async_copy(
                source.at[block[0] * tiles + t],
                both_in.at[t, pl.ds(half * n_tokens, n_tokens)],
                in_sem.at[half, t],
            )
            for half, source in enumerate((codes, weighed))
        ]

    def start(t):
        for copy in fetch(t):
            copy.start()

    start(0)
    if prepared:
        own_copies = [pltpu.make_async_copy(given, operands, own_sem.at[0])]
    else:
        own_copies = [
            pltpu.make_async_copy(turned, own, own_sem.at[0]),
            pltpu.make_async_copy(given, factors, own_sem.at[1]),
        ]
    for copy in own_copies:
        copy.start()
    for t in range(1, min(NEAR, tiles)):
        start(t)

    if prepared:
        own_copies[0].wait()
    else:
        for copy in own_copies:
            copy.wait()
        scale, offset = factors[:1], factors[8:9]
        grad, token = own[0].astype(F32), own[1].astype(F32)
        operands[:, :n_tokens] = (scale * grad + offset * token).astype(BF16)
        operands[:, n_tokens:] = (scale * token).astype(BF16)
        keep = pltpu.make_async_copy(operands, kept, own_sem.at[0])
        keep.start()

    def send(t):
        return pltpu.make_async_copy(
            result.at[t], out.at[pl.ds(t * width, width)], out_sem.at[t]
        )

    wide = min(WIDE, width)
    steps = [(t, slice(c, c + wide)) for t in range(tiles) for c in range(0, width, wide)]

    def product(step):
        t, c = step
        if c.start == 0:
            for copy in fetch(t):
                copy.wait()
            if t + NEAR < tiles:
                start(t + NEAR)
        return dot(operands[...], both_in[t, :, c])

    ahead = product(steps[0])
    for k, (t, c) in enumerate(steps):
        value = ahead
        if k + 1 < len(steps):
            ahead = product(steps[k + 1])
        if prepared:
            out[t * width + c.start : t * width + c.stop] = value.astype(BF16).T
        else:
            result[t, c] = value.astype(BF16).T
            if c.stop == width:
                send(t).start()
    if not prepared:
        keep.wait()
        for t in range(tiles):
            send(t).wait()


def add_kernel(n_parts, *refs):
    parts, own, out, mark = refs[: n_parts - 1], refs[n_parts - 1], refs[n_parts], refs[n_parts + 1]
    held, result, in_sem, out_sem = refs[n_parts + 2 :]
    mark[...] = jnp.zeros(mark.shape, F32)
    steps, rows, _ = result.shape

    def fetch(i):
        at = pl.ds(i * rows, rows)
        return [
            pltpu.make_async_copy(part.at[at], held.at[j, i], in_sem.at[j, i])
            for j, part in enumerate(parts)
        ]

    def send(i):
        return pltpu.make_async_copy(result.at[i], out.at[pl.ds(i * rows, rows)], out_sem.at[i])

    for i in range(steps):
        for copy in fetch(i):
            copy.start()
    for i in range(steps):
        for copy in fetch(i):
            copy.wait()
        mine = own[i * rows : (i + 1) * rows].astype(F32)
        result[i] = sum((held[j, i].astype(F32) for j in range(len(parts))), mine)
        send(i).start()
    for i in range(steps):
        send(i).wait()


def unpack_kernel(gathered, _, quantized, gradient, both, out_sem):
    n_code, rows, width = gathered.shape
    dim = width // 2
    steps = min(n_code, 4)
    group = n_code // steps

    def send(i):
        at = pl.ds(i * group * rows, group * rows)
        return [
            pltpu.make_async_copy(both.at[k, at], target.at[at], out_sem.at[k, i])
            for k, target in enumerate((quantized, gradient))
        ]

    for i in range(steps):
        for g in range(i * group, (i + 1) * group):
            at = slice(g * rows, (g + 1) * rows)
            both[0, at] = gathered[g, :, :dim].astype(F32)
            both[1, at] = gathered[g, :, dim:].astype(F32)
        for copy in send(i):
            copy.start()
    for i in range(steps):
        for copy in send(i):
            copy.wait()


def swap(value, axis, size, mask):
    return lax.ppermute(value, axis, [(i, i ^ mask) for i in range(size)])


def local(n_dp, n_code, tokens, codebook, noise, grad_out):
    n_tokens, dim = tokens.shape
    n_codes = codebook.shape[0]
    rows = n_tokens // n_code
    block = n_codes // n_dp
    width = min(1024, block)
    wide = min(WIDE, width)
    tiles_in = n_codes // wide
    tiles = n_codes // width
    piece = rows * (2 * dim // 128) + stat_lanes(n_tokens) // 128 * PACK
    products = 2 * n_tokens * n_codes * dim

    sent, sides = pl.pallas_call(
        functools.partial(forward_kernel, n_code),
        out_shape=(
            jax.ShapeDtypeStruct((n_code, piece, 128), BF16),
            jax.ShapeDtypeStruct((n_tokens, 128), F32),
        ),
        in_specs=[ANY, ANY, ANY, ANY],
        out_specs=(ANY, ANY),
        scratch_shapes=[
            pltpu.VMEM((2, n_tokens, dim), BF16),
            pltpu.VMEM((2 * n_tokens, dim), BF16),
            pltpu.VMEM((tiles, width, dim), BF16),
            pltpu.VMEM((tiles, n_tokens, width), BF16),
            pltpu.VMEM((2 * n_tokens, width), BF16),
            pltpu.VMEM((2 * n_tokens, width), BF16),
            pltpu.VMEM((n_tokens, 128), F32),
            pltpu.VMEM((n_tokens, 128), F32),
            pltpu.VMEM((2 * n_tokens, dim), F32),
            pltpu.VMEM((n_code, piece, 128), BF16),
            pltpu.VMEM((n_tokens, 128), F32),
            pltpu.SemaphoreType.DMA((2,)),
            pltpu.SemaphoreType.DMA((tiles,)),
            pltpu.SemaphoreType.DMA((tiles,)),
            pltpu.SemaphoreType.DMA((2, 2)),
            pltpu.SemaphoreType.DMA((1 + min(n_code, 4),)),
        ],
        compiler_params=FULL,
        cost_estimate=pl.CostEstimate(
            flops=4 * products, bytes_accessed=12 * MIB, transcendentals=n_tokens * n_codes
        ),
        name="forward",
    )(tokens, grad_out, codebook, noise)

    received = lax.all_to_all(sent, "code", 0, 0, tiled=True)
    codes, weighed, turned = pl.pallas_call(
        weigh_kernel,
        out_shape=(pltpu.HBM((tiles_in, n_tokens, wide), BF16),) * 2
        + (jax.ShapeDtypeStruct((2, dim, n_tokens), BF16),),
        in_specs=[VMEM, VMEM, ANY, ANY, VMEM],
        out_specs=(ANY, ANY, ANY),
        scratch_shapes=[
            pltpu.VMEM((tiles, width, dim), BF16),
            pltpu.VMEM((tiles, n_tokens, width), BF16),
            pltpu.VMEM((tiles_in, n_tokens, wide), BF16),
            pltpu.VMEM((tiles_in, n_tokens, wide), BF16),
            pltpu.VMEM((n_tokens, dim), BF16),
            pltpu.VMEM((n_tokens, 128), F32),
            pltpu.VMEM((n_tokens, 128), F32),
            pltpu.VMEM((2, dim, n_tokens), BF16),
            pltpu.SemaphoreType.DMA((tiles,)),
            pltpu.SemaphoreType.DMA((tiles,)),
            pltpu.SemaphoreType.DMA((2, tiles_in)),
            pltpu.SemaphoreType.DMA,
        ],
        compiler_params=FULL,
        cost_estimate=pl.CostEstimate(
            flops=2 * products, bytes_accessed=28 * MIB, transcendentals=n_tokens * n_codes
        ),
        name="weigh",
    )(tokens, grad_out, codebook, noise, sides)
    received, weighed = lax.optimization_barrier((received, weighed))
    code_at = lax.axis_index("code")
    spread, factors = pl.pallas_call(
        merge_kernel,
        out_shape=(
            jax.ShapeDtypeStruct((n_code, rows, 2 * dim), BF16),
            pltpu.HBM((16, n_tokens), F32),
        ),
        in_specs=[SMEM, VMEM],
        out_specs=(VMEM, ANY),
        scratch_shapes=[
            pltpu.VMEM((n_tokens, 128), F32),
            pltpu.VMEM((16, n_tokens), F32),
            pltpu.SemaphoreType.DMA,
        ],
        compiler_params=SOME,
        name="merge",
    )(code_at[None], received)
    spread, factors = lax.optimization_barrier((spread, factors))
    gathered = lax.all_to_all(spread, "code", 0, 0, tiled=True)
    block_tiles = block // wide
    streams = [
        pltpu.VMEM((block_tiles, 2 * n_tokens, wide), BF16),
        pltpu.VMEM((dim, 2 * n_tokens), BF16),
        pltpu.SemaphoreType.DMA((2, block_tiles)),
        pltpu.SemaphoreType.DMA((2,)),
    ]
    common = dict(
        compiler_params=MOST,
        cost_estimate=pl.CostEstimate(flops=1, bytes_accessed=1, transcendentals=0),
    )
    dp_at = lax.axis_index("dp")
    first, operands = pl.pallas_call(
        functools.partial(backward_kernel, False),
        out_shape=(
            jax.ShapeDtypeStruct((block, dim), BF16),
            jax.ShapeDtypeStruct((dim, 2 * n_tokens), BF16),
        ),
        in_specs=[SMEM, ANY, ANY, ANY, ANY],
        out_specs=(ANY, ANY),
        scratch_shapes=[
            pltpu.VMEM((2, dim, n_tokens), BF16),
            pltpu.VMEM((16, n_tokens), F32),
        ] + streams + [
            pltpu.VMEM((block_tiles, wide, dim), BF16),
            pltpu.SemaphoreType.DMA((block_tiles,)),
        ],
        name="backward_first",
        **common,
    )((dp_at ^ (n_dp - 1))[None], turned, codes, weighed, factors)

    def backward(at):
        return pl.pallas_call(
            functools.partial(backward_kernel, True),
            out_shape=pltpu.VMEM((block, dim), BF16),
            in_specs=[SMEM, ANY, ANY, ANY],
            out_specs=VMEM,
            scratch_shapes=streams,
            name="backward",
            compiler_params=MOST,
            cost_estimate=pl.CostEstimate(
                flops=100 * products, bytes_accessed=400 * MIB, transcendentals=0
            ),
        )(at[None], codes, weighed, operands)

    blocks = [swap(first, "dp", n_dp, n_dp - 1)]
    blocks += [swap(backward(dp_at ^ d), "dp", n_dp, d) for d in range(1, n_dp - 1)]
    blocks.append(backward(dp_at))
    steps = max(block // 512, 1)
    own_rows, mark = pl.pallas_call(
        functools.partial(add_kernel, n_dp),
        out_shape=(
            jax.ShapeDtypeStruct((block, dim), F32),
            jax.ShapeDtypeStruct((8, 128), F32),
        ),
        in_specs=[ANY] * (n_dp - 1) + [VMEM],
        out_specs=(ANY, VMEM),
        scratch_shapes=[
            pltpu.VMEM((n_dp - 1, steps, block // steps, dim), BF16),
            pltpu.VMEM((steps, block // steps, dim), F32),
            pltpu.SemaphoreType.DMA((n_dp - 1, steps)),
            pltpu.SemaphoreType.DMA((steps,)),
        ],
        compiler_params=SOME,
        cost_estimate=pl.CostEstimate(
            flops=0, bytes_accessed=(2 * n_dp + 4) * block * dim, transcendentals=0
        ),
        name="add",
    )(*blocks)
    quantized, token_gradient = pl.pallas_call(
        unpack_kernel,
        out_shape=(jax.ShapeDtypeStruct((n_tokens, dim), F32),) * 2,
        in_specs=[VMEM, VMEM],
        out_specs=(ANY, ANY),
        scratch_shapes=[
            pltpu.VMEM((2, n_tokens, dim), F32),
            pltpu.SemaphoreType.DMA((2, min(n_code, 4))),
        ],
        compiler_params=SOME,
        cost_estimate=pl.CostEstimate(
            flops=0, bytes_accessed=12 * n_tokens * dim, transcendentals=0
        ),
        name="unpack",
    )(gathered, mark)
    return quantized, token_gradient, own_rows[None]


def solution(mesh):
    n_dp, n_code = mesh.shape["dp"], mesh.shape["code"]
    in_specs = (P("dp", None), P("code", None), P("dp", "code"), P("dp", None))
    out_specs = (P("dp", None), P("dp", None), P("code", "dp", None))
    return jax.shard_map(
        functools.partial(local, n_dp, n_code),
        mesh=mesh, in_specs=in_specs, out_specs=out_specs, check_vma=False,
    )
```
